32 devices in a mesh: groups: 2 (over y), seq: 4 (over z), head: 2 (over x), sub: 2 (over core).
Axes of the slice: x: 2, y: 2, z: 4, core: 2. Of those that a mesh axis runs over, the one named last changes fastest.
Arguments:
- hidden: bfloat16 [4096, 2048], P(('groups', 'seq', 'sub')), parts along dimension 0, may hold values from -6 to 6
- w_query: bfloat16 [2048, 2048], P('sub', 'head')
- w_key: bfloat16 [2048, 2048], P('sub', 'head')
- w_value: bfloat16 [2048, 2048], P('sub', 'head'), may hold values from -0.125 to 0.125
- cluster_rank: int32 [512], P('groups'), parts along dimension 0, may hold values from 0 to 255, as said below
- assign: int32 [16, 4096], P('head', ('groups', 'seq', 'sub')), parts along dimension 1, may hold values from 0 to 255, as said below
- d_attended: bfloat16 [4096, 2048], P(('groups', 'seq', 'sub'), 'head'), parts along dimension 0, may hold values from -6 to 6
Outputs:
- attended: bfloat16 [4096, 2048], P(('groups', 'seq', 'sub'), 'head'), parts along dimension 0
- d_hidden: bfloat16 [4096, 2048], P(('groups', 'seq', 'sub'), 'head'), parts along dimension 0
- centroid_sums: float32 [16, 512, 128], P('head', ('groups', 'seq', 'sub')), parts along dimension 1
The draws below stay inside these ranges and needn't reach their ends.
There are 2 independent parts, one for each index of `groups`. The reference program is written for one: setup_inputs(seed, part) draws one part's arguments, and reference() takes and returns one part's arrays. A program takes and returns all parts, laid end to end along the dimension named above; an argument that names none is the same for every part. Nothing has to cross between parts.
Inputs may be any that keep to these rules, and one draw needn't show every extreme that they name: `cluster_rank` is `cluster_rank` is a permutation; cluster c belongs to owner cluster_rank[c] // 32, owners numbered like the shards of seq+sub. `assign`: in each head and each aligned block of 256 tokens at most 64 tokens have clusters of one owner, exactly 64 for some owners of every block; in every head one owner has exactly 64 from every block.
All inputs are finite; a program needn't handle non-finite values.
Results may differ from the reference program's by a relative error of at most 0.011.
Values may be sent and summed in bfloat16 or wider, within the bound.
No kernel may reach another device: no remote copies, remote signals or barrier semaphores. Data moves between devices by JAX's collectives and lax.ppermute only.
A program may use at most 128 MiB of HBM per device.

```python
import jax
import jax.numpy as jnp
from jax import lax

D = 2048
H = 16
DH = 128
CLUSTERS = 256
TOK_DEV = 256
OWNERS = 8
TOKENS = 2048
SEND_CAP = 64
CL_OWN = 32
HEADS_DEV = 8


def routing_tables(key):
    owner_count = TOKENS // TOK_DEV
    capacity = 2 * TOK_DEV // owner_count
    quarter = owner_count // 4
    per_owner = CLUSTERS // owner_count
    cluster_order = jax.random.permutation(jax.random.fold_in(key, 101), CLUSTERS).astype(jnp.int32)
    by_order = jnp.argsort(cluster_order, stable=True).astype(jnp.int32)
    full_owner = jax.random.randint(jax.random.fold_in(key, 102), (H,), 0, owner_count)
    positions = jnp.arange(TOK_DEV, dtype=jnp.int32)
    profile = jnp.where(positions < quarter * capacity, positions // capacity, quarter + (positions - quarter * capacity) // (capacity // 2))

    def block_clusters(head_idx, block_idx):
        block_key = jax.random.fold_in(jax.random.fold_in(key, 103), head_idx * owner_count + block_idx)
        owner_perm = jax.random.permutation(jax.random.fold_in(block_key, 1), owner_count).astype(jnp.int32)
        chosen = full_owner[head_idx].astype(jnp.int32)
        spot_index = jnp.argmax(owner_perm == chosen)
        first_owner = owner_perm[0]
        owner_perm = owner_perm.at[spot_index].set(first_owner)
        owner_perm = owner_perm.at[0].set(chosen)
        owner_ids = owner_perm[profile]
        owner_ids = owner_ids[jax.random.permutation(jax.random.fold_in(block_key, 2), TOK_DEV)]
        inner_slot = jax.random.randint(jax.random.fold_in(block_key, 3), (TOK_DEV,), 0, per_owner)
        return by_order[owner_ids * per_owner + inner_slot]

    def per_head(head_idx):
        return jax.vmap(lambda block_idx: block_clusters(head_idx, block_idx))(jnp.arange(owner_count))
    assign = jax.vmap(per_head)(jnp.arange(H)).reshape(H, TOKENS)
    return (cluster_order, assign.astype(jnp.int32))


def shared_weight(key):
    return jax.random.normal(jax.random.fold_in(key, 201), (D, H * DH), jnp.float32) * D ** (-0.5)


def draw_cluster_rank(key, part):
    tables = routing_tables(key)
    return tables[0]


def draw_assign(key, part):
    tables = routing_tables(key)
    return tables[1]


def draw_hidden(key, part):
    key = jax.random.fold_in(key, 3)
    values = jax.random.normal(jax.random.fold_in(key, 5), (TOKENS, D), jnp.float32)
    return jnp.clip(values, -6.0, 6.0).astype(jnp.bfloat16)


def draw_w_query(key, part):
    return shared_weight(key).astype(jnp.bfloat16)


def draw_w_key(key, part):
    key = jax.random.fold_in(key, 6)
    fresh = jax.random.normal(jax.random.fold_in(key, 1), (D, H * DH), jnp.float32) * D ** (-0.5)
    return fresh.astype(jnp.bfloat16)


def level_of(rng, dims, pieces, smallest, largest):
    loudness, own = 1.0, jax.random.fold_in(rng, 6)
    for position, shards_of in pieces:
        steps = jnp.exp(jax.random.uniform(jax.random.fold_in(own, position), (shards_of,), jnp.float32, smallest / len(pieces), largest / len(pieces)))
        loudness = loudness * jnp.repeat(steps, dims[position] // shards_of).reshape([-1 if axis == position else 1 for axis in range(len(dims))])
    return loudness


def scatter_about(own_key, dims, deviation, most, pieces=(), held_as=jnp.bfloat16):
    values = deviation * jax.random.normal(own_key, dims, jnp.float32)
    if pieces:
        values = values * level_of(own_key, dims, pieces, -0.22, 0.18)
    return jnp.clip(values, -most, most).astype(held_as)


def setup_inputs(seed: int = 0, part: int = 0) -> dict:
    key_list = jax.random.split(jax.random.key(seed), 8)
    part_keys = jax.random.split(jax.random.fold_in(key_list[7], part), 8)
    hidden = draw_hidden(jax.random.fold_in(jax.random.fold_in(key_list[7], part), 71), part)
    w_query = draw_w_query(jax.random.fold_in(key_list[7], 71), part)
    w_key = draw_w_key(jax.random.fold_in(key_list[7], 71), part)
    w_value = scatter_about(key_list[3], (D, H * DH), D ** -0.5, 0.125, ((0, 2), (1, 2)))
    cluster_rank = draw_cluster_rank(jax.random.fold_in(jax.random.fold_in(key_list[7], part), 71), part)
    assign = draw_assign(jax.random.fold_in(jax.random.fold_in(key_list[7], part), 71), part)
    d_attended = scatter_about(part_keys[6], (TOKENS, H * DH), 1.0, 6.0, ((0, 8), (1, 2)))
    return dict(hidden=hidden, w_query=w_query, w_key=w_key, w_value=w_value, cluster_rank=cluster_rank, assign=assign, d_attended=d_attended)


epsilon = 1e-06

def keep_mask(filled, cluster_ids, positions):
    count = filled.shape[0]
    same = filled[:, None] & filled[None, :] & (cluster_ids[:, None] == cluster_ids[None, :])
    causal = positions[None, :] <= positions[:, None]
    diagonal = jnp.arange(count)[:, None] == jnp.arange(count)[None, :]
    return same & causal | diagonal

def attend_group(queries, keys_in, values, grads_in, filled, cluster_ids, positions):
    scale = DH ** (-0.5)
    contract_last = (((1,), (1,)), ((), ()))
    contract_first = (((0,), (0,)), ((), ()))
    scores = lax.dot_general(queries, keys_in, contract_last, preferred_element_type=jnp.float32) * scale
    allowed = keep_mask(filled, cluster_ids, positions)
    row_top = lax.optimization_barrier(jnp.max(jnp.where(allowed, scores, -jnp.inf), axis=1))
    expd = jnp.where(allowed, jnp.exp(scores - row_top[:, None]), 0.0)
    row_total = lax.optimization_barrier(jnp.sum(expd, axis=1))
    probs = expd / row_total[:, None]
    probs_low = probs.astype(jnp.bfloat16)
    outputs = jnp.dot(probs_low, values, preferred_element_type=jnp.float32).astype(jnp.bfloat16)
    grad_probs = lax.dot_general(grads_in, values, contract_last, preferred_element_type=jnp.float32)
    delta_rows = lax.optimization_barrier(jnp.sum(probs * grad_probs, axis=1))
    grad_low = (probs * (grad_probs - delta_rows[:, None]) * scale).astype(jnp.bfloat16)
    grad_query = jnp.dot(grad_low, keys_in, preferred_element_type=jnp.float32).astype(jnp.bfloat16)
    grad_key = lax.dot_general(grad_low, queries, contract_first, preferred_element_type=jnp.float32).astype(jnp.bfloat16)
    grad_value = lax.dot_general(probs_low, grads_in, contract_first, preferred_element_type=jnp.float32).astype(jnp.bfloat16)
    return (outputs, grad_query, grad_key, grad_value)

def reference(hidden, w_query, w_key, w_value, cluster_rank, assign, d_attended):

    def project(weight):
        rows_out = jnp.dot(hidden, weight, preferred_element_type=jnp.float32).astype(jnp.bfloat16)
        return rows_out.reshape(TOKENS, H, DH).transpose(1, 0, 2)
    queries = project(w_query)
    keys_all = project(w_key)
    values = project(w_value)
    grads_all = d_attended.reshape(TOKENS, H, DH).transpose(1, 0, 2)
    rank_tok = cluster_rank[assign].astype(jnp.int32)
    token_ids = jnp.arange(TOKENS, dtype=jnp.int32)
    slot_count = OWNERS * SEND_CAP

    def one_head(packed):
        head_q, head_k, head_v, head_g, head_rank, head_assign = packed
        owner_ids = head_rank // CL_OWN
        owner_hot = (owner_ids[:, None] == jnp.arange(OWNERS, dtype=jnp.int32)[None, :]).astype(jnp.int32)
        within = lax.optimization_barrier(jnp.sum(owner_hot * (jnp.cumsum(owner_hot, axis=0) - 1), axis=1))
        table = jnp.full((OWNERS, slot_count), -1, jnp.int32).at[owner_ids, within].set(token_ids)

        def one_group(members):
            filled = members >= 0
            safe_ids = jnp.maximum(members, 0)

            def select_rows(source):
                return jnp.where(filled[:, None], source[safe_ids], jnp.zeros((), source.dtype))
            cluster_ids = jnp.where(filled, head_assign[safe_ids], -1)
            return attend_group(select_rows(head_q), select_rows(head_k), select_rows(head_v), select_rows(head_g), filled, cluster_ids, safe_ids)
        grouped = lax.map(one_group, table)
        return tuple((grouped_arr[owner_ids, within] for grouped_arr in grouped))
    outputs, grad_q, grad_k, grad_v = lax.map(one_head, (queries, keys_all, values, grads_all, rank_tok, assign))

    def merge_heads(per_head):
        return per_head.transpose(1, 0, 2).reshape(TOKENS, H * DH)
    attended = merge_heads(outputs)
    width_dev = HEADS_DEV * DH
    running_sum = jnp.zeros((TOKENS, D), jnp.float32)
    pairs = ((merge_heads(grad_q), w_query), (merge_heads(grad_k), w_key), (merge_heads(grad_v), w_value))
    for group_idx in range(H // HEADS_DEV):
        column_lo = group_idx * width_dev
        partial_sum = jnp.zeros((TOKENS, D), jnp.float32)
        for grad_flat, weight in pairs:
            partial_sum = partial_sum + jnp.dot(grad_flat[:, column_lo:column_lo + width_dev], weight[:, column_lo:column_lo + width_dev].T, preferred_element_type=jnp.float32)
        rounded = lax.optimization_barrier(partial_sum.astype(jnp.bfloat16))
        running_sum = running_sum + rounded.astype(jnp.float32)
    d_hidden = running_sum.astype(jnp.bfloat16)
    keys_float = keys_all.astype(jnp.float32)
    unit_keys = keys_float * lax.rsqrt(lax.optimization_barrier(jnp.sum(keys_float * keys_float, axis=2, keepdims=True)) + epsilon)
    centroid_sums = jax.vmap(lambda unit_rows, rank_row: jax.ops.segment_sum(unit_rows, rank_row, num_segments=CLUSTERS))(unit_keys, rank_tok)
    return (attended, d_hidden, centroid_sums)
```

```python
from functools import partial

import jax
import jax.numpy as jnp
from jax import lax
from jax.experimental import pallas as pl
from jax.experimental.pallas import tpu as pltpu
from jax.sharding import PartitionSpec as P

epsilon = 1e-06


def keep_mask(filled, cluster_ids, positions):
    count = filled.shape[0]
    same = filled[:, None] & filled[None, :] & (cluster_ids[:, None] == cluster_ids[None, :])
    causal = positions[None, :] <= positions[:, None]
    diagonal = jnp.arange(count)[:, None] == jnp.arange(count)[None, :]
    return same & causal | diagonal


def head_forward(packed, scale):
    queries, keys_in, values, filled, cluster_ids, positions = packed
    scores = (
        lax.dot_general(
            queries, keys_in, (((1,), (1,)), ((), ())), preferred_element_type=jnp.float32
        )
        * scale
    )
    allowed = keep_mask(filled, cluster_ids, positions)
    row_top = jnp.max(jnp.where(allowed, scores, -jnp.inf), axis=1)
    expd = jnp.where(allowed, jnp.exp(scores - row_top[:, None]), 0.0)
    row_total = jnp.sum(expd, axis=1)
    probs_low = (expd / row_total[:, None]).astype(jnp.bfloat16)
    outputs = jnp.dot(probs_low, values, preferred_element_type=jnp.float32).astype(jnp.bfloat16)
    return (outputs, row_top, row_total)


def head_backward(packed, scale):
    queries, keys_in, values, grads_in, filled, cluster_ids, positions, row_top, row_total = packed
    contract_last = (((1,), (1,)), ((), ()))
    contract_first = (((0,), (0,)), ((), ()))
    scores = (
        lax.dot_general(queries, keys_in, contract_last, preferred_element_type=jnp.float32) * scale
    )
    allowed = keep_mask(filled, cluster_ids, positions)
    probs = jnp.where(allowed, jnp.exp(scores - row_top[:, None]), 0.0) / row_total[:, None]
    probs_low = probs.astype(jnp.bfloat16)
    grad_probs = lax.dot_general(
        grads_in, values, contract_last, preferred_element_type=jnp.float32
    )
    delta_rows = jnp.sum(probs * grad_probs, axis=1)
    grad_low = (probs * (grad_probs - delta_rows[:, None]) * scale).astype(jnp.bfloat16)
    grad_query = jnp.dot(grad_low, keys_in, preferred_element_type=jnp.float32).astype(jnp.bfloat16)
    grad_key = lax.dot_general(
        grad_low, queries, contract_first, preferred_element_type=jnp.float32
    ).astype(jnp.bfloat16)
    grad_value = lax.dot_general(
        probs_low, grads_in, contract_first, preferred_element_type=jnp.float32
    ).astype(jnp.bfloat16)
    return (grad_query, grad_key, grad_value)


def by_owner(hidden, w_query, w_key, w_value, cluster_rank, assign, d_attended):
    tok_rows = hidden.shape[0]
    heads_here = assign.shape[0]
    head_dim = w_query.shape[1] // heads_here
    clusters = cluster_rank.shape[0]
    seq_count = lax.axis_size("seq")
    sub_count = lax.axis_size("sub")
    owners = seq_count * sub_count
    capacity = 2 * tok_rows // owners
    slot_count = owners * capacity
    per_owner = clusters // owners
    scale = head_dim ** (-0.5)
    pieces = (
        lax.all_gather(w_query, "sub", axis=0, tiled=True),
        lax.all_gather(w_key, "sub", axis=0, tiled=True),
        lax.all_gather(w_value, "sub", axis=0, tiled=True),
    )
    projected = tuple(
        (
            jnp.dot(hidden, weight_piece, preferred_element_type=jnp.float32)
            for weight_piece in pieces
        )
    )

    def split_heads(matrix):
        return (
            matrix.astype(jnp.bfloat16).reshape(tok_rows, heads_here, head_dim).transpose(1, 0, 2)
        )

    queries, keys_all, values = tuple((split_heads(matrix) for matrix in projected))
    cluster_range = jnp.arange(clusters, dtype=jnp.int32)
    rank_tok = jnp.sum(jnp.where(assign[:, :, None] == cluster_range, cluster_rank, 0), axis=2)
    owner_ids = rank_tok // per_owner
    owner_hot = (owner_ids[:, :, None] == jnp.arange(owners, dtype=jnp.int32)).astype(jnp.int32)
    within = jnp.sum(owner_hot * (jnp.cumsum(owner_hot, axis=1) - 1), axis=2)
    slot_tok = owner_ids * capacity + within
    token_ids = jnp.arange(tok_rows, dtype=jnp.int32)
    slot_range = jnp.arange(slot_count, dtype=jnp.int32)
    slot_match = slot_tok[:, None, :] == slot_range[None, :, None]
    slot_hot = slot_match.astype(jnp.bfloat16)

    def to_slots(rows_in):
        kept = jnp.einsum(
            "hst,htd->hsd", slot_hot, rows_in, preferred_element_type=jnp.float32
        ).astype(jnp.bfloat16)
        return kept.reshape(heads_here, owners, capacity, head_dim)

    def from_slots(slotted):
        flat_slots = slotted.reshape(heads_here, slot_count, head_dim)
        return jnp.einsum(
            "hst,hsd->htd", slot_hot, flat_slots, preferred_element_type=jnp.float32
        ).astype(jnp.bfloat16)

    def exchange_three(first, second, third):
        return (
            lax.all_to_all(first, ("seq", "sub"), split_axis=1, concat_axis=1, tiled=True),
            lax.all_to_all(second, ("seq", "sub"), split_axis=1, concat_axis=1, tiled=True),
            lax.all_to_all(third, ("seq", "sub"), split_axis=1, concat_axis=1, tiled=True),
        )

    sent = exchange_three(to_slots(queries), to_slots(keys_all), to_slots(values))
    tag_tok = assign * tok_rows + token_ids
    slot_tag = jnp.sum(jnp.where(slot_match, tag_tok[:, None, :] + 1, 0), axis=2) - 1
    tags = lax.all_to_all(
        slot_tag.reshape(heads_here, owners, capacity),
        ("seq", "sub"),
        split_axis=1,
        concat_axis=1,
        tiled=True,
    )
    tags = tags.reshape(heads_here, slot_count)
    owner_q, owner_k, owner_v = tuple(
        (member.reshape(heads_here, slot_count, head_dim) for member in sent)
    )
    filled = tags >= 0
    cluster_ids = jnp.where(filled, tags // tok_rows, -1)
    positions = slot_range // capacity * tok_rows + tags % tok_rows
    outputs, row_top, row_total = lax.map(
        partial(head_forward, scale=scale),
        (owner_q, owner_k, owner_v, filled, cluster_ids, positions),
    )
    returned = lax.all_to_all(
        outputs.reshape(heads_here, owners, capacity, head_dim),
        ("seq", "sub"),
        split_axis=1,
        concat_axis=1,
        tiled=True,
    )

    def merge_heads(slotted):
        return from_slots(slotted).transpose(1, 0, 2).reshape(tok_rows, heads_here * head_dim)

    attended = merge_heads(returned)
    grads_tok = d_attended.reshape(tok_rows, heads_here, head_dim).transpose(1, 0, 2)
    owner_g = lax.all_to_all(
        to_slots(grads_tok), ("seq", "sub"), split_axis=1, concat_axis=1, tiled=True
    ).reshape(heads_here, slot_count, head_dim)
    grad_q, grad_k, grad_v = lax.map(
        partial(head_backward, scale=scale),
        (owner_q, owner_k, owner_v, owner_g, filled, cluster_ids, positions, row_top, row_total),
    )
    shape_four = (heads_here, owners, capacity, head_dim)
    back = exchange_three(
        grad_q.reshape(shape_four), grad_k.reshape(shape_four), grad_v.reshape(shape_four)
    )
    token_grads = tuple((merge_heads(member) for member in back))
    pieces = lax.all_gather((w_query, w_key, w_value), "sub", axis=0, tiled=True)
    terms = [
        jnp.einsum("tc,rc->tr", grad_rows_in, weight_piece, preferred_element_type=jnp.float32)
        for grad_rows_in, weight_piece in zip(token_grads, pieces)
    ]
    partial_grad = terms[0] + terms[1] + terms[2]
    d_hidden = lax.psum_scatter(
        partial_grad.astype(jnp.bfloat16), "head", scatter_dimension=1, tiled=True
    )
    keys_float = keys_all.astype(jnp.float32)
    unit_keys = keys_float * lax.rsqrt(
        jnp.sum(keys_float * keys_float, axis=2, keepdims=True) + epsilon
    )
    member_hot = (rank_tok[:, :, None] == cluster_range).astype(jnp.float32)
    local_sums = jnp.einsum("htr,htd->hrd", member_hot, unit_keys, precision=lax.Precision.HIGHEST)
    centroid_sums = lax.psum_scatter(
        local_sums.astype(jnp.bfloat16), ("seq", "sub"), scatter_dimension=1, tiled=True
    ).astype(jnp.float32)
    return (attended, d_hidden, centroid_sums)


contract_last = (((1,), (1,)), ((), ()))
log2_e = 1.4426950408889634


def masked_scores(keys_in, query_rows, col_ids, row_ids, block, factor):
    seen = keys_in.shape[0]
    count = query_rows.shape[0]
    scores = (
        lax.dot_general(keys_in, query_rows, contract_last, preferred_element_type=jnp.float32)
        * factor
    )
    same = col_ids == row_ids
    key_at = lax.broadcasted_iota(jnp.int32, (count, count), 0)
    query_at = lax.broadcasted_iota(jnp.int32, (count, count), 1)
    last = same[seen - count :] & (key_at <= query_at)
    if block == 0:
        allowed = last
    else:
        allowed = jnp.concatenate([same[: seen - count], last], axis=0)
    return jnp.where(allowed, scores, -jnp.inf)


def forward_kernel(factor, packed_ref, col_ref, row_ref, out_ref, lse_ref):
    blocks, triple, head_dim = packed_ref.shape
    rows = triple // 3
    for block in range(blocks):
        seen = (block + 1) * rows
        keys_in = packed_ref[: block + 1, rows : 2 * rows, :].reshape(seen, head_dim)
        values = packed_ref[: block + 1, 2 * rows :, :].reshape(seen, head_dim)
        scores = masked_scores(
            keys_in,
            packed_ref[block, :rows, :],
            col_ref[:seen, :],
            row_ref[block : block + 1, :],
            block,
            factor,
        )
        top = jnp.max(scores, axis=0, keepdims=True)
        expd = jnp.exp2(scores - top)
        total = jnp.sum(expd, axis=0, keepdims=True)
        probs_low = (expd * (1.0 / total)).astype(jnp.bfloat16)
        flipped = lax.dot_general(
            values, probs_low, (((0,), (0,)), ((), ())), preferred_element_type=jnp.float32
        )
        out_ref[block] = flipped.T.astype(jnp.bfloat16)
        lse_ref[block : block + 1, :] = top + jnp.log2(total)


def backward_kernel(
    factor, scale, packed_ref, grads_ref, col_ref, row_ref, rank_ref, lse_ref, out_ref, dk_ref, dv_ref
):
    blocks, triple, head_dim = packed_ref.shape
    rows = triple // 3
    tokens = blocks * rows
    clusters = rank_ref.shape[1]
    owned = clusters // blocks
    dk_ref[...] = jnp.zeros_like(dk_ref)
    dv_ref[...] = jnp.zeros_like(dv_ref)
    for block in range(blocks):
        seen = (block + 1) * rows
        keys_in = packed_ref[: block + 1, rows : 2 * rows, :].reshape(seen, head_dim)
        values = packed_ref[: block + 1, 2 * rows :, :].reshape(seen, head_dim)
        query_rows = packed_ref[block, :rows, :]
        grad_rows = grads_ref[block, :rows, :]
        scores = masked_scores(
            keys_in, query_rows, col_ref[:seen, :], row_ref[block : block + 1, :], block, factor
        )
        probs = jnp.exp2(scores - lse_ref[block : block + 1, :])
        grad_probs = lax.dot_general(
            values, grad_rows, contract_last, preferred_element_type=jnp.float32
        )
        weighted = probs * grad_probs
        delta = jnp.sum(weighted, axis=0, keepdims=True)
        grad_low = (weighted - probs * delta).astype(jnp.bfloat16)
        dv_ref[:seen, :] += jnp.dot(
            probs.astype(jnp.bfloat16), grad_rows, preferred_element_type=jnp.float32
        )
        dk_ref[:seen, :] += jnp.dot(grad_low, query_rows, preferred_element_type=jnp.float32)
        flipped = lax.dot_general(
            keys_in, grad_low, (((0,), (0,)), ((), ())), preferred_element_type=jnp.float32
        )
        out_ref[block, :rows, :] = (flipped.T * scale).astype(jnp.bfloat16)
    out_ref[:, rows : 2 * rows, :] = (
        (dk_ref[...] * scale).astype(jnp.bfloat16).reshape(blocks, rows, head_dim)
    )
    out_ref[:, 2 * rows : triple, :] = (
        dv_ref[...].astype(jnp.bfloat16).reshape(blocks, rows, head_dim)
    )
    sums = jnp.zeros((clusters, head_dim), jnp.float32)
    cluster_at = lax.broadcasted_iota(jnp.int32, (clusters, rows), 0)
    for block in range(blocks):
        keys_float = packed_ref[block, rows : 2 * rows, :].astype(jnp.float32)
        unit = keys_float * lax.rsqrt(
            jnp.sum(keys_float * keys_float, axis=1, keepdims=True) + epsilon
        )
        unit_high = unit.astype(jnp.bfloat16)
        unit_low = (unit - unit_high.astype(jnp.float32)).astype(jnp.bfloat16)
        member = jnp.where(cluster_at == row_ref[block : block + 1, :], 1.0, 0.0).astype(
            jnp.bfloat16
        )
        sums += jnp.dot(member, unit_high, preferred_element_type=jnp.float32)
        sums += jnp.dot(member, unit_low, preferred_element_type=jnp.float32)
    rank_at = lax.broadcasted_iota(jnp.int32, (clusters, clusters), 0)
    ordered = jnp.where(rank_at == rank_ref[...], 1.0, 0.0).astype(jnp.bfloat16)
    ranked = jnp.dot(ordered, sums.astype(jnp.bfloat16), preferred_element_type=jnp.float32)
    out_ref[:, triple:, :] = ranked.astype(jnp.bfloat16).reshape(blocks, owned, head_dim)


def by_head(hidden, w_query, w_key, w_value, cluster_rank, assign, d_attended):
    rows = hidden.shape[0]
    blocks = assign.shape[0]
    head_dim = w_query.shape[1] // blocks
    width = w_query.shape[1]
    half = w_query.shape[0]
    tokens = blocks * rows
    clusters = cluster_rank.shape[0]
    owned = clusters // blocks
    scale = head_dim ** (-0.5)
    factor = scale * log2_e
    line = ("seq", "sub")
    vmem = pl.BlockSpec(memory_space=pltpu.VMEM)
    params = pltpu.CompilerParams(vmem_limit_bytes=48 * 1024 * 1024)
    pairs_seen = tokens * (tokens + rows) // 2

    def exchange(packed):
        return lax.all_to_all(packed, line, split_axis=0, concat_axis=0, tiled=True)

    def split_heads(matrix):
        return matrix.reshape(rows, blocks, head_dim).transpose(1, 0, 2)

    tag_rows = -(-rows // head_dim // 16) * 16
    tags = assign.astype(jnp.bfloat16).reshape(blocks, rows // head_dim, head_dim)
    tags = jnp.pad(tags, ((0, 0), (0, tag_rows - rows // head_dim), (0, 0)))
    grads = exchange(jnp.concatenate([split_heads(d_attended), tags], axis=1))
    row_ids = (
        grads[:, rows : rows + rows // head_dim, :].reshape(blocks, rows).astype(jnp.int32)
    )
    col_ids = row_ids.reshape(tokens, 1)

    swap = [(0, 1), (1, 0)]
    side = lax.axis_index("sub")
    near = lax.dynamic_slice_in_dim(hidden, side * half, half, axis=1)
    far = lax.dynamic_slice_in_dim(hidden, (1 - side) * half, half, axis=1)
    own = (w_query, w_key, w_value)
    other = tuple(lax.ppermute(piece, "sub", swap) for piece in own)
    projected = [
        split_heads(
            (
                jnp.dot(near, mine, preferred_element_type=jnp.float32)
                + jnp.dot(far, theirs, preferred_element_type=jnp.float32)
            ).astype(jnp.bfloat16)
        )
        for mine, theirs in zip(own, other)
    ]
    packed = exchange(jnp.concatenate(projected, axis=1))

    outputs, lse = pl.pallas_call(
        partial(forward_kernel, factor),
        out_shape=(
            jax.ShapeDtypeStruct((blocks, rows, head_dim), jnp.bfloat16),
            jax.ShapeDtypeStruct((blocks, rows), jnp.float32),
        ),
        in_specs=[vmem] * 3,
        out_specs=(vmem, vmem),
        compiler_params=params,
        cost_estimate=pl.CostEstimate(
            flops=4 * pairs_seen * head_dim,
            bytes_accessed=8 * tokens * head_dim,
            transcendentals=pairs_seen,
        ),
    )(packed, col_ids, row_ids)
    returned = exchange(outputs)
    attended = returned.transpose(1, 0, 2).reshape(rows, width)

    grads_out = pl.pallas_call(
        partial(backward_kernel, factor, scale),
        out_shape=jax.ShapeDtypeStruct((blocks, 3 * rows + owned, head_dim), jnp.bfloat16),
        in_specs=[vmem] * 6,
        out_specs=vmem,
        scratch_shapes=[
            pltpu.VMEM((tokens, head_dim), jnp.float32),
            pltpu.VMEM((tokens, head_dim), jnp.float32),
        ],
        compiler_params=params,
        cost_estimate=pl.CostEstimate(
            flops=10 * pairs_seen * head_dim,
            bytes_accessed=14 * tokens * head_dim,
            transcendentals=pairs_seen,
        ),
    )(packed, grads, col_ids, row_ids, cluster_rank.reshape(1, clusters), lse)
    back = exchange(grads_out)
    centroid_sums = back[:, 3 * rows :, :].astype(jnp.float32)
    token_grads = [
        back[:, index * rows : (index + 1) * rows, :].transpose(1, 0, 2).reshape(rows, width)
        for index in range(3)
    ]

    def input_part(pieces):
        terms = [
            jnp.einsum("tc,rc->tr", grad_rows, piece, preferred_element_type=jnp.float32)
            for grad_rows, piece in zip(token_grads, pieces)
        ]
        return terms[0] + terms[1] + terms[2]

    straight = side == lax.axis_index("head")
    part_own, part_other = input_part(own), input_part(other)
    sent = jnp.where(straight, part_other, part_own).astype(jnp.bfloat16)
    kept = jnp.where(straight, part_own, part_other)
    arrived = lax.ppermute(sent, "head", swap)
    d_hidden = (kept + arrived.astype(jnp.float32)).astype(jnp.bfloat16)
    return (attended, d_hidden, centroid_sums)


def per_device(hidden, w_query, w_key, w_value, cluster_rank, assign, d_attended):
    owners = lax.axis_size("seq") * lax.axis_size("sub")
    halves = lax.axis_size("sub") == 2 and lax.axis_size("head") == 2
    plan = by_head if assign.shape[0] == owners and halves else by_owner
    return plan(hidden, w_query, w_key, w_value, cluster_rank, assign, d_attended)


def solution(mesh):
    placed = (
        P(("groups", "seq", "sub"), None),
        P("sub", "head"),
        P("sub", "head"),
        P("sub", "head"),
        P("groups"),
        P("head", ("groups", "seq", "sub")),
        P(("groups", "seq", "sub"), "head"),
    )
    return jax.shard_map(
        per_device,
        mesh=mesh,
        in_specs=placed,
        out_specs=(
            P(("groups", "seq", "sub"), "head"),
            P(("groups", "seq", "sub"), "head"),
            P("head", ("groups", "seq", "sub"), None),
        ),
        check_vma=False,
    )
```

```python
from functools import partial

import jax
import jax.numpy as jnp
from jax import lax
from jax.experimental import pallas as pl
from jax.experimental.pallas import tpu as pltpu
from jax.sharding import PartitionSpec as P

epsilon = 1e-06


def keep_mask(filled, cluster_ids, positions):
    count = filled.shape[0]
    same = filled[:, None] & filled[None, :] & (cluster_ids[:, None] == cluster_ids[None, :])
    causal = positions[None, :] <= positions[:, None]
    diagonal = jnp.arange(count)[:, None] == jnp.arange(count)[None, :]
    return same & causal | diagonal


def head_forward(packed, scale):
    queries, keys_in, values, filled, cluster_ids, positions = packed
    scores = (
        lax.dot_general(
            queries, keys_in, (((1,), (1,)), ((), ())), preferred_element_type=jnp.float32
        )
        * scale
    )
    allowed = keep_mask(filled, cluster_ids, positions)
    row_top = jnp.max(jnp.where(allowed, scores, -jnp.inf), axis=1)
    expd = jnp.where(allowed, jnp.exp(scores - row_top[:, None]), 0.0)
    row_total = jnp.sum(expd, axis=1)
    probs_low = (expd / row_total[:, None]).astype(jnp.bfloat16)
    outputs = jnp.dot(probs_low, values, preferred_element_type=jnp.float32).astype(jnp.bfloat16)
    return (outputs, row_top, row_total)


def head_backward(packed, scale):
    queries, keys_in, values, grads_in, filled, cluster_ids, positions, row_top, row_total = packed
    contract_last = (((1,), (1,)), ((), ()))
    contract_first = (((0,), (0,)), ((), ()))
    scores = (
        lax.dot_general(queries, keys_in, contract_last, preferred_element_type=jnp.float32) * scale
    )
    allowed = keep_mask(filled, cluster_ids, positions)
    probs = jnp.where(allowed, jnp.exp(scores - row_top[:, None]), 0.0) / row_total[:, None]
    probs_low = probs.astype(jnp.bfloat16)
    grad_probs = lax.dot_general(
        grads_in, values, contract_last, preferred_element_type=jnp.float32
    )
    delta_rows = jnp.sum(probs * grad_probs, axis=1)
    grad_low = (probs * (grad_probs - delta_rows[:, None]) * scale).astype(jnp.bfloat16)
    grad_query = jnp.dot(grad_low, keys_in, preferred_element_type=jnp.float32).astype(jnp.bfloat16)
    grad_key = lax.dot_general(
        grad_low, queries, contract_first, preferred_element_type=jnp.float32
    ).astype(jnp.bfloat16)
    grad_value = lax.dot_general(
        probs_low, grads_in, contract_first, preferred_element_type=jnp.float32
    ).astype(jnp.bfloat16)
    return (grad_query, grad_key, grad_value)


def by_owner(hidden, w_query, w_key, w_value, cluster_rank, assign, d_attended):
    tok_rows = hidden.shape[0]
    heads_here = assign.shape[0]
    head_dim = w_query.shape[1] // heads_here
    clusters = cluster_rank.shape[0]
    seq_count = lax.axis_size("seq")
    sub_count = lax.axis_size("sub")
    owners = seq_count * sub_count
    capacity = 2 * tok_rows // owners
    slot_count = owners * capacity
    per_owner = clusters // owners
    scale = head_dim ** (-0.5)
    pieces = (
        lax.all_gather(w_query, "sub", axis=0, tiled=True),
        lax.all_gather(w_key, "sub", axis=0, tiled=True),
        lax.all_gather(w_value, "sub", axis=0, tiled=True),
    )
    projected = tuple(
        (
            jnp.dot(hidden, weight_piece, preferred_element_type=jnp.float32)
            for weight_piece in pieces
        )
    )

    def split_heads(matrix):
        return (
            matrix.astype(jnp.bfloat16).reshape(tok_rows, heads_here, head_dim).transpose(1, 0, 2)
        )

    queries, keys_all, values = tuple((split_heads(matrix) for matrix in projected))
    cluster_range = jnp.arange(clusters, dtype=jnp.int32)
    rank_tok = jnp.sum(jnp.where(assign[:, :, None] == cluster_range, cluster_rank, 0), axis=2)
    owner_ids = rank_tok // per_owner
    owner_hot = (owner_ids[:, :, None] == jnp.arange(owners, dtype=jnp.int32)).astype(jnp.int32)
    within = jnp.sum(owner_hot * (jnp.cumsum(owner_hot, axis=1) - 1), axis=2)
    slot_tok = owner_ids * capacity + within
    token_ids = jnp.arange(tok_rows, dtype=jnp.int32)
    slot_range = jnp.arange(slot_count, dtype=jnp.int32)
    slot_match = slot_tok[:, None, :] == slot_range[None, :, None]
    slot_hot = slot_match.astype(jnp.bfloat16)

    def to_slots(rows_in):
        kept = jnp.einsum(
            "hst,htd->hsd", slot_hot, rows_in, preferred_element_type=jnp.float32
        ).astype(jnp.bfloat16)
        return kept.reshape(heads_here, owners, capacity, head_dim)

    def from_slots(slotted):
        flat_slots = slotted.reshape(heads_here, slot_count, head_dim)
        return jnp.einsum(
            "hst,hsd->htd", slot_hot, flat_slots, preferred_element_type=jnp.float32
        ).astype(jnp.bfloat16)

    def exchange_three(first, second, third):
        return (
            lax.all_to_all(first, ("seq", "sub"), split_axis=1, concat_axis=1, tiled=True),
            lax.all_to_all(second, ("seq", "sub"), split_axis=1, concat_axis=1, tiled=True),
            lax.all_to_all(third, ("seq", "sub"), split_axis=1, concat_axis=1, tiled=True),
        )

    sent = exchange_three(to_slots(queries), to_slots(keys_all), to_slots(values))
    tag_tok = assign * tok_rows + token_ids
    slot_tag = jnp.sum(jnp.where(slot_match, tag_tok[:, None, :] + 1, 0), axis=2) - 1
    tags = lax.all_to_all(
        slot_tag.reshape(heads_here, owners, capacity),
        ("seq", "sub"),
        split_axis=1,
        concat_axis=1,
        tiled=True,
    )
    tags = tags.reshape(heads_here, slot_count)
    owner_q, owner_k, owner_v = tuple(
        (member.reshape(heads_here, slot_count, head_dim) for member in sent)
    )
    filled = tags >= 0
    cluster_ids = jnp.where(filled, tags // tok_rows, -1)
    positions = slot_range // capacity * tok_rows + tags % tok_rows
    outputs, row_top, row_total = lax.map(
        partial(head_forward, scale=scale),
        (owner_q, owner_k, owner_v, filled, cluster_ids, positions),
    )
    returned = lax.all_to_all(
        outputs.reshape(heads_here, owners, capacity, head_dim),
        ("seq", "sub"),
        split_axis=1,
        concat_axis=1,
        tiled=True,
    )

    def merge_heads(slotted):
        return from_slots(slotted).transpose(1, 0, 2).reshape(tok_rows, heads_here * head_dim)

    attended = merge_heads(returned)
    grads_tok = d_attended.reshape(tok_rows, heads_here, head_dim).transpose(1, 0, 2)
    owner_g = lax.all_to_all(
        to_slots(grads_tok), ("seq", "sub"), split_axis=1, concat_axis=1, tiled=True
    ).reshape(heads_here, slot_count, head_dim)
    grad_q, grad_k, grad_v = lax.map(
        partial(head_backward, scale=scale),
        (owner_q, owner_k, owner_v, owner_g, filled, cluster_ids, positions, row_top, row_total),
    )
    shape_four = (heads_here, owners, capacity, head_dim)
    back = exchange_three(
        grad_q.reshape(shape_four), grad_k.reshape(shape_four), grad_v.reshape(shape_four)
    )
    token_grads = tuple((merge_heads(member) for member in back))
    pieces = lax.all_gather((w_query, w_key, w_value), "sub", axis=0, tiled=True)
    terms = [
        jnp.einsum("tc,rc->tr", grad_rows_in, weight_piece, preferred_element_type=jnp.float32)
        for grad_rows_in, weight_piece in zip(token_grads, pieces)
    ]
    partial_grad = terms[0] + terms[1] + terms[2]
    d_hidden = lax.psum_scatter(
        partial_grad.astype(jnp.bfloat16), "head", scatter_dimension=1, tiled=True
    )
    keys_float = keys_all.astype(jnp.float32)
    unit_keys = keys_float * lax.rsqrt(
        jnp.sum(keys_float * keys_float, axis=2, keepdims=True) + epsilon
    )
    member_hot = (rank_tok[:, :, None] == cluster_range).astype(jnp.float32)
    local_sums = jnp.einsum("htr,htd->hrd", member_hot, unit_keys, precision=lax.Precision.HIGHEST)
    centroid_sums = lax.psum_scatter(
        local_sums.astype(jnp.bfloat16), ("seq", "sub"), scatter_dimension=1, tiled=True
    ).astype(jnp.float32)
    return (attended, d_hidden, centroid_sums)


contract_last = (((1,), (1,)), ((), ()))
contract_first = (((0,), (0,)), ((), ()))
log2_e = 1.4426950408889634
vmem_bytes = 48 * 1024 * 1024


def pack_kernel(grads_ref, assign_ref, out_ref):
    blocks, padded, head_dim = out_ref.shape
    rows = grads_ref.shape[0]
    spare = padded - rows - rows // head_dim
    for head in range(blocks):
        out_ref[head, :rows, :] = grads_ref[:, head * head_dim : (head + 1) * head_dim]
        ids = assign_ref[head : head + 1, :].astype(jnp.float32)
        lines = [
            ids[:, start : start + head_dim] for start in range(0, rows, head_dim)
        ] + [jnp.zeros((spare, head_dim), jnp.float32)]
        out_ref[head, rows:, :] = jnp.concatenate(lines, axis=0).astype(jnp.bfloat16)


def project_kernel(side_ref, hidden_ref, *refs):
    out_ref = refs[-1]
    heads, triple, head_dim = out_ref.shape
    rows = triple // 3
    half = refs[0].shape[0]
    side = side_ref[0]
    near = hidden_ref[:, pl.ds(pl.multiple_of(side * half, half), half)]
    far = hidden_ref[:, pl.ds(pl.multiple_of((1 - side) * half, half), half)]
    for index in range(3):
        total = jnp.dot(near, refs[index][...], preferred_element_type=jnp.float32)
        total += jnp.dot(far, refs[3 + index][...], preferred_element_type=jnp.float32)
        low = total.astype(jnp.bfloat16)
        for head in range(heads):
            out_ref[head, index * rows : (index + 1) * rows, :] = low[
                :, head * head_dim : (head + 1) * head_dim
            ]


def attend_kernel(factor, scale, packed_ref, grads_ref, rank_ref, out_ref, grad_ref, ids_ref, dk_ref, dv_ref):
    blocks, triple, head_dim = packed_ref.shape
    rows = triple // 3
    clusters = rank_ref.shape[1]
    owned = clusters // blocks
    id_rows = []
    for block in range(blocks):
        lines = grads_ref[block, rows : rows + 16, :].astype(jnp.float32)
        ids = jnp.concatenate([lines[at : at + 1, :] for at in range(rows // head_dim)], axis=1)
        id_rows.append(ids)
        ids_ref[block * rows : (block + 1) * rows, :] = jnp.broadcast_to(ids, (head_dim, rows)).T
    key_at = lax.broadcasted_iota(jnp.int32, (rows, rows), 0)
    query_at = lax.broadcasted_iota(jnp.int32, (rows, rows), 1)
    dk_ref[...] = jnp.zeros_like(dk_ref)
    dv_ref[...] = jnp.zeros_like(dv_ref)
    for block in range(blocks):
        seen = (block + 1) * rows
        keys_in = packed_ref[: block + 1, rows : 2 * rows, :].reshape(seen, head_dim)
        values = packed_ref[: block + 1, 2 * rows :, :].reshape(seen, head_dim)
        query_rows = packed_ref[block, :rows, :]
        grad_rows = grads_ref[block, :rows, :]
        scores = lax.dot_general(
            keys_in, query_rows, contract_last, preferred_element_type=jnp.float32
        )
        grad_probs = lax.dot_general(
            values, grad_rows, contract_last, preferred_element_type=jnp.float32
        )
        ids = ids_ref[:seen, :]
        same = jnp.concatenate(
            [
                ids == id_rows[block][:, start : start + head_dim]
                for start in range(0, rows, head_dim)
            ],
            axis=1,
        )
        last = same[seen - rows :] & (key_at <= query_at)
        allowed = last if block == 0 else jnp.concatenate([same[: seen - rows], last], axis=0)
        scores = jnp.where(allowed, scores * factor, -jnp.inf)
        top = jnp.max(scores, axis=0, keepdims=True)
        expd = jnp.exp2(scores - top)
        total = jnp.sum(expd, axis=0, keepdims=True)
        probs = expd * (1.0 / total)
        weighted = probs * grad_probs
        delta = jnp.sum(weighted, axis=0, keepdims=True)
        grad_low = (weighted - probs * delta).astype(jnp.bfloat16)
        probs_low = probs.astype(jnp.bfloat16)
        flipped = lax.dot_general(
            values, probs_low, contract_first, preferred_element_type=jnp.float32
        )
        out_ref[block] = flipped.T.astype(jnp.bfloat16)
        dv_ref[:seen, :] += jnp.dot(probs_low, grad_rows, preferred_element_type=jnp.float32)
        dk_ref[:seen, :] += jnp.dot(grad_low, query_rows, preferred_element_type=jnp.float32)
        flipped = lax.dot_general(
            keys_in, grad_low, contract_first, preferred_element_type=jnp.float32
        )
        grad_ref[block, :rows, :] = (flipped.T * scale).astype(jnp.bfloat16)
    grad_ref[:, rows : 2 * rows, :] = (
        (dk_ref[...] * scale).astype(jnp.bfloat16).reshape(blocks, rows, head_dim)
    )
    grad_ref[:, 2 * rows : triple, :] = (
        dv_ref[...].astype(jnp.bfloat16).reshape(blocks, rows, head_dim)
    )
    sums = jnp.zeros((clusters, head_dim), jnp.float32)
    cluster_at = lax.broadcasted_iota(jnp.int32, (clusters, rows), 0).astype(jnp.float32)
    for block in range(blocks):
        keys_float = packed_ref[block, rows : 2 * rows, :].astype(jnp.float32)
        unit = keys_float * lax.rsqrt(
            jnp.sum(keys_float * keys_float, axis=1, keepdims=True) + epsilon
        )
        unit_high = unit.astype(jnp.bfloat16)
        unit_low = (unit - unit_high.astype(jnp.float32)).astype(jnp.bfloat16)
        member = jnp.where(cluster_at == id_rows[block], 1.0, 0.0).astype(jnp.bfloat16)
        sums += jnp.dot(member, unit_high, preferred_element_type=jnp.float32)
        sums += jnp.dot(member, unit_low, preferred_element_type=jnp.float32)
    rank_at = lax.broadcasted_iota(jnp.int32, (clusters, clusters), 0)
    ordered = jnp.where(rank_at == rank_ref[...], 1.0, 0.0).astype(jnp.bfloat16)
    ranked = jnp.dot(ordered, sums.astype(jnp.bfloat16), preferred_element_type=jnp.float32)
    grad_ref[:, triple:, :] = ranked.astype(jnp.bfloat16).reshape(blocks, owned, head_dim)


def input_kernel(pick_ref, back_ref, *refs):
    out_ref, gathered_ref = refs[-2:]
    blocks, padded, head_dim = back_ref.shape
    rows = out_ref.shape[0]
    width = blocks * head_dim

    @pl.when(pl.program_id(0) == 0)
    def gather():
        for index in range(3):
            for head in range(blocks):
                at = index * width + head * head_dim
                gathered_ref[:, at : at + head_dim] = back_ref[
                    head, index * rows : (index + 1) * rows, :
                ]

    def multiply(first):
        total = None
        for index in range(3):
            term = lax.dot_general(
                gathered_ref[:, index * width : (index + 1) * width],
                refs[first + index][...],
                contract_last,
                preferred_element_type=jnp.float32,
            )
            total = term if total is None else total + term
        out_ref[...] = total.astype(out_ref.dtype)

    pl.when(pick_ref[0] == 0)(lambda: multiply(0))
    pl.when(pick_ref[0] != 0)(lambda: multiply(3))


def by_head(hidden, w_query, w_key, w_value, cluster_rank, assign, d_attended):
    rows = hidden.shape[0]
    blocks = assign.shape[0]
    half, width = w_query.shape
    head_dim = width // blocks
    tokens = blocks * rows
    clusters = cluster_rank.shape[0]
    owned = clusters // blocks
    scale = head_dim ** (-0.5)
    factor = scale * log2_e
    line = ("seq", "sub")
    vmem = pl.BlockSpec(memory_space=pltpu.VMEM)
    params = pltpu.CompilerParams(vmem_limit_bytes=vmem_bytes)
    pairs_seen = tokens * (tokens + rows) // 2
    wide = 2 * head_dim

    def exchange(packed):
        return lax.all_to_all(packed, line, split_axis=0, concat_axis=0, tiled=True)

    id_rows = -(-(rows // head_dim) // 16) * 16
    grads = exchange(
        pl.pallas_call(
            pack_kernel,
            out_shape=jax.ShapeDtypeStruct((blocks, rows + id_rows, head_dim), jnp.bfloat16),
            in_specs=[vmem] * 2,
            out_specs=vmem,
            compiler_params=params,
        )(d_attended, assign)
    )

    swap = [(0, 1), (1, 0)]
    side = lax.axis_index("sub")
    own = (w_query, w_key, w_value)
    other = tuple(lax.ppermute(piece, "sub", swap) for piece in own)
    projected = pl.pallas_call(
        project_kernel,
        out_shape=jax.ShapeDtypeStruct((blocks, 3 * rows, head_dim), jnp.bfloat16),
        grid_spec=pltpu.PrefetchScalarGridSpec(
            num_scalar_prefetch=1,
            grid=(width // wide,),
            in_specs=[pl.BlockSpec((rows, 2 * half), lambda step, side_at: (0, 0))]
            + [pl.BlockSpec((half, wide), lambda step, side_at: (0, step))] * 6,
            out_specs=pl.BlockSpec((2, 3 * rows, head_dim), lambda step, side_at: (step, 0, 0)),
        ),
        compiler_params=params,
        cost_estimate=pl.CostEstimate(
            flops=12 * rows * half * width, bytes_accessed=14 * half * width, transcendentals=0
        ),
    )(side.reshape(1), hidden, *own, *other)
    packed = exchange(projected)

    outputs, grads_out = pl.pallas_call(
        partial(attend_kernel, factor, scale),
        out_shape=(
            jax.ShapeDtypeStruct((blocks, rows, head_dim), jnp.bfloat16),
            jax.ShapeDtypeStruct((blocks, 3 * rows + owned, head_dim), jnp.bfloat16),
        ),
        in_specs=[vmem] * 3,
        out_specs=(vmem, vmem),
        scratch_shapes=[pltpu.VMEM((tokens, head_dim), jnp.float32)] * 3,
        compiler_params=params,
        cost_estimate=pl.CostEstimate(
            flops=12 * pairs_seen * head_dim,
            bytes_accessed=16 * tokens * head_dim,
            transcendentals=pairs_seen,
        ),
    )(packed, grads, cluster_rank.reshape(1, clusters))
    back = exchange(grads_out)
    returned = exchange(outputs)
    attended = returned.transpose(1, 0, 2).reshape(rows, width)
    centroid_sums = back[:, 3 * rows :, :].astype(jnp.float32)

    def input_part(pick, kept_type):
        def rows_of(first):
            return lambda step, pick_at: (jnp.where(pick_at[0] == first, step, 0), 0)

        return pl.pallas_call(
            input_kernel,
            out_shape=jax.ShapeDtypeStruct((rows, half), kept_type),
            grid_spec=pltpu.PrefetchScalarGridSpec(
                num_scalar_prefetch=1,
                grid=(half // wide,),
                in_specs=[pl.BlockSpec(back.shape, lambda step, pick_at: (0, 0, 0))]
                + [pl.BlockSpec((wide, width), rows_of(0))] * 3
                + [pl.BlockSpec((wide, width), rows_of(1))] * 3,
                out_specs=pl.BlockSpec((rows, wide), lambda step, pick_at: (0, step)),
                scratch_shapes=[pltpu.VMEM((rows, 3 * width), jnp.bfloat16)],
            ),
            compiler_params=params,
            cost_estimate=pl.CostEstimate(
                flops=6 * rows * half * width, bytes_accessed=10 * half * width, transcendentals=0
            ),
        )(pick.reshape(1), back, *own, *other)

    crossed = (side != lax.axis_index("head")).astype(jnp.int32)
    arrived = lax.ppermute(input_part(1 - crossed, jnp.bfloat16), "head", swap)
    kept = input_part(crossed, jnp.float32)
    d_hidden = (kept + arrived.astype(jnp.float32)).astype(jnp.bfloat16)
    return (attended, d_hidden, centroid_sums)


def per_device(hidden, w_query, w_key, w_value, cluster_rank, assign, d_attended):
    owners = lax.axis_size("seq") * lax.axis_size("sub")
    halves = lax.axis_size("sub") == 2 and lax.axis_size("head") == 2
    plan = by_head if assign.shape[0] == owners and halves else by_owner
    return plan(hidden, w_query, w_key, w_value, cluster_rank, assign, d_attended)


def solution(mesh):
    placed = (
        P(("groups", "seq", "sub"), None),
        P("sub", "head"),
        P("sub", "head"),
        P("sub", "head"),
        P("groups"),
        P("head", ("groups", "seq", "sub")),
        P(("groups", "seq", "sub"), "head"),
    )
    return jax.shard_map(
        per_device,
        mesh=mesh,
        in_specs=placed,
        out_specs=(
            P(("groups", "seq", "sub"), "head"),
            P(("groups", "seq", "sub"), "head"),
            P("head", ("groups", "seq", "sub"), None),
        ),
        check_vma=False,
    )
```

```python
from functools import partial

import jax
import jax.numpy as jnp
from jax import lax
from jax.experimental import pallas as pl
from jax.experimental.pallas import tpu as pltpu
from jax.sharding import PartitionSpec as P

epsilon = 1e-06


def keep_mask(filled, cluster_ids, positions):
    count = filled.shape[0]
    same = filled[:, None] & filled[None, :] & (cluster_ids[:, None] == cluster_ids[None, :])
    causal = positions[None, :] <= positions[:, None]
    diagonal = jnp.arange(count)[:, None] == jnp.arange(count)[None, :]
    return same & causal | diagonal


def head_forward(packed, scale):
    queries, keys_in, values, filled, cluster_ids, positions = packed
    scores = (
        lax.dot_general(
            queries, keys_in, (((1,), (1,)), ((), ())), preferred_element_type=jnp.float32
        )
        * scale
    )
    allowed = keep_mask(filled, cluster_ids, positions)
    row_top = jnp.max(jnp.where(allowed, scores, -jnp.inf), axis=1)
    expd = jnp.where(allowed, jnp.exp(scores - row_top[:, None]), 0.0)
    row_total = jnp.sum(expd, axis=1)
    probs_low = (expd / row_total[:, None]).astype(jnp.bfloat16)
    outputs = jnp.dot(probs_low, values, preferred_element_type=jnp.float32).astype(jnp.bfloat16)
    return (outputs, row_top, row_total)


def head_backward(packed, scale):
    queries, keys_in, values, grads_in, filled, cluster_ids, positions, row_top, row_total = packed
    contract_last = (((1,), (1,)), ((), ()))
    contract_first = (((0,), (0,)), ((), ()))
    scores = (
        lax.dot_general(queries, keys_in, contract_last, preferred_element_type=jnp.float32) * scale
    )
    allowed = keep_mask(filled, cluster_ids, positions)
    probs = jnp.where(allowed, jnp.exp(scores - row_top[:, None]), 0.0) / row_total[:, None]
    probs_low = probs.astype(jnp.bfloat16)
    grad_probs = lax.dot_general(
        grads_in, values, contract_last, preferred_element_type=jnp.float32
    )
    delta_rows = jnp.sum(probs * grad_probs, axis=1)
    grad_low = (probs * (grad_probs - delta_rows[:, None]) * scale).astype(jnp.bfloat16)
    grad_query = jnp.dot(grad_low, keys_in, preferred_element_type=jnp.float32).astype(jnp.bfloat16)
    grad_key = lax.dot_general(
        grad_low, queries, contract_first, preferred_element_type=jnp.float32
    ).astype(jnp.bfloat16)
    grad_value = lax.dot_general(
        probs_low, grads_in, contract_first, preferred_element_type=jnp.float32
    ).astype(jnp.bfloat16)
    return (grad_query, grad_key, grad_value)


def by_owner(hidden, w_query, w_key, w_value, cluster_rank, assign, d_attended):
    tok_rows = hidden.shape[0]
    heads_here = assign.shape[0]
    head_dim = w_query.shape[1] // heads_here
    clusters = cluster_rank.shape[0]
    seq_count = lax.axis_size("seq")
    sub_count = lax.axis_size("sub")
    owners = seq_count * sub_count
    capacity = 2 * tok_rows // owners
    slot_count = owners * capacity
    per_owner = clusters // owners
    scale = head_dim ** (-0.5)
    pieces = (
        lax.all_gather(w_query, "sub", axis=0, tiled=True),
        lax.all_gather(w_key, "sub", axis=0, tiled=True),
        lax.all_gather(w_value, "sub", axis=0, tiled=True),
    )
    projected = tuple(
        (
            jnp.dot(hidden, weight_piece, preferred_element_type=jnp.float32)
            for weight_piece in pieces
        )
    )

    def split_heads(matrix):
        return (
            matrix.astype(jnp.bfloat16).reshape(tok_rows, heads_here, head_dim).transpose(1, 0, 2)
        )

    queries, keys_all, values = tuple((split_heads(matrix) for matrix in projected))
    cluster_range = jnp.arange(clusters, dtype=jnp.int32)
    rank_tok = jnp.sum(jnp.where(assign[:, :, None] == cluster_range, cluster_rank, 0), axis=2)
    owner_ids = rank_tok // per_owner
    owner_hot = (owner_ids[:, :, None] == jnp.arange(owners, dtype=jnp.int32)).astype(jnp.int32)
    within = jnp.sum(owner_hot * (jnp.cumsum(owner_hot, axis=1) - 1), axis=2)
    slot_tok = owner_ids * capacity + within
    token_ids = jnp.arange(tok_rows, dtype=jnp.int32)
    slot_range = jnp.arange(slot_count, dtype=jnp.int32)
    slot_match = slot_tok[:, None, :] == slot_range[None, :, None]
    slot_hot = slot_match.astype(jnp.bfloat16)

    def to_slots(rows_in):
        kept = jnp.einsum(
            "hst,htd->hsd", slot_hot, rows_in, preferred_element_type=jnp.float32
        ).astype(jnp.bfloat16)
        return kept.reshape(heads_here, owners, capacity, head_dim)

    def from_slots(slotted):
        flat_slots = slotted.reshape(heads_here, slot_count, head_dim)
        return jnp.einsum(
            "hst,hsd->htd", slot_hot, flat_slots, preferred_element_type=jnp.float32
        ).astype(jnp.bfloat16)

    def exchange_three(first, second, third):
        return (
            lax.all_to_all(first, ("seq", "sub"), split_axis=1, concat_axis=1, tiled=True),
            lax.all_to_all(second, ("seq", "sub"), split_axis=1, concat_axis=1, tiled=True),
            lax.all_to_all(third, ("seq", "sub"), split_axis=1, concat_axis=1, tiled=True),
        )

    sent = exchange_three(to_slots(queries), to_slots(keys_all), to_slots(values))
    tag_tok = assign * tok_rows + token_ids
    slot_tag = jnp.sum(jnp.where(slot_match, tag_tok[:, None, :] + 1, 0), axis=2) - 1
    tags = lax.all_to_all(
        slot_tag.reshape(heads_here, owners, capacity),
        ("seq", "sub"),
        split_axis=1,
        concat_axis=1,
        tiled=True,
    )
    tags = tags.reshape(heads_here, slot_count)
    owner_q, owner_k, owner_v = tuple(
        (member.reshape(heads_here, slot_count, head_dim) for member in sent)
    )
    filled = tags >= 0
    cluster_ids = jnp.where(filled, tags // tok_rows, -1)
    positions = slot_range // capacity * tok_rows + tags % tok_rows
    outputs, row_top, row_total = lax.map(
        partial(head_forward, scale=scale),
        (owner_q, owner_k, owner_v, filled, cluster_ids, positions),
    )
    returned = lax.all_to_all(
        outputs.reshape(heads_here, owners, capacity, head_dim),
        ("seq", "sub"),
        split_axis=1,
        concat_axis=1,
        tiled=True,
    )

    def merge_heads(slotted):
        return from_slots(slotted).transpose(1, 0, 2).reshape(tok_rows, heads_here * head_dim)

    attended = merge_heads(returned)
    grads_tok = d_attended.reshape(tok_rows, heads_here, head_dim).transpose(1, 0, 2)
    owner_g = lax.all_to_all(
        to_slots(grads_tok), ("seq", "sub"), split_axis=1, concat_axis=1, tiled=True
    ).reshape(heads_here, slot_count, head_dim)
    grad_q, grad_k, grad_v = lax.map(
        partial(head_backward, scale=scale),
        (owner_q, owner_k, owner_v, owner_g, filled, cluster_ids, positions, row_top, row_total),
    )
    shape_four = (heads_here, owners, capacity, head_dim)
    back = exchange_three(
        grad_q.reshape(shape_four), grad_k.reshape(shape_four), grad_v.reshape(shape_four)
    )
    token_grads = tuple((merge_heads(member) for member in back))
    pieces = lax.all_gather((w_query, w_key, w_value), "sub", axis=0, tiled=True)
    terms = [
        jnp.einsum("tc,rc->tr", grad_rows_in, weight_piece, preferred_element_type=jnp.float32)
        for grad_rows_in, weight_piece in zip(token_grads, pieces)
    ]
    partial_grad = terms[0] + terms[1] + terms[2]
    d_hidden = lax.psum_scatter(
        partial_grad.astype(jnp.bfloat16), "head", scatter_dimension=1, tiled=True
    )
    keys_float = keys_all.astype(jnp.float32)
    unit_keys = keys_float * lax.rsqrt(
        jnp.sum(keys_float * keys_float, axis=2, keepdims=True) + epsilon
    )
    member_hot = (rank_tok[:, :, None] == cluster_range).astype(jnp.float32)
    local_sums = jnp.einsum("htr,htd->hrd", member_hot, unit_keys, precision=lax.Precision.HIGHEST)
    centroid_sums = lax.psum_scatter(
        local_sums.astype(jnp.bfloat16), ("seq", "sub"), scatter_dimension=1, tiled=True
    ).astype(jnp.float32)
    return (attended, d_hidden, centroid_sums)


contract_last = (((1,), (1,)), ((), ()))
contract_first = (((0,), (0,)), ((), ()))
log2_e = 1.4426950408889634
vmem_bytes = 48 * 1024 * 1024


def pack_kernel(place_ref, grads_ref, assign_ref, *out_refs):
    padded, head_dim = out_refs[0].shape
    rows = grads_ref.shape[0]
    spare = padded - rows - rows // head_dim
    for offset, out_ref in enumerate(out_refs):
        head = place_ref[0] ^ offset
        at = pl.multiple_of(head * head_dim, head_dim)
        out_ref[:rows, :] = grads_ref[:, pl.ds(at, head_dim)]
        ids = assign_ref[pl.ds(head, 1), :].astype(jnp.float32)
        lines = [
            ids[:, start : start + head_dim] for start in range(0, rows, head_dim)
        ] + [jnp.zeros((spare, head_dim), jnp.float32)]
        out_ref[rows:, :] = jnp.concatenate(lines, axis=0).astype(jnp.bfloat16)


def project_kernel(count, place_ref, hidden_ref, *refs):
    weights, out_refs = refs[: 2 * count], refs[2 * count :]
    triple, head_dim = out_refs[0].shape
    rows = triple // count
    half = weights[0].shape[0]
    odd = place_ref[0] % 2
    near = hidden_ref[:, pl.ds(pl.multiple_of(odd * half, half), half)]
    far = hidden_ref[:, pl.ds(pl.multiple_of((1 - odd) * half, half), half)]
    for index in range(count):
        total = jnp.dot(near, weights[index][...], preferred_element_type=jnp.float32)
        total += jnp.dot(far, weights[count + index][...], preferred_element_type=jnp.float32)
        low = total.astype(jnp.bfloat16)
        first = jnp.where(odd == 0, low[:, :head_dim], low[:, head_dim:])
        second = jnp.where(odd == 0, low[:, head_dim:], low[:, :head_dim])
        for pair in range(len(out_refs) // 2):

            @pl.when(pl.program_id(0) == pair)
            def store(pair=pair, index=index, first=first, second=second):
                out_refs[2 * pair][index * rows : (index + 1) * rows, :] = first
                out_refs[2 * pair + 1][index * rows : (index + 1) * rows, :] = second


def take_ids(grads_ref, rows):
    head_dim = grads_ref.shape[1]
    lines = grads_ref[rows : rows + 16, :].astype(jnp.float32)
    return jnp.concatenate([lines[at : at + 1, :] for at in range(rows // head_dim)], axis=1)


def in_order(place, parts, rows, ordered):
    for offset, part in enumerate(parts):
        for index, held in enumerate(ordered):
            held[place ^ offset] = part[index * rows : (index + 1) * rows, :]


def order_ids(place, grads, rows, id_rows, id_cols):
    for offset, part in enumerate(grads):
        ids = take_ids(part, rows)
        id_rows[place ^ offset] = jnp.broadcast_to(ids, id_rows.shape[1:])
        id_cols[place ^ offset] = jnp.broadcast_to(ids, (id_cols.shape[2], rows)).T


def block_scores(factor, block, queries, keys_in, id_rows, id_cols):
    rows, head_dim = queries.shape[1:]
    seen = (block + 1) * rows
    scores = lax.dot_general(
        keys_in[: block + 1].reshape(seen, head_dim),
        queries[block],
        contract_last,
        preferred_element_type=jnp.float32,
    )
    ids = id_cols[: block + 1].reshape(seen, head_dim)
    mine = id_rows[block][:1, :]
    same = jnp.concatenate(
        [ids == mine[:, start : start + head_dim] for start in range(0, rows, head_dim)], axis=1
    )
    key_at = lax.broadcasted_iota(jnp.int32, (rows, rows), 0)
    query_at = lax.broadcasted_iota(jnp.int32, (rows, rows), 1)
    last = same[seen - rows :] & (key_at <= query_at)
    allowed = last if block == 0 else jnp.concatenate([same[: seen - rows], last], axis=0)
    return jnp.where(allowed, scores * factor, -jnp.inf)


def value_grad_kernel(factor, count, place_ref, *refs):
    packed, grads = refs[:count], refs[count : 2 * count]
    out_refs, lse_ref = refs[2 * count : 3 * count], refs[3 * count]
    queries, keys_in, grad_rows, id_rows, id_cols, total_ref = refs[3 * count + 1 :]
    rows, head_dim = queries.shape[1:]
    place = place_ref[0]
    in_order(place, packed, rows, (queries, keys_in))
    in_order(place, grads, rows, (grad_rows,))
    order_ids(place, grads, rows, id_rows, id_cols)
    total_ref[...] = jnp.zeros_like(total_ref)
    for block in range(count):
        seen = (block + 1) * rows
        scores = block_scores(factor, block, queries, keys_in, id_rows, id_cols)
        top = jnp.max(scores, axis=0, keepdims=True)
        expd = jnp.exp2(scores - top)
        total = jnp.sum(expd, axis=0, keepdims=True)
        lse_ref[block : block + 1, :] = top + jnp.log2(total)
        probs_low = (expd * (1.0 / total)).astype(jnp.bfloat16)
        total_ref[:seen, :] += jnp.dot(
            probs_low, grad_rows[block], preferred_element_type=jnp.float32
        )
    for offset in range(count):
        at = pl.multiple_of((place ^ offset) * rows, rows)
        out_refs[offset][...] = total_ref[pl.ds(at, rows), :].astype(jnp.bfloat16)


def query_grad_kernel(factor, scale, count, place_ref, *refs):
    packed, valued, grads = refs[:count], refs[count : 2 * count], refs[2 * count : 3 * count]
    lse_ref, rank_ref = refs[3 * count : 3 * count + 2]
    grad_refs, out_refs = refs[3 * count + 2 : 4 * count + 2], refs[4 * count + 2 : 5 * count + 2]
    queries, keys_in, values, grad_rows, id_rows, id_cols, total_ref, dq_ref, attended_ref = refs[
        5 * count + 2 :
    ]
    rows, head_dim = queries.shape[1:]
    clusters = rank_ref.shape[1]
    owned = clusters // count
    place = place_ref[0]
    in_order(place, packed, rows, (queries, keys_in))
    in_order(place, valued, rows, (values,))
    in_order(place, grads, rows, (grad_rows,))
    order_ids(place, grads, rows, id_rows, id_cols)
    total_ref[...] = jnp.zeros_like(total_ref)
    for block in range(count):
        seen = (block + 1) * rows
        scores = block_scores(factor, block, queries, keys_in, id_rows, id_cols)
        probs = jnp.exp2(scores - lse_ref[block : block + 1, :])
        seen_values = values[: block + 1].reshape(seen, head_dim)
        grad_probs = lax.dot_general(
            seen_values, grad_rows[block], contract_last, preferred_element_type=jnp.float32
        )
        flipped = lax.dot_general(
            seen_values,
            probs.astype(jnp.bfloat16),
            contract_first,
            preferred_element_type=jnp.float32,
        )
        attended_ref[block] = flipped.T.astype(jnp.bfloat16)
        weighted = probs * grad_probs
        delta = jnp.sum(weighted, axis=0, keepdims=True)
        grad_low = (weighted - probs * delta).astype(jnp.bfloat16)
        total_ref[:seen, :] += jnp.dot(
            grad_low, queries[block], preferred_element_type=jnp.float32
        )
        flipped = lax.dot_general(
            keys_in[: block + 1].reshape(seen, head_dim),
            grad_low,
            contract_first,
            preferred_element_type=jnp.float32,
        )
        dq_ref[block] = (flipped.T * scale).astype(jnp.bfloat16)
    sums = jnp.zeros((clusters, head_dim), jnp.float32)
    cluster_at = lax.broadcasted_iota(jnp.int32, (clusters, rows), 0).astype(jnp.float32)
    for block in range(count):
        keys_float = keys_in[block].astype(jnp.float32)
        unit = keys_float * lax.rsqrt(
            jnp.sum(keys_float * keys_float, axis=1, keepdims=True) + epsilon
        )
        unit_high = unit.astype(jnp.bfloat16)
        unit_low = (unit - unit_high.astype(jnp.float32)).astype(jnp.bfloat16)
        member = jnp.where(cluster_at == id_rows[block][:1, :], 1.0, 0.0).astype(jnp.bfloat16)
        sums += jnp.dot(member, unit_high, preferred_element_type=jnp.float32)
        sums += jnp.dot(member, unit_low, preferred_element_type=jnp.float32)
    rank_at = lax.broadcasted_iota(jnp.int32, (clusters, clusters), 0)
    ordered = jnp.where(rank_at == rank_ref[...], 1.0, 0.0).astype(jnp.bfloat16)
    ranked = jnp.dot(ordered, sums.astype(jnp.bfloat16), preferred_element_type=jnp.float32)
    ranked_low = ranked.astype(jnp.bfloat16).reshape(count, owned, head_dim)
    dq_end = rows
    for part in range(count):
        attended_ref[count + part, :owned, :] = ranked_low[part]
    for offset in range(count):
        owner = place ^ offset
        at = pl.multiple_of(owner * rows, rows)
        grad_refs[offset][:dq_end, :] = dq_ref[owner]
        grad_refs[offset][dq_end:, :] = (total_ref[pl.ds(at, rows), :] * scale).astype(jnp.bfloat16)
        out_refs[offset][:rows, :] = attended_ref[owner]
        out_refs[offset][rows:, :] = attended_ref[count + owner, :owned, :]


def finish_kernel(count, place_ref, *refs):
    parts, attended_ref, sums_ref = refs[:count], refs[count], refs[count + 1]
    rows = attended_ref.shape[0]
    head_dim = sums_ref.shape[2]
    for offset, part in enumerate(parts):
        head = place_ref[0] ^ offset
        at = pl.multiple_of(head * head_dim, head_dim)
        attended_ref[:, pl.ds(at, head_dim)] = part[:rows, :]
        sums_ref[head] = part[rows:, :].astype(jnp.float32)


def input_kernel(count, place_ref, *refs):
    parts, valued, weights = refs[:count], refs[count : 2 * count], refs[2 * count : 2 * count + 6]
    out_ref, gathered_ref = refs[2 * count + 6 :]
    rows = out_ref.shape[0]
    head_dim = parts[0].shape[1]
    width = count * head_dim

    @pl.when(pl.program_id(0) == 0)
    def gather():
        for offset in range(count):
            at = (place_ref[0] ^ offset) * head_dim
            for index, piece in enumerate(
                (parts[offset][:rows, :], parts[offset][rows:, :], valued[offset][...])
            ):
                start = pl.multiple_of(index * width + at, head_dim)
                gathered_ref[:, pl.ds(start, head_dim)] = piece

    def multiply(first):
        total = None
        for index in range(3):
            term = lax.dot_general(
                gathered_ref[:, index * width : (index + 1) * width],
                weights[first + index][...],
                contract_last,
                preferred_element_type=jnp.float32,
            )
            total = term if total is None else total + term
        out_ref[...] = total.astype(out_ref.dtype)

    pl.when(place_ref[1] == 0)(lambda: multiply(0))
    pl.when(place_ref[1] != 0)(lambda: multiply(3))


def by_head(hidden, w_query, w_key, w_value, cluster_rank, assign, d_attended):
    rows = hidden.shape[0]
    count = assign.shape[0]
    half, width = w_query.shape
    head_dim = width // count
    tokens = count * rows
    clusters = cluster_rank.shape[0]
    owned = clusters // count
    scale = head_dim ** (-0.5)
    factor = scale * log2_e
    line = ("seq", "sub")
    smem = pl.BlockSpec(memory_space=pltpu.SMEM)
    vmem = pl.BlockSpec(memory_space=pltpu.VMEM)
    params = pltpu.CompilerParams(vmem_limit_bytes=vmem_bytes)
    pairs_seen = tokens * (tokens + rows) // 2
    wide = 2 * head_dim
    side = lax.axis_index("sub")
    place = lax.axis_index("seq") * 2 + side
    here = place.reshape(1)

    def buffers(height):
        return (jax.ShapeDtypeStruct((height, head_dim), jnp.bfloat16),) * count

    def exchange(parts):
        moved = [
            lax.ppermute(parts[offset], line, [(at, at ^ offset) for at in range(count)])
            for offset in range(count - 1, 0, -1)
        ]
        return (parts[0], *moved[::-1])

    def scratch(kind):
        return pltpu.VMEM((count, rows, head_dim), kind)

    id_scratch = [
        pltpu.VMEM((count, 8, rows), jnp.float32),
        pltpu.VMEM((count, rows, head_dim), jnp.float32),
    ]
    total_scratch = [pltpu.VMEM((tokens, head_dim), jnp.float32)]

    id_height = -(-(rows // head_dim) // 16) * 16
    grads = exchange(
        pl.pallas_call(
            pack_kernel,
            out_shape=buffers(rows + id_height),
            in_specs=[smem] + [vmem] * 2,
            out_specs=(vmem,) * count,
            compiler_params=params,
        )(here, d_attended, assign)
    )

    swap = [(0, 1), (1, 0)]
    own = (w_query, w_key, w_value)
    other = tuple(lax.ppermute(piece, "sub", swap) for piece in own)

    def project(mine, theirs):
        number = len(mine)
        return pl.pallas_call(
            partial(project_kernel, number),
            out_shape=buffers(number * rows),
            grid_spec=pltpu.PrefetchScalarGridSpec(
                num_scalar_prefetch=1,
                grid=(count // 2,),
                in_specs=[pl.BlockSpec((rows, 2 * half), lambda step, at: (0, 0))]
                + [pl.BlockSpec((half, wide), lambda step, at: (0, (at[0] // 2) ^ step))]
                * (2 * number),
                out_specs=[pl.BlockSpec((number * rows, head_dim), lambda step, at: (0, 0))]
                * count,
            ),
            compiler_params=params,
            cost_estimate=pl.CostEstimate(
                flops=4 * number * rows * half * width,
                bytes_accessed=5 * number * half * width,
                transcendentals=0,
            ),
        )(here, hidden, *mine, *theirs)

    packed = exchange(project(own[:2], other[:2]))
    valued = exchange(project(own[2:], other[2:]))

    *value_grads, lse = pl.pallas_call(
        partial(value_grad_kernel, factor, count),
        out_shape=(*buffers(rows), jax.ShapeDtypeStruct((count, rows), jnp.float32)),
        in_specs=[smem] + [vmem] * (2 * count),
        out_specs=(vmem,) * (count + 1),
        scratch_shapes=[scratch(jnp.bfloat16)] * 3 + id_scratch + total_scratch,
        compiler_params=params,
        cost_estimate=pl.CostEstimate(
            flops=4 * pairs_seen * head_dim,
            bytes_accessed=8 * tokens * head_dim,
            transcendentals=pairs_seen,
        ),
    )(here, *packed, *grads)
    value_back = exchange(value_grads)

    results = pl.pallas_call(
        partial(query_grad_kernel, factor, scale, count),
        out_shape=(*buffers(2 * rows), *buffers(rows + owned)),
        in_specs=[smem] + [vmem] * (3 * count + 2),
        out_specs=(vmem,) * (2 * count),
        scratch_shapes=[scratch(jnp.bfloat16)] * 4
        + id_scratch
        + total_scratch
        + [scratch(jnp.bfloat16), pltpu.VMEM((2 * count, rows, head_dim), jnp.bfloat16)],
        compiler_params=params,
        cost_estimate=pl.CostEstimate(
            flops=10 * pairs_seen * head_dim,
            bytes_accessed=14 * tokens * head_dim,
            transcendentals=pairs_seen,
        ),
    )(here, *packed, *valued, *grads, lse, cluster_rank.reshape(1, clusters))
    back = exchange(results[:count])
    returned = exchange(results[count:])

    def input_part(pick, kept_type):
        def rows_of(first):
            return lambda step, at: (jnp.where(at[1] == first, step, 0), 0)

        return pl.pallas_call(
            partial(input_kernel, count),
            out_shape=jax.ShapeDtypeStruct((rows, half), kept_type),
            grid_spec=pltpu.PrefetchScalarGridSpec(
                num_scalar_prefetch=1,
                grid=(half // wide,),
                in_specs=[pl.BlockSpec((2 * rows, head_dim), lambda step, at: (0, 0))] * count
                + [pl.BlockSpec((rows, head_dim), lambda step, at: (0, 0))] * count
                + [pl.BlockSpec((wide, width), rows_of(0))] * 3
                + [pl.BlockSpec((wide, width), rows_of(1))] * 3,
                out_specs=pl.BlockSpec((rows, wide), lambda step, at: (0, step)),
                scratch_shapes=[pltpu.VMEM((rows, 3 * width), jnp.bfloat16)],
            ),
            compiler_params=params,
            cost_estimate=pl.CostEstimate(
                flops=6 * rows * half * width, bytes_accessed=10 * half * width, transcendentals=0
            ),
        )(jnp.stack([place, pick]), *back, *value_back, *own, *other)

    crossed = (side != lax.axis_index("head")).astype(jnp.int32)
    arrived = lax.ppermute(input_part(1 - crossed, jnp.bfloat16), "head", swap)
    kept = input_part(crossed, jnp.float32)
    attended, centroid_sums = pl.pallas_call(
        partial(finish_kernel, count),
        out_shape=(
            jax.ShapeDtypeStruct((rows, width), jnp.bfloat16),
            jax.ShapeDtypeStruct((count, owned, head_dim), jnp.float32),
        ),
        in_specs=[smem] + [vmem] * count,
        out_specs=(vmem, vmem),
        compiler_params=params,
    )(here, *returned)
    d_hidden = (kept + arrived.astype(jnp.float32)).astype(jnp.bfloat16)
    return (attended, d_hidden, centroid_sums)


def per_device(hidden, w_query, w_key, w_value, cluster_rank, assign, d_attended):
    owners = lax.axis_size("seq") * lax.axis_size("sub")
    halves = lax.axis_size("sub") == 2 and lax.axis_size("head") == 2
    paired = owners & (owners - 1) == 0
    plan = by_head if assign.shape[0] == owners and halves and paired else by_owner
    return plan(hidden, w_query, w_key, w_value, cluster_rank, assign, d_attended)


def solution(mesh):
    placed = (
        P(("groups", "seq", "sub"), None),
        P("sub", "head"),
        P("sub", "head"),
        P("sub", "head"),
        P("groups"),
        P("head", ("groups", "seq", "sub")),
        P(("groups", "seq", "sub"), "head"),
    )
    return jax.shard_map(
        per_device,
        mesh=mesh,
        in_specs=placed,
        out_specs=(
            P(("groups", "seq", "sub"), "head"),
            P(("groups", "seq", "sub"), "head"),
            P("head", ("groups", "seq", "sub"), None),
        ),
        check_vma=False,
    )
```

```python
from functools import partial

import jax
import jax.numpy as jnp
from jax import lax
from jax.experimental import pallas as pl
from jax.experimental.pallas import tpu as pltpu
from jax.sharding import PartitionSpec as P

epsilon = 1e-06


def keep_mask(filled, cluster_ids, positions):
    count = filled.shape[0]
    same = filled[:, None] & filled[None, :] & (cluster_ids[:, None] == cluster_ids[None, :])
    causal = positions[None, :] <= positions[:, None]
    diagonal = jnp.arange(count)[:, None] == jnp.arange(count)[None, :]
    return same & causal | diagonal


def head_forward(packed, scale):
    queries, keys_in, values, filled, cluster_ids, positions = packed
    scores = (
        lax.dot_general(
            queries, keys_in, (((1,), (1,)), ((), ())), preferred_element_type=jnp.float32
        )
        * scale
    )
    allowed = keep_mask(filled, cluster_ids, positions)
    row_top = jnp.max(jnp.where(allowed, scores, -jnp.inf), axis=1)
    expd = jnp.where(allowed, jnp.exp(scores - row_top[:, None]), 0.0)
    row_total = jnp.sum(expd, axis=1)
    probs_low = (expd / row_total[:, None]).astype(jnp.bfloat16)
    outputs = jnp.dot(probs_low, values, preferred_element_type=jnp.float32).astype(jnp.bfloat16)
    return (outputs, row_top, row_total)


def head_backward(packed, scale):
    queries, keys_in, values, grads_in, filled, cluster_ids, positions, row_top, row_total = packed
    contract_last = (((1,), (1,)), ((), ()))
    contract_first = (((0,), (0,)), ((), ()))
    scores = (
        lax.dot_general(queries, keys_in, contract_last, preferred_element_type=jnp.float32) * scale
    )
    allowed = keep_mask(filled, cluster_ids, positions)
    probs = jnp.where(allowed, jnp.exp(scores - row_top[:, None]), 0.0) / row_total[:, None]
    probs_low = probs.astype(jnp.bfloat16)
    grad_probs = lax.dot_general(
        grads_in, values, contract_last, preferred_element_type=jnp.float32
    )
    delta_rows = jnp.sum(probs * grad_probs, axis=1)
    grad_low = (probs * (grad_probs - delta_rows[:, None]) * scale).astype(jnp.bfloat16)
    grad_query = jnp.dot(grad_low, keys_in, preferred_element_type=jnp.float32).astype(jnp.bfloat16)
    grad_key = lax.dot_general(
        grad_low, queries, contract_first, preferred_element_type=jnp.float32
    ).astype(jnp.bfloat16)
    grad_value = lax.dot_general(
        probs_low, grads_in, contract_first, preferred_element_type=jnp.float32
    ).astype(jnp.bfloat16)
    return (grad_query, grad_key, grad_value)


def by_owner(hidden, w_query, w_key, w_value, cluster_rank, assign, d_attended):
    tok_rows = hidden.shape[0]
    heads_here = assign.shape[0]
    head_dim = w_query.shape[1] // heads_here
    clusters = cluster_rank.shape[0]
    seq_count = lax.axis_size("seq")
    sub_count = lax.axis_size("sub")
    owners = seq_count * sub_count
    capacity = 2 * tok_rows // owners
    slot_count = owners * capacity
    per_owner = clusters // owners
    scale = head_dim ** (-0.5)
    pieces = (
        lax.all_gather(w_query, "sub", axis=0, tiled=True),
        lax.all_gather(w_key, "sub", axis=0, tiled=True),
        lax.all_gather(w_value, "sub", axis=0, tiled=True),
    )
    projected = tuple(
        (
            jnp.dot(hidden, weight_piece, preferred_element_type=jnp.float32)
            for weight_piece in pieces
        )
    )

    def split_heads(matrix):
        return (
            matrix.astype(jnp.bfloat16).reshape(tok_rows, heads_here, head_dim).transpose(1, 0, 2)
        )

    queries, keys_all, values = tuple((split_heads(matrix) for matrix in projected))
    cluster_range = jnp.arange(clusters, dtype=jnp.int32)
    rank_tok = jnp.sum(jnp.where(assign[:, :, None] == cluster_range, cluster_rank, 0), axis=2)
    owner_ids = rank_tok // per_owner
    owner_hot = (owner_ids[:, :, None] == jnp.arange(owners, dtype=jnp.int32)).astype(jnp.int32)
    within = jnp.sum(owner_hot * (jnp.cumsum(owner_hot, axis=1) - 1), axis=2)
    slot_tok = owner_ids * capacity + within
    token_ids = jnp.arange(tok_rows, dtype=jnp.int32)
    slot_range = jnp.arange(slot_count, dtype=jnp.int32)
    slot_match = slot_tok[:, None, :] == slot_range[None, :, None]
    slot_hot = slot_match.astype(jnp.bfloat16)

    def to_slots(rows_in):
        kept = jnp.einsum(
            "hst,htd->hsd", slot_hot, rows_in, preferred_element_type=jnp.float32
        ).astype(jnp.bfloat16)
        return kept.reshape(heads_here, owners, capacity, head_dim)

    def from_slots(slotted):
        flat_slots = slotted.reshape(heads_here, slot_count, head_dim)
        return jnp.einsum(
            "hst,hsd->htd", slot_hot, flat_slots, preferred_element_type=jnp.float32
        ).astype(jnp.bfloat16)

    def exchange_three(first, second, third):
        return (
            lax.all_to_all(first, ("seq", "sub"), split_axis=1, concat_axis=1, tiled=True),
            lax.all_to_all(second, ("seq", "sub"), split_axis=1, concat_axis=1, tiled=True),
            lax.all_to_all(third, ("seq", "sub"), split_axis=1, concat_axis=1, tiled=True),
        )

    sent = exchange_three(to_slots(queries), to_slots(keys_all), to_slots(values))
    tag_tok = assign * tok_rows + token_ids
    slot_tag = jnp.sum(jnp.where(slot_match, tag_tok[:, None, :] + 1, 0), axis=2) - 1
    tags = lax.all_to_all(
        slot_tag.reshape(heads_here, owners, capacity),
        ("seq", "sub"),
        split_axis=1,
        concat_axis=1,
        tiled=True,
    )
    tags = tags.reshape(heads_here, slot_count)
    owner_q, owner_k, owner_v = tuple(
        (member.reshape(heads_here, slot_count, head_dim) for member in sent)
    )
    filled = tags >= 0
    cluster_ids = jnp.where(filled, tags // tok_rows, -1)
    positions = slot_range // capacity * tok_rows + tags % tok_rows
    outputs, row_top, row_total = lax.map(
        partial(head_forward, scale=scale),
        (owner_q, owner_k, owner_v, filled, cluster_ids, positions),
    )
    returned = lax.all_to_all(
        outputs.reshape(heads_here, owners, capacity, head_dim),
        ("seq", "sub"),
        split_axis=1,
        concat_axis=1,
        tiled=True,
    )

    def merge_heads(slotted):
        return from_slots(slotted).transpose(1, 0, 2).reshape(tok_rows, heads_here * head_dim)

    attended = merge_heads(returned)
    grads_tok = d_attended.reshape(tok_rows, heads_here, head_dim).transpose(1, 0, 2)
    owner_g = lax.all_to_all(
        to_slots(grads_tok), ("seq", "sub"), split_axis=1, concat_axis=1, tiled=True
    ).reshape(heads_here, slot_count, head_dim)
    grad_q, grad_k, grad_v = lax.map(
        partial(head_backward, scale=scale),
        (owner_q, owner_k, owner_v, owner_g, filled, cluster_ids, positions, row_top, row_total),
    )
    shape_four = (heads_here, owners, capacity, head_dim)
    back = exchange_three(
        grad_q.reshape(shape_four), grad_k.reshape(shape_four), grad_v.reshape(shape_four)
    )
    token_grads = tuple((merge_heads(member) for member in back))
    pieces = lax.all_gather((w_query, w_key, w_value), "sub", axis=0, tiled=True)
    terms = [
        jnp.einsum("tc,rc->tr", grad_rows_in, weight_piece, preferred_element_type=jnp.float32)
        for grad_rows_in, weight_piece in zip(token_grads, pieces)
    ]
    partial_grad = terms[0] + terms[1] + terms[2]
    d_hidden = lax.psum_scatter(
        partial_grad.astype(jnp.bfloat16), "head", scatter_dimension=1, tiled=True
    )
    keys_float = keys_all.astype(jnp.float32)
    unit_keys = keys_float * lax.rsqrt(
        jnp.sum(keys_float * keys_float, axis=2, keepdims=True) + epsilon
    )
    member_hot = (rank_tok[:, :, None] == cluster_range).astype(jnp.float32)
    local_sums = jnp.einsum("htr,htd->hrd", member_hot, unit_keys, precision=lax.Precision.HIGHEST)
    centroid_sums = lax.psum_scatter(
        local_sums.astype(jnp.bfloat16), ("seq", "sub"), scatter_dimension=1, tiled=True
    ).astype(jnp.float32)
    return (attended, d_hidden, centroid_sums)


contract_last = (((1,), (1,)), ((), ()))
contract_first = (((0,), (0,)), ((), ()))
log2_e = 1.4426950408889634
vmem_bytes = 40 * 1024 * 1024


def pack_kernel(grads_ref, assign_ref, out_ref):
    count, padded, head_dim = out_ref.shape
    rows = grads_ref.shape[0]
    spare = padded - rows - rows // head_dim
    for device in range(count):
        head = device % 2 * (count // 2) + device // 2
        out_ref[device, :rows, :] = grads_ref[:, head * head_dim : (head + 1) * head_dim]
        ids = assign_ref[head : head + 1, :].astype(jnp.float32)
        lines = [
            ids[:, start : start + head_dim] for start in range(0, rows, head_dim)
        ] + [jnp.zeros((spare, head_dim), jnp.float32)]
        out_ref[device, rows:, :] = jnp.concatenate(lines, axis=0).astype(jnp.bfloat16)


def project_kernel(chips, place_ref, mine_ref, theirs_ref, *refs):
    weights, out_refs, hidden_ref = refs[:6], refs[6 : 6 + chips], refs[6 + chips]
    rows = mine_ref.shape[0]
    tall = 2 * rows
    half = weights[0].shape[0]
    head_dim = out_refs[0].shape[1]
    odd = place_ref[0] % 2
    side = place_ref[1]

    @pl.when(pl.program_id(0) == 0)
    def join():
        hidden_ref[pl.ds(pl.multiple_of(side * rows, rows), rows), :] = mine_ref[...]
        hidden_ref[pl.ds(pl.multiple_of((1 - side) * rows, rows), rows), :] = theirs_ref[...]

    near = hidden_ref[:, pl.ds(pl.multiple_of(side * half, half), half)]
    far = hidden_ref[:, pl.ds(pl.multiple_of((1 - side) * half, half), half)]
    for index in range(3):
        total = jnp.dot(near, weights[index][...], preferred_element_type=jnp.float32)
        total += jnp.dot(far, weights[3 + index][...], preferred_element_type=jnp.float32)
        low = total.astype(jnp.bfloat16)
        first = jnp.where(odd == 0, low[:, :head_dim], low[:, head_dim:])
        second = jnp.where(odd == 0, low[:, head_dim:], low[:, :head_dim])
        for pair in range(chips // 2):

            @pl.when(pl.program_id(0) == pair)
            def store(pair=pair, index=index, first=first, second=second):
                out_refs[2 * pair][index * tall : (index + 1) * tall, :] = first
                out_refs[2 * pair + 1][index * tall : (index + 1) * tall, :] = second


def attend_kernel(factor, scale, chips, place_ref, *refs):
    packed, grads_ref, rank_ref = refs[:chips], refs[chips], refs[chips + 1]
    back_refs, out_ref = refs[chips + 2 : 2 * chips + 2], refs[2 * chips + 2]
    queries, keys_in, values, ids_ref, dq_ref, dk_ref, dv_ref = refs[2 * chips + 3 :]
    place = place_ref[0]
    blocks = grads_ref.shape[0]
    tokens, head_dim = queries.shape
    rows = tokens // blocks
    tall = 2 * rows
    clusters = rank_ref.shape[1]
    owned = clusters // blocks
    for offset in range(chips):
        at = pl.ds(pl.multiple_of((place ^ offset) * tall, tall), tall)
        for index, held in enumerate((queries, keys_in, values)):
            held[at, :] = packed[offset][index * tall : (index + 1) * tall, :]
    id_rows = []
    for block in range(blocks):
        lines = grads_ref[block, rows : rows + 16, :].astype(jnp.float32)
        ids = jnp.concatenate([lines[at : at + 1, :] for at in range(rows // head_dim)], axis=1)
        id_rows.append(ids)
        ids_ref[block * rows : (block + 1) * rows, :] = jnp.broadcast_to(ids, (head_dim, rows)).T
    key_at = lax.broadcasted_iota(jnp.int32, (rows, rows), 0)
    query_at = lax.broadcasted_iota(jnp.int32, (rows, rows), 1)
    dk_ref[...] = jnp.zeros_like(dk_ref)
    dv_ref[...] = jnp.zeros_like(dv_ref)
    for block in range(blocks):
        seen = (block + 1) * rows
        seen_keys = keys_in[:seen, :]
        seen_values = values[:seen, :]
        query_rows = queries[block * rows : seen, :]
        grad_rows = grads_ref[block, :rows, :]
        scores = lax.dot_general(
            seen_keys, query_rows, contract_last, preferred_element_type=jnp.float32
        )
        grad_probs = lax.dot_general(
            seen_values, grad_rows, contract_last, preferred_element_type=jnp.float32
        )
        ids = ids_ref[:seen, :]
        same = jnp.concatenate(
            [
                ids == id_rows[block][:, start : start + head_dim]
                for start in range(0, rows, head_dim)
            ],
            axis=1,
        )
        last = same[seen - rows :] & (key_at <= query_at)
        allowed = last if block == 0 else jnp.concatenate([same[: seen - rows], last], axis=0)
        scores = jnp.where(allowed, scores * factor, -jnp.inf)
        top = jnp.max(scores, axis=0, keepdims=True)
        expd = jnp.exp2(scores - top)
        total = jnp.sum(expd, axis=0, keepdims=True)
        probs = expd * (1.0 / total)
        weighted = probs * grad_probs
        delta = jnp.sum(weighted, axis=0, keepdims=True)
        grad_low = (weighted - probs * delta).astype(jnp.bfloat16)
        probs_low = probs.astype(jnp.bfloat16)
        flipped = lax.dot_general(
            seen_values, probs_low, contract_first, preferred_element_type=jnp.float32
        )
        out_ref[block, :rows, :] = flipped.T.astype(jnp.bfloat16)
        dv_ref[:seen, :] += jnp.dot(probs_low, grad_rows, preferred_element_type=jnp.float32)
        dk_ref[:seen, :] += jnp.dot(grad_low, query_rows, preferred_element_type=jnp.float32)
        flipped = lax.dot_general(
            seen_keys, grad_low, contract_first, preferred_element_type=jnp.float32
        )
        dq_ref[block * rows : seen, :] = (flipped.T * scale).astype(jnp.bfloat16)
    for offset in range(chips):
        at = pl.ds(pl.multiple_of((place ^ offset) * tall, tall), tall)
        back_refs[offset][:tall, :] = dq_ref[at, :]
        back_refs[offset][tall : 2 * tall, :] = (dk_ref[at, :] * scale).astype(jnp.bfloat16)
        back_refs[offset][2 * tall :, :] = dv_ref[at, :].astype(jnp.bfloat16)
    sums = jnp.zeros((clusters, head_dim), jnp.float32)
    cluster_at = lax.broadcasted_iota(jnp.int32, (clusters, rows), 0).astype(jnp.float32)
    for block in range(blocks):
        keys_float = keys_in[block * rows : (block + 1) * rows, :].astype(jnp.float32)
        unit = keys_float * lax.rsqrt(
            jnp.sum(keys_float * keys_float, axis=1, keepdims=True) + epsilon
        )
        unit_high = unit.astype(jnp.bfloat16)
        unit_low = (unit - unit_high.astype(jnp.float32)).astype(jnp.bfloat16)
        member = jnp.where(cluster_at == id_rows[block], 1.0, 0.0).astype(jnp.bfloat16)
        sums += jnp.dot(member, unit_high, preferred_element_type=jnp.float32)
        sums += jnp.dot(member, unit_low, preferred_element_type=jnp.float32)
    rank_at = lax.broadcasted_iota(jnp.int32, (clusters, clusters), 0)
    ordered = jnp.where(rank_at == rank_ref[...], 1.0, 0.0).astype(jnp.bfloat16)
    ranked = jnp.dot(ordered, sums.astype(jnp.bfloat16), preferred_element_type=jnp.float32)
    out_ref[:, rows:, :] = ranked.astype(jnp.bfloat16).reshape(blocks, owned, head_dim)


def input_kernel(chips, place_ref, *refs):
    parts, weights = refs[:chips], refs[chips : chips + 6]
    out_ref, gathered_ref = refs[chips + 6 :]
    rows = out_ref.shape[0]
    head_dim = parts[0].shape[1]
    width = chips * head_dim
    steps = pl.num_programs(0) // 2

    @pl.when(pl.program_id(0) == 0)
    def gather():
        for offset in range(chips):
            at = (place_ref[0] ^ offset) * head_dim
            for index in range(3):
                start = pl.multiple_of(index * width + at, head_dim)
                first = pl.multiple_of((2 * index + place_ref[2]) * rows, rows)
                gathered_ref[:, pl.ds(start, head_dim)] = parts[offset][pl.ds(first, rows), :]

    def multiply(first):
        total = None
        for index in range(3):
            term = lax.dot_general(
                gathered_ref[:, index * width : (index + 1) * width],
                weights[first + index][...],
                contract_last,
                preferred_element_type=jnp.float32,
            )
            total = term if total is None else total + term
        out_ref[...] = total.astype(out_ref.dtype)

    mine = pl.program_id(0) // steps == place_ref[1]
    pl.when(mine)(lambda: multiply(0))
    pl.when(jnp.logical_not(mine))(lambda: multiply(3))


def cross_kernel(place_ref, mine_ref, theirs_ref, out_ref):
    out_ref[...] = (mine_ref[...] + theirs_ref[...].astype(jnp.float32)).astype(jnp.bfloat16)


def finish_kernel(place_ref, mine_ref, theirs_ref, crossed_ref, returned_ref, hidden_ref, attended_ref, sums_ref):
    total = mine_ref[...] + theirs_ref[...].astype(jnp.float32)
    hidden_ref[...] = (total + crossed_ref[...].astype(jnp.float32)).astype(jnp.bfloat16)
    rows = attended_ref.shape[0]
    count, owned, head_dim = sums_ref.shape
    for device in range(count):
        head = device % 2 * (count // 2) + device // 2
        attended_ref[:, head * head_dim : (head + 1) * head_dim] = returned_ref[device, :rows, :]
        sums_ref[head] = returned_ref[device, rows:, :].astype(jnp.float32)


def by_head(hidden, w_query, w_key, w_value, cluster_rank, assign, d_attended):
    rows = hidden.shape[0]
    count = assign.shape[0]
    chips = count // 2
    half, width = w_query.shape
    head_dim = width // count
    tokens = count * rows
    clusters = cluster_rank.shape[0]
    owned = clusters // count
    scale = head_dim ** (-0.5)
    factor = scale * log2_e
    line = ("seq", "sub")
    smem = pl.BlockSpec(memory_space=pltpu.SMEM)
    vmem = pl.BlockSpec(memory_space=pltpu.VMEM)
    params = pltpu.CompilerParams(vmem_limit_bytes=vmem_bytes)
    pairs_seen = tokens * (tokens + rows) // 2
    wide = 2 * head_dim
    swap = [(0, 1), (1, 0)]
    chip, side, column = (lax.axis_index(name) for name in ("seq", "sub", "head"))
    place = jnp.stack([chip, side, side, column])
    place_sibling = jnp.stack([chip, side, 1 - side, column])

    def whole(array):
        return pl.BlockSpec(array.shape, lambda step, at: (0,) * len(array.shape))

    def exchange(packed):
        return lax.all_to_all(packed, line, split_axis=0, concat_axis=0, tiled=True)

    def exchange_chips(parts):
        moved = {
            offset: lax.ppermute(parts[offset], "seq", [(at, at ^ offset) for at in range(chips)])
            for offset in (2, 3, 1)
        }
        return (parts[0], moved[1], moved[2], moved[3])

    def buffers(height):
        return (jax.ShapeDtypeStruct((height, head_dim), jnp.bfloat16),) * chips

    hidden_other = lax.ppermute(hidden, "sub", swap)
    own = (w_query, w_key, w_value)
    other = tuple(lax.ppermute(piece, "sub", swap) for piece in own)

    id_height = -(-(rows // head_dim) // 16) * 16
    grads = exchange(
        pl.pallas_call(
            pack_kernel,
            out_shape=jax.ShapeDtypeStruct((count, rows + id_height, head_dim), jnp.bfloat16),
            in_specs=[vmem] * 2,
            out_specs=vmem,
            compiler_params=params,
        )(d_attended, assign)
    )

    projected = pl.pallas_call(
        partial(project_kernel, chips),
        out_shape=buffers(6 * rows),
        grid_spec=pltpu.PrefetchScalarGridSpec(
            num_scalar_prefetch=1,
            grid=(chips // 2,),
            in_specs=[whole(hidden)] * 2
            + [
                pl.BlockSpec(
                    (half, wide), lambda step, at: (0, at[1] * (chips // 2) + ((at[0] // 2) ^ step))
                )
            ]
            * 6,
            out_specs=[pl.BlockSpec((6 * rows, head_dim), lambda step, at: (0, 0))] * chips,
            scratch_shapes=[pltpu.VMEM((2 * rows, 2 * half), jnp.bfloat16)],
        ),
        compiler_params=params,
        cost_estimate=pl.CostEstimate(
            flops=12 * rows * half * width, bytes_accessed=8 * half * width, transcendentals=0
        ),
    )(place, hidden, hidden_other, *own, *other)
    packed = exchange_chips(projected)

    *grads_out, outputs = pl.pallas_call(
        partial(attend_kernel, factor, scale, chips),
        out_shape=(
            *buffers(6 * rows),
            jax.ShapeDtypeStruct((count, rows + owned, head_dim), jnp.bfloat16),
        ),
        in_specs=[smem] + [vmem] * (chips + 2),
        out_specs=(vmem,) * (chips + 1),
        scratch_shapes=[pltpu.VMEM((tokens, head_dim), jnp.bfloat16)] * 3
        + [pltpu.VMEM((tokens, head_dim), jnp.float32)]
        + [pltpu.VMEM((tokens, head_dim), jnp.bfloat16)]
        + [pltpu.VMEM((tokens, head_dim), jnp.float32)] * 2,
        compiler_params=params,
        cost_estimate=pl.CostEstimate(
            flops=12 * pairs_seen * head_dim,
            bytes_accessed=16 * tokens * head_dim,
            transcendentals=pairs_seen,
        ),
    )(place, *packed, grads, cluster_rank.reshape(1, clusters))
    back = exchange_chips(grads_out)

    steps = half // wide

    def input_part(at, kind):
        def rows_of(first):
            return lambda step, at: (
                jnp.where((step // steps == at[1]) == first, step % steps, 0),
                at[1],
            )

        return pl.pallas_call(
            partial(input_kernel, chips),
            out_shape=jax.ShapeDtypeStruct((rows, 2 * half), kind),
            grid_spec=pltpu.PrefetchScalarGridSpec(
                num_scalar_prefetch=1,
                grid=(2 * steps,),
                in_specs=[whole(back[0])] * chips
                + [pl.BlockSpec((wide, width // 2), rows_of(True))] * 3
                + [pl.BlockSpec((wide, width // 2), rows_of(False))] * 3,
                out_specs=pl.BlockSpec((rows, wide), lambda step, at: (0, step)),
                scratch_shapes=[pltpu.VMEM((rows, 3 * width // 2), jnp.bfloat16)],
            ),
            compiler_params=params,
            cost_estimate=pl.CostEstimate(
                flops=6 * rows * half * width, bytes_accessed=10 * half * width, transcendentals=0
            ),
        )(at, *back, *own, *other)

    theirs = lax.ppermute(input_part(place_sibling, jnp.bfloat16), "sub", swap)
    mine = input_part(place, jnp.float32)

    def half_of(pick):
        return pl.BlockSpec((rows, half), lambda step, at: (0, pick(at)))

    crossing = pl.pallas_call(
        cross_kernel,
        out_shape=jax.ShapeDtypeStruct((rows, half), jnp.bfloat16),
        grid_spec=pltpu.PrefetchScalarGridSpec(
            num_scalar_prefetch=1,
            grid=(1,),
            in_specs=[half_of(lambda at: 1 - at[3])] * 2,
            out_specs=pl.BlockSpec((rows, half), lambda step, at: (0, 0)),
        ),
        compiler_params=params,
    )(place, mine, theirs)
    crossed = lax.ppermute(crossing, "head", swap)
    outputs, _ = lax.optimization_barrier((outputs, back[1]))
    returned = exchange(outputs)
    d_hidden, attended, centroid_sums = pl.pallas_call(
        finish_kernel,
        out_shape=(
            jax.ShapeDtypeStruct((rows, half), jnp.bfloat16),
            jax.ShapeDtypeStruct((rows, width), jnp.bfloat16),
            jax.ShapeDtypeStruct((count, owned, head_dim), jnp.float32),
        ),
        grid_spec=pltpu.PrefetchScalarGridSpec(
            num_scalar_prefetch=1,
            grid=(1,),
            in_specs=[half_of(lambda at: at[3])] * 2 + [whole(crossed), whole(returned)],
            out_specs=(
                pl.BlockSpec((rows, half), lambda step, at: (0, 0)),
                pl.BlockSpec((rows, width), lambda step, at: (0, 0)),
                pl.BlockSpec((count, owned, head_dim), lambda step, at: (0, 0, 0)),
            ),
        ),
        compiler_params=params,
    )(place, mine, theirs, crossed, returned)
    return (attended, d_hidden, centroid_sums)


def per_device(hidden, w_query, w_key, w_value, cluster_rank, assign, d_attended):
    chips = lax.axis_size("seq")
    fits = chips == 4 and lax.axis_size("sub") == 2 and lax.axis_size("head") == 2
    plan = by_head if fits and assign.shape[0] == 2 * chips else by_owner
    return plan(hidden, w_query, w_key, w_value, cluster_rank, assign, d_attended)


def solution(mesh):
    placed = (
        P(("groups", "seq", "sub"), None),
        P("sub", "head"),
        P("sub", "head"),
        P("sub", "head"),
        P("groups"),
        P("head", ("groups", "seq", "sub")),
        P(("groups", "seq", "sub"), "head"),
    )
    return jax.shard_map(
        per_device,
        mesh=mesh,
        in_specs=placed,
        out_specs=(
            P(("groups", "seq", "sub"), "head"),
            P(("groups", "seq", "sub"), "head"),
            P("head", ("groups", "seq", "sub"), None),
        ),
        check_vma=False,
    )
```

```python
from functools import partial

import jax
import jax.numpy as jnp
from jax import lax
from jax.experimental import pallas as pl
from jax.experimental.pallas import tpu as pltpu
from jax.sharding import PartitionSpec as P

epsilon = 1e-06


def keep_mask(filled, cluster_ids, positions):
    count = filled.shape[0]
    same = filled[:, None] & filled[None, :] & (cluster_ids[:, None] == cluster_ids[None, :])
    causal = positions[None, :] <= positions[:, None]
    diagonal = jnp.arange(count)[:, None] == jnp.arange(count)[None, :]
    return same & causal | diagonal


def head_forward(packed, scale):
    queries, keys_in, values, filled, cluster_ids, positions = packed
    scores = (
        lax.dot_general(
            queries, keys_in, (((1,), (1,)), ((), ())), preferred_element_type=jnp.float32
        )
        * scale
    )
    allowed = keep_mask(filled, cluster_ids, positions)
    row_top = jnp.max(jnp.where(allowed, scores, -jnp.inf), axis=1)
    expd = jnp.where(allowed, jnp.exp(scores - row_top[:, None]), 0.0)
    row_total = jnp.sum(expd, axis=1)
    probs_low = (expd / row_total[:, None]).astype(jnp.bfloat16)
    outputs = jnp.dot(probs_low, values, preferred_element_type=jnp.float32).astype(jnp.bfloat16)
    return (outputs, row_top, row_total)


def head_backward(packed, scale):
    queries, keys_in, values, grads_in, filled, cluster_ids, positions, row_top, row_total = packed
    contract_last = (((1,), (1,)), ((), ()))
    contract_first = (((0,), (0,)), ((), ()))
    scores = (
        lax.dot_general(queries, keys_in, contract_last, preferred_element_type=jnp.float32) * scale
    )
    allowed = keep_mask(filled, cluster_ids, positions)
    probs = jnp.where(allowed, jnp.exp(scores - row_top[:, None]), 0.0) / row_total[:, None]
    probs_low = probs.astype(jnp.bfloat16)
    grad_probs = lax.dot_general(
        grads_in, values, contract_last, preferred_element_type=jnp.float32
    )
    delta_rows = jnp.sum(probs * grad_probs, axis=1)
    grad_low = (probs * (grad_probs - delta_rows[:, None]) * scale).astype(jnp.bfloat16)
    grad_query = jnp.dot(grad_low, keys_in, preferred_element_type=jnp.float32).astype(jnp.bfloat16)
    grad_key = lax.dot_general(
        grad_low, queries, contract_first, preferred_element_type=jnp.float32
    ).astype(jnp.bfloat16)
    grad_value = lax.dot_general(
        probs_low, grads_in, contract_first, preferred_element_type=jnp.float32
    ).astype(jnp.bfloat16)
    return (grad_query, grad_key, grad_value)


def by_owner(hidden, w_query, w_key, w_value, cluster_rank, assign, d_attended):
    tok_rows = hidden.shape[0]
    heads_here = assign.shape[0]
    head_dim = w_query.shape[1] // heads_here
    clusters = cluster_rank.shape[0]
    seq_count = lax.axis_size("seq")
    sub_count = lax.axis_size("sub")
    owners = seq_count * sub_count
    capacity = 2 * tok_rows // owners
    slot_count = owners * capacity
    per_owner = clusters // owners
    scale = head_dim ** (-0.5)
    pieces = (
        lax.all_gather(w_query, "sub", axis=0, tiled=True),
        lax.all_gather(w_key, "sub", axis=0, tiled=True),
        lax.all_gather(w_value, "sub", axis=0, tiled=True),
    )
    projected = tuple(
        (
            jnp.dot(hidden, weight_piece, preferred_element_type=jnp.float32)
            for weight_piece in pieces
        )
    )

    def split_heads(matrix):
        return (
            matrix.astype(jnp.bfloat16).reshape(tok_rows, heads_here, head_dim).transpose(1, 0, 2)
        )

    queries, keys_all, values = tuple((split_heads(matrix) for matrix in projected))
    cluster_range = jnp.arange(clusters, dtype=jnp.int32)
    rank_tok = jnp.sum(jnp.where(assign[:, :, None] == cluster_range, cluster_rank, 0), axis=2)
    owner_ids = rank_tok // per_owner
    owner_hot = (owner_ids[:, :, None] == jnp.arange(owners, dtype=jnp.int32)).astype(jnp.int32)
    within = jnp.sum(owner_hot * (jnp.cumsum(owner_hot, axis=1) - 1), axis=2)
    slot_tok = owner_ids * capacity + within
    token_ids = jnp.arange(tok_rows, dtype=jnp.int32)
    slot_range = jnp.arange(slot_count, dtype=jnp.int32)
    slot_match = slot_tok[:, None, :] == slot_range[None, :, None]
    slot_hot = slot_match.astype(jnp.bfloat16)

    def to_slots(rows_in):
        kept = jnp.einsum(
            "hst,htd->hsd", slot_hot, rows_in, preferred_element_type=jnp.float32
        ).astype(jnp.bfloat16)
        return kept.reshape(heads_here, owners, capacity, head_dim)

    def from_slots(slotted):
        flat_slots = slotted.reshape(heads_here, slot_count, head_dim)
        return jnp.einsum(
            "hst,hsd->htd", slot_hot, flat_slots, preferred_element_type=jnp.float32
        ).astype(jnp.bfloat16)

    def exchange_three(first, second, third):
        return (
            lax.all_to_all(first, ("seq", "sub"), split_axis=1, concat_axis=1, tiled=True),
            lax.all_to_all(second, ("seq", "sub"), split_axis=1, concat_axis=1, tiled=True),
            lax.all_to_all(third, ("seq", "sub"), split_axis=1, concat_axis=1, tiled=True),
        )

    sent = exchange_three(to_slots(queries), to_slots(keys_all), to_slots(values))
    tag_tok = assign * tok_rows + token_ids
    slot_tag = jnp.sum(jnp.where(slot_match, tag_tok[:, None, :] + 1, 0), axis=2) - 1
    tags = lax.all_to_all(
        slot_tag.reshape(heads_here, owners, capacity),
        ("seq", "sub"),
        split_axis=1,
        concat_axis=1,
        tiled=True,
    )
    tags = tags.reshape(heads_here, slot_count)
    owner_q, owner_k, owner_v = tuple(
        (member.reshape(heads_here, slot_count, head_dim) for member in sent)
    )
    filled = tags >= 0
    cluster_ids = jnp.where(filled, tags // tok_rows, -1)
    positions = slot_range // capacity * tok_rows + tags % tok_rows
    outputs, row_top, row_total = lax.map(
        partial(head_forward, scale=scale),
        (owner_q, owner_k, owner_v, filled, cluster_ids, positions),
    )
    returned = lax.all_to_all(
        outputs.reshape(heads_here, owners, capacity, head_dim),
        ("seq", "sub"),
        split_axis=1,
        concat_axis=1,
        tiled=True,
    )

    def merge_heads(slotted):
        return from_slots(slotted).transpose(1, 0, 2).reshape(tok_rows, heads_here * head_dim)

    attended = merge_heads(returned)
    grads_tok = d_attended.reshape(tok_rows, heads_here, head_dim).transpose(1, 0, 2)
    owner_g = lax.all_to_all(
        to_slots(grads_tok), ("seq", "sub"), split_axis=1, concat_axis=1, tiled=True
    ).reshape(heads_here, slot_count, head_dim)
    grad_q, grad_k, grad_v = lax.map(
        partial(head_backward, scale=scale),
        (owner_q, owner_k, owner_v, owner_g, filled, cluster_ids, positions, row_top, row_total),
    )
    shape_four = (heads_here, owners, capacity, head_dim)
    back = exchange_three(
        grad_q.reshape(shape_four), grad_k.reshape(shape_four), grad_v.reshape(shape_four)
    )
    token_grads = tuple((merge_heads(member) for member in back))
    pieces = lax.all_gather((w_query, w_key, w_value), "sub", axis=0, tiled=True)
    terms = [
        jnp.einsum("tc,rc->tr", grad_rows_in, weight_piece, preferred_element_type=jnp.float32)
        for grad_rows_in, weight_piece in zip(token_grads, pieces)
    ]
    partial_grad = terms[0] + terms[1] + terms[2]
    d_hidden = lax.psum_scatter(
        partial_grad.astype(jnp.bfloat16), "head", scatter_dimension=1, tiled=True
    )
    keys_float = keys_all.astype(jnp.float32)
    unit_keys = keys_float * lax.rsqrt(
        jnp.sum(keys_float * keys_float, axis=2, keepdims=True) + epsilon
    )
    member_hot = (rank_tok[:, :, None] == cluster_range).astype(jnp.float32)
    local_sums = jnp.einsum("htr,htd->hrd", member_hot, unit_keys, precision=lax.Precision.HIGHEST)
    centroid_sums = lax.psum_scatter(
        local_sums.astype(jnp.bfloat16), ("seq", "sub"), scatter_dimension=1, tiled=True
    ).astype(jnp.float32)
    return (attended, d_hidden, centroid_sums)


contract_last = (((1,), (1,)), ((), ()))
contract_first = (((0,), (0,)), ((), ()))
log2_e = 1.4426950408889634
mebi = 1024 * 1024


def pack_kernel(grads_ref, assign_ref, out_ref):
    count, padded, head_dim = out_ref.shape
    rows = grads_ref.shape[0]
    spare = padded - rows - rows // head_dim
    for device in range(count):
        head = device % 2 * (count // 2) + device // 2
        out_ref[device, :rows, :] = grads_ref[:, head * head_dim : (head + 1) * head_dim]
        ids = assign_ref[head : head + 1, :].astype(jnp.float32)
        lines = [
            ids[:, start : start + head_dim] for start in range(0, rows, head_dim)
        ] + [jnp.zeros((spare, head_dim), jnp.float32)]
        out_ref[device, rows:, :] = jnp.concatenate(lines, axis=0).astype(jnp.bfloat16)


def join_rows(side, mine_ref, theirs_ref, start, joined_ref):
    rows, columns = mine_ref.shape[0], joined_ref.shape[1]
    at = pl.ds(pl.multiple_of(start, columns), columns)
    joined_ref[pl.ds(pl.multiple_of(side * rows, rows), rows), :] = mine_ref[:, at]
    joined_ref[pl.ds(pl.multiple_of((1 - side) * rows, rows), rows), :] = theirs_ref[:, at]


def fetch_columns(side, weights, held_ref, sems):
    columns = held_ref.shape[2]
    at = pl.ds(pl.multiple_of(side * columns, columns), columns)
    copies = [
        pltpu.make_async_copy(weight.at[:, at], held_ref.at[index], sems.at[index])
        for index, weight in enumerate(weights)
    ]
    for copy in copies:
        copy.start()
    return copies


def near_kernel(place_ref, mine_ref, theirs_ref, *refs):
    weights, out_ref, joined_ref, held_ref, sems = refs[:3], *refs[3:]
    side = place_ref[1]
    copies = fetch_columns(side, weights, held_ref, sems)
    join_rows(side, mine_ref, theirs_ref, side * joined_ref.shape[1], joined_ref)
    for index, copy in enumerate(copies):
        copy.wait()
        out_ref[index] = jnp.dot(
            joined_ref[...], held_ref[index], preferred_element_type=jnp.float32
        )


def far_kernel(place_ref, mine_ref, theirs_ref, near_ref, *refs):
    weights, refs = refs[:3], refs[3:]
    out_refs, (joined_ref, held_ref, low_ref, sems) = refs[:-4], refs[-4:]
    chips = len(out_refs)
    tall, head_dim = joined_ref.shape[0], out_refs[0].shape[1]
    side = place_ref[1]
    copies = fetch_columns(side, weights, held_ref, sems)
    join_rows(side, mine_ref, theirs_ref, (1 - side) * joined_ref.shape[1], joined_ref)
    for index, copy in enumerate(copies):
        copy.wait()
        total = near_ref[index] + jnp.dot(
            joined_ref[...], held_ref[index], preferred_element_type=jnp.float32
        )
        low_ref[...] = total.astype(jnp.bfloat16)
        for offset in range(chips):
            at = pl.multiple_of((place_ref[0] ^ offset) * head_dim, head_dim)
            out_refs[offset][index * tall : (index + 1) * tall, :] = low_ref[:, pl.ds(at, head_dim)]


def attend_kernel(factor, scale, chips, place_ref, *refs):
    packed, grads_ref, rank_ref = refs[:chips], refs[chips], refs[chips + 1]
    back_refs, out_ref = refs[chips + 2 : 3 * chips + 2], refs[3 * chips + 2]
    queries, keys_in, values, ids_ref, dq_ref, dk_ref, dv_ref = refs[3 * chips + 3 :]
    place, side = place_ref[0], place_ref[1]
    blocks = grads_ref.shape[0]
    tokens, head_dim = queries.shape
    rows = tokens // blocks
    tall = 2 * rows
    clusters = rank_ref.shape[1]
    owned = clusters // blocks
    for offset in range(chips):
        at = pl.ds(pl.multiple_of((place ^ offset) * tall, tall), tall)
        for index, held in enumerate((queries, keys_in, values)):
            held[at, :] = packed[offset][index * tall : (index + 1) * tall, :]
    id_rows = []
    for block in range(blocks):
        lines = grads_ref[block, rows : rows + 16, :].astype(jnp.float32)
        ids = jnp.concatenate([lines[at : at + 1, :] for at in range(rows // head_dim)], axis=1)
        id_rows.append(ids)
        ids_ref[block * rows : (block + 1) * rows, :] = jnp.broadcast_to(ids, (head_dim, rows)).T
    key_at = lax.broadcasted_iota(jnp.int32, (rows, rows), 0)
    query_at = lax.broadcasted_iota(jnp.int32, (rows, rows), 1)
    dk_ref[...] = jnp.zeros_like(dk_ref)
    dv_ref[...] = jnp.zeros_like(dv_ref)
    for block in range(blocks):
        seen = (block + 1) * rows
        seen_keys = keys_in[:seen, :]
        seen_values = values[:seen, :]
        query_rows = queries[block * rows : seen, :]
        grad_rows = grads_ref[block, :rows, :]
        scores = lax.dot_general(
            seen_keys, query_rows, contract_last, preferred_element_type=jnp.float32
        )
        grad_probs = lax.dot_general(
            seen_values, grad_rows, contract_last, preferred_element_type=jnp.float32
        )
        ids = ids_ref[:seen, :]
        same = jnp.concatenate(
            [
                ids == id_rows[block][:, start : start + head_dim]
                for start in range(0, rows, head_dim)
            ],
            axis=1,
        )
        last = same[seen - rows :] & (key_at <= query_at)
        allowed = last if block == 0 else jnp.concatenate([same[: seen - rows], last], axis=0)
        scores = jnp.where(allowed, scores * factor, -jnp.inf)
        top = jnp.max(scores, axis=0, keepdims=True)
        expd = jnp.exp2(scores - top)
        total = jnp.sum(expd, axis=0, keepdims=True)
        probs = expd * (1.0 / total)
        weighted = probs * grad_probs
        delta = jnp.sum(weighted, axis=0, keepdims=True)
        grad_low = (weighted - probs * delta).astype(jnp.bfloat16)
        probs_low = probs.astype(jnp.bfloat16)
        flipped = lax.dot_general(
            seen_values, probs_low, contract_first, preferred_element_type=jnp.float32
        )
        out_ref[block, :rows, :] = flipped.T.astype(jnp.bfloat16)
        dv_ref[:seen, :] += jnp.dot(probs_low, grad_rows, preferred_element_type=jnp.float32)
        dk_ref[:seen, :] += jnp.dot(grad_low, query_rows, preferred_element_type=jnp.float32)
        flipped = lax.dot_general(
            seen_keys, grad_low, contract_first, preferred_element_type=jnp.float32
        )
        dq_ref[block * rows : seen, :] = (flipped.T * scale).astype(jnp.bfloat16)
    for turn in range(2):
        for offset in range(chips):
            back_ref = back_refs[turn * chips + offset]
            shard = (place ^ offset) * 2 + (side ^ turn)
            at = pl.ds(pl.multiple_of(shard * rows, rows), rows)
            back_ref[:rows, :] = dq_ref[at, :]
            back_ref[rows : 2 * rows, :] = (dk_ref[at, :] * scale).astype(jnp.bfloat16)
            back_ref[2 * rows :, :] = dv_ref[at, :].astype(jnp.bfloat16)
    sums = jnp.zeros((clusters, head_dim), jnp.float32)
    cluster_at = lax.broadcasted_iota(jnp.int32, (clusters, rows), 0).astype(jnp.float32)
    for block in range(blocks):
        keys_float = keys_in[block * rows : (block + 1) * rows, :].astype(jnp.float32)
        unit = keys_float * lax.rsqrt(
            jnp.sum(keys_float * keys_float, axis=1, keepdims=True) + epsilon
        )
        unit_high = unit.astype(jnp.bfloat16)
        unit_low = (unit - unit_high.astype(jnp.float32)).astype(jnp.bfloat16)
        member = jnp.where(cluster_at == id_rows[block], 1.0, 0.0).astype(jnp.bfloat16)
        sums += jnp.dot(member, unit_high, preferred_element_type=jnp.float32)
        sums += jnp.dot(member, unit_low, preferred_element_type=jnp.float32)
    rank_at = lax.broadcasted_iota(jnp.int32, (clusters, clusters), 0)
    ordered = jnp.where(rank_at == rank_ref[...], 1.0, 0.0).astype(jnp.bfloat16)
    ranked = jnp.dot(ordered, sums.astype(jnp.bfloat16), preferred_element_type=jnp.float32)
    out_ref[:, rows:, :] = ranked.astype(jnp.bfloat16).reshape(blocks, owned, head_dim)


def input_kernel(place_ref, *refs):
    parts, weights, (out_ref, gathered_ref, held_ref, sems) = refs[:-10], refs[-10:-4], refs[-4:]
    chips = len(parts) // 2
    rows, width = out_ref.shape[0], held_ref.shape[2]
    head_dim = parts[0].shape[1]

    def fetch(first):
        for index in range(3):
            pltpu.make_async_copy(
                weights[first + index], held_ref.at[index], sems.at[index]
            ).start()

    pl.when(place_ref[2] == 0)(lambda: fetch(0))
    pl.when(place_ref[2] != 0)(lambda: fetch(3))
    for turn in range(2):
        for offset in range(chips):
            head = (place_ref[1] ^ turn) * chips + (place_ref[0] ^ offset)
            for index in range(3):
                start = pl.multiple_of(index * width + head * head_dim, head_dim)
                gathered_ref[:, pl.ds(start, head_dim)] = parts[turn * chips + offset][
                    index * rows : (index + 1) * rows, :
                ]
    flipped = None
    for index in range(3):
        pltpu.make_async_copy(weights[index], held_ref.at[index], sems.at[index]).wait()
        term = lax.dot_general(
            held_ref[index],
            gathered_ref[:, index * width : (index + 1) * width],
            contract_last,
            preferred_element_type=jnp.float32,
        )
        flipped = term if flipped is None else flipped + term
    out_ref[...] = flipped.T.astype(out_ref.dtype)


def finish_kernel(kept_ref, crossed_ref, returned_ref, hidden_ref, attended_ref, sums_ref):
    hidden_ref[...] = (kept_ref[...] + crossed_ref[...].astype(jnp.float32)).astype(jnp.bfloat16)
    rows = attended_ref.shape[0]
    count, owned, head_dim = sums_ref.shape
    for device in range(count):
        head = device % 2 * (count // 2) + device // 2
        attended_ref[:, head * head_dim : (head + 1) * head_dim] = returned_ref[device, :rows, :]
        sums_ref[head] = returned_ref[device, rows:, :].astype(jnp.float32)


def by_head(hidden, w_query, w_key, w_value, cluster_rank, assign, d_attended):
    rows = hidden.shape[0]
    count = assign.shape[0]
    chips = count // 2
    half, width = w_query.shape
    head_dim = width // count
    tokens = count * rows
    clusters = cluster_rank.shape[0]
    owned = clusters // count
    scale = head_dim ** (-0.5)
    factor = scale * log2_e
    line = ("seq", "sub")
    smem = pl.BlockSpec(memory_space=pltpu.SMEM)
    vmem = pl.BlockSpec(memory_space=pltpu.VMEM)
    anywhere = pl.BlockSpec(memory_space=pl.ANY)
    params = pltpu.CompilerParams(vmem_limit_bytes=32 * mebi)
    project_params = pltpu.CompilerParams(vmem_limit_bytes=56 * mebi)
    input_params = pltpu.CompilerParams(vmem_limit_bytes=58 * mebi)
    pairs_seen = tokens * (tokens + rows) // 2
    swap = [(0, 1), (1, 0)]
    chip, side, column = (lax.axis_index(name) for name in ("seq", "sub", "head"))
    crossed_over = (side != column).astype(jnp.int32)

    def exchange(packed):
        return lax.all_to_all(packed, line, split_axis=0, concat_axis=0, tiled=True)

    def exchange_chips(parts):
        moved = {
            offset: lax.ppermute(parts[offset], "seq", [(at, at ^ offset) for at in range(chips)])
            for offset in (2, 3, 1)
        }
        return (parts[0], moved[1], moved[2], moved[3])

    def buffers(height, number=chips):
        return (jax.ShapeDtypeStruct((height, head_dim), jnp.bfloat16),) * number

    hidden_other = lax.ppermute(hidden, "sub", swap)
    own = (w_query, w_key, w_value)
    other = tuple(lax.ppermute(piece, "sub", swap) for piece in own)

    id_height = -(-(rows // head_dim) // 16) * 16
    grads = exchange(
        pl.pallas_call(
            pack_kernel,
            out_shape=jax.ShapeDtypeStruct((count, rows + id_height, head_dim), jnp.bfloat16),
            in_specs=[vmem] * 2,
            out_specs=vmem,
            compiler_params=params,
        )(d_attended, assign)
    )

    place = jnp.stack([chip, side])
    project_scratch = [
        pltpu.VMEM((2 * rows, half), jnp.bfloat16),
        pltpu.VMEM((3, half, width // 2), jnp.bfloat16),
    ]
    project_cost = pl.CostEstimate(
        flops=6 * rows * half * width, bytes_accessed=8 * half * width, transcendentals=0
    )
    near = pl.pallas_call(
        near_kernel,
        out_shape=jax.ShapeDtypeStruct((3, 2 * rows, width // 2), jnp.float32),
        in_specs=[smem] + [vmem] * 2 + [anywhere] * 3,
        out_specs=vmem,
        scratch_shapes=project_scratch + [pltpu.SemaphoreType.DMA((3,))],
        compiler_params=project_params,
        cost_estimate=project_cost,
    )(place, hidden, hidden_other, *own)
    projected = pl.pallas_call(
        far_kernel,
        out_shape=buffers(6 * rows),
        in_specs=[smem] + [vmem] * 3 + [anywhere] * 3,
        out_specs=(vmem,) * chips,
        scratch_shapes=project_scratch
        + [
            pltpu.VMEM((2 * rows, width // 2), jnp.bfloat16),
            pltpu.SemaphoreType.DMA((3,)),
        ],
        compiler_params=project_params,
        cost_estimate=project_cost,
    )(place, hidden, hidden_other, near, *other)
    packed = exchange_chips(projected)

    *grads_out, outputs = pl.pallas_call(
        partial(attend_kernel, factor, scale, chips),
        out_shape=(
            *buffers(3 * rows, count),
            jax.ShapeDtypeStruct((count, rows + owned, head_dim), jnp.bfloat16),
        ),
        in_specs=[smem] + [vmem] * (chips + 2),
        out_specs=(vmem,) * (count + 1),
        scratch_shapes=[pltpu.VMEM((tokens, head_dim), jnp.bfloat16)] * 3
        + [pltpu.VMEM((tokens, head_dim), jnp.float32)]
        + [pltpu.VMEM((tokens, head_dim), jnp.bfloat16)]
        + [pltpu.VMEM((tokens, head_dim), jnp.float32)] * 2,
        compiler_params=params,
        cost_estimate=pl.CostEstimate(
            flops=12 * pairs_seen * head_dim,
            bytes_accessed=16 * tokens * head_dim,
            transcendentals=pairs_seen,
        ),
    )(place, *packed, grads, cluster_rank.reshape(1, clusters))
    passing = exchange_chips(grads_out[chips:])
    back = exchange_chips(grads_out[:chips])
    back = (*back, *(lax.ppermute(part, "sub", swap) for part in passing))

    def input_part(pick, kind):
        return pl.pallas_call(
            input_kernel,
            out_shape=jax.ShapeDtypeStruct((rows, half), kind),
            in_specs=[smem] + [vmem] * count + [anywhere] * 6,
            out_specs=vmem,
            scratch_shapes=[
                pltpu.VMEM((rows, 3 * width), jnp.bfloat16),
                pltpu.VMEM((3, half, width), jnp.bfloat16),
                pltpu.SemaphoreType.DMA((3,)),
            ],
            compiler_params=input_params,
            cost_estimate=pl.CostEstimate(
                flops=6 * rows * half * width, bytes_accessed=10 * half * width, transcendentals=0
            ),
        )(jnp.stack([chip, side, pick]), *back, *own, *other)

    crossing = input_part(1 - crossed_over, jnp.bfloat16)
    crossed = lax.ppermute(crossing, "head", swap)
    outputs, _ = lax.optimization_barrier((outputs, crossing))
    returned = exchange(outputs)
    kept = input_part(crossed_over, jnp.float32)
    d_hidden, attended, centroid_sums = pl.pallas_call(
        finish_kernel,
        out_shape=(
            jax.ShapeDtypeStruct((rows, half), jnp.bfloat16),
            jax.ShapeDtypeStruct((rows, width), jnp.bfloat16),
            jax.ShapeDtypeStruct((count, owned, head_dim), jnp.float32),
        ),
        in_specs=[vmem] * 3,
        out_specs=(vmem,) * 3,
        compiler_params=params,
    )(kept, crossed, returned)
    return (attended, d_hidden, centroid_sums)


def per_device(hidden, w_query, w_key, w_value, cluster_rank, assign, d_attended):
    chips = lax.axis_size("seq")
    fits = chips == 4 and lax.axis_size("sub") == 2 and lax.axis_size("head") == 2
    plan = by_head if fits and assign.shape[0] == 2 * chips else by_owner
    return plan(hidden, w_query, w_key, w_value, cluster_rank, assign, d_attended)


def solution(mesh):
    placed = (
        P(("groups", "seq", "sub"), None),
        P("sub", "head"),
        P("sub", "head"),
        P("sub", "head"),
        P("groups"),
        P("head", ("groups", "seq", "sub")),
        P(("groups", "seq", "sub"), "head"),
    )
    return jax.shard_map(
        per_device,
        mesh=mesh,
        in_specs=placed,
        out_specs=(
            P(("groups", "seq", "sub"), "head"),
            P(("groups", "seq", "sub"), "head"),
            P("head", ("groups", "seq", "sub"), None),
        ),
        check_vma=False,
    )
```

```python
from functools import partial

import jax
import jax.numpy as jnp
from jax import lax
from jax.experimental import pallas as pl
from jax.experimental.pallas import tpu as pltpu
from jax.sharding import PartitionSpec as P

epsilon = 1e-06


def keep_mask(filled, cluster_ids, positions):
    count = filled.shape[0]
    same = filled[:, None] & filled[None, :] & (cluster_ids[:, None] == cluster_ids[None, :])
    causal = positions[None, :] <= positions[:, None]
    diagonal = jnp.arange(count)[:, None] == jnp.arange(count)[None, :]
    return same & causal | diagonal


def head_forward(packed, scale):
    queries, keys_in, values, filled, cluster_ids, positions = packed
    scores = (
        lax.dot_general(
            queries, keys_in, (((1,), (1,)), ((), ())), preferred_element_type=jnp.float32
        )
        * scale
    )
    allowed = keep_mask(filled, cluster_ids, positions)
    row_top = jnp.max(jnp.where(allowed, scores, -jnp.inf), axis=1)
    expd = jnp.where(allowed, jnp.exp(scores - row_top[:, None]), 0.0)
    row_total = jnp.sum(expd, axis=1)
    probs_low = (expd / row_total[:, None]).astype(jnp.bfloat16)
    outputs = jnp.dot(probs_low, values, preferred_element_type=jnp.float32).astype(jnp.bfloat16)
    return (outputs, row_top, row_total)


def head_backward(packed, scale):
    queries, keys_in, values, grads_in, filled, cluster_ids, positions, row_top, row_total = packed
    contract_last = (((1,), (1,)), ((), ()))
    contract_first = (((0,), (0,)), ((), ()))
    scores = (
        lax.dot_general(queries, keys_in, contract_last, preferred_element_type=jnp.float32) * scale
    )
    allowed = keep_mask(filled, cluster_ids, positions)
    probs = jnp.where(allowed, jnp.exp(scores - row_top[:, None]), 0.0) / row_total[:, None]
    probs_low = probs.astype(jnp.bfloat16)
    grad_probs = lax.dot_general(
        grads_in, values, contract_last, preferred_element_type=jnp.float32
    )
    delta_rows = jnp.sum(probs * grad_probs, axis=1)
    grad_low = (probs * (grad_probs - delta_rows[:, None]) * scale).astype(jnp.bfloat16)
    grad_query = jnp.dot(grad_low, keys_in, preferred_element_type=jnp.float32).astype(jnp.bfloat16)
    grad_key = lax.dot_general(
        grad_low, queries, contract_first, preferred_element_type=jnp.float32
    ).astype(jnp.bfloat16)
    grad_value = lax.dot_general(
        probs_low, grads_in, contract_first, preferred_element_type=jnp.float32
    ).astype(jnp.bfloat16)
    return (grad_query, grad_key, grad_value)


def by_owner(hidden, w_query, w_key, w_value, cluster_rank, assign, d_attended):
    tok_rows = hidden.shape[0]
    heads_here = assign.shape[0]
    head_dim = w_query.shape[1] // heads_here
    clusters = cluster_rank.shape[0]
    seq_count = lax.axis_size("seq")
    sub_count = lax.axis_size("sub")
    owners = seq_count * sub_count
    capacity = 2 * tok_rows // owners
    slot_count = owners * capacity
    per_owner = clusters // owners
    scale = head_dim ** (-0.5)
    pieces = (
        lax.all_gather(w_query, "sub", axis=0, tiled=True),
        lax.all_gather(w_key, "sub", axis=0, tiled=True),
        lax.all_gather(w_value, "sub", axis=0, tiled=True),
    )
    projected = tuple(
        (
            jnp.dot(hidden, weight_piece, preferred_element_type=jnp.float32)
            for weight_piece in pieces
        )
    )

    def split_heads(matrix):
        return (
            matrix.astype(jnp.bfloat16).reshape(tok_rows, heads_here, head_dim).transpose(1, 0, 2)
        )

    queries, keys_all, values = tuple((split_heads(matrix) for matrix in projected))
    cluster_range = jnp.arange(clusters, dtype=jnp.int32)
    rank_tok = jnp.sum(jnp.where(assign[:, :, None] == cluster_range, cluster_rank, 0), axis=2)
    owner_ids = rank_tok // per_owner
    owner_hot = (owner_ids[:, :, None] == jnp.arange(owners, dtype=jnp.int32)).astype(jnp.int32)
    within = jnp.sum(owner_hot * (jnp.cumsum(owner_hot, axis=1) - 1), axis=2)
    slot_tok = owner_ids * capacity + within
    token_ids = jnp.arange(tok_rows, dtype=jnp.int32)
    slot_range = jnp.arange(slot_count, dtype=jnp.int32)
    slot_match = slot_tok[:, None, :] == slot_range[None, :, None]
    slot_hot = slot_match.astype(jnp.bfloat16)

    def to_slots(rows_in):
        kept = jnp.einsum(
            "hst,htd->hsd", slot_hot, rows_in, preferred_element_type=jnp.float32
        ).astype(jnp.bfloat16)
        return kept.reshape(heads_here, owners, capacity, head_dim)

    def from_slots(slotted):
        flat_slots = slotted.reshape(heads_here, slot_count, head_dim)
        return jnp.einsum(
            "hst,hsd->htd", slot_hot, flat_slots, preferred_element_type=jnp.float32
        ).astype(jnp.bfloat16)

    def exchange_three(first, second, third):
        return (
            lax.all_to_all(first, ("seq", "sub"), split_axis=1, concat_axis=1, tiled=True),
            lax.all_to_all(second, ("seq", "sub"), split_axis=1, concat_axis=1, tiled=True),
            lax.all_to_all(third, ("seq", "sub"), split_axis=1, concat_axis=1, tiled=True),
        )

    sent = exchange_three(to_slots(queries), to_slots(keys_all), to_slots(values))
    tag_tok = assign * tok_rows + token_ids
    slot_tag = jnp.sum(jnp.where(slot_match, tag_tok[:, None, :] + 1, 0), axis=2) - 1
    tags = lax.all_to_all(
        slot_tag.reshape(heads_here, owners, capacity),
        ("seq", "sub"),
        split_axis=1,
        concat_axis=1,
        tiled=True,
    )
    tags = tags.reshape(heads_here, slot_count)
    owner_q, owner_k, owner_v = tuple(
        (member.reshape(heads_here, slot_count, head_dim) for member in sent)
    )
    filled = tags >= 0
    cluster_ids = jnp.where(filled, tags // tok_rows, -1)
    positions = slot_range // capacity * tok_rows + tags % tok_rows
    outputs, row_top, row_total = lax.map(
        partial(head_forward, scale=scale),
        (owner_q, owner_k, owner_v, filled, cluster_ids, positions),
    )
    returned = lax.all_to_all(
        outputs.reshape(heads_here, owners, capacity, head_dim),
        ("seq", "sub"),
        split_axis=1,
        concat_axis=1,
        tiled=True,
    )

    def merge_heads(slotted):
        return from_slots(slotted).transpose(1, 0, 2).reshape(tok_rows, heads_here * head_dim)

    attended = merge_heads(returned)
    grads_tok = d_attended.reshape(tok_rows, heads_here, head_dim).transpose(1, 0, 2)
    owner_g = lax.all_to_all(
        to_slots(grads_tok), ("seq", "sub"), split_axis=1, concat_axis=1, tiled=True
    ).reshape(heads_here, slot_count, head_dim)
    grad_q, grad_k, grad_v = lax.map(
        partial(head_backward, scale=scale),
        (owner_q, owner_k, owner_v, owner_g, filled, cluster_ids, positions, row_top, row_total),
    )
    shape_four = (heads_here, owners, capacity, head_dim)
    back = exchange_three(
        grad_q.reshape(shape_four), grad_k.reshape(shape_four), grad_v.reshape(shape_four)
    )
    token_grads = tuple((merge_heads(member) for member in back))
    pieces = lax.all_gather((w_query, w_key, w_value), "sub", axis=0, tiled=True)
    terms = [
        jnp.einsum("tc,rc->tr", grad_rows_in, weight_piece, preferred_element_type=jnp.float32)
        for grad_rows_in, weight_piece in zip(token_grads, pieces)
    ]
    partial_grad = terms[0] + terms[1] + terms[2]
    d_hidden = lax.psum_scatter(
        partial_grad.astype(jnp.bfloat16), "head", scatter_dimension=1, tiled=True
    )
    keys_float = keys_all.astype(jnp.float32)
    unit_keys = keys_float * lax.rsqrt(
        jnp.sum(keys_float * keys_float, axis=2, keepdims=True) + epsilon
    )
    member_hot = (rank_tok[:, :, None] == cluster_range).astype(jnp.float32)
    local_sums = jnp.einsum("htr,htd->hrd", member_hot, unit_keys, precision=lax.Precision.HIGHEST)
    centroid_sums = lax.psum_scatter(
        local_sums.astype(jnp.bfloat16), ("seq", "sub"), scatter_dimension=1, tiled=True
    ).astype(jnp.float32)
    return (attended, d_hidden, centroid_sums)


contract_last = (((1,), (1,)), ((), ()))
contract_first = (((0,), (0,)), ((), ()))
log2_e = 1.4426950408889634
mebi = 1024 * 1024


def id_lines(rows, head_dim):
    return -(-(rows // head_dim) // 16) * 16


def pack_kernel(place_ref, grads_ref, assign_ref, mine_ref, theirs_ref):
    chips, padded, head_dim = mine_ref.shape
    rows = grads_ref.shape[0]
    spare = padded - rows - rows // head_dim
    for turn, out_ref in enumerate((mine_ref, theirs_ref)):
        for chip in range(chips):
            head = (place_ref[1] ^ turn) * chips + chip
            at = pl.multiple_of(head * head_dim, head_dim)
            out_ref[chip, :rows, :] = grads_ref[:, pl.ds(at, head_dim)]
            ids = assign_ref[pl.ds(head, 1), :].astype(jnp.float32)
            lines = [
                ids[:, start : start + head_dim] for start in range(0, rows, head_dim)
            ] + [jnp.zeros((spare, head_dim), jnp.float32)]
            out_ref[chip, rows:, :] = jnp.concatenate(lines, axis=0).astype(jnp.bfloat16)


def merge_kernel(place_ref, mine_ref, theirs_ref, *out_refs):
    height = mine_ref.shape[1]
    for turn, held_ref in enumerate((mine_ref, theirs_ref)):
        at = pl.ds(pl.multiple_of((place_ref[1] ^ turn) * height, height), height)
        for offset, out_ref in enumerate(out_refs):
            out_ref[at, :] = held_ref[place_ref[0] ^ offset]


def fetch_columns(half, weights, held_ref, sems):
    chunks = sems.shape[1]
    columns = held_ref.shape[2]
    rows = held_ref.shape[1] // chunks
    at = pl.ds(pl.multiple_of(half * columns, columns), columns)
    copies = []
    for index, weight in enumerate(weights):
        for chunk in range(chunks):
            lines = pl.ds(chunk * rows, rows)
            copy = pltpu.make_async_copy(
                weight.at[lines, at], held_ref.at[index, lines], sems.at[index, chunk]
            )
            copy.start()
            copies.append(copy)
    return copies


def project_kernel(count, turn, place_ref, mine_ref, theirs_ref, *refs):
    weights, refs = refs[:count], refs[count:]
    if turn == 0:
        arrived_ref, refs = refs[0], refs[1:]
    out_refs, (joined_ref, held_ref, low_ref, sems) = refs[:-4], refs[-4:]
    side = place_ref[1]
    rows, depth = mine_ref.shape[0], joined_ref.shape[1]
    tall = 2 * rows
    copies = fetch_columns(side ^ turn, weights, held_ref, sems)
    near = pl.ds(pl.multiple_of(side * depth, depth), depth)
    joined_ref[pl.ds(pl.multiple_of(side * rows, rows), rows), :] = mine_ref[:, near]
    joined_ref[pl.ds(pl.multiple_of((1 - side) * rows, rows), rows), :] = theirs_ref[:, near]
    chunks = sems.shape[1]
    for index in range(count):
        for chunk in range(chunks):
            copies[index * chunks + chunk].wait()
        total = jnp.dot(joined_ref[...], held_ref[index], preferred_element_type=jnp.float32)
        if turn == 1:
            out_refs[0][index] = total.astype(jnp.bfloat16)
            continue
        low_ref[...] = (total + arrived_ref[index].astype(jnp.float32)).astype(jnp.bfloat16)
        for offset, out_ref in enumerate(out_refs):
            head_dim = out_ref.shape[1]
            at = pl.multiple_of((place_ref[0] ^ offset) * head_dim, head_dim)
            out_ref[index * tall : (index + 1) * tall, :] = low_ref[:, pl.ds(at, head_dim)]


def in_order(place, parts, start, ordered):
    for offset, part in enumerate(parts):
        tall = ordered.shape[0] // len(parts)
        at = pl.ds(pl.multiple_of((place ^ offset) * tall, tall), tall)
        ordered[at, :] = part[start : start + tall, :]


def order_grads(place, parts, rows, grad_rows, id_rows, id_cols):
    head_dim = grad_rows.shape[1]
    height = parts[0].shape[0] // 2
    for offset, part in enumerate(parts):
        for core in range(2):
            block = (place ^ offset) * 2 + core
            at = pl.ds(pl.multiple_of(block * rows, rows), rows)
            start = core * height
            grad_rows[at, :] = part[start : start + rows, :]
            lines = part[start + rows : start + rows + 16, :].astype(jnp.float32)
            ids = jnp.concatenate(
                [lines[line : line + 1, :] for line in range(rows // head_dim)], axis=1
            )
            id_rows[block] = jnp.broadcast_to(ids, id_rows.shape[1:])
            id_cols[at, :] = jnp.broadcast_to(ids, (head_dim, rows)).T


def block_scores(factor, block, rows, queries, keys_in, id_rows, id_cols):
    head_dim = queries.shape[1]
    seen = (block + 1) * rows
    scores = lax.dot_general(
        keys_in[:seen, :],
        queries[block * rows : seen, :],
        contract_last,
        preferred_element_type=jnp.float32,
    )
    ids = id_cols[:seen, :]
    mine = id_rows[block][:1, :]
    same = jnp.concatenate(
        [ids == mine[:, start : start + head_dim] for start in range(0, rows, head_dim)], axis=1
    )
    key_at = lax.broadcasted_iota(jnp.int32, (rows, rows), 0)
    query_at = lax.broadcasted_iota(jnp.int32, (rows, rows), 1)
    last = same[seen - rows :] & (key_at <= query_at)
    allowed = last if block == 0 else jnp.concatenate([same[: seen - rows], last], axis=0)
    return jnp.where(allowed, scores * factor, -jnp.inf)


def value_grad_kernel(factor, chips, rows, place_ref, *refs):
    packed, grads = refs[:chips], refs[chips : 2 * chips]
    out_refs, lse_ref = refs[2 * chips : 3 * chips], refs[3 * chips]
    queries, keys_in, grad_rows, id_rows, id_cols, total_ref = refs[3 * chips + 1 :]
    tall = 2 * rows
    place = place_ref[0]
    in_order(place, packed, 0, queries)
    in_order(place, packed, tall, keys_in)
    order_grads(place, grads, rows, grad_rows, id_rows, id_cols)
    total_ref[...] = jnp.zeros_like(total_ref)
    for block in range(2 * chips):
        seen = (block + 1) * rows
        scores = block_scores(factor, block, rows, queries, keys_in, id_rows, id_cols)
        top = jnp.max(scores, axis=0, keepdims=True)
        expd = jnp.exp2(scores - top)
        total = jnp.sum(expd, axis=0, keepdims=True)
        lse_ref[block : block + 1, :] = top + jnp.log2(total)
        total_ref[:seen, :] += jnp.dot(
            (expd * (1.0 / total)).astype(jnp.bfloat16),
            grad_rows[block * rows : seen, :],
            preferred_element_type=jnp.float32,
        )
    for offset, out_ref in enumerate(out_refs):
        at = pl.multiple_of((place ^ offset) * tall, tall)
        out_ref[...] = total_ref[pl.ds(at, tall), :].astype(jnp.bfloat16)


def query_grad_kernel(factor, scale, chips, rows, place_ref, *refs):
    packed, valued, grads = refs[:chips], refs[chips : 2 * chips], refs[2 * chips : 3 * chips]
    lse_ref, rank_ref = refs[3 * chips : 3 * chips + 2]
    refs = refs[3 * chips + 2 :]
    grad_refs, out_refs, refs = refs[:chips], refs[chips : 2 * chips], refs[2 * chips :]
    queries, keys_in, values, grad_rows, id_rows, id_cols, total_ref, dq_ref, attended_ref = refs
    head_dim = queries.shape[1]
    clusters = rank_ref.shape[1]
    tall = 2 * rows
    place = place_ref[0]
    in_order(place, packed, 0, queries)
    in_order(place, packed, tall, keys_in)
    in_order(place, valued, 0, values)
    order_grads(place, grads, rows, grad_rows, id_rows, id_cols)
    total_ref[...] = jnp.zeros_like(total_ref)
    for block in range(2 * chips):
        seen = (block + 1) * rows
        mine = slice(block * rows, seen)
        scores = block_scores(factor, block, rows, queries, keys_in, id_rows, id_cols)
        probs = jnp.exp2(scores - lse_ref[block : block + 1, :])
        seen_values = values[:seen, :]
        grad_probs = lax.dot_general(
            seen_values, grad_rows[mine, :], contract_last, preferred_element_type=jnp.float32
        )
        flipped = lax.dot_general(
            seen_values,
            probs.astype(jnp.bfloat16),
            contract_first,
            preferred_element_type=jnp.float32,
        )
        attended_ref[mine, :] = flipped.T.astype(jnp.bfloat16)
        weighted = probs * grad_probs
        delta = jnp.sum(weighted, axis=0, keepdims=True)
        grad_low = (weighted - probs * delta).astype(jnp.bfloat16)
        total_ref[:seen, :] += jnp.dot(
            grad_low, queries[mine, :], preferred_element_type=jnp.float32
        )
        flipped = lax.dot_general(
            keys_in[:seen, :], grad_low, contract_first, preferred_element_type=jnp.float32
        )
        dq_ref[mine, :] = (flipped.T * scale).astype(jnp.bfloat16)
    sums = jnp.zeros((clusters, head_dim), jnp.float32)
    cluster_at = lax.broadcasted_iota(jnp.int32, (clusters, rows), 0).astype(jnp.float32)
    for block in range(2 * chips):
        keys_float = keys_in[block * rows : (block + 1) * rows, :].astype(jnp.float32)
        unit = keys_float * lax.rsqrt(
            jnp.sum(keys_float * keys_float, axis=1, keepdims=True) + epsilon
        )
        unit_high = unit.astype(jnp.bfloat16)
        unit_low = (unit - unit_high.astype(jnp.float32)).astype(jnp.bfloat16)
        member = jnp.where(cluster_at == id_rows[block][:1, :], 1.0, 0.0).astype(jnp.bfloat16)
        sums += jnp.dot(member, unit_high, preferred_element_type=jnp.float32)
        sums += jnp.dot(member, unit_low, preferred_element_type=jnp.float32)
    rank_at = lax.broadcasted_iota(jnp.int32, (clusters, clusters), 0)
    ordered = jnp.where(rank_at == rank_ref[...], 1.0, 0.0).astype(jnp.bfloat16)
    ranked = jnp.dot(ordered, sums.astype(jnp.bfloat16), preferred_element_type=jnp.float32)
    attended_ref[2 * chips * rows :, :] = ranked.astype(jnp.bfloat16)
    owned = clusters // (2 * chips)
    for offset in range(chips):
        at = pl.ds(pl.multiple_of((place ^ offset) * tall, tall), tall)
        grad_refs[offset][:tall, :] = dq_ref[at, :]
        grad_refs[offset][tall:, :] = (total_ref[at, :] * scale).astype(jnp.bfloat16)
        for core in range(2):
            shard = (place ^ offset) * 2 + core
            start = core * (rows + owned)
            at = pl.ds(pl.multiple_of(shard * rows, rows), rows)
            out_refs[offset][start : start + rows, :] = attended_ref[at, :]
            at = pl.ds(pl.multiple_of(2 * chips * rows + shard * owned, owned), owned)
            out_refs[offset][start + rows : start + rows + owned, :] = attended_ref[at, :]


def stage_kernel(*refs):
    weights, (held_ref, sems) = refs[:-2], refs[-2:]
    copies = [
        pltpu.make_async_copy(weight, held_ref.at[index], sems.at[index])
        for index, weight in enumerate(weights)
    ]
    for copy in copies:
        copy.start()
    for copy in copies:
        copy.wait()


def input_kernel(chips, place_ref, *refs):
    held_ref, out_ref, gathered_ref = refs[4 * chips :]
    rows, width = out_ref.shape[0], held_ref.shape[2]
    head_dim = width // (2 * chips)
    for turn in range(2):
        parts = refs[turn * chips : (turn + 1) * chips]
        valued = refs[(2 + turn) * chips : (3 + turn) * chips]
        for offset in range(chips):
            head = (place_ref[1] ^ turn) * chips + (place_ref[0] ^ offset)
            for index in range(3):
                source = parts[offset] if index < 2 else valued[offset]
                at = pl.multiple_of((2 * (index % 2) + place_ref[2]) * rows, rows)
                start = pl.multiple_of(index * width + head * head_dim, head_dim)
                gathered_ref[:, pl.ds(start, head_dim)] = source[pl.ds(at, rows), :]
    flipped = None
    for index in range(3):
        term = lax.dot_general(
            held_ref[index],
            gathered_ref[:, index * width : (index + 1) * width],
            contract_last,
            preferred_element_type=jnp.float32,
        )
        flipped = term if flipped is None else flipped + term
    out_ref[...] = flipped.T.astype(out_ref.dtype)


def finish_kernel(chips, place_ref, first_ref, second_ref, kept_ref, *refs):
    parts, (hidden_ref, attended_ref, sums_ref) = refs[: 2 * chips], refs[2 * chips :]
    side = place_ref[1]
    second = jnp.where(place_ref[2] == side, kept_ref[...], second_ref[...])
    total = first_ref[...].astype(jnp.float32) + second.astype(jnp.float32)
    hidden_ref[...] = total.astype(jnp.bfloat16)
    rows = attended_ref.shape[0]
    head_dim = sums_ref.shape[2]
    height = parts[0].shape[0] // 2
    start = pl.multiple_of(side * height, height)
    for turn in range(2):
        for offset in range(chips):
            part = parts[turn * chips + offset]
            head = (side ^ turn) * chips + (place_ref[0] ^ offset)
            at = pl.multiple_of(head * head_dim, head_dim)
            attended_ref[:, pl.ds(at, head_dim)] = part[pl.ds(start, rows), :]
            sums_ref[head] = part[pl.ds(start + rows, height - rows), :].astype(jnp.float32)


def by_head(hidden, w_query, w_key, w_value, cluster_rank, assign, d_attended):
    rows = hidden.shape[0]
    count = assign.shape[0]
    chips = count // 2
    half, width = w_query.shape
    head_dim = width // count
    tokens = count * rows
    clusters = cluster_rank.shape[0]
    owned = clusters // count
    scale = head_dim ** (-0.5)
    factor = scale * log2_e
    smem = pl.BlockSpec(memory_space=pltpu.SMEM)
    vmem = pl.BlockSpec(memory_space=pltpu.VMEM)
    anywhere = pl.BlockSpec(memory_space=pl.ANY)
    params = pltpu.CompilerParams(vmem_limit_bytes=32 * mebi)
    project_params = pltpu.CompilerParams(vmem_limit_bytes=48 * mebi)
    swap = [(0, 1), (1, 0)]
    chip, side, column = (lax.axis_index(name) for name in ("seq", "sub", "head"))
    place = jnp.stack([chip, side])

    def call(kernel, outs, *operands, scratch=(), hbm=0, limits=params, takes=1):
        return pl.pallas_call(
            kernel,
            out_shape=outs,
            in_specs=[smem] + [vmem] * (len(operands) - 1 - hbm) + [anywhere] * hbm,
            out_specs=jax.tree.map(lambda _: vmem, outs),
            scratch_shapes=list(scratch),
            compiler_params=limits,
            cost_estimate=pl.CostEstimate(
                flops=int(takes * 1.15e9), bytes_accessed=mebi, transcendentals=0
            ),
        )(*operands)

    def low(*shape):
        return jax.ShapeDtypeStruct(shape, jnp.bfloat16)

    def buffers(height):
        return (low(height, head_dim),) * chips

    def exchange(parts):
        moved = {
            offset: lax.ppermute(parts[offset], "seq", [(at, at ^ offset) for at in range(chips)])
            for offset in (2, 3, 1)
        }
        return (parts[0], moved[1], moved[2], moved[3])

    def to_sibling(piece):
        return lax.ppermute(piece, "sub", swap)

    hidden_other = to_sibling(hidden)
    block = low(chips, rows + id_lines(rows, head_dim), head_dim)
    grads_mine, grads_theirs = call(pack_kernel, (block, block), place, d_attended, assign)
    grads_other = to_sibling(grads_theirs)

    def project(turn, weights, *arrived):
        number = len(weights)
        outs = buffers(2 * number * rows) if turn == 0 else low(number, 2 * rows, width // 2)

        def kernel(place_ref, mine_ref, theirs_ref, *refs):
            early, refs = refs[: 1 - turn], refs[1 - turn :]
            project_kernel(
                number, turn, place_ref, mine_ref, theirs_ref, *refs[:number], *early, *refs[number:]
            )

        return call(
            kernel,
            outs,
            place,
            hidden,
            hidden_other,
            *arrived,
            *weights,
            scratch=[
                pltpu.VMEM((2 * rows, half), jnp.bfloat16),
                pltpu.VMEM((number, half, width // 2), jnp.bfloat16),
                pltpu.VMEM((2 * rows, width // 2), jnp.bfloat16),
                pltpu.SemaphoreType.DMA((number, 4)),
            ],
            hbm=number,
            limits=project_params,
            takes=1 + 1.5 * number,
        )

    early, late = (w_query, w_key), (w_value,)
    early_arrived = to_sibling(project(1, early))
    late_arrived = to_sibling(project(1, late))
    grads = exchange(call(merge_kernel, buffers(2 * block.shape[1]), place, grads_mine, grads_other))
    early_arrived, _ = lax.optimization_barrier((early_arrived, grads[0]))
    early_projected = project(0, early, early_arrived)
    packed = exchange(early_projected)
    late_arrived, _, _ = lax.optimization_barrier((late_arrived, early_projected[0], grads))
    late_projected = project(0, late, late_arrived)
    valued = exchange(late_projected)
    packed = lax.optimization_barrier((*packed, late_projected[0]))[:chips]

    def held(kind):
        return pltpu.VMEM((tokens, head_dim), kind)

    id_scratch = [pltpu.VMEM((count, 8, rows), jnp.float32), held(jnp.float32)]
    *value_grads, lse = call(
        partial(value_grad_kernel, factor, chips, rows),
        (*buffers(2 * rows), jax.ShapeDtypeStruct((count, rows), jnp.float32)),
        place,
        *packed,
        *grads,
        scratch=[held(jnp.bfloat16)] * 3 + id_scratch + [held(jnp.float32)],
        takes=7,
    )
    value_back = exchange(value_grads)
    results = call(
        partial(query_grad_kernel, factor, scale, chips, rows),
        (*buffers(4 * rows), *buffers(2 * (rows + owned))),
        place,
        *packed,
        *valued,
        *grads,
        lse,
        cluster_rank.reshape(1, clusters),
        scratch=[held(jnp.bfloat16)] * 4
        + id_scratch
        + [
            held(jnp.float32),
            held(jnp.bfloat16),
            pltpu.VMEM((tokens + clusters, head_dim), jnp.bfloat16),
        ],
        takes=10,
    )
    *ready, _, _ = lax.optimization_barrier((*results[:chips], value_back[2], value_back[3]))
    back = exchange(ready)

    *own, _ = lax.optimization_barrier((w_query, w_key, w_value, results[0]))
    staged = pl.pallas_call(
        stage_kernel,
        out_shape=pltpu.VMEM((3, half, width), jnp.bfloat16),
        in_specs=[anywhere] * 3,
        out_specs=vmem,
        scratch_shapes=[pltpu.SemaphoreType.DMA((3,))],
        compiler_params=pltpu.CompilerParams(vmem_limit_bytes=16 * mebi),
        cost_estimate=pl.CostEstimate(
            flops=0, bytes_accessed=18 * half * width, transcendentals=0
        ),
    )(*own)
    back = (*lax.optimization_barrier((back[0], staged))[:1], *back[1:])

    back_other = tuple(to_sibling(part) for part in back)
    value_other = tuple(to_sibling(part) for part in value_back)

    def input_part(shard):
        return call(
            partial(input_kernel, chips),
            low(rows, half),
            jnp.stack([chip, side, shard]),
            *back,
            *back_other,
            *value_back,
            *value_other,
            staged,
            scratch=[pltpu.VMEM((rows, 3 * width), jnp.bfloat16)],
            takes=3,
        )

    square = ("head", "sub")
    first = lax.ppermute(input_part(1 - column), square, [(0, 1), (1, 3), (3, 2), (2, 0)])
    kept = input_part(column)
    second = lax.ppermute(kept, square, [(1, 2), (2, 1)])
    *outputs, _ = lax.optimization_barrier((*results[chips:], back[2]))
    returned = exchange(outputs)
    returned_other = tuple(to_sibling(part) for part in returned)
    d_hidden, attended, centroid_sums = call(
        partial(finish_kernel, chips),
        (
            low(rows, half),
            low(rows, width),
            jax.ShapeDtypeStruct((count, owned, head_dim), jnp.float32),
        ),
        jnp.stack([chip, side, column]),
        first,
        second,
        kept,
        *returned,
        *returned_other,
    )
    return (attended, d_hidden, centroid_sums)


def per_device(hidden, w_query, w_key, w_value, cluster_rank, assign, d_attended):
    chips = lax.axis_size("seq")
    fits = chips == 4 and lax.axis_size("sub") == 2 and lax.axis_size("head") == 2
    plan = by_head if fits and assign.shape[0] == 2 * chips else by_owner
    return plan(hidden, w_query, w_key, w_value, cluster_rank, assign, d_attended)


def solution(mesh):
    placed = (
        P(("groups", "seq", "sub"), None),
        P("sub", "head"),
        P("sub", "head"),
        P("sub", "head"),
        P("groups"),
        P("head", ("groups", "seq", "sub")),
        P(("groups", "seq", "sub"), "head"),
    )
    return jax.shard_map(
        per_device,
        mesh=mesh,
        in_specs=placed,
        out_specs=(
            P(("groups", "seq", "sub"), "head"),
            P(("groups", "seq", "sub"), "head"),
            P("head", ("groups", "seq", "sub"), None),
        ),
        check_vma=False,
    )
```

```python
from functools import partial

import jax
import jax.numpy as jnp
from jax import lax
from jax.experimental import pallas as pl
from jax.experimental.pallas import tpu as pltpu
from jax.sharding import PartitionSpec as P

epsilon = 1e-06


def keep_mask(filled, cluster_ids, positions):
    count = filled.shape[0]
    same = filled[:, None] & filled[None, :] & (cluster_ids[:, None] == cluster_ids[None, :])
    causal = positions[None, :] <= positions[:, None]
    diagonal = jnp.arange(count)[:, None] == jnp.arange(count)[None, :]
    return same & causal | diagonal


def head_forward(packed, scale):
    queries, keys_in, values, filled, cluster_ids, positions = packed
    scores = (
        lax.dot_general(
            queries, keys_in, (((1,), (1,)), ((), ())), preferred_element_type=jnp.float32
        )
        * scale
    )
    allowed = keep_mask(filled, cluster_ids, positions)
    row_top = jnp.max(jnp.where(allowed, scores, -jnp.inf), axis=1)
    expd = jnp.where(allowed, jnp.exp(scores - row_top[:, None]), 0.0)
    row_total = jnp.sum(expd, axis=1)
    probs_low = (expd / row_total[:, None]).astype(jnp.bfloat16)
    outputs = jnp.dot(probs_low, values, preferred_element_type=jnp.float32).astype(jnp.bfloat16)
    return (outputs, row_top, row_total)


def head_backward(packed, scale):
    queries, keys_in, values, grads_in, filled, cluster_ids, positions, row_top, row_total = packed
    contract_last = (((1,), (1,)), ((), ()))
    contract_first = (((0,), (0,)), ((), ()))
    scores = (
        lax.dot_general(queries, keys_in, contract_last, preferred_element_type=jnp.float32) * scale
    )
    allowed = keep_mask(filled, cluster_ids, positions)
    probs = jnp.where(allowed, jnp.exp(scores - row_top[:, None]), 0.0) / row_total[:, None]
    probs_low = probs.astype(jnp.bfloat16)
    grad_probs = lax.dot_general(
        grads_in, values, contract_last, preferred_element_type=jnp.float32
    )
    delta_rows = jnp.sum(probs * grad_probs, axis=1)
    grad_low = (probs * (grad_probs - delta_rows[:, None]) * scale).astype(jnp.bfloat16)
    grad_query = jnp.dot(grad_low, keys_in, preferred_element_type=jnp.float32).astype(jnp.bfloat16)
    grad_key = lax.dot_general(
        grad_low, queries, contract_first, preferred_element_type=jnp.float32
    ).astype(jnp.bfloat16)
    grad_value = lax.dot_general(
        probs_low, grads_in, contract_first, preferred_element_type=jnp.float32
    ).astype(jnp.bfloat16)
    return (grad_query, grad_key, grad_value)


def by_owner(hidden, w_query, w_key, w_value, cluster_rank, assign, d_attended):
    tok_rows = hidden.shape[0]
    heads_here = assign.shape[0]
    head_dim = w_query.shape[1] // heads_here
    clusters = cluster_rank.shape[0]
    seq_count = lax.axis_size("seq")
    sub_count = lax.axis_size("sub")
    owners = seq_count * sub_count
    capacity = 2 * tok_rows // owners
    slot_count = owners * capacity
    per_owner = clusters // owners
    scale = head_dim ** (-0.5)
    pieces = (
        lax.all_gather(w_query, "sub", axis=0, tiled=True),
        lax.all_gather(w_key, "sub", axis=0, tiled=True),
        lax.all_gather(w_value, "sub", axis=0, tiled=True),
    )
    projected = tuple(
        (
            jnp.dot(hidden, weight_piece, preferred_element_type=jnp.float32)
            for weight_piece in pieces
        )
    )

    def split_heads(matrix):
        return (
            matrix.astype(jnp.bfloat16).reshape(tok_rows, heads_here, head_dim).transpose(1, 0, 2)
        )

    queries, keys_all, values = tuple((split_heads(matrix) for matrix in projected))
    cluster_range = jnp.arange(clusters, dtype=jnp.int32)
    rank_tok = jnp.sum(jnp.where(assign[:, :, None] == cluster_range, cluster_rank, 0), axis=2)
    owner_ids = rank_tok // per_owner
    owner_hot = (owner_ids[:, :, None] == jnp.arange(owners, dtype=jnp.int32)).astype(jnp.int32)
    within = jnp.sum(owner_hot * (jnp.cumsum(owner_hot, axis=1) - 1), axis=2)
    slot_tok = owner_ids * capacity + within
    token_ids = jnp.arange(tok_rows, dtype=jnp.int32)
    slot_range = jnp.arange(slot_count, dtype=jnp.int32)
    slot_match = slot_tok[:, None, :] == slot_range[None, :, None]
    slot_hot = slot_match.astype(jnp.bfloat16)

    def to_slots(rows_in):
        kept = jnp.einsum(
            "hst,htd->hsd", slot_hot, rows_in, preferred_element_type=jnp.float32
        ).astype(jnp.bfloat16)
        return kept.reshape(heads_here, owners, capacity, head_dim)

    def from_slots(slotted):
        flat_slots = slotted.reshape(heads_here, slot_count, head_dim)
        return jnp.einsum(
            "hst,hsd->htd", slot_hot, flat_slots, preferred_element_type=jnp.float32
        ).astype(jnp.bfloat16)

    def exchange_three(first, second, third):
        return (
            lax.all_to_all(first, ("seq", "sub"), split_axis=1, concat_axis=1, tiled=True),
            lax.all_to_all(second, ("seq", "sub"), split_axis=1, concat_axis=1, tiled=True),
            lax.all_to_all(third, ("seq", "sub"), split_axis=1, concat_axis=1, tiled=True),
        )

    sent = exchange_three(to_slots(queries), to_slots(keys_all), to_slots(values))
    tag_tok = assign * tok_rows + token_ids
    slot_tag = jnp.sum(jnp.where(slot_match, tag_tok[:, None, :] + 1, 0), axis=2) - 1
    tags = lax.all_to_all(
        slot_tag.reshape(heads_here, owners, capacity),
        ("seq", "sub"),
        split_axis=1,
        concat_axis=1,
        tiled=True,
    )
    tags = tags.reshape(heads_here, slot_count)
    owner_q, owner_k, owner_v = tuple(
        (member.reshape(heads_here, slot_count, head_dim) for member in sent)
    )
    filled = tags >= 0
    cluster_ids = jnp.where(filled, tags // tok_rows, -1)
    positions = slot_range // capacity * tok_rows + tags % tok_rows
    outputs, row_top, row_total = lax.map(
        partial(head_forward, scale=scale),
        (owner_q, owner_k, owner_v, filled, cluster_ids, positions),
    )
    returned = lax.all_to_all(
        outputs.reshape(heads_here, owners, capacity, head_dim),
        ("seq", "sub"),
        split_axis=1,
        concat_axis=1,
        tiled=True,
    )

    def merge_heads(slotted):
        return from_slots(slotted).transpose(1, 0, 2).reshape(tok_rows, heads_here * head_dim)

    attended = merge_heads(returned)
    grads_tok = d_attended.reshape(tok_rows, heads_here, head_dim).transpose(1, 0, 2)
    owner_g = lax.all_to_all(
        to_slots(grads_tok), ("seq", "sub"), split_axis=1, concat_axis=1, tiled=True
    ).reshape(heads_here, slot_count, head_dim)
    grad_q, grad_k, grad_v = lax.map(
        partial(head_backward, scale=scale),
        (owner_q, owner_k, owner_v, owner_g, filled, cluster_ids, positions, row_top, row_total),
    )
    shape_four = (heads_here, owners, capacity, head_dim)
    back = exchange_three(
        grad_q.reshape(shape_four), grad_k.reshape(shape_four), grad_v.reshape(shape_four)
    )
    token_grads = tuple((merge_heads(member) for member in back))
    pieces = lax.all_gather((w_query, w_key, w_value), "sub", axis=0, tiled=True)
    terms = [
        jnp.einsum("tc,rc->tr", grad_rows_in, weight_piece, preferred_element_type=jnp.float32)
        for grad_rows_in, weight_piece in zip(token_grads, pieces)
    ]
    partial_grad = terms[0] + terms[1] + terms[2]
    d_hidden = lax.psum_scatter(
        partial_grad.astype(jnp.bfloat16), "head", scatter_dimension=1, tiled=True
    )
    keys_float = keys_all.astype(jnp.float32)
    unit_keys = keys_float * lax.rsqrt(
        jnp.sum(keys_float * keys_float, axis=2, keepdims=True) + epsilon
    )
    member_hot = (rank_tok[:, :, None] == cluster_range).astype(jnp.float32)
    local_sums = jnp.einsum("htr,htd->hrd", member_hot, unit_keys, precision=lax.Precision.HIGHEST)
    centroid_sums = lax.psum_scatter(
        local_sums.astype(jnp.bfloat16), ("seq", "sub"), scatter_dimension=1, tiled=True
    ).astype(jnp.float32)
    return (attended, d_hidden, centroid_sums)


contract_last = (((1,), (1,)), ((), ()))
contract_first = (((0,), (0,)), ((), ()))
log2_e = 1.4426950408889634
mebi = 1024 * 1024


def id_lines(rows, head_dim):
    return -(-(rows // head_dim) // 16) * 16


def pack_kernel(place_ref, grads_ref, assign_ref, mine_ref, theirs_ref):
    chips, padded, head_dim = mine_ref.shape
    rows = grads_ref.shape[0]
    spare = padded - rows - rows // head_dim
    for turn, out_ref in enumerate((mine_ref, theirs_ref)):
        for chip in range(chips):
            head = (place_ref[1] ^ turn) * chips + chip
            at = pl.multiple_of(head * head_dim, head_dim)
            out_ref[chip, :rows, :] = grads_ref[:, pl.ds(at, head_dim)]
            ids = assign_ref[pl.ds(head, 1), :].astype(jnp.float32)
            lines = [
                ids[:, start : start + head_dim] for start in range(0, rows, head_dim)
            ] + [jnp.zeros((spare, head_dim), jnp.float32)]
            out_ref[chip, rows:, :] = jnp.concatenate(lines, axis=0).astype(jnp.bfloat16)


def merge_kernel(place_ref, mine_ref, theirs_ref, *out_refs):
    height = mine_ref.shape[1]
    for turn, held_ref in enumerate((mine_ref, theirs_ref)):
        at = pl.ds(pl.multiple_of((place_ref[1] ^ turn) * height, height), height)
        for offset, out_ref in enumerate(out_refs):
            out_ref[at, :] = held_ref[place_ref[0] ^ offset]


def fetch_columns(half, weights, held_ref, sems):
    chunks = sems.shape[1]
    columns = held_ref.shape[2]
    rows = held_ref.shape[1] // chunks
    at = pl.ds(pl.multiple_of(half * columns, columns), columns)
    copies = []
    for index, weight in enumerate(weights):
        for chunk in range(chunks):
            lines = pl.ds(chunk * rows, rows)
            copy = pltpu.make_async_copy(
                weight.at[lines, at], held_ref.at[index, lines], sems.at[index, chunk]
            )
            copy.start()
            copies.append(copy)
    return copies


def project_kernel(count, turn, place_ref, *refs):
    if turn == 0:
        arrived_ref, refs = refs[0], refs[1:]
    tokens, weights, refs = refs[:2], refs[2 : 2 + count], refs[2 + count :]
    out_refs, (joined_ref, held_ref, low_ref, sems, token_sems) = refs[:-5], refs[-5:]
    side = place_ref[1]
    tall, depth = joined_ref.shape
    rows = tall // 2
    near = pl.ds(pl.multiple_of(side * depth, depth), depth)
    joins = []
    for core, source in enumerate(tokens):
        at = pl.ds(pl.multiple_of((side ^ core) * rows, rows), rows)
        joins.append(
            pltpu.make_async_copy(source.at[:, near], joined_ref.at[at], token_sems.at[core])
        )
        joins[core].start()
    copies = fetch_columns(side ^ turn, weights, held_ref, sems)
    for copy in joins:
        copy.wait()
    chunks = sems.shape[1]
    for index in range(count):
        for chunk in range(chunks):
            copies[index * chunks + chunk].wait()
        total = jnp.dot(joined_ref[...], held_ref[index], preferred_element_type=jnp.float32)
        if turn == 1:
            out_refs[0][index] = total.astype(jnp.bfloat16)
            continue
        low_ref[...] = (total + arrived_ref[index].astype(jnp.float32)).astype(jnp.bfloat16)
        for offset, out_ref in enumerate(out_refs):
            head_dim = out_ref.shape[1]
            at = pl.multiple_of((place_ref[0] ^ offset) * head_dim, head_dim)
            out_ref[index * tall : (index + 1) * tall, :] = low_ref[:, pl.ds(at, head_dim)]


def in_order(place, parts, start, ordered):
    for offset, part in enumerate(parts):
        tall = ordered.shape[0] // len(parts)
        at = pl.ds(pl.multiple_of((place ^ offset) * tall, tall), tall)
        ordered[at, :] = part[start : start + tall, :]


def order_grads(place, parts, rows, grad_rows, id_rows, id_cols):
    head_dim = grad_rows.shape[1]
    height = parts[0].shape[0] // 2
    for offset, part in enumerate(parts):
        for core in range(2):
            block = (place ^ offset) * 2 + core
            at = pl.ds(pl.multiple_of(block * rows, rows), rows)
            start = core * height
            grad_rows[at, :] = part[start : start + rows, :]
            lines = part[start + rows : start + rows + 16, :].astype(jnp.float32)
            ids = jnp.concatenate(
                [lines[line : line + 1, :] for line in range(rows // head_dim)], axis=1
            )
            id_rows[block] = jnp.broadcast_to(ids, id_rows.shape[1:])
            id_cols[at, :] = jnp.broadcast_to(ids, (head_dim, rows)).T


def block_scores(factor, block, rows, queries, keys_in, id_rows, id_cols):
    head_dim = queries.shape[1]
    seen = (block + 1) * rows
    scores = lax.dot_general(
        keys_in[:seen, :],
        queries[block * rows : seen, :],
        contract_last,
        preferred_element_type=jnp.float32,
    )
    ids = id_cols[:seen, :]
    mine = id_rows[block][:1, :]
    same = jnp.concatenate(
        [ids == mine[:, start : start + head_dim] for start in range(0, rows, head_dim)], axis=1
    )
    key_at = lax.broadcasted_iota(jnp.int32, (rows, rows), 0)
    query_at = lax.broadcasted_iota(jnp.int32, (rows, rows), 1)
    last = same[seen - rows :] & (key_at <= query_at)
    allowed = last if block == 0 else jnp.concatenate([same[: seen - rows], last], axis=0)
    return jnp.where(allowed, scores * factor, -jnp.inf)


def value_grad_kernel(factor, chips, rows, place_ref, *refs):
    packed, grads = refs[:chips], refs[chips : 2 * chips]
    out_refs, lse_ref = refs[2 * chips : 3 * chips], refs[3 * chips]
    queries, keys_in, grad_rows, id_rows, id_cols, total_ref = refs[3 * chips + 1 :]
    tall = 2 * rows
    place = place_ref[0]
    in_order(place, packed, 0, queries)
    in_order(place, packed, tall, keys_in)
    order_grads(place, grads, rows, grad_rows, id_rows, id_cols)
    total_ref[...] = jnp.zeros_like(total_ref)
    for block in range(2 * chips):
        seen = (block + 1) * rows
        scores = block_scores(factor, block, rows, queries, keys_in, id_rows, id_cols)
        top = jnp.max(scores, axis=0, keepdims=True)
        expd = jnp.exp2(scores - top)
        total = jnp.sum(expd, axis=0, keepdims=True)
        lse_ref[block : block + 1, :] = top + jnp.log2(total)
        total_ref[:seen, :] += jnp.dot(
            (expd * (1.0 / total)).astype(jnp.bfloat16),
            grad_rows[block * rows : seen, :],
            preferred_element_type=jnp.float32,
        )
    for offset, out_ref in enumerate(out_refs):
        at = pl.multiple_of((place ^ offset) * tall, tall)
        out_ref[...] = total_ref[pl.ds(at, tall), :].astype(jnp.bfloat16)


def query_grad_kernel(factor, scale, chips, rows, place_ref, *refs):
    packed, valued, grads = refs[:chips], refs[chips : 2 * chips], refs[2 * chips : 3 * chips]
    lse_ref, rank_ref = refs[3 * chips : 3 * chips + 2]
    refs = refs[3 * chips + 2 :]
    grad_refs, out_refs, refs = refs[:chips], refs[chips : chips + 2], refs[chips + 2 :]
    queries, keys_in, values, grad_rows, id_rows, id_cols, total_ref, dq_ref, attended_ref = refs
    head_dim = queries.shape[1]
    clusters = rank_ref.shape[1]
    tall = 2 * rows
    place = place_ref[0]
    in_order(place, packed, 0, queries)
    in_order(place, packed, tall, keys_in)
    in_order(place, valued, 0, values)
    order_grads(place, grads, rows, grad_rows, id_rows, id_cols)
    total_ref[...] = jnp.zeros_like(total_ref)
    for block in range(2 * chips):
        seen = (block + 1) * rows
        mine = slice(block * rows, seen)
        scores = block_scores(factor, block, rows, queries, keys_in, id_rows, id_cols)
        probs = jnp.exp2(scores - lse_ref[block : block + 1, :])
        seen_values = values[:seen, :]
        grad_probs = lax.dot_general(
            seen_values, grad_rows[mine, :], contract_last, preferred_element_type=jnp.float32
        )
        flipped = lax.dot_general(
            seen_values,
            probs.astype(jnp.bfloat16),
            contract_first,
            preferred_element_type=jnp.float32,
        )
        attended_ref[mine, :] = flipped.T.astype(jnp.bfloat16)
        weighted = probs * grad_probs
        delta = jnp.sum(weighted, axis=0, keepdims=True)
        grad_low = (weighted - probs * delta).astype(jnp.bfloat16)
        total_ref[:seen, :] += jnp.dot(
            grad_low, queries[mine, :], preferred_element_type=jnp.float32
        )
        flipped = lax.dot_general(
            keys_in[:seen, :], grad_low, contract_first, preferred_element_type=jnp.float32
        )
        dq_ref[mine, :] = (flipped.T * scale).astype(jnp.bfloat16)
    sums = jnp.zeros((clusters, head_dim), jnp.float32)
    cluster_at = lax.broadcasted_iota(jnp.int32, (clusters, rows), 0).astype(jnp.float32)
    for block in range(2 * chips):
        keys_float = keys_in[block * rows : (block + 1) * rows, :].astype(jnp.float32)
        unit = keys_float * lax.rsqrt(
            jnp.sum(keys_float * keys_float, axis=1, keepdims=True) + epsilon
        )
        unit_high = unit.astype(jnp.bfloat16)
        unit_low = (unit - unit_high.astype(jnp.float32)).astype(jnp.bfloat16)
        member = jnp.where(cluster_at == id_rows[block][:1, :], 1.0, 0.0).astype(jnp.bfloat16)
        sums += jnp.dot(member, unit_high, preferred_element_type=jnp.float32)
        sums += jnp.dot(member, unit_low, preferred_element_type=jnp.float32)
    rank_at = lax.broadcasted_iota(jnp.int32, (clusters, clusters), 0)
    ordered = jnp.where(rank_at == rank_ref[...], 1.0, 0.0).astype(jnp.bfloat16)
    ranked = jnp.dot(ordered, sums.astype(jnp.bfloat16), preferred_element_type=jnp.float32)
    attended_ref[2 * chips * rows :, :] = ranked.astype(jnp.bfloat16)
    owned = clusters // (2 * chips)
    for offset in range(chips):
        at = pl.ds(pl.multiple_of((place ^ offset) * tall, tall), tall)
        grad_refs[offset][:tall, :] = dq_ref[at, :]
        grad_refs[offset][tall:, :] = (total_ref[at, :] * scale).astype(jnp.bfloat16)
    for turn, out_ref in enumerate(out_refs):
        for chip in range(chips):
            shard = chip * 2 + (place_ref[1] ^ turn)
            at = pl.ds(pl.multiple_of(shard * rows, rows), rows)
            out_ref[chip, :rows, :] = attended_ref[at, :]
            at = pl.ds(pl.multiple_of(2 * chips * rows + shard * owned, owned), owned)
            out_ref[chip, rows:, :] = attended_ref[at, :]


def input_kernel(chips, place_ref, *refs):
    weights, (out_ref, gathered_ref) = refs[4 * chips : -2], refs[-2:]
    rows, width = out_ref.shape[0], weights[0].shape[1]
    head_dim = width // (2 * chips)
    for turn in range(2):
        parts = refs[turn * chips : (turn + 1) * chips]
        valued = refs[(2 + turn) * chips : (3 + turn) * chips]
        for offset in range(chips):
            head = (place_ref[1] ^ turn) * chips + (place_ref[0] ^ offset)
            for index in range(3):
                source = parts[offset] if index < 2 else valued[offset]
                at = pl.multiple_of((2 * (index % 2) + place_ref[2]) * rows, rows)
                start = pl.multiple_of(index * width + head * head_dim, head_dim)
                gathered_ref[:, pl.ds(start, head_dim)] = source[pl.ds(at, rows), :]
    flipped = None
    for index in range(3):
        term = lax.dot_general(
            weights[index][...],
            gathered_ref[:, index * width : (index + 1) * width],
            contract_last,
            preferred_element_type=jnp.float32,
        )
        flipped = term if flipped is None else flipped + term
    out_ref[...] = flipped.T.astype(out_ref.dtype)


def attended_kernel(chips, place_ref, *refs):
    parts, (attended_ref, sums_ref) = refs[:chips], refs[chips:]
    rows = attended_ref.shape[0]
    head_dim = sums_ref.shape[2]
    height = parts[0].shape[0] // 2
    for core in range(2):
        start = core * height
        for offset, part in enumerate(parts):
            head = core * chips + (place_ref[0] ^ offset)
            at = pl.multiple_of(head * head_dim, head_dim)
            attended_ref[:, pl.ds(at, head_dim)] = part[start : start + rows, :]
            sums_ref[head] = part[start + rows : start + height, :].astype(jnp.float32)


def sum_kernel(place_ref, first_ref, second_ref, kept_ref, hidden_ref):
    keeps = place_ref[2] == place_ref[1]
    second = jnp.where(keeps, kept_ref[...], second_ref[...]).astype(jnp.float32)
    hidden_ref[...] = (first_ref[...].astype(jnp.float32) + second).astype(jnp.bfloat16)


def by_head(hidden, w_query, w_key, w_value, cluster_rank, assign, d_attended):
    rows = hidden.shape[0]
    count = assign.shape[0]
    chips = count // 2
    half, width = w_query.shape
    head_dim = width // count
    tokens = count * rows
    clusters = cluster_rank.shape[0]
    owned = clusters // count
    scale = head_dim ** (-0.5)
    factor = scale * log2_e
    smem = pl.BlockSpec(memory_space=pltpu.SMEM)
    vmem = pl.BlockSpec(memory_space=pltpu.VMEM)
    anywhere = pl.BlockSpec(memory_space=pl.ANY)
    params = pltpu.CompilerParams(vmem_limit_bytes=32 * mebi)
    project_params = pltpu.CompilerParams(vmem_limit_bytes=32 * mebi)
    swap = [(0, 1), (1, 0)]
    chip, side, column = (lax.axis_index(name) for name in ("seq", "sub", "head"))
    place = jnp.stack([chip, side])

    def call(kernel, outs, *operands, scratch=(), hbm=0, limits=params, takes=1):
        return pl.pallas_call(
            kernel,
            out_shape=outs,
            in_specs=[smem] + [vmem] * (len(operands) - 1 - hbm) + [anywhere] * hbm,
            out_specs=jax.tree.map(lambda _: vmem, outs),
            scratch_shapes=list(scratch),
            compiler_params=limits,
            cost_estimate=pl.CostEstimate(
                flops=int(takes * 1.15e9), bytes_accessed=mebi, transcendentals=0
            ),
        )(*operands)

    def low(*shape):
        return jax.ShapeDtypeStruct(shape, jnp.bfloat16)

    def buffers(height):
        return (low(height, head_dim),) * chips

    def exchange(parts):
        moved = {
            offset: lax.ppermute(parts[offset], "seq", [(at, at ^ offset) for at in range(chips)])
            for offset in (2, 3, 1)
        }
        return (parts[0], moved[1], moved[2], moved[3])

    def to_sibling(piece):
        return lax.ppermute(piece, "sub", swap)

    hidden_other = to_sibling(hidden)
    block = low(chips, rows + id_lines(rows, head_dim), head_dim)
    grads_mine, grads_theirs = call(pack_kernel, (block, block), place, d_attended, assign)
    grads_other = to_sibling(grads_theirs)

    def stay(array):
        return pltpu.with_memory_space_constraint(array, pltpu.HBM)

    def project(turn, weights, *arrived):
        number = len(weights)
        outs = buffers(2 * number * rows) if turn == 0 else low(number, 2 * rows, width // 2)

        return call(
            partial(project_kernel, number, turn),
            outs,
            place,
            *arrived,
            stay(hidden),
            hidden_other,
            *(stay(weight) for weight in weights),
            scratch=[
                pltpu.VMEM((2 * rows, half), jnp.bfloat16),
                pltpu.VMEM((number, half, width // 2), jnp.bfloat16),
                pltpu.VMEM((2 * rows, width // 2), jnp.bfloat16),
                pltpu.SemaphoreType.DMA((number, 4)),
                pltpu.SemaphoreType.DMA((2,)),
            ],
            hbm=2 + number,
            limits=project_params,
            takes=(8 if number == 2 else 0.1) if turn == 0 else 0.1,
        )

    merged = call(merge_kernel, buffers(2 * block.shape[1]), place, grads_mine, grads_other)
    grads = exchange(merged)
    hidden_other, _ = lax.optimization_barrier((hidden_other, merged[0]))
    early, late = (w_query, w_key), (w_value,)
    early_arrived = to_sibling(project(1, early))
    late_arrived = to_sibling(project(1, late))
    grads = exchange(call(merge_kernel, buffers(2 * block.shape[1]), place, grads_mine, grads_other))
    early_arrived, _ = lax.optimization_barrier((early_arrived, grads[0]))
    early_projected = project(0, early, early_arrived)
    packed = exchange(early_projected)
    late_arrived, _, _ = lax.optimization_barrier((late_arrived, early_projected[0], (grads[2], grads[3])))
    late_projected = project(0, late, late_arrived)
    valued = exchange(late_projected)
    packed = lax.optimization_barrier((*packed, late_projected[0]))[:chips]

    def held(kind):
        return pltpu.VMEM((tokens, head_dim), kind)

    id_scratch = [pltpu.VMEM((count, 8, rows), jnp.float32), held(jnp.float32)]
    *value_grads, lse = call(
        partial(value_grad_kernel, factor, chips, rows),
        (*buffers(2 * rows), jax.ShapeDtypeStruct((count, rows), jnp.float32)),
        place,
        *packed,
        *grads,
        scratch=[held(jnp.bfloat16)] * 3 + id_scratch + [held(jnp.float32)],
        takes=7,
    )
    value_back = exchange(value_grads)
    results = call(
        partial(query_grad_kernel, factor, scale, chips, rows),
        (*buffers(4 * rows), *(low(chips, rows + owned, head_dim),) * 2),
        place,
        *packed,
        *valued,
        *grads,
        lse,
        cluster_rank.reshape(1, clusters),
        scratch=[held(jnp.bfloat16)] * 4
        + id_scratch
        + [
            held(jnp.float32),
            held(jnp.bfloat16),
            pltpu.VMEM((tokens + clusters, head_dim), jnp.bfloat16),
        ],
        takes=10,
    )
    *ready, _, _ = lax.optimization_barrier((*results[:chips], value_back[2], value_back[3]))
    back = exchange(ready)

    attended_mine, attended_theirs = results[chips:]
    outputs = call(
        merge_kernel, buffers(2 * (rows + owned)), place, attended_mine, to_sibling(attended_theirs)
    )
    back_other = tuple(to_sibling(part) for part in back)
    value_other = tuple(to_sibling(part) for part in value_back)

    def input_part(shard):
        return call(
            partial(input_kernel, chips),
            low(rows, half),
            jnp.stack([chip, side, shard]),
            *back,
            *back_other,
            *value_back,
            *value_other,
            w_query,
            w_key,
            w_value,
            scratch=[pltpu.VMEM((rows, 3 * width), jnp.bfloat16)],
            takes=3,
        )

    square = ("head", "sub")
    crossing = input_part(1 - column)
    first = lax.ppermute(crossing, square, [(0, 1), (1, 3), (3, 2), (2, 0)])
    kept = input_part(lax.optimization_barrier((column, crossing))[0])
    second = lax.ppermute(kept, square, [(1, 2), (2, 1)])
    *outputs, _, _ = lax.optimization_barrier((*outputs, back[2], back[3]))
    returned = exchange(outputs)
    corner = jnp.stack([chip, side, column])
    *returned, _ = lax.optimization_barrier((*returned, first))
    attended, centroid_sums = call(
        partial(attended_kernel, chips),
        (low(rows, width), jax.ShapeDtypeStruct((count, owned, head_dim), jnp.float32)),
        corner,
        *returned,
    )
    first, _ = lax.optimization_barrier((first, attended))
    d_hidden = call(sum_kernel, low(rows, half), corner, first, second, kept)
    return (attended, d_hidden, centroid_sums)


def per_device(hidden, w_query, w_key, w_value, cluster_rank, assign, d_attended):
    chips = lax.axis_size("seq")
    fits = chips == 4 and lax.axis_size("sub") == 2 and lax.axis_size("head") == 2
    plan = by_head if fits and assign.shape[0] == 2 * chips else by_owner
    return plan(hidden, w_query, w_key, w_value, cluster_rank, assign, d_attended)


def solution(mesh):
    placed = (
        P(("groups", "seq", "sub"), None),
        P("sub", "head"),
        P("sub", "head"),
        P("sub", "head"),
        P("groups"),
        P("head", ("groups", "seq", "sub")),
        P(("groups", "seq", "sub"), "head"),
    )
    return jax.shard_map(
        per_device,
        mesh=mesh,
        in_specs=placed,
        out_specs=(
            P(("groups", "seq", "sub"), "head"),
            P(("groups", "seq", "sub"), "head"),
            P("head", ("groups", "seq", "sub"), None),
        ),
        check_vma=False,
    )
```

```python
from functools import partial

import jax
import jax.numpy as jnp
from jax import lax
from jax.experimental import pallas as pl
from jax.experimental.pallas import tpu as pltpu
from jax.sharding import PartitionSpec as P

epsilon = 1e-06


def keep_mask(filled, cluster_ids, positions):
    count = filled.shape[0]
    same = filled[:, None] & filled[None, :] & (cluster_ids[:, None] == cluster_ids[None, :])
    causal = positions[None, :] <= positions[:, None]
    diagonal = jnp.arange(count)[:, None] == jnp.arange(count)[None, :]
    return same & causal | diagonal


def head_forward(packed, scale):
    queries, keys_in, values, filled, cluster_ids, positions = packed
    scores = (
        lax.dot_general(
            queries, keys_in, (((1,), (1,)), ((), ())), preferred_element_type=jnp.float32
        )
        * scale
    )
    allowed = keep_mask(filled, cluster_ids, positions)
    row_top = jnp.max(jnp.where(allowed, scores, -jnp.inf), axis=1)
    expd = jnp.where(allowed, jnp.exp(scores - row_top[:, None]), 0.0)
    row_total = jnp.sum(expd, axis=1)
    probs_low = (expd / row_total[:, None]).astype(jnp.bfloat16)
    outputs = jnp.dot(probs_low, values, preferred_element_type=jnp.float32).astype(jnp.bfloat16)
    return (outputs, row_top, row_total)


def head_backward(packed, scale):
    queries, keys_in, values, grads_in, filled, cluster_ids, positions, row_top, row_total = packed
    contract_last = (((1,), (1,)), ((), ()))
    contract_first = (((0,), (0,)), ((), ()))
    scores = (
        lax.dot_general(queries, keys_in, contract_last, preferred_element_type=jnp.float32) * scale
    )
    allowed = keep_mask(filled, cluster_ids, positions)
    probs = jnp.where(allowed, jnp.exp(scores - row_top[:, None]), 0.0) / row_total[:, None]
    probs_low = probs.astype(jnp.bfloat16)
    grad_probs = lax.dot_general(
        grads_in, values, contract_last, preferred_element_type=jnp.float32
    )
    delta_rows = jnp.sum(probs * grad_probs, axis=1)
    grad_low = (probs * (grad_probs - delta_rows[:, None]) * scale).astype(jnp.bfloat16)
    grad_query = jnp.dot(grad_low, keys_in, preferred_element_type=jnp.float32).astype(jnp.bfloat16)
    grad_key = lax.dot_general(
        grad_low, queries, contract_first, preferred_element_type=jnp.float32
    ).astype(jnp.bfloat16)
    grad_value = lax.dot_general(
        probs_low, grads_in, contract_first, preferred_element_type=jnp.float32
    ).astype(jnp.bfloat16)
    return (grad_query, grad_key, grad_value)


def by_owner(hidden, w_query, w_key, w_value, cluster_rank, assign, d_attended):
    tok_rows = hidden.shape[0]
    heads_here = assign.shape[0]
    head_dim = w_query.shape[1] // heads_here
    clusters = cluster_rank.shape[0]
    seq_count = lax.axis_size("seq")
    sub_count = lax.axis_size("sub")
    owners = seq_count * sub_count
    capacity = 2 * tok_rows // owners
    slot_count = owners * capacity
    per_owner = clusters // owners
    scale = head_dim ** (-0.5)
    pieces = (
        lax.all_gather(w_query, "sub", axis=0, tiled=True),
        lax.all_gather(w_key, "sub", axis=0, tiled=True),
        lax.all_gather(w_value, "sub", axis=0, tiled=True),
    )
    projected = tuple(
        (
            jnp.dot(hidden, weight_piece, preferred_element_type=jnp.float32)
            for weight_piece in pieces
        )
    )

    def split_heads(matrix):
        return (
            matrix.astype(jnp.bfloat16).reshape(tok_rows, heads_here, head_dim).transpose(1, 0, 2)
        )

    queries, keys_all, values = tuple((split_heads(matrix) for matrix in projected))
    cluster_range = jnp.arange(clusters, dtype=jnp.int32)
    rank_tok = jnp.sum(jnp.where(assign[:, :, None] == cluster_range, cluster_rank, 0), axis=2)
    owner_ids = rank_tok // per_owner
    owner_hot = (owner_ids[:, :, None] == jnp.arange(owners, dtype=jnp.int32)).astype(jnp.int32)
    within = jnp.sum(owner_hot * (jnp.cumsum(owner_hot, axis=1) - 1), axis=2)
    slot_tok = owner_ids * capacity + within
    token_ids = jnp.arange(tok_rows, dtype=jnp.int32)
    slot_range = jnp.arange(slot_count, dtype=jnp.int32)
    slot_match = slot_tok[:, None, :] == slot_range[None, :, None]
    slot_hot = slot_match.astype(jnp.bfloat16)

    def to_slots(rows_in):
        kept = jnp.einsum(
            "hst,htd->hsd", slot_hot, rows_in, preferred_element_type=jnp.float32
        ).astype(jnp.bfloat16)
        return kept.reshape(heads_here, owners, capacity, head_dim)

    def from_slots(slotted):
        flat_slots = slotted.reshape(heads_here, slot_count, head_dim)
        return jnp.einsum(
            "hst,hsd->htd", slot_hot, flat_slots, preferred_element_type=jnp.float32
        ).astype(jnp.bfloat16)

    def exchange_three(first, second, third):
        return (
            lax.all_to_all(first, ("seq", "sub"), split_axis=1, concat_axis=1, tiled=True),
            lax.all_to_all(second, ("seq", "sub"), split_axis=1, concat_axis=1, tiled=True),
            lax.all_to_all(third, ("seq", "sub"), split_axis=1, concat_axis=1, tiled=True),
        )

    sent = exchange_three(to_slots(queries), to_slots(keys_all), to_slots(values))
    tag_tok = assign * tok_rows + token_ids
    slot_tag = jnp.sum(jnp.where(slot_match, tag_tok[:, None, :] + 1, 0), axis=2) - 1
    tags = lax.all_to_all(
        slot_tag.reshape(heads_here, owners, capacity),
        ("seq", "sub"),
        split_axis=1,
        concat_axis=1,
        tiled=True,
    )
    tags = tags.reshape(heads_here, slot_count)
    owner_q, owner_k, owner_v = tuple(
        (member.reshape(heads_here, slot_count, head_dim) for member in sent)
    )
    filled = tags >= 0
    cluster_ids = jnp.where(filled, tags // tok_rows, -1)
    positions = slot_range // capacity * tok_rows + tags % tok_rows
    outputs, row_top, row_total = lax.map(
        partial(head_forward, scale=scale),
        (owner_q, owner_k, owner_v, filled, cluster_ids, positions),
    )
    returned = lax.all_to_all(
        outputs.reshape(heads_here, owners, capacity, head_dim),
        ("seq", "sub"),
        split_axis=1,
        concat_axis=1,
        tiled=True,
    )

    def merge_heads(slotted):
        return from_slots(slotted).transpose(1, 0, 2).reshape(tok_rows, heads_here * head_dim)

    attended = merge_heads(returned)
    grads_tok = d_attended.reshape(tok_rows, heads_here, head_dim).transpose(1, 0, 2)
    owner_g = lax.all_to_all(
        to_slots(grads_tok), ("seq", "sub"), split_axis=1, concat_axis=1, tiled=True
    ).reshape(heads_here, slot_count, head_dim)
    grad_q, grad_k, grad_v = lax.map(
        partial(head_backward, scale=scale),
        (owner_q, owner_k, owner_v, owner_g, filled, cluster_ids, positions, row_top, row_total),
    )
    shape_four = (heads_here, owners, capacity, head_dim)
    back = exchange_three(
        grad_q.reshape(shape_four), grad_k.reshape(shape_four), grad_v.reshape(shape_four)
    )
    token_grads = tuple((merge_heads(member) for member in back))
    pieces = lax.all_gather((w_query, w_key, w_value), "sub", axis=0, tiled=True)
    terms = [
        jnp.einsum("tc,rc->tr", grad_rows_in, weight_piece, preferred_element_type=jnp.float32)
        for grad_rows_in, weight_piece in zip(token_grads, pieces)
    ]
    partial_grad = terms[0] + terms[1] + terms[2]
    d_hidden = lax.psum_scatter(
        partial_grad.astype(jnp.bfloat16), "head", scatter_dimension=1, tiled=True
    )
    keys_float = keys_all.astype(jnp.float32)
    unit_keys = keys_float * lax.rsqrt(
        jnp.sum(keys_float * keys_float, axis=2, keepdims=True) + epsilon
    )
    member_hot = (rank_tok[:, :, None] == cluster_range).astype(jnp.float32)
    local_sums = jnp.einsum("htr,htd->hrd", member_hot, unit_keys, precision=lax.Precision.HIGHEST)
    centroid_sums = lax.psum_scatter(
        local_sums.astype(jnp.bfloat16), ("seq", "sub"), scatter_dimension=1, tiled=True
    ).astype(jnp.float32)
    return (attended, d_hidden, centroid_sums)


contract_last = (((1,), (1,)), ((), ()))
contract_first = (((0,), (0,)), ((), ()))
log2_e = 1.4426950408889634
mebi = 1024 * 1024


def id_lines(rows, head_dim):
    return -(-(rows // head_dim) // 16) * 16


def pack_kernel(place_ref, grads_ref, assign_ref, mine_ref, theirs_ref):
    chips, padded, head_dim = mine_ref.shape
    rows = grads_ref.shape[0]
    spare = padded - rows - rows // head_dim
    for turn, out_ref in enumerate((mine_ref, theirs_ref)):
        for chip in range(chips):
            head = (place_ref[1] ^ turn) * chips + chip
            at = pl.multiple_of(head * head_dim, head_dim)
            out_ref[chip, :rows, :] = grads_ref[:, pl.ds(at, head_dim)]
            ids = assign_ref[pl.ds(head, 1), :].astype(jnp.float32)
            lines = [
                ids[:, start : start + head_dim] for start in range(0, rows, head_dim)
            ] + [jnp.zeros((spare, head_dim), jnp.float32)]
            out_ref[chip, rows:, :] = jnp.concatenate(lines, axis=0).astype(jnp.bfloat16)


def merge_kernel(place_ref, mine_ref, theirs_ref, *out_refs):
    height = mine_ref.shape[1]
    for turn, held_ref in enumerate((mine_ref, theirs_ref)):
        at = pl.ds(pl.multiple_of((place_ref[1] ^ turn) * height, height), height)
        for offset, out_ref in enumerate(out_refs):
            out_ref[at, :] = held_ref[place_ref[0] ^ offset]


def fetch_columns(half, weights, held_ref, sems):
    chunks = sems.shape[1]
    columns = held_ref.shape[2]
    rows = held_ref.shape[1] // chunks
    at = pl.ds(pl.multiple_of(half * columns, columns), columns)
    copies = []
    for index, weight in enumerate(weights):
        for chunk in range(chunks):
            lines = pl.ds(chunk * rows, rows)
            copy = pltpu.make_async_copy(
                weight.at[lines, at], held_ref.at[index, lines], sems.at[index, chunk]
            )
            copy.start()
            copies.append(copy)
    return copies


def project_kernel(count, turn, place_ref, *refs):
    if turn == 0:
        arrived_ref, refs = refs[0], refs[1:]
    tokens, weights, refs = refs[:2], refs[2 : 2 + count], refs[2 + count :]
    out_refs, (joined_ref, held_ref, low_ref, sems, token_sems) = refs[:-5], refs[-5:]
    side = place_ref[1]
    tall, depth = joined_ref.shape
    rows = tall // 2
    near = pl.ds(pl.multiple_of(side * depth, depth), depth)
    joins = []
    for core, source in enumerate(tokens):
        at = pl.ds(pl.multiple_of((side ^ core) * rows, rows), rows)
        joins.append(
            pltpu.make_async_copy(source.at[:, near], joined_ref.at[at], token_sems.at[core])
        )
        joins[core].start()
    copies = fetch_columns(side ^ turn, weights, held_ref, sems)
    for copy in joins:
        copy.wait()
    chunks = sems.shape[1]
    for index in range(count):
        for chunk in range(chunks):
            copies[index * chunks + chunk].wait()
        total = jnp.dot(joined_ref[...], held_ref[index], preferred_element_type=jnp.float32)
        if turn == 1:
            out_refs[0][index] = total.astype(jnp.bfloat16)
            continue
        low_ref[...] = (total + arrived_ref[index].astype(jnp.float32)).astype(jnp.bfloat16)
        for offset, out_ref in enumerate(out_refs):
            head_dim = out_ref.shape[1]
            at = pl.multiple_of((place_ref[0] ^ offset) * head_dim, head_dim)
            out_ref[index * tall : (index + 1) * tall, :] = low_ref[:, pl.ds(at, head_dim)]


def in_order(place, parts, start, ordered):
    for offset, part in enumerate(parts):
        tall = ordered.shape[0] // len(parts)
        at = pl.ds(pl.multiple_of((place ^ offset) * tall, tall), tall)
        ordered[at, :] = part[start : start + tall, :]


def order_grads(place, parts, rows, grad_rows, id_rows, id_cols):
    head_dim = grad_rows.shape[1]
    height = parts[0].shape[0] // 2
    for offset, part in enumerate(parts):
        for core in range(2):
            block = (place ^ offset) * 2 + core
            at = pl.ds(pl.multiple_of(block * rows, rows), rows)
            start = core * height
            grad_rows[at, :] = part[start : start + rows, :]
            lines = part[start + rows : start + rows + 16, :].astype(jnp.float32)
            ids = jnp.concatenate(
                [lines[line : line + 1, :] for line in range(rows // head_dim)], axis=1
            )
            id_rows[block] = jnp.broadcast_to(ids, id_rows.shape[1:])
            id_cols[at, :] = jnp.broadcast_to(ids, (head_dim, rows)).T


def block_scores(factor, block, rows, queries, keys_in, id_rows, id_cols):
    head_dim = queries.shape[1]
    seen = (block + 1) * rows
    scores = lax.dot_general(
        keys_in[:seen, :],
        queries[block * rows : seen, :],
        contract_last,
        preferred_element_type=jnp.float32,
    )
    ids = id_cols[:seen, :]
    mine = id_rows[block][:1, :]
    same = jnp.concatenate(
        [ids == mine[:, start : start + head_dim] for start in range(0, rows, head_dim)], axis=1
    )
    key_at = lax.broadcasted_iota(jnp.int32, (rows, rows), 0)
    query_at = lax.broadcasted_iota(jnp.int32, (rows, rows), 1)
    last = same[seen - rows :] & (key_at <= query_at)
    allowed = last if block == 0 else jnp.concatenate([same[: seen - rows], last], axis=0)
    return jnp.where(allowed, scores * factor, -jnp.inf)


def value_grad_kernel(factor, chips, rows, place_ref, *refs):
    packed, grads = refs[:chips], refs[chips : 2 * chips]
    out_refs, lse_ref = refs[2 * chips : 3 * chips], refs[3 * chips]
    queries, keys_in, grad_rows, id_rows, id_cols, total_ref = refs[3 * chips + 1 :]
    tall = 2 * rows
    place = place_ref[0]
    in_order(place, packed, 0, queries)
    in_order(place, packed, tall, keys_in)
    order_grads(place, grads, rows, grad_rows, id_rows, id_cols)
    total_ref[...] = jnp.zeros_like(total_ref)
    for block in range(2 * chips):
        seen = (block + 1) * rows
        scores = block_scores(factor, block, rows, queries, keys_in, id_rows, id_cols)
        top = jnp.max(scores, axis=0, keepdims=True)
        expd = jnp.exp2(scores - top)
        total = jnp.sum(expd, axis=0, keepdims=True)
        lse_ref[block : block + 1, :] = top + jnp.log2(total)
        total_ref[:seen, :] += jnp.dot(
            (expd * (1.0 / total)).astype(jnp.bfloat16),
            grad_rows[block * rows : seen, :],
            preferred_element_type=jnp.float32,
        )
    for offset, out_ref in enumerate(out_refs):
        at = pl.multiple_of((place ^ offset) * tall, tall)
        out_ref[...] = total_ref[pl.ds(at, tall), :].astype(jnp.bfloat16)


def query_grad_kernel(factor, scale, chips, rows, place_ref, *refs):
    packed, valued, grads = refs[:chips], refs[chips : 2 * chips], refs[2 * chips : 3 * chips]
    lse_ref, rank_ref = refs[3 * chips : 3 * chips + 2]
    refs = refs[3 * chips + 2 :]
    grad_refs, out_refs, refs = refs[:chips], refs[chips : chips + 2], refs[chips + 2 :]
    queries, keys_in, values, grad_rows, id_rows, id_cols, total_ref, dq_ref, attended_ref = refs
    head_dim = queries.shape[1]
    clusters = rank_ref.shape[1]
    tall = 2 * rows
    place = place_ref[0]
    in_order(place, packed, 0, queries)
    in_order(place, packed, tall, keys_in)
    in_order(place, valued, 0, values)
    order_grads(place, grads, rows, grad_rows, id_rows, id_cols)
    total_ref[...] = jnp.zeros_like(total_ref)
    for block in range(2 * chips):
        seen = (block + 1) * rows
        mine = slice(block * rows, seen)
        scores = block_scores(factor, block, rows, queries, keys_in, id_rows, id_cols)
        probs = jnp.exp2(scores - lse_ref[block : block + 1, :])
        seen_values = values[:seen, :]
        grad_probs = lax.dot_general(
            seen_values, grad_rows[mine, :], contract_last, preferred_element_type=jnp.float32
        )
        flipped = lax.dot_general(
            seen_values,
            probs.astype(jnp.bfloat16),
            contract_first,
            preferred_element_type=jnp.float32,
        )
        attended_ref[mine, :] = flipped.T.astype(jnp.bfloat16)
        weighted = probs * grad_probs
        delta = jnp.sum(weighted, axis=0, keepdims=True)
        grad_low = (weighted - probs * delta).astype(jnp.bfloat16)
        total_ref[:seen, :] += jnp.dot(
            grad_low, queries[mine, :], preferred_element_type=jnp.float32
        )
        flipped = lax.dot_general(
            keys_in[:seen, :], grad_low, contract_first, preferred_element_type=jnp.float32
        )
        dq_ref[mine, :] = (flipped.T * scale).astype(jnp.bfloat16)
    sums = jnp.zeros((clusters, head_dim), jnp.float32)
    cluster_at = lax.broadcasted_iota(jnp.int32, (clusters, rows), 0).astype(jnp.float32)
    for block in range(2 * chips):
        keys_float = keys_in[block * rows : (block + 1) * rows, :].astype(jnp.float32)
        unit = keys_float * lax.rsqrt(
            jnp.sum(keys_float * keys_float, axis=1, keepdims=True) + epsilon
        )
        unit_high = unit.astype(jnp.bfloat16)
        unit_low = (unit - unit_high.astype(jnp.float32)).astype(jnp.bfloat16)
        member = jnp.where(cluster_at == id_rows[block][:1, :], 1.0, 0.0).astype(jnp.bfloat16)
        sums += jnp.dot(member, unit_high, preferred_element_type=jnp.float32)
        sums += jnp.dot(member, unit_low, preferred_element_type=jnp.float32)
    rank_at = lax.broadcasted_iota(jnp.int32, (clusters, clusters), 0)
    ordered = jnp.where(rank_at == rank_ref[...], 1.0, 0.0).astype(jnp.bfloat16)
    ranked = jnp.dot(ordered, sums.astype(jnp.bfloat16), preferred_element_type=jnp.float32)
    attended_ref[2 * chips * rows :, :] = ranked.astype(jnp.bfloat16)
    owned = clusters // (2 * chips)
    for offset in range(chips):
        at = pl.ds(pl.multiple_of((place ^ offset) * tall, tall), tall)
        grad_refs[offset][:tall, :] = dq_ref[at, :]
        grad_refs[offset][tall:, :] = (total_ref[at, :] * scale).astype(jnp.bfloat16)
    for turn, out_ref in enumerate(out_refs):
        for chip in range(chips):
            shard = chip * 2 + (place_ref[1] ^ turn)
            at = pl.ds(pl.multiple_of(shard * rows, rows), rows)
            out_ref[chip, :rows, :] = attended_ref[at, :]
            at = pl.ds(pl.multiple_of(2 * chips * rows + shard * owned, owned), owned)
            out_ref[chip, rows:, :] = attended_ref[at, :]


def input_kernel(chips, which, place_ref, *refs):
    weights, (out_ref, gathered_ref) = refs[4 * chips : -2], refs[-2:]
    rows, width = out_ref.shape[0], weights[0].shape[1]
    head_dim = width // (2 * chips)
    for turn in range(2):
        parts = refs[turn * chips : (turn + 1) * chips]
        valued = refs[(2 + turn) * chips : (3 + turn) * chips]
        for offset in range(chips):
            head = (place_ref[1] ^ turn) * chips + (place_ref[0] ^ offset)
            for index in range(3):
                source = parts[offset] if index < 2 else valued[offset]
                at = pl.multiple_of((2 * (index % 2) + place_ref[which]) * rows, rows)
                start = pl.multiple_of(index * width + head * head_dim, head_dim)
                gathered_ref[:, pl.ds(start, head_dim)] = source[pl.ds(at, rows), :]
    flipped = None
    for index in range(3):
        term = lax.dot_general(
            weights[index][...],
            gathered_ref[:, index * width : (index + 1) * width],
            contract_last,
            preferred_element_type=jnp.float32,
        )
        flipped = term if flipped is None else flipped + term
    out_ref[...] = flipped.T.astype(out_ref.dtype)


def attended_kernel(chips, place_ref, *refs):
    parts, (attended_ref, sums_ref) = refs[:chips], refs[chips:]
    rows = attended_ref.shape[0]
    head_dim = sums_ref.shape[2]
    height = parts[0].shape[0] // 2
    for core in range(2):
        start = core * height
        for offset, part in enumerate(parts):
            head = core * chips + (place_ref[0] ^ offset)
            at = pl.multiple_of(head * head_dim, head_dim)
            attended_ref[:, pl.ds(at, head_dim)] = part[start : start + rows, :]
            sums_ref[head] = part[start + rows : start + height, :].astype(jnp.float32)


def sum_kernel(place_ref, first_ref, second_ref, kept_ref, hidden_ref):
    keeps = place_ref[2] == place_ref[1]
    second = jnp.where(keeps, kept_ref[...], second_ref[...]).astype(jnp.float32)
    hidden_ref[...] = (first_ref[...].astype(jnp.float32) + second).astype(jnp.bfloat16)


def by_head(hidden, w_query, w_key, w_value, cluster_rank, assign, d_attended):
    rows = hidden.shape[0]
    count = assign.shape[0]
    chips = count // 2
    half, width = w_query.shape
    head_dim = width // count
    tokens = count * rows
    clusters = cluster_rank.shape[0]
    owned = clusters // count
    scale = head_dim ** (-0.5)
    factor = scale * log2_e
    smem = pl.BlockSpec(memory_space=pltpu.SMEM)
    vmem = pl.BlockSpec(memory_space=pltpu.VMEM)
    anywhere = pl.BlockSpec(memory_space=pl.ANY)
    params = pltpu.CompilerParams(vmem_limit_bytes=32 * mebi)
    project_params = pltpu.CompilerParams(vmem_limit_bytes=32 * mebi)
    swap = [(0, 1), (1, 0)]
    chip, side, column = (lax.axis_index(name) for name in ("seq", "sub", "head"))
    place = jnp.stack([chip, side, column, 1 - column])

    def call(kernel, outs, *operands, scratch=(), hbm=0, limits=params, takes=1):
        return pl.pallas_call(
            kernel,
            out_shape=outs,
            in_specs=[smem] + [vmem] * (len(operands) - 1 - hbm) + [anywhere] * hbm,
            out_specs=jax.tree.map(lambda _: vmem, outs),
            scratch_shapes=list(scratch),
            compiler_params=limits,
            cost_estimate=pl.CostEstimate(
                flops=int(takes * 1.15e9), bytes_accessed=mebi, transcendentals=0
            ),
        )(*operands)

    def low(*shape):
        return jax.ShapeDtypeStruct(shape, jnp.bfloat16)

    def buffers(height):
        return (low(height, head_dim),) * chips

    def exchange(parts):
        moved = {
            offset: lax.ppermute(parts[offset], "seq", [(at, at ^ offset) for at in range(chips)])
            for offset in (2, 3, 1)
        }
        return (parts[0], moved[1], moved[2], moved[3])

    def to_sibling(piece):
        return lax.ppermute(piece, "sub", swap)

    hidden_other = to_sibling(hidden)
    block = low(chips, rows + id_lines(rows, head_dim), head_dim)
    grads_mine, grads_theirs = call(pack_kernel, (block, block), place, d_attended, assign)
    grads_other = to_sibling(grads_theirs)

    def stay(array):
        return pltpu.with_memory_space_constraint(array, pltpu.HBM)

    def project(turn, weights, *arrived):
        number = len(weights)
        outs = buffers(2 * number * rows) if turn == 0 else low(number, 2 * rows, width // 2)

        return call(
            partial(project_kernel, number, turn),
            outs,
            place,
            *arrived,
            stay(hidden),
            hidden_other,
            *(stay(weight) for weight in weights),
            scratch=[
                pltpu.VMEM((2 * rows, half), jnp.bfloat16),
                pltpu.VMEM((number, half, width // 2), jnp.bfloat16),
                pltpu.VMEM((2 * rows, width // 2), jnp.bfloat16),
                pltpu.SemaphoreType.DMA((number, 4)),
                pltpu.SemaphoreType.DMA((2,)),
            ],
            hbm=2 + number,
            limits=project_params,
            takes=(8 if number == 2 else 0.1) if turn == 0 else 0.1,
        )

    merged = call(merge_kernel, buffers(2 * block.shape[1]), place, grads_mine, grads_other)
    grads = exchange(merged)
    hidden_other, _ = lax.optimization_barrier((hidden_other, merged[0]))
    early, late = (w_query, w_key), (w_value,)
    early_arrived = to_sibling(project(1, early))
    late_arrived = to_sibling(project(1, late))
    grads = exchange(call(merge_kernel, buffers(2 * block.shape[1]), place, grads_mine, grads_other))
    early_arrived, _ = lax.optimization_barrier((early_arrived, grads[0]))
    early_projected = project(0, early, early_arrived)
    packed = exchange(early_projected)
    late_arrived, _, _ = lax.optimization_barrier((late_arrived, early_projected[0], (grads[2], grads[3])))
    late_projected = project(0, late, late_arrived)
    valued = exchange(late_projected)
    packed = lax.optimization_barrier((*packed, late_projected[0]))[:chips]

    def held(kind):
        return pltpu.VMEM((tokens, head_dim), kind)

    id_scratch = [pltpu.VMEM((count, 8, rows), jnp.float32), held(jnp.float32)]
    *value_grads, lse = call(
        partial(value_grad_kernel, factor, chips, rows),
        (*buffers(2 * rows), jax.ShapeDtypeStruct((count, rows), jnp.float32)),
        place,
        *packed,
        *grads,
        scratch=[held(jnp.bfloat16)] * 3 + id_scratch + [held(jnp.float32)],
        takes=7,
    )
    value_back = exchange(value_grads)
    results = call(
        partial(query_grad_kernel, factor, scale, chips, rows),
        (*buffers(4 * rows), *(low(chips, rows + owned, head_dim),) * 2),
        place,
        *packed,
        *valued,
        *grads,
        lse,
        cluster_rank.reshape(1, clusters),
        scratch=[held(jnp.bfloat16)] * 4
        + id_scratch
        + [
            held(jnp.float32),
            held(jnp.bfloat16),
            pltpu.VMEM((tokens + clusters, head_dim), jnp.bfloat16),
        ],
        takes=10,
    )
    *ready, _, _ = lax.optimization_barrier((*results[:chips], value_back[2], value_back[3]))
    back = exchange(ready)

    attended_mine, attended_theirs = results[chips:]
    outputs = call(
        merge_kernel, buffers(2 * (rows + owned)), place, attended_mine, to_sibling(attended_theirs)
    )
    back_other = tuple(to_sibling(part) for part in back)
    value_other = tuple(to_sibling(part) for part in value_back)

    def input_part(which, place):
        return call(
            partial(input_kernel, chips, which),
            low(rows, half),
            place,
            *back,
            *back_other,
            *value_back,
            *value_other,
            w_query,
            w_key,
            w_value,
            scratch=[pltpu.VMEM((rows, 3 * width), jnp.bfloat16)],
            takes=3,
        )

    square = ("head", "sub")
    crossing = input_part(3, place)
    first = lax.ppermute(crossing, square, [(0, 1), (1, 3), (3, 2), (2, 0)])
    kept = input_part(2, lax.optimization_barrier((place, crossing))[0])
    second = lax.ppermute(kept, square, [(1, 2), (2, 1)])
    *outputs, _, _ = lax.optimization_barrier((*outputs, back[2], back[3]))
    returned = exchange(outputs)
    *returned, _ = lax.optimization_barrier((*returned, first))
    attended, centroid_sums = call(
        partial(attended_kernel, chips),
        (low(rows, width), jax.ShapeDtypeStruct((count, owned, head_dim), jnp.float32)),
        place,
        *returned,
    )
    first, _ = lax.optimization_barrier((first, attended))
    d_hidden = call(sum_kernel, low(rows, half), place, first, second, kept)
    return (attended, d_hidden, centroid_sums)


def per_device(hidden, w_query, w_key, w_value, cluster_rank, assign, d_attended):
    chips = lax.axis_size("seq")
    fits = chips == 4 and lax.axis_size("sub") == 2 and lax.axis_size("head") == 2
    plan = by_head if fits and assign.shape[0] == 2 * chips else by_owner
    return plan(hidden, w_query, w_key, w_value, cluster_rank, assign, d_attended)


def solution(mesh):
    placed = (
        P(("groups", "seq", "sub"), None),
        P("sub", "head"),
        P("sub", "head"),
        P("sub", "head"),
        P("groups"),
        P("head", ("groups", "seq", "sub")),
        P(("groups", "seq", "sub"), "head"),
    )
    return jax.shard_map(
        per_device,
        mesh=mesh,
        in_specs=placed,
        out_specs=(
            P(("groups", "seq", "sub"), "head"),
            P(("groups", "seq", "sub"), "head"),
            P("head", ("groups", "seq", "sub"), None),
        ),
        check_vma=False,
    )
```

```python
from functools import partial

import jax
import jax.numpy as jnp
from jax import lax
from jax.experimental import pallas as pl
from jax.experimental.pallas import tpu as pltpu
from jax.sharding import PartitionSpec as P

epsilon = 1e-06


def keep_mask(filled, cluster_ids, positions):
    count = filled.shape[0]
    same = filled[:, None] & filled[None, :] & (cluster_ids[:, None] == cluster_ids[None, :])
    causal = positions[None, :] <= positions[:, None]
    diagonal = jnp.arange(count)[:, None] == jnp.arange(count)[None, :]
    return same & causal | diagonal


def head_forward(packed, scale):
    queries, keys_in, values, filled, cluster_ids, positions = packed
    scores = (
        lax.dot_general(
            queries, keys_in, (((1,), (1,)), ((), ())), preferred_element_type=jnp.float32
        )
        * scale
    )
    allowed = keep_mask(filled, cluster_ids, positions)
    row_top = jnp.max(jnp.where(allowed, scores, -jnp.inf), axis=1)
    expd = jnp.where(allowed, jnp.exp(scores - row_top[:, None]), 0.0)
    row_total = jnp.sum(expd, axis=1)
    probs_low = (expd / row_total[:, None]).astype(jnp.bfloat16)
    outputs = jnp.dot(probs_low, values, preferred_element_type=jnp.float32).astype(jnp.bfloat16)
    return (outputs, row_top, row_total)


def head_backward(packed, scale):
    queries, keys_in, values, grads_in, filled, cluster_ids, positions, row_top, row_total = packed
    contract_last = (((1,), (1,)), ((), ()))
    contract_first = (((0,), (0,)), ((), ()))
    scores = (
        lax.dot_general(queries, keys_in, contract_last, preferred_element_type=jnp.float32) * scale
    )
    allowed = keep_mask(filled, cluster_ids, positions)
    probs = jnp.where(allowed, jnp.exp(scores - row_top[:, None]), 0.0) / row_total[:, None]
    probs_low = probs.astype(jnp.bfloat16)
    grad_probs = lax.dot_general(
        grads_in, values, contract_last, preferred_element_type=jnp.float32
    )
    delta_rows = jnp.sum(probs * grad_probs, axis=1)
    grad_low = (probs * (grad_probs - delta_rows[:, None]) * scale).astype(jnp.bfloat16)
    grad_query = jnp.dot(grad_low, keys_in, preferred_element_type=jnp.float32).astype(jnp.bfloat16)
    grad_key = lax.dot_general(
        grad_low, queries, contract_first, preferred_element_type=jnp.float32
    ).astype(jnp.bfloat16)
    grad_value = lax.dot_general(
        probs_low, grads_in, contract_first, preferred_element_type=jnp.float32
    ).astype(jnp.bfloat16)
    return (grad_query, grad_key, grad_value)


def by_owner(hidden, w_query, w_key, w_value, cluster_rank, assign, d_attended):
    tok_rows = hidden.shape[0]
    heads_here = assign.shape[0]
    head_dim = w_query.shape[1] // heads_here
    clusters = cluster_rank.shape[0]
    seq_count = lax.axis_size("seq")
    sub_count = lax.axis_size("sub")
    owners = seq_count * sub_count
    capacity = 2 * tok_rows // owners
    slot_count = owners * capacity
    per_owner = clusters // owners
    scale = head_dim ** (-0.5)
    pieces = (
        lax.all_gather(w_query, "sub", axis=0, tiled=True),
        lax.all_gather(w_key, "sub", axis=0, tiled=True),
        lax.all_gather(w_value, "sub", axis=0, tiled=True),
    )
    projected = tuple(
        (
            jnp.dot(hidden, weight_piece, preferred_element_type=jnp.float32)
            for weight_piece in pieces
        )
    )

    def split_heads(matrix):
        return (
            matrix.astype(jnp.bfloat16).reshape(tok_rows, heads_here, head_dim).transpose(1, 0, 2)
        )

    queries, keys_all, values = tuple((split_heads(matrix) for matrix in projected))
    cluster_range = jnp.arange(clusters, dtype=jnp.int32)
    rank_tok = jnp.sum(jnp.where(assign[:, :, None] == cluster_range, cluster_rank, 0), axis=2)
    owner_ids = rank_tok // per_owner
    owner_hot = (owner_ids[:, :, None] == jnp.arange(owners, dtype=jnp.int32)).astype(jnp.int32)
    within = jnp.sum(owner_hot * (jnp.cumsum(owner_hot, axis=1) - 1), axis=2)
    slot_tok = owner_ids * capacity + within
    token_ids = jnp.arange(tok_rows, dtype=jnp.int32)
    slot_range = jnp.arange(slot_count, dtype=jnp.int32)
    slot_match = slot_tok[:, None, :] == slot_range[None, :, None]
    slot_hot = slot_match.astype(jnp.bfloat16)

    def to_slots(rows_in):
        kept = jnp.einsum(
            "hst,htd->hsd", slot_hot, rows_in, preferred_element_type=jnp.float32
        ).astype(jnp.bfloat16)
        return kept.reshape(heads_here, owners, capacity, head_dim)

    def from_slots(slotted):
        flat_slots = slotted.reshape(heads_here, slot_count, head_dim)
        return jnp.einsum(
            "hst,hsd->htd", slot_hot, flat_slots, preferred_element_type=jnp.float32
        ).astype(jnp.bfloat16)

    def exchange_three(first, second, third):
        return (
            lax.all_to_all(first, ("seq", "sub"), split_axis=1, concat_axis=1, tiled=True),
            lax.all_to_all(second, ("seq", "sub"), split_axis=1, concat_axis=1, tiled=True),
            lax.all_to_all(third, ("seq", "sub"), split_axis=1, concat_axis=1, tiled=True),
        )

    sent = exchange_three(to_slots(queries), to_slots(keys_all), to_slots(values))
    tag_tok = assign * tok_rows + token_ids
    slot_tag = jnp.sum(jnp.where(slot_match, tag_tok[:, None, :] + 1, 0), axis=2) - 1
    tags = lax.all_to_all(
        slot_tag.reshape(heads_here, owners, capacity),
        ("seq", "sub"),
        split_axis=1,
        concat_axis=1,
        tiled=True,
    )
    tags = tags.reshape(heads_here, slot_count)
    owner_q, owner_k, owner_v = tuple(
        (member.reshape(heads_here, slot_count, head_dim) for member in sent)
    )
    filled = tags >= 0
    cluster_ids = jnp.where(filled, tags // tok_rows, -1)
    positions = slot_range // capacity * tok_rows + tags % tok_rows
    outputs, row_top, row_total = lax.map(
        partial(head_forward, scale=scale),
        (owner_q, owner_k, owner_v, filled, cluster_ids, positions),
    )
    returned = lax.all_to_all(
        outputs.reshape(heads_here, owners, capacity, head_dim),
        ("seq", "sub"),
        split_axis=1,
        concat_axis=1,
        tiled=True,
    )

    def merge_heads(slotted):
        return from_slots(slotted).transpose(1, 0, 2).reshape(tok_rows, heads_here * head_dim)

    attended = merge_heads(returned)
    grads_tok = d_attended.reshape(tok_rows, heads_here, head_dim).transpose(1, 0, 2)
    owner_g = lax.all_to_all(
        to_slots(grads_tok), ("seq", "sub"), split_axis=1, concat_axis=1, tiled=True
    ).reshape(heads_here, slot_count, head_dim)
    grad_q, grad_k, grad_v = lax.map(
        partial(head_backward, scale=scale),
        (owner_q, owner_k, owner_v, owner_g, filled, cluster_ids, positions, row_top, row_total),
    )
    shape_four = (heads_here, owners, capacity, head_dim)
    back = exchange_three(
        grad_q.reshape(shape_four), grad_k.reshape(shape_four), grad_v.reshape(shape_four)
    )
    token_grads = tuple((merge_heads(member) for member in back))
    pieces = lax.all_gather((w_query, w_key, w_value), "sub", axis=0, tiled=True)
    terms = [
        jnp.einsum("tc,rc->tr", grad_rows_in, weight_piece, preferred_element_type=jnp.float32)
        for grad_rows_in, weight_piece in zip(token_grads, pieces)
    ]
    partial_grad = terms[0] + terms[1] + terms[2]
    d_hidden = lax.psum_scatter(
        partial_grad.astype(jnp.bfloat16), "head", scatter_dimension=1, tiled=True
    )
    keys_float = keys_all.astype(jnp.float32)
    unit_keys = keys_float * lax.rsqrt(
        jnp.sum(keys_float * keys_float, axis=2, keepdims=True) + epsilon
    )
    member_hot = (rank_tok[:, :, None] == cluster_range).astype(jnp.float32)
    local_sums = jnp.einsum("htr,htd->hrd", member_hot, unit_keys, precision=lax.Precision.HIGHEST)
    centroid_sums = lax.psum_scatter(
        local_sums.astype(jnp.bfloat16), ("seq", "sub"), scatter_dimension=1, tiled=True
    ).astype(jnp.float32)
    return (attended, d_hidden, centroid_sums)


contract_last = (((1,), (1,)), ((), ()))
contract_first = (((0,), (0,)), ((), ()))
log2_e = 1.4426950408889634
mebi = 1024 * 1024


def id_lines(rows, head_dim):
    return -(-(rows // head_dim) // 16) * 16


def open_kernel(place_ref, grads_ref, assign_ref, *refs):
    weights, (held_ref, mine_ref, theirs_ref, ids_ref, sems, id_sem) = refs[:3], refs[3:]
    chips, padded, head_dim = mine_ref.shape
    rows = grads_ref.shape[0]
    spare = padded - rows - rows // head_dim
    ids_copy = pltpu.make_async_copy(assign_ref, ids_ref, id_sem.at[0])
    ids_copy.start()
    copies = []
    for turn, out_ref in enumerate((mine_ref, theirs_ref)):
        for chip in range(chips):
            head = (place_ref[1] ^ turn) * chips + chip
            at = pl.multiple_of(head * head_dim, head_dim)
            copies.append((grads_ref.at[:, pl.ds(at, head_dim)], out_ref.at[chip, pl.ds(0, rows)]))
    chunk = held_ref.shape[1] // 4
    for index, weight in enumerate(weights):
        for part in range(4):
            at = pl.ds(part * chunk, chunk)
            copies.append((weight.at[at], held_ref.at[index, at]))
    copies = [
        pltpu.make_async_copy(source, target, sems.at[index])
        for index, (source, target) in enumerate(copies)
    ]
    for copy in copies:
        copy.start()
    ids_copy.wait()
    for turn, out_ref in enumerate((mine_ref, theirs_ref)):
        for chip in range(chips):
            head = (place_ref[1] ^ turn) * chips + chip
            ids = ids_ref[pl.ds(head, 1), :].astype(jnp.float32)
            lines = [
                ids[:, start : start + head_dim] for start in range(0, rows, head_dim)
            ] + [jnp.zeros((spare, head_dim), jnp.float32)]
            out_ref[chip, rows:, :] = jnp.concatenate(lines, axis=0).astype(jnp.bfloat16)
    for copy in copies:
        copy.wait()


def merge_kernel(place_ref, mine_ref, theirs_ref, *out_refs):
    height = mine_ref.shape[1]
    for turn, held_ref in enumerate((mine_ref, theirs_ref)):
        at = pl.ds(pl.multiple_of((place_ref[1] ^ turn) * height, height), height)
        for offset, out_ref in enumerate(out_refs):
            out_ref[at, :] = held_ref[place_ref[0] ^ offset]


def project(indices, turn, place_ref, joined_ref, held_ref, finish):
    columns = held_ref.shape[2] // 2
    at = pl.ds(pl.multiple_of((place_ref[1] ^ turn) * columns, columns), columns)
    for slot, index in enumerate(indices):
        finish(
            slot,
            jnp.dot(joined_ref[...], held_ref[index, :, at], preferred_element_type=jnp.float32),
        )


def sibling_kernel(indices, place_ref, joined_ref, held_ref, out_ref):
    def finish(slot, total):
        out_ref[slot] = total.astype(jnp.bfloat16)

    project(indices, 1, place_ref, joined_ref, held_ref, finish)


def first_kernel(indices, place_ref, held_ref, mine_ref, theirs_ref, out_ref, joined_ref, sems):
    side = place_ref[1]
    tall, depth = joined_ref.shape
    rows = tall // 2
    near = pl.ds(pl.multiple_of(side * depth, depth), depth)
    copies = []
    for core, source in enumerate((mine_ref, theirs_ref)):
        at = pl.ds(pl.multiple_of((side ^ core) * rows, rows), rows)
        copies.append(
            pltpu.make_async_copy(source.at[:, near], joined_ref.at[at], sems.at[core])
        )
        copies[core].start()
    for copy in copies:
        copy.wait()
    sibling_kernel(indices, place_ref, joined_ref, held_ref, out_ref)


def own_kernel(indices, place_ref, joined_ref, held_ref, arrived_ref, *refs):
    out_refs, low_ref = refs[:-1], refs[-1]
    tall = joined_ref.shape[0]

    def finish(slot, total):
        low_ref[...] = (total + arrived_ref[slot].astype(jnp.float32)).astype(jnp.bfloat16)
        for offset, out_ref in enumerate(out_refs):
            head_dim = out_ref.shape[1]
            at = pl.multiple_of((place_ref[0] ^ offset) * head_dim, head_dim)
            out_ref[slot * tall : (slot + 1) * tall, :] = low_ref[:, pl.ds(at, head_dim)]

    project(indices, 0, place_ref, joined_ref, held_ref, finish)


def in_order(place, parts, start, ordered):
    for offset, part in enumerate(parts):
        tall = ordered.shape[0] // len(parts)
        at = pl.ds(pl.multiple_of((place ^ offset) * tall, tall), tall)
        ordered[at, :] = part[start : start + tall, :]


def order_grads(place, parts, rows, grad_rows, id_rows, id_cols):
    head_dim = grad_rows.shape[1]
    height = parts[0].shape[0] // 2
    for offset, part in enumerate(parts):
        for core in range(2):
            block = (place ^ offset) * 2 + core
            at = pl.ds(pl.multiple_of(block * rows, rows), rows)
            start = core * height
            grad_rows[at, :] = part[start : start + rows, :]
            lines = part[start + rows : start + rows + 16, :].astype(jnp.float32)
            ids = jnp.concatenate(
                [lines[line : line + 1, :] for line in range(rows // head_dim)], axis=1
            )
            id_rows[block] = jnp.broadcast_to(ids, id_rows.shape[1:])
            id_cols[at, :] = jnp.broadcast_to(ids, (head_dim, rows)).T


def block_scores(factor, block, rows, queries, keys_in, id_rows, id_cols):
    head_dim = queries.shape[1]
    seen = (block + 1) * rows
    scores = lax.dot_general(
        keys_in[:seen, :],
        queries[block * rows : seen, :],
        contract_last,
        preferred_element_type=jnp.float32,
    )
    ids = id_cols[:seen, :]
    mine = id_rows[block][:1, :]
    same = jnp.concatenate(
        [ids == mine[:, start : start + head_dim] for start in range(0, rows, head_dim)], axis=1
    )
    key_at = lax.broadcasted_iota(jnp.int32, (rows, rows), 0)
    query_at = lax.broadcasted_iota(jnp.int32, (rows, rows), 1)
    last = same[seen - rows :] & (key_at <= query_at)
    allowed = last if block == 0 else jnp.concatenate([same[: seen - rows], last], axis=0)
    return jnp.where(allowed, scores * factor, -jnp.inf)


def value_grad_kernel(factor, chips, rows, place_ref, *refs):
    packed, grads = refs[:chips], refs[chips : 2 * chips]
    out_refs, lse_ref = refs[2 * chips : 3 * chips], refs[3 * chips]
    queries, keys_in, grad_rows, id_rows, id_cols, total_ref = refs[3 * chips + 1 :]
    tall = 2 * rows
    place = place_ref[0]
    in_order(place, packed, 0, queries)
    in_order(place, packed, tall, keys_in)
    order_grads(place, grads, rows, grad_rows, id_rows, id_cols)
    total_ref[...] = jnp.zeros_like(total_ref)
    for block in range(2 * chips):
        seen = (block + 1) * rows
        scores = block_scores(factor, block, rows, queries, keys_in, id_rows, id_cols)
        top = jnp.max(scores, axis=0, keepdims=True)
        expd = jnp.exp2(scores - top)
        total = jnp.sum(expd, axis=0, keepdims=True)
        lse_ref[block : block + 1, :] = top + jnp.log2(total)
        total_ref[:seen, :] += jnp.dot(
            (expd * (1.0 / total)).astype(jnp.bfloat16),
            grad_rows[block * rows : seen, :],
            preferred_element_type=jnp.float32,
        )
    for offset, out_ref in enumerate(out_refs):
        at = pl.multiple_of((place ^ offset) * tall, tall)
        out_ref[...] = total_ref[pl.ds(at, tall), :].astype(jnp.bfloat16)


def query_grad_kernel(factor, scale, chips, rows, place_ref, *refs):
    packed, valued, grads = refs[:chips], refs[chips : 2 * chips], refs[2 * chips : 3 * chips]
    lse_ref, rank_ref = refs[3 * chips : 3 * chips + 2]
    refs = refs[3 * chips + 2 :]
    grad_refs, out_refs, refs = refs[:chips], refs[chips : chips + 2], refs[chips + 2 :]
    queries, keys_in, values, grad_rows, id_rows, id_cols, total_ref, dq_ref, attended_ref = refs
    head_dim = queries.shape[1]
    clusters = rank_ref.shape[1]
    tall = 2 * rows
    place = place_ref[0]
    in_order(place, packed, 0, queries)
    in_order(place, packed, tall, keys_in)
    in_order(place, valued, 0, values)
    order_grads(place, grads, rows, grad_rows, id_rows, id_cols)
    total_ref[...] = jnp.zeros_like(total_ref)
    for block in range(2 * chips):
        seen = (block + 1) * rows
        mine = slice(block * rows, seen)
        scores = block_scores(factor, block, rows, queries, keys_in, id_rows, id_cols)
        probs = jnp.exp2(scores - lse_ref[block : block + 1, :])
        seen_values = values[:seen, :]
        grad_probs = lax.dot_general(
            seen_values, grad_rows[mine, :], contract_last, preferred_element_type=jnp.float32
        )
        flipped = lax.dot_general(
            seen_values,
            probs.astype(jnp.bfloat16),
            contract_first,
            preferred_element_type=jnp.float32,
        )
        attended_ref[mine, :] = flipped.T.astype(jnp.bfloat16)
        weighted = probs * grad_probs
        delta = jnp.sum(weighted, axis=0, keepdims=True)
        grad_low = (weighted - probs * delta).astype(jnp.bfloat16)
        total_ref[:seen, :] += jnp.dot(
            grad_low, queries[mine, :], preferred_element_type=jnp.float32
        )
        flipped = lax.dot_general(
            keys_in[:seen, :], grad_low, contract_first, preferred_element_type=jnp.float32
        )
        dq_ref[mine, :] = (flipped.T * scale).astype(jnp.bfloat16)
    sums = jnp.zeros((clusters, head_dim), jnp.float32)
    cluster_at = lax.broadcasted_iota(jnp.int32, (clusters, rows), 0).astype(jnp.float32)
    for block in range(2 * chips):
        keys_float = keys_in[block * rows : (block + 1) * rows, :].astype(jnp.float32)
        unit = keys_float * lax.rsqrt(
            jnp.sum(keys_float * keys_float, axis=1, keepdims=True) + epsilon
        )
        unit_high = unit.astype(jnp.bfloat16)
        unit_low = (unit - unit_high.astype(jnp.float32)).astype(jnp.bfloat16)
        member = jnp.where(cluster_at == id_rows[block][:1, :], 1.0, 0.0).astype(jnp.bfloat16)
        sums += jnp.dot(member, unit_high, preferred_element_type=jnp.float32)
        sums += jnp.dot(member, unit_low, preferred_element_type=jnp.float32)
    rank_at = lax.broadcasted_iota(jnp.int32, (clusters, clusters), 0)
    ordered = jnp.where(rank_at == rank_ref[...], 1.0, 0.0).astype(jnp.bfloat16)
    ranked = jnp.dot(ordered, sums.astype(jnp.bfloat16), preferred_element_type=jnp.float32)
    attended_ref[2 * chips * rows :, :] = ranked.astype(jnp.bfloat16)
    owned = clusters // (2 * chips)
    for offset in range(chips):
        at = pl.ds(pl.multiple_of((place ^ offset) * tall, tall), tall)
        grad_refs[offset][:tall, :] = dq_ref[at, :]
        grad_refs[offset][tall:, :] = (total_ref[at, :] * scale).astype(jnp.bfloat16)
    for turn, out_ref in enumerate(out_refs):
        for chip in range(chips):
            shard = chip * 2 + (place_ref[1] ^ turn)
            at = pl.ds(pl.multiple_of(shard * rows, rows), rows)
            out_ref[chip, :rows, :] = attended_ref[at, :]
            at = pl.ds(pl.multiple_of(2 * chips * rows + shard * owned, owned), owned)
            out_ref[chip, rows:, :] = attended_ref[at, :]


def input_kernel(chips, which, place_ref, *refs):
    held_ref, out_ref, gathered_ref = refs[4 * chips :]
    rows, width = out_ref.shape[0], held_ref.shape[2]
    head_dim = width // (2 * chips)
    for turn in range(2):
        parts = refs[turn * chips : (turn + 1) * chips]
        valued = refs[(2 + turn) * chips : (3 + turn) * chips]
        for offset in range(chips):
            head = (place_ref[1] ^ turn) * chips + (place_ref[0] ^ offset)
            for index in range(3):
                source = parts[offset] if index < 2 else valued[offset]
                at = pl.multiple_of((2 * (index % 2) + place_ref[which]) * rows, rows)
                start = pl.multiple_of(index * width + head * head_dim, head_dim)
                gathered_ref[:, pl.ds(start, head_dim)] = source[pl.ds(at, rows), :]
    flipped = None
    for index in range(3):
        term = lax.dot_general(
            held_ref[index],
            gathered_ref[:, index * width : (index + 1) * width],
            contract_last,
            preferred_element_type=jnp.float32,
        )
        flipped = term if flipped is None else flipped + term
    out_ref[...] = flipped.T.astype(out_ref.dtype)


def attended_kernel(chips, place_ref, *refs):
    parts, (attended_ref, sums_ref) = refs[:chips], refs[chips:]
    rows = attended_ref.shape[0]
    head_dim = sums_ref.shape[2]
    height = parts[0].shape[0] // 2
    for core in range(2):
        start = core * height
        for offset, part in enumerate(parts):
            head = core * chips + (place_ref[0] ^ offset)
            at = pl.multiple_of(head * head_dim, head_dim)
            attended_ref[:, pl.ds(at, head_dim)] = part[start : start + rows, :]
            sums_ref[head] = part[start + rows : start + height, :].astype(jnp.float32)


def sum_kernel(place_ref, first_ref, second_ref, kept_ref, hidden_ref):
    keeps = place_ref[2] == place_ref[1]
    second = jnp.where(keeps, kept_ref[...], second_ref[...]).astype(jnp.float32)
    hidden_ref[...] = (first_ref[...].astype(jnp.float32) + second).astype(jnp.bfloat16)


def by_head(hidden, w_query, w_key, w_value, cluster_rank, assign, d_attended):
    rows = hidden.shape[0]
    count = assign.shape[0]
    chips = count // 2
    half, width = w_query.shape
    head_dim = width // count
    tokens = count * rows
    clusters = cluster_rank.shape[0]
    owned = clusters // count
    scale = head_dim ** (-0.5)
    factor = scale * log2_e
    smem = pl.BlockSpec(memory_space=pltpu.SMEM)
    vmem = pl.BlockSpec(memory_space=pltpu.VMEM)
    anywhere = pl.BlockSpec(memory_space=pl.ANY)
    params = pltpu.CompilerParams(vmem_limit_bytes=32 * mebi)
    swap = [(0, 1), (1, 0)]
    chip, side, column = (lax.axis_index(name) for name in ("seq", "sub", "head"))
    place = jnp.stack([chip, side, column, 1 - column])

    def call(kernel, outs, *operands, scratch=(), hbm=0, limits=params, takes=1):
        return pl.pallas_call(
            kernel,
            out_shape=outs,
            in_specs=[smem] + [vmem] * (len(operands) - 1 - hbm) + [anywhere] * hbm,
            out_specs=jax.tree.map(lambda _: vmem, outs),
            scratch_shapes=list(scratch),
            compiler_params=limits,
            cost_estimate=pl.CostEstimate(
                flops=int(takes * 1.15e9), bytes_accessed=mebi, transcendentals=0
            ),
        )(*operands)

    def low(*shape):
        return jax.ShapeDtypeStruct(shape, jnp.bfloat16)

    def buffers(height):
        return (low(height, head_dim),) * chips

    def exchange(parts):
        moved = {
            offset: lax.ppermute(parts[offset], "seq", [(at, at ^ offset) for at in range(chips)])
            for offset in (2, 3, 1)
        }
        return (parts[0], moved[1], moved[2], moved[3])

    def to_sibling(piece):
        return lax.ppermute(piece, "sub", swap)

    def stay(array):
        return pltpu.with_memory_space_constraint(array, pltpu.HBM)

    hidden_other = to_sibling(hidden)
    block = low(chips, rows + id_lines(rows, head_dim), head_dim)
    weights, grads_mine, grads_theirs = call(
        open_kernel,
        (pltpu.VMEM((3, half, width), jnp.bfloat16), block, block),
        place,
        stay(d_attended),
        stay(assign),
        *(stay(weight) for weight in (w_query, w_key, w_value)),
        scratch=[
            pltpu.VMEM(assign.shape, jnp.int32),
            pltpu.SemaphoreType.DMA((count + 12,)),
            pltpu.SemaphoreType.DMA((1,)),
        ],
        hbm=5,
    )
    grads_other = to_sibling(grads_theirs)
    merged = call(merge_kernel, buffers(2 * block.shape[1]), place, grads_mine, grads_other)
    grads = exchange(merged)
    early_part, joined = call(
        partial(first_kernel, (0, 1)),
        (low(2, 2 * rows, width // 2), low(2 * rows, half)),
        place,
        weights,
        stay(hidden),
        hidden_other,
        scratch=[pltpu.SemaphoreType.DMA((2,))],
        hbm=2,
        takes=0.1,
    )
    late_part = call(
        partial(sibling_kernel, (2,)), low(1, 2 * rows, width // 2), place, joined, weights, takes=0.1
    )
    early_arrived, late_arrived = to_sibling(early_part), to_sibling(late_part)

    def own_heads(indices, arrived, takes):
        return call(
            partial(own_kernel, indices),
            buffers(2 * len(indices) * rows),
            place,
            joined,
            weights,
            arrived,
            scratch=[pltpu.VMEM((2 * rows, width // 2), jnp.bfloat16)],
            takes=takes,
        )

    early_arrived, _ = lax.optimization_barrier((early_arrived, merged[0]))
    early_projected = own_heads((0, 1), early_arrived, 8)
    packed = exchange(early_projected)
    late_arrived, *_ = lax.optimization_barrier(
        (late_arrived, early_projected[0], grads[2], grads[3])
    )
    late_projected = own_heads((2,), late_arrived, 0.1)
    valued = exchange(late_projected)
    packed = lax.optimization_barrier((*packed, late_projected[0]))[:chips]

    def held(kind):
        return pltpu.VMEM((tokens, head_dim), kind)

    id_scratch = [pltpu.VMEM((count, 8, rows), jnp.float32), held(jnp.float32)]
    *value_grads, lse = call(
        partial(value_grad_kernel, factor, chips, rows),
        (*buffers(2 * rows), jax.ShapeDtypeStruct((count, rows), jnp.float32)),
        place,
        *packed,
        *grads,
        scratch=[held(jnp.bfloat16)] * 3 + id_scratch + [held(jnp.float32)],
        takes=7,
    )
    value_back = exchange(value_grads)
    results = call(
        partial(query_grad_kernel, factor, scale, chips, rows),
        (*buffers(4 * rows), *(low(chips, rows + owned, head_dim),) * 2),
        place,
        *packed,
        *valued,
        *grads,
        lse,
        cluster_rank.reshape(1, clusters),
        scratch=[held(jnp.bfloat16)] * 4
        + id_scratch
        + [
            held(jnp.float32),
            held(jnp.bfloat16),
            pltpu.VMEM((tokens + clusters, head_dim), jnp.bfloat16),
        ],
        takes=10,
    )
    *ready, _, _ = lax.optimization_barrier((*results[:chips], value_back[2], value_back[3]))
    back = exchange(ready)

    attended_mine, attended_theirs = results[chips:]
    outputs = call(
        merge_kernel, buffers(2 * (rows + owned)), place, attended_mine, to_sibling(attended_theirs)
    )
    back_other = tuple(to_sibling(part) for part in back)
    value_other = tuple(to_sibling(part) for part in value_back)

    def input_part(which, place):
        return call(
            partial(input_kernel, chips, which),
            low(rows, half),
            place,
            *back,
            *back_other,
            *value_back,
            *value_other,
            weights,
            scratch=[pltpu.VMEM((rows, 3 * width), jnp.bfloat16)],
        )

    *outputs, _, _ = lax.optimization_barrier((*outputs, back[2], back[3]))
    returned = exchange(outputs)
    square = ("head", "sub")
    crossing = input_part(3, place)
    first = lax.ppermute(crossing, square, [(0, 1), (1, 3), (3, 2), (2, 0)])
    kept = input_part(2, lax.optimization_barrier((place, crossing))[0])
    second = lax.ppermute(kept, square, [(1, 2), (2, 1)])
    attended, centroid_sums = call(
        partial(attended_kernel, chips),
        (low(rows, width), jax.ShapeDtypeStruct((count, owned, head_dim), jnp.float32)),
        place,
        *returned,
        takes=8,
    )
    first, second, _ = lax.optimization_barrier((first, second, attended))
    d_hidden = call(sum_kernel, low(rows, half), place, first, second, kept)
    return (attended, d_hidden, centroid_sums)


def per_device(hidden, w_query, w_key, w_value, cluster_rank, assign, d_attended):
    chips = lax.axis_size("seq")
    fits = chips == 4 and lax.axis_size("sub") == 2 and lax.axis_size("head") == 2
    plan = by_head if fits and assign.shape[0] == 2 * chips else by_owner
    return plan(hidden, w_query, w_key, w_value, cluster_rank, assign, d_attended)


def solution(mesh):
    placed = (
        P(("groups", "seq", "sub"), None),
        P("sub", "head"),
        P("sub", "head"),
        P("sub", "head"),
        P("groups"),
        P("head", ("groups", "seq", "sub")),
        P(("groups", "seq", "sub"), "head"),
    )
    return jax.shard_map(
        per_device,
        mesh=mesh,
        in_specs=placed,
        out_specs=(
            P(("groups", "seq", "sub"), "head"),
            P(("groups", "seq", "sub"), "head"),
            P("head", ("groups", "seq", "sub"), None),
        ),
        check_vma=False,
    )
```

```python
from functools import partial

import jax
import jax.numpy as jnp
from jax import lax
from jax.experimental import pallas as pl
from jax.experimental.pallas import tpu as pltpu
from jax.sharding import PartitionSpec as P

epsilon = 1e-06


def keep_mask(filled, cluster_ids, positions):
    count = filled.shape[0]
    same = filled[:, None] & filled[None, :] & (cluster_ids[:, None] == cluster_ids[None, :])
    causal = positions[None, :] <= positions[:, None]
    diagonal = jnp.arange(count)[:, None] == jnp.arange(count)[None, :]
    return same & causal | diagonal


def head_forward(packed, scale):
    queries, keys_in, values, filled, cluster_ids, positions = packed
    scores = (
        lax.dot_general(
            queries, keys_in, (((1,), (1,)), ((), ())), preferred_element_type=jnp.float32
        )
        * scale
    )
    allowed = keep_mask(filled, cluster_ids, positions)
    row_top = jnp.max(jnp.where(allowed, scores, -jnp.inf), axis=1)
    expd = jnp.where(allowed, jnp.exp(scores - row_top[:, None]), 0.0)
    row_total = jnp.sum(expd, axis=1)
    probs_low = (expd / row_total[:, None]).astype(jnp.bfloat16)
    outputs = jnp.dot(probs_low, values, preferred_element_type=jnp.float32).astype(jnp.bfloat16)
    return (outputs, row_top, row_total)


def head_backward(packed, scale):
    queries, keys_in, values, grads_in, filled, cluster_ids, positions, row_top, row_total = packed
    contract_last = (((1,), (1,)), ((), ()))
    contract_first = (((0,), (0,)), ((), ()))
    scores = (
        lax.dot_general(queries, keys_in, contract_last, preferred_element_type=jnp.float32) * scale
    )
    allowed = keep_mask(filled, cluster_ids, positions)
    probs = jnp.where(allowed, jnp.exp(scores - row_top[:, None]), 0.0) / row_total[:, None]
    probs_low = probs.astype(jnp.bfloat16)
    grad_probs = lax.dot_general(
        grads_in, values, contract_last, preferred_element_type=jnp.float32
    )
    delta_rows = jnp.sum(probs * grad_probs, axis=1)
    grad_low = (probs * (grad_probs - delta_rows[:, None]) * scale).astype(jnp.bfloat16)
    grad_query = jnp.dot(grad_low, keys_in, preferred_element_type=jnp.float32).astype(jnp.bfloat16)
    grad_key = lax.dot_general(
        grad_low, queries, contract_first, preferred_element_type=jnp.float32
    ).astype(jnp.bfloat16)
    grad_value = lax.dot_general(
        probs_low, grads_in, contract_first, preferred_element_type=jnp.float32
    ).astype(jnp.bfloat16)
    return (grad_query, grad_key, grad_value)


def by_owner(hidden, w_query, w_key, w_value, cluster_rank, assign, d_attended):
    tok_rows = hidden.shape[0]
    heads_here = assign.shape[0]
    head_dim = w_query.shape[1] // heads_here
    clusters = cluster_rank.shape[0]
    seq_count = lax.axis_size("seq")
    sub_count = lax.axis_size("sub")
    owners = seq_count * sub_count
    capacity = 2 * tok_rows // owners
    slot_count = owners * capacity
    per_owner = clusters // owners
    scale = head_dim ** (-0.5)
    pieces = (
        lax.all_gather(w_query, "sub", axis=0, tiled=True),
        lax.all_gather(w_key, "sub", axis=0, tiled=True),
        lax.all_gather(w_value, "sub", axis=0, tiled=True),
    )
    projected = tuple(
        (
            jnp.dot(hidden, weight_piece, preferred_element_type=jnp.float32)
            for weight_piece in pieces
        )
    )

    def split_heads(matrix):
        return (
            matrix.astype(jnp.bfloat16).reshape(tok_rows, heads_here, head_dim).transpose(1, 0, 2)
        )

    queries, keys_all, values = tuple((split_heads(matrix) for matrix in projected))
    cluster_range = jnp.arange(clusters, dtype=jnp.int32)
    rank_tok = jnp.sum(jnp.where(assign[:, :, None] == cluster_range, cluster_rank, 0), axis=2)
    owner_ids = rank_tok // per_owner
    owner_hot = (owner_ids[:, :, None] == jnp.arange(owners, dtype=jnp.int32)).astype(jnp.int32)
    within = jnp.sum(owner_hot * (jnp.cumsum(owner_hot, axis=1) - 1), axis=2)
    slot_tok = owner_ids * capacity + within
    token_ids = jnp.arange(tok_rows, dtype=jnp.int32)
    slot_range = jnp.arange(slot_count, dtype=jnp.int32)
    slot_match = slot_tok[:, None, :] == slot_range[None, :, None]
    slot_hot = slot_match.astype(jnp.bfloat16)

    def to_slots(rows_in):
        kept = jnp.einsum(
            "hst,htd->hsd", slot_hot, rows_in, preferred_element_type=jnp.float32
        ).astype(jnp.bfloat16)
        return kept.reshape(heads_here, owners, capacity, head_dim)

    def from_slots(slotted):
        flat_slots = slotted.reshape(heads_here, slot_count, head_dim)
        return jnp.einsum(
            "hst,hsd->htd", slot_hot, flat_slots, preferred_element_type=jnp.float32
        ).astype(jnp.bfloat16)

    def exchange_three(first, second, third):
        return (
            lax.all_to_all(first, ("seq", "sub"), split_axis=1, concat_axis=1, tiled=True),
            lax.all_to_all(second, ("seq", "sub"), split_axis=1, concat_axis=1, tiled=True),
            lax.all_to_all(third, ("seq", "sub"), split_axis=1, concat_axis=1, tiled=True),
        )

    sent = exchange_three(to_slots(queries), to_slots(keys_all), to_slots(values))
    tag_tok = assign * tok_rows + token_ids
    slot_tag = jnp.sum(jnp.where(slot_match, tag_tok[:, None, :] + 1, 0), axis=2) - 1
    tags = lax.all_to_all(
        slot_tag.reshape(heads_here, owners, capacity),
        ("seq", "sub"),
        split_axis=1,
        concat_axis=1,
        tiled=True,
    )
    tags = tags.reshape(heads_here, slot_count)
    owner_q, owner_k, owner_v = tuple(
        (member.reshape(heads_here, slot_count, head_dim) for member in sent)
    )
    filled = tags >= 0
    cluster_ids = jnp.where(filled, tags // tok_rows, -1)
    positions = slot_range // capacity * tok_rows + tags % tok_rows
    outputs, row_top, row_total = lax.map(
        partial(head_forward, scale=scale),
        (owner_q, owner_k, owner_v, filled, cluster_ids, positions),
    )
    returned = lax.all_to_all(
        outputs.reshape(heads_here, owners, capacity, head_dim),
        ("seq", "sub"),
        split_axis=1,
        concat_axis=1,
        tiled=True,
    )

    def merge_heads(slotted):
        return from_slots(slotted).transpose(1, 0, 2).reshape(tok_rows, heads_here * head_dim)

    attended = merge_heads(returned)
    grads_tok = d_attended.reshape(tok_rows, heads_here, head_dim).transpose(1, 0, 2)
    owner_g = lax.all_to_all(
        to_slots(grads_tok), ("seq", "sub"), split_axis=1, concat_axis=1, tiled=True
    ).reshape(heads_here, slot_count, head_dim)
    grad_q, grad_k, grad_v = lax.map(
        partial(head_backward, scale=scale),
        (owner_q, owner_k, owner_v, owner_g, filled, cluster_ids, positions, row_top, row_total),
    )
    shape_four = (heads_here, owners, capacity, head_dim)
    back = exchange_three(
        grad_q.reshape(shape_four), grad_k.reshape(shape_four), grad_v.reshape(shape_four)
    )
    token_grads = tuple((merge_heads(member) for member in back))
    pieces = lax.all_gather((w_query, w_key, w_value), "sub", axis=0, tiled=True)
    terms = [
        jnp.einsum("tc,rc->tr", grad_rows_in, weight_piece, preferred_element_type=jnp.float32)
        for grad_rows_in, weight_piece in zip(token_grads, pieces)
    ]
    partial_grad = terms[0] + terms[1] + terms[2]
    d_hidden = lax.psum_scatter(
        partial_grad.astype(jnp.bfloat16), "head", scatter_dimension=1, tiled=True
    )
    keys_float = keys_all.astype(jnp.float32)
    unit_keys = keys_float * lax.rsqrt(
        jnp.sum(keys_float * keys_float, axis=2, keepdims=True) + epsilon
    )
    member_hot = (rank_tok[:, :, None] == cluster_range).astype(jnp.float32)
    local_sums = jnp.einsum("htr,htd->hrd", member_hot, unit_keys, precision=lax.Precision.HIGHEST)
    centroid_sums = lax.psum_scatter(
        local_sums.astype(jnp.bfloat16), ("seq", "sub"), scatter_dimension=1, tiled=True
    ).astype(jnp.float32)
    return (attended, d_hidden, centroid_sums)


contract_last = (((1,), (1,)), ((), ()))
contract_first = (((0,), (0,)), ((), ()))
log2_e = 1.4426950408889634
mebi = 1024 * 1024


def id_lines(rows, head_dim):
    return -(-(rows // head_dim) // 16) * 16


def pack_kernel(place_ref, grads_ref, assign_ref, mine_ref, theirs_ref, ids_ref, sems):
    chips, padded, head_dim = mine_ref.shape
    rows = grads_ref.shape[0]
    spare = padded - rows - rows // head_dim
    copies = [pltpu.make_async_copy(assign_ref, ids_ref, sems.at[2 * chips])]
    for turn, out_ref in enumerate((mine_ref, theirs_ref)):
        for chip in range(chips):
            head = (place_ref[1] ^ turn) * chips + chip
            at = pl.multiple_of(head * head_dim, head_dim)
            copies.append(
                pltpu.make_async_copy(
                    grads_ref.at[:, pl.ds(at, head_dim)],
                    out_ref.at[chip, pl.ds(0, rows)],
                    sems.at[turn * chips + chip],
                )
            )
    for copy in copies:
        copy.start()
    copies[0].wait()
    for turn, out_ref in enumerate((mine_ref, theirs_ref)):
        for chip in range(chips):
            head = (place_ref[1] ^ turn) * chips + chip
            ids = ids_ref[pl.ds(head, 1), :].astype(jnp.float32)
            lines = [
                ids[:, start : start + head_dim] for start in range(0, rows, head_dim)
            ] + [jnp.zeros((spare, head_dim), jnp.float32)]
            out_ref[chip, rows:, :] = jnp.concatenate(lines, axis=0).astype(jnp.bfloat16)
    for copy in copies[1:]:
        copy.wait()


def merge_kernel(place_ref, mine_ref, theirs_ref, *out_refs):
    height = mine_ref.shape[1]
    for turn, held_ref in enumerate((mine_ref, theirs_ref)):
        at = pl.ds(pl.multiple_of((place_ref[1] ^ turn) * height, height), height)
        for offset, out_ref in enumerate(out_refs):
            out_ref[at, :] = held_ref[place_ref[0] ^ offset]


def fetch_columns(half, weights, held_ref, sems):
    chunks = sems.shape[1]
    columns = held_ref.shape[2]
    rows = held_ref.shape[1] // chunks
    at = pl.ds(pl.multiple_of(half * columns, columns), columns)
    copies = []
    for index, weight in enumerate(weights):
        for chunk in range(chunks):
            lines = pl.ds(chunk * rows, rows)
            copy = pltpu.make_async_copy(
                weight.at[lines, at], held_ref.at[index, lines], sems.at[index, chunk]
            )
            copy.start()
            copies.append(copy)
    return copies


def project_kernel(count, turn, place_ref, *refs):
    if turn == 0:
        arrived_ref, refs = refs[0], refs[1:]
    tokens, weights, refs = refs[:2], refs[2 : 2 + count], refs[2 + count :]
    out_refs, (joined_ref, held_ref, low_ref, sems, token_sems) = refs[:-5], refs[-5:]
    side = place_ref[1]
    tall, depth = joined_ref.shape
    rows = tall // 2
    near = pl.ds(pl.multiple_of(side * depth, depth), depth)
    joins = []
    for core, source in enumerate(tokens):
        at = pl.ds(pl.multiple_of((side ^ core) * rows, rows), rows)
        joins.append(
            pltpu.make_async_copy(source.at[:, near], joined_ref.at[at], token_sems.at[core])
        )
        joins[core].start()
    copies = fetch_columns(side ^ turn, weights, held_ref, sems)
    for copy in joins:
        copy.wait()
    chunks = sems.shape[1]
    for index in range(count):
        for chunk in range(chunks):
            copies[index * chunks + chunk].wait()
        total = jnp.dot(joined_ref[...], held_ref[index], preferred_element_type=jnp.float32)
        if turn == 1:
            out_refs[0][index] = total.astype(jnp.bfloat16)
            continue
        low_ref[...] = (total + arrived_ref[index].astype(jnp.float32)).astype(jnp.bfloat16)
        for offset, out_ref in enumerate(out_refs):
            head_dim = out_ref.shape[1]
            at = pl.multiple_of((place_ref[0] ^ offset) * head_dim, head_dim)
            out_ref[index * tall : (index + 1) * tall, :] = low_ref[:, pl.ds(at, head_dim)]


def in_order(place, parts, start, ordered):
    for offset, part in enumerate(parts):
        tall = ordered.shape[0] // len(parts)
        at = pl.ds(pl.multiple_of((place ^ offset) * tall, tall), tall)
        ordered[at, :] = part[start : start + tall, :]


def order_grads(place, parts, rows, grad_rows, id_rows, id_cols):
    head_dim = grad_rows.shape[1]
    height = parts[0].shape[0] // 2
    for offset, part in enumerate(parts):
        for core in range(2):
            block = (place ^ offset) * 2 + core
            at = pl.ds(pl.multiple_of(block * rows, rows), rows)
            start = core * height
            grad_rows[at, :] = part[start : start + rows, :]
            lines = part[start + rows : start + rows + 16, :].astype(jnp.float32)
            ids = jnp.concatenate(
                [lines[line : line + 1, :] for line in range(rows // head_dim)], axis=1
            )
            id_rows[block] = jnp.broadcast_to(ids, id_rows.shape[1:])
            id_cols[at, :] = jnp.broadcast_to(ids, (head_dim, rows)).T


def block_scores(factor, block, rows, queries, keys_in, id_rows, id_cols):
    head_dim = queries.shape[1]
    seen = (block + 1) * rows
    scores = lax.dot_general(
        keys_in[:seen, :],
        queries[block * rows : seen, :],
        contract_last,
        preferred_element_type=jnp.float32,
    )
    ids = id_cols[:seen, :]
    mine = id_rows[block][:1, :]
    same = jnp.concatenate(
        [ids == mine[:, start : start + head_dim] for start in range(0, rows, head_dim)], axis=1
    )
    key_at = lax.broadcasted_iota(jnp.int32, (rows, rows), 0)
    query_at = lax.broadcasted_iota(jnp.int32, (rows, rows), 1)
    last = same[seen - rows :] & (key_at <= query_at)
    allowed = last if block == 0 else jnp.concatenate([same[: seen - rows], last], axis=0)
    return jnp.where(allowed, scores * factor, -jnp.inf)


def value_grad_kernel(factor, chips, rows, place_ref, *refs):
    packed, grads = refs[:chips], refs[chips : 2 * chips]
    out_refs, lse_ref = refs[2 * chips : 3 * chips], refs[3 * chips]
    queries, keys_in, grad_rows, id_rows, id_cols, total_ref = refs[3 * chips + 1 :]
    tall = 2 * rows
    place = place_ref[0]
    in_order(place, packed, 0, queries)
    in_order(place, packed, tall, keys_in)
    order_grads(place, grads, rows, grad_rows, id_rows, id_cols)
    total_ref[...] = jnp.zeros_like(total_ref)
    for block in range(2 * chips):
        seen = (block + 1) * rows
        scores = block_scores(factor, block, rows, queries, keys_in, id_rows, id_cols)
        top = jnp.max(scores, axis=0, keepdims=True)
        expd = jnp.exp2(scores - top)
        total = jnp.sum(expd, axis=0, keepdims=True)
        lse_ref[block : block + 1, :] = top + jnp.log2(total)
        total_ref[:seen, :] += jnp.dot(
            (expd * (1.0 / total)).astype(jnp.bfloat16),
            grad_rows[block * rows : seen, :],
            preferred_element_type=jnp.float32,
        )
    for offset, out_ref in enumerate(out_refs):
        at = pl.multiple_of((place ^ offset) * tall, tall)
        out_ref[...] = total_ref[pl.ds(at, tall), :].astype(jnp.bfloat16)


def query_grad_kernel(factor, scale, chips, rows, place_ref, *refs):
    packed, valued, grads = refs[:chips], refs[chips : 2 * chips], refs[2 * chips : 3 * chips]
    lse_ref, rank_ref = refs[3 * chips : 3 * chips + 2]
    refs = refs[3 * chips + 2 :]
    grad_refs, out_refs, refs = refs[:chips], refs[chips : chips + 2], refs[chips + 2 :]
    queries, keys_in, values, grad_rows, id_rows, id_cols, total_ref, dq_ref, attended_ref = refs
    head_dim = queries.shape[1]
    clusters = rank_ref.shape[1]
    tall = 2 * rows
    place = place_ref[0]
    in_order(place, packed, 0, queries)
    in_order(place, packed, tall, keys_in)
    in_order(place, valued, 0, values)
    order_grads(place, grads, rows, grad_rows, id_rows, id_cols)
    total_ref[...] = jnp.zeros_like(total_ref)
    for block in range(2 * chips):
        seen = (block + 1) * rows
        mine = slice(block * rows, seen)
        scores = block_scores(factor, block, rows, queries, keys_in, id_rows, id_cols)
        probs = jnp.exp2(scores - lse_ref[block : block + 1, :])
        seen_values = values[:seen, :]
        grad_probs = lax.dot_general(
            seen_values, grad_rows[mine, :], contract_last, preferred_element_type=jnp.float32
        )
        flipped = lax.dot_general(
            seen_values,
            probs.astype(jnp.bfloat16),
            contract_first,
            preferred_element_type=jnp.float32,
        )
        attended_ref[mine, :] = flipped.T.astype(jnp.bfloat16)
        weighted = probs * grad_probs
        delta = jnp.sum(weighted, axis=0, keepdims=True)
        grad_low = (weighted - probs * delta).astype(jnp.bfloat16)
        total_ref[:seen, :] += jnp.dot(
            grad_low, queries[mine, :], preferred_element_type=jnp.float32
        )
        flipped = lax.dot_general(
            keys_in[:seen, :], grad_low, contract_first, preferred_element_type=jnp.float32
        )
        dq_ref[mine, :] = (flipped.T * scale).astype(jnp.bfloat16)
    sums = jnp.zeros((clusters, head_dim), jnp.float32)
    cluster_at = lax.broadcasted_iota(jnp.int32, (clusters, rows), 0).astype(jnp.float32)
    for block in range(2 * chips):
        keys_float = keys_in[block * rows : (block + 1) * rows, :].astype(jnp.float32)
        unit = keys_float * lax.rsqrt(
            jnp.sum(keys_float * keys_float, axis=1, keepdims=True) + epsilon
        )
        unit_high = unit.astype(jnp.bfloat16)
        unit_low = (unit - unit_high.astype(jnp.float32)).astype(jnp.bfloat16)
        member = jnp.where(cluster_at == id_rows[block][:1, :], 1.0, 0.0).astype(jnp.bfloat16)
        sums += jnp.dot(member, unit_high, preferred_element_type=jnp.float32)
        sums += jnp.dot(member, unit_low, preferred_element_type=jnp.float32)
    rank_at = lax.broadcasted_iota(jnp.int32, (clusters, clusters), 0)
    ordered = jnp.where(rank_at == rank_ref[...], 1.0, 0.0).astype(jnp.bfloat16)
    ranked = jnp.dot(ordered, sums.astype(jnp.bfloat16), preferred_element_type=jnp.float32)
    attended_ref[2 * chips * rows :, :] = ranked.astype(jnp.bfloat16)
    owned = clusters // (2 * chips)
    for offset in range(chips):
        at = pl.ds(pl.multiple_of((place ^ offset) * tall, tall), tall)
        grad_refs[offset][:tall, :] = dq_ref[at, :]
        grad_refs[offset][tall:, :] = (total_ref[at, :] * scale).astype(jnp.bfloat16)
    for turn, out_ref in enumerate(out_refs):
        for chip in range(chips):
            shard = chip * 2 + (place_ref[1] ^ turn)
            at = pl.ds(pl.multiple_of(shard * rows, rows), rows)
            out_ref[chip, :rows, :] = attended_ref[at, :]
            at = pl.ds(pl.multiple_of(2 * chips * rows + shard * owned, owned), owned)
            out_ref[chip, rows:, :] = attended_ref[at, :]


def input_kernel(chips, which, place_ref, *refs):
    weights, (out_ref, gathered_ref) = refs[4 * chips : -2], refs[-2:]
    rows, width = out_ref.shape[0], weights[0].shape[1]
    head_dim = width // (2 * chips)
    for turn in range(2):
        parts = refs[turn * chips : (turn + 1) * chips]
        valued = refs[(2 + turn) * chips : (3 + turn) * chips]
        for offset in range(chips):
            head = (place_ref[1] ^ turn) * chips + (place_ref[0] ^ offset)
            for index in range(3):
                source = parts[offset] if index < 2 else valued[offset]
                at = pl.multiple_of((2 * (index % 2) + place_ref[which]) * rows, rows)
                start = pl.multiple_of(index * width + head * head_dim, head_dim)
                gathered_ref[:, pl.ds(start, head_dim)] = source[pl.ds(at, rows), :]
    flipped = None
    for index in range(3):
        term = lax.dot_general(
            weights[index][...],
            gathered_ref[:, index * width : (index + 1) * width],
            contract_last,
            preferred_element_type=jnp.float32,
        )
        flipped = term if flipped is None else flipped + term
    out_ref[...] = flipped.T.astype(out_ref.dtype)


def attended_kernel(chips, place_ref, *refs):
    parts, (attended_ref, sums_ref) = refs[:chips], refs[chips:]
    rows = attended_ref.shape[0]
    head_dim = sums_ref.shape[2]
    height = parts[0].shape[0] // 2
    for core in range(2):
        start = core * height
        for offset, part in enumerate(parts):
            head = core * chips + (place_ref[0] ^ offset)
            at = pl.multiple_of(head * head_dim, head_dim)
            attended_ref[:, pl.ds(at, head_dim)] = part[start : start + rows, :]
            sums_ref[head] = part[start + rows : start + height, :].astype(jnp.float32)


def sum_kernel(place_ref, first_ref, second_ref, kept_ref, hidden_ref):
    keeps = place_ref[2] == place_ref[1]
    second = jnp.where(keeps, kept_ref[...], second_ref[...]).astype(jnp.float32)
    hidden_ref[...] = (first_ref[...].astype(jnp.float32) + second).astype(jnp.bfloat16)


def by_head(hidden, w_query, w_key, w_value, cluster_rank, assign, d_attended):
    rows = hidden.shape[0]
    count = assign.shape[0]
    chips = count // 2
    half, width = w_query.shape
    head_dim = width // count
    tokens = count * rows
    clusters = cluster_rank.shape[0]
    owned = clusters // count
    scale = head_dim ** (-0.5)
    factor = scale * log2_e
    smem = pl.BlockSpec(memory_space=pltpu.SMEM)
    vmem = pl.BlockSpec(memory_space=pltpu.VMEM)
    anywhere = pl.BlockSpec(memory_space=pl.ANY)
    params = pltpu.CompilerParams(vmem_limit_bytes=32 * mebi)
    project_params = pltpu.CompilerParams(vmem_limit_bytes=32 * mebi)
    swap = [(0, 1), (1, 0)]
    chip, side, column = (lax.axis_index(name) for name in ("seq", "sub", "head"))
    place = jnp.stack([chip, side, column, 1 - column])

    def call(kernel, outs, *operands, scratch=(), hbm=0, limits=params, takes=1):
        return pl.pallas_call(
            kernel,
            out_shape=outs,
            in_specs=[smem] + [vmem] * (len(operands) - 1 - hbm) + [anywhere] * hbm,
            out_specs=jax.tree.map(lambda _: vmem, outs),
            scratch_shapes=list(scratch),
            compiler_params=limits,
            cost_estimate=pl.CostEstimate(
                flops=int(takes * 1.15e9), bytes_accessed=mebi, transcendentals=0
            ),
        )(*operands)

    def low(*shape):
        return jax.ShapeDtypeStruct(shape, jnp.bfloat16)

    def buffers(height):
        return (low(height, head_dim),) * chips

    def exchange(parts):
        moved = {
            offset: lax.ppermute(parts[offset], "seq", [(at, at ^ offset) for at in range(chips)])
            for offset in (2, 3, 1)
        }
        return (parts[0], moved[1], moved[2], moved[3])

    def to_sibling(piece):
        return lax.ppermute(piece, "sub", swap)

    def stay(array):
        return pltpu.with_memory_space_constraint(array, pltpu.HBM)

    hidden_other = to_sibling(hidden)
    block = low(chips, rows + id_lines(rows, head_dim), head_dim)
    grads_mine, grads_theirs = call(
        pack_kernel,
        (block, block),
        place,
        stay(d_attended),
        stay(assign),
        scratch=[pltpu.VMEM(assign.shape, jnp.int32), pltpu.SemaphoreType.DMA((count + 1,))],
        hbm=2,
    )
    grads_other = to_sibling(grads_theirs)

    def project(turn, weights, *arrived):
        number = len(weights)
        outs = buffers(2 * number * rows) if turn == 0 else low(number, 2 * rows, width // 2)

        return call(
            partial(project_kernel, number, turn),
            outs,
            place,
            *arrived,
            stay(hidden),
            hidden_other,
            *(stay(weight) for weight in weights),
            scratch=[
                pltpu.VMEM((2 * rows, half), jnp.bfloat16),
                pltpu.VMEM((number, half, width // 2), jnp.bfloat16),
                pltpu.VMEM((2 * rows, width // 2), jnp.bfloat16),
                pltpu.SemaphoreType.DMA((number, 4)),
                pltpu.SemaphoreType.DMA((2,)),
            ],
            hbm=2 + number,
            limits=project_params,
            takes=(8 if number == 2 else 0.1) if turn == 0 else 0.1,
        )

    merged = call(merge_kernel, buffers(2 * block.shape[1]), place, grads_mine, grads_other)
    grads = exchange(merged)
    hidden_other, _ = lax.optimization_barrier((hidden_other, merged[0]))
    early, late = (w_query, w_key), (w_value,)
    early_arrived = to_sibling(project(1, early))
    late_arrived = to_sibling(project(1, late))
    grads = exchange(call(merge_kernel, buffers(2 * block.shape[1]), place, grads_mine, grads_other))
    early_arrived, _ = lax.optimization_barrier((early_arrived, grads[0]))
    early_projected = project(0, early, early_arrived)
    packed = exchange(early_projected)
    late_arrived, _, _ = lax.optimization_barrier((late_arrived, early_projected[0], (grads[2], grads[3])))
    late_projected = project(0, late, late_arrived)
    valued = exchange(late_projected)
    packed = lax.optimization_barrier((*packed, late_projected[0]))[:chips]

    def held(kind):
        return pltpu.VMEM((tokens, head_dim), kind)

    id_scratch = [pltpu.VMEM((count, 8, rows), jnp.float32), held(jnp.float32)]
    *value_grads, lse = call(
        partial(value_grad_kernel, factor, chips, rows),
        (*buffers(2 * rows), jax.ShapeDtypeStruct((count, rows), jnp.float32)),
        place,
        *packed,
        *grads,
        scratch=[held(jnp.bfloat16)] * 3 + id_scratch + [held(jnp.float32)],
        takes=7,
    )
    value_back = exchange(value_grads)
    results = call(
        partial(query_grad_kernel, factor, scale, chips, rows),
        (*buffers(4 * rows), *(low(chips, rows + owned, head_dim),) * 2),
        place,
        *packed,
        *valued,
        *grads,
        lse,
        cluster_rank.reshape(1, clusters),
        scratch=[held(jnp.bfloat16)] * 4
        + id_scratch
        + [
            held(jnp.float32),
            held(jnp.bfloat16),
            pltpu.VMEM((tokens + clusters, head_dim), jnp.bfloat16),
        ],
        takes=10,
    )
    *ready, _, _ = lax.optimization_barrier((*results[:chips], value_back[2], value_back[3]))
    back = exchange(ready)

    attended_mine, attended_theirs = results[chips:]
    outputs = call(
        merge_kernel, buffers(2 * (rows + owned)), place, attended_mine, to_sibling(attended_theirs)
    )
    back_other = tuple(to_sibling(part) for part in back)
    value_other = tuple(to_sibling(part) for part in value_back)

    def input_part(which, place):
        return call(
            partial(input_kernel, chips, which),
            low(rows, half),
            place,
            *back,
            *back_other,
            *value_back,
            *value_other,
            w_query,
            w_key,
            w_value,
            scratch=[pltpu.VMEM((rows, 3 * width), jnp.bfloat16)],
        )

    *outputs, _, _ = lax.optimization_barrier((*outputs, back[2], back[3]))
    returned = exchange(outputs)
    square = ("head", "sub")
    crossing = input_part(3, place)
    first = lax.ppermute(crossing, square, [(0, 1), (1, 3), (3, 2), (2, 0)])
    kept = input_part(2, lax.optimization_barrier((place, crossing))[0])
    second = lax.ppermute(kept, square, [(1, 2), (2, 1)])
    attended, centroid_sums = call(
        partial(attended_kernel, chips),
        (low(rows, width), jax.ShapeDtypeStruct((count, owned, head_dim), jnp.float32)),
        place,
        *returned,
        takes=8,
    )
    first, second, _ = lax.optimization_barrier((first, second, attended))
    d_hidden = call(sum_kernel, low(rows, half), place, first, second, kept)
    return (attended, d_hidden, centroid_sums)


def per_device(hidden, w_query, w_key, w_value, cluster_rank, assign, d_attended):
    chips = lax.axis_size("seq")
    fits = chips == 4 and lax.axis_size("sub") == 2 and lax.axis_size("head") == 2
    plan = by_head if fits and assign.shape[0] == 2 * chips else by_owner
    return plan(hidden, w_query, w_key, w_value, cluster_rank, assign, d_attended)


def solution(mesh):
    placed = (
        P(("groups", "seq", "sub"), None),
        P("sub", "head"),
        P("sub", "head"),
        P("sub", "head"),
        P("groups"),
        P("head", ("groups", "seq", "sub")),
        P(("groups", "seq", "sub"), "head"),
    )
    return jax.shard_map(
        per_device,
        mesh=mesh,
        in_specs=placed,
        out_specs=(
            P(("groups", "seq", "sub"), "head"),
            P(("groups", "seq", "sub"), "head"),
            P("head", ("groups", "seq", "sub"), None),
        ),
        check_vma=False,
    )
```

```python
from functools import partial

import jax
import jax.numpy as jnp
from jax import lax
from jax.experimental import pallas as pl
from jax.experimental.pallas import tpu as pltpu
from jax.sharding import PartitionSpec as P

epsilon = 1e-06


def keep_mask(filled, cluster_ids, positions):
    count = filled.shape[0]
    same = filled[:, None] & filled[None, :] & (cluster_ids[:, None] == cluster_ids[None, :])
    causal = positions[None, :] <= positions[:, None]
    diagonal = jnp.arange(count)[:, None] == jnp.arange(count)[None, :]
    return same & causal | diagonal


def head_forward(packed, scale):
    queries, keys_in, values, filled, cluster_ids, positions = packed
    scores = (
        lax.dot_general(
            queries, keys_in, (((1,), (1,)), ((), ())), preferred_element_type=jnp.float32
        )
        * scale
    )
    allowed = keep_mask(filled, cluster_ids, positions)
    row_top = jnp.max(jnp.where(allowed, scores, -jnp.inf), axis=1)
    expd = jnp.where(allowed, jnp.exp(scores - row_top[:, None]), 0.0)
    row_total = jnp.sum(expd, axis=1)
    probs_low = (expd / row_total[:, None]).astype(jnp.bfloat16)
    outputs = jnp.dot(probs_low, values, preferred_element_type=jnp.float32).astype(jnp.bfloat16)
    return (outputs, row_top, row_total)


def head_backward(packed, scale):
    queries, keys_in, values, grads_in, filled, cluster_ids, positions, row_top, row_total = packed
    contract_last = (((1,), (1,)), ((), ()))
    contract_first = (((0,), (0,)), ((), ()))
    scores = (
        lax.dot_general(queries, keys_in, contract_last, preferred_element_type=jnp.float32) * scale
    )
    allowed = keep_mask(filled, cluster_ids, positions)
    probs = jnp.where(allowed, jnp.exp(scores - row_top[:, None]), 0.0) / row_total[:, None]
    probs_low = probs.astype(jnp.bfloat16)
    grad_probs = lax.dot_general(
        grads_in, values, contract_last, preferred_element_type=jnp.float32
    )
    delta_rows = jnp.sum(probs * grad_probs, axis=1)
    grad_low = (probs * (grad_probs - delta_rows[:, None]) * scale).astype(jnp.bfloat16)
    grad_query = jnp.dot(grad_low, keys_in, preferred_element_type=jnp.float32).astype(jnp.bfloat16)
    grad_key = lax.dot_general(
        grad_low, queries, contract_first, preferred_element_type=jnp.float32
    ).astype(jnp.bfloat16)
    grad_value = lax.dot_general(
        probs_low, grads_in, contract_first, preferred_element_type=jnp.float32
    ).astype(jnp.bfloat16)
    return (grad_query, grad_key, grad_value)


def by_owner(hidden, w_query, w_key, w_value, cluster_rank, assign, d_attended):
    tok_rows = hidden.shape[0]
    heads_here = assign.shape[0]
    head_dim = w_query.shape[1] // heads_here
    clusters = cluster_rank.shape[0]
    seq_count = lax.axis_size("seq")
    sub_count = lax.axis_size("sub")
    owners = seq_count * sub_count
    capacity = 2 * tok_rows // owners
    slot_count = owners * capacity
    per_owner = clusters // owners
    scale = head_dim ** (-0.5)
    pieces = (
        lax.all_gather(w_query, "sub", axis=0, tiled=True),
        lax.all_gather(w_key, "sub", axis=0, tiled=True),
        lax.all_gather(w_value, "sub", axis=0, tiled=True),
    )
    projected = tuple(
        (
            jnp.dot(hidden, weight_piece, preferred_element_type=jnp.float32)
            for weight_piece in pieces
        )
    )

    def split_heads(matrix):
        return (
            matrix.astype(jnp.bfloat16).reshape(tok_rows, heads_here, head_dim).transpose(1, 0, 2)
        )

    queries, keys_all, values = tuple((split_heads(matrix) for matrix in projected))
    cluster_range = jnp.arange(clusters, dtype=jnp.int32)
    rank_tok = jnp.sum(jnp.where(assign[:, :, None] == cluster_range, cluster_rank, 0), axis=2)
    owner_ids = rank_tok // per_owner
    owner_hot = (owner_ids[:, :, None] == jnp.arange(owners, dtype=jnp.int32)).astype(jnp.int32)
    within = jnp.sum(owner_hot * (jnp.cumsum(owner_hot, axis=1) - 1), axis=2)
    slot_tok = owner_ids * capacity + within
    token_ids = jnp.arange(tok_rows, dtype=jnp.int32)
    slot_range = jnp.arange(slot_count, dtype=jnp.int32)
    slot_match = slot_tok[:, None, :] == slot_range[None, :, None]
    slot_hot = slot_match.astype(jnp.bfloat16)

    def to_slots(rows_in):
        kept = jnp.einsum(
            "hst,htd->hsd", slot_hot, rows_in, preferred_element_type=jnp.float32
        ).astype(jnp.bfloat16)
        return kept.reshape(heads_here, owners, capacity, head_dim)

    def from_slots(slotted):
        flat_slots = slotted.reshape(heads_here, slot_count, head_dim)
        return jnp.einsum(
            "hst,hsd->htd", slot_hot, flat_slots, preferred_element_type=jnp.float32
        ).astype(jnp.bfloat16)

    def exchange_three(first, second, third):
        return (
            lax.all_to_all(first, ("seq", "sub"), split_axis=1, concat_axis=1, tiled=True),
            lax.all_to_all(second, ("seq", "sub"), split_axis=1, concat_axis=1, tiled=True),
            lax.all_to_all(third, ("seq", "sub"), split_axis=1, concat_axis=1, tiled=True),
        )

    sent = exchange_three(to_slots(queries), to_slots(keys_all), to_slots(values))
    tag_tok = assign * tok_rows + token_ids
    slot_tag = jnp.sum(jnp.where(slot_match, tag_tok[:, None, :] + 1, 0), axis=2) - 1
    tags = lax.all_to_all(
        slot_tag.reshape(heads_here, owners, capacity),
        ("seq", "sub"),
        split_axis=1,
        concat_axis=1,
        tiled=True,
    )
    tags = tags.reshape(heads_here, slot_count)
    owner_q, owner_k, owner_v = tuple(
        (member.reshape(heads_here, slot_count, head_dim) for member in sent)
    )
    filled = tags >= 0
    cluster_ids = jnp.where(filled, tags // tok_rows, -1)
    positions = slot_range // capacity * tok_rows + tags % tok_rows
    outputs, row_top, row_total = lax.map(
        partial(head_forward, scale=scale),
        (owner_q, owner_k, owner_v, filled, cluster_ids, positions),
    )
    returned = lax.all_to_all(
        outputs.reshape(heads_here, owners, capacity, head_dim),
        ("seq", "sub"),
        split_axis=1,
        concat_axis=1,
        tiled=True,
    )

    def merge_heads(slotted):
        return from_slots(slotted).transpose(1, 0, 2).reshape(tok_rows, heads_here * head_dim)

    attended = merge_heads(returned)
    grads_tok = d_attended.reshape(tok_rows, heads_here, head_dim).transpose(1, 0, 2)
    owner_g = lax.all_to_all(
        to_slots(grads_tok), ("seq", "sub"), split_axis=1, concat_axis=1, tiled=True
    ).reshape(heads_here, slot_count, head_dim)
    grad_q, grad_k, grad_v = lax.map(
        partial(head_backward, scale=scale),
        (owner_q, owner_k, owner_v, owner_g, filled, cluster_ids, positions, row_top, row_total),
    )
    shape_four = (heads_here, owners, capacity, head_dim)
    back = exchange_three(
        grad_q.reshape(shape_four), grad_k.reshape(shape_four), grad_v.reshape(shape_four)
    )
    token_grads = tuple((merge_heads(member) for member in back))
    pieces = lax.all_gather((w_query, w_key, w_value), "sub", axis=0, tiled=True)
    terms = [
        jnp.einsum("tc,rc->tr", grad_rows_in, weight_piece, preferred_element_type=jnp.float32)
        for grad_rows_in, weight_piece in zip(token_grads, pieces)
    ]
    partial_grad = terms[0] + terms[1] + terms[2]
    d_hidden = lax.psum_scatter(
        partial_grad.astype(jnp.bfloat16), "head", scatter_dimension=1, tiled=True
    )
    keys_float = keys_all.astype(jnp.float32)
    unit_keys = keys_float * lax.rsqrt(
        jnp.sum(keys_float * keys_float, axis=2, keepdims=True) + epsilon
    )
    member_hot = (rank_tok[:, :, None] == cluster_range).astype(jnp.float32)
    local_sums = jnp.einsum("htr,htd->hrd", member_hot, unit_keys, precision=lax.Precision.HIGHEST)
    centroid_sums = lax.psum_scatter(
        local_sums.astype(jnp.bfloat16), ("seq", "sub"), scatter_dimension=1, tiled=True
    ).astype(jnp.float32)
    return (attended, d_hidden, centroid_sums)


contract_last = (((1,), (1,)), ((), ()))
contract_first = (((0,), (0,)), ((), ()))
log2_e = 1.4426950408889634
mebi = 1024 * 1024


def id_lines(rows, head_dim):
    return -(-(rows // head_dim) // 16) * 16


def pack_kernel(place_ref, grads_ref, assign_ref, mine_ref, theirs_ref, ids_ref, sems):
    chips, padded, head_dim = mine_ref.shape
    rows = grads_ref.shape[0]
    spare = padded - rows - rows // head_dim
    copies = [pltpu.make_async_copy(assign_ref, ids_ref, sems.at[2 * chips])]
    for turn, out_ref in enumerate((mine_ref, theirs_ref)):
        for chip in range(chips):
            head = (place_ref[1] ^ turn) * chips + chip
            at = pl.multiple_of(head * head_dim, head_dim)
            copies.append(
                pltpu.make_async_copy(
                    grads_ref.at[:, pl.ds(at, head_dim)],
                    out_ref.at[chip, pl.ds(0, rows)],
                    sems.at[turn * chips + chip],
                )
            )
    for copy in copies:
        copy.start()
    copies[0].wait()
    for turn, out_ref in enumerate((mine_ref, theirs_ref)):
        for chip in range(chips):
            head = (place_ref[1] ^ turn) * chips + chip
            ids = ids_ref[pl.ds(head, 1), :].astype(jnp.float32)
            lines = [
                ids[:, start : start + head_dim] for start in range(0, rows, head_dim)
            ] + [jnp.zeros((spare, head_dim), jnp.float32)]
            out_ref[chip, rows:, :] = jnp.concatenate(lines, axis=0).astype(jnp.bfloat16)
    for copy in copies[1:]:
        copy.wait()


def merge_kernel(place_ref, mine_ref, theirs_ref, *out_refs):
    height = mine_ref.shape[1]
    for turn, held_ref in enumerate((mine_ref, theirs_ref)):
        at = pl.ds(pl.multiple_of((place_ref[1] ^ turn) * height, height), height)
        for offset, out_ref in enumerate(out_refs):
            out_ref[at, :] = held_ref[place_ref[0] ^ offset]


def fetch_columns(half, weights, held_ref, sems):
    chunks = sems.shape[1]
    columns = held_ref.shape[2]
    rows = held_ref.shape[1] // chunks
    at = pl.ds(pl.multiple_of(half * columns, columns), columns)
    copies = []
    for index, weight in enumerate(weights):
        for chunk in range(chunks):
            lines = pl.ds(chunk * rows, rows)
            copy = pltpu.make_async_copy(
                weight.at[lines, at], held_ref.at[index, lines], sems.at[index, chunk]
            )
            copy.start()
            copies.append(copy)
    return copies


def project_kernel(count, turn, place_ref, *refs):
    if turn == 0:
        arrived_ref, refs = refs[0], refs[1:]
    tokens, weights, refs = refs[:2], refs[2 : 2 + count], refs[2 + count :]
    out_refs, (joined_ref, held_ref, low_ref, sems, token_sems) = refs[:-5], refs[-5:]
    side = place_ref[1]
    tall, depth = joined_ref.shape
    rows = tall // 2
    near = pl.ds(pl.multiple_of(side * depth, depth), depth)
    joins = []
    for core, source in enumerate(tokens):
        at = pl.ds(pl.multiple_of((side ^ core) * rows, rows), rows)
        joins.append(
            pltpu.make_async_copy(source.at[:, near], joined_ref.at[at], token_sems.at[core])
        )
        joins[core].start()
    copies = fetch_columns(side ^ turn, weights, held_ref, sems)
    for copy in joins:
        copy.wait()
    chunks = sems.shape[1]
    for index in range(count):
        for chunk in range(chunks):
            copies[index * chunks + chunk].wait()
        total = jnp.dot(joined_ref[...], held_ref[index], preferred_element_type=jnp.float32)
        if turn == 1:
            out_refs[0][index] = total.astype(jnp.bfloat16)
            continue
        low_ref[...] = (total + arrived_ref[index].astype(jnp.float32)).astype(jnp.bfloat16)
        for offset, out_ref in enumerate(out_refs):
            head_dim = out_ref.shape[1]
            at = pl.multiple_of((place_ref[0] ^ offset) * head_dim, head_dim)
            out_ref[index * tall : (index + 1) * tall, :] = low_ref[:, pl.ds(at, head_dim)]


def in_order(place, parts, start, ordered):
    for offset, part in enumerate(parts):
        tall = ordered.shape[0] // len(parts)
        at = pl.ds(pl.multiple_of((place ^ offset) * tall, tall), tall)
        ordered[at, :] = part[start : start + tall, :]


def order_grads(place, parts, rows, grad_rows, id_rows, id_cols):
    head_dim = grad_rows.shape[1]
    height = parts[0].shape[0] // 2
    for offset, part in enumerate(parts):
        for core in range(2):
            block = (place ^ offset) * 2 + core
            at = pl.ds(pl.multiple_of(block * rows, rows), rows)
            start = core * height
            grad_rows[at, :] = part[start : start + rows, :]
            lines = part[start + rows : start + rows + 16, :].astype(jnp.float32)
            ids = jnp.concatenate(
                [lines[line : line + 1, :] for line in range(rows // head_dim)], axis=1
            )
            id_rows[block] = jnp.broadcast_to(ids, id_rows.shape[1:])
            id_cols[at, :] = jnp.broadcast_to(ids, (head_dim, rows)).T


def order_rows(place, parts, rows, ordered):
    height = parts[0].shape[0] // 2
    for offset, part in enumerate(parts):
        for core in range(2):
            at = pl.ds(pl.multiple_of(((place ^ offset) * 2 + core) * rows, rows), rows)
            ordered[at, :] = part[core * height : core * height + rows, :]


def block_scores(factor, block, rows, queries, keys_in, id_rows, id_cols):
    head_dim = queries.shape[1]
    seen = (block + 1) * rows
    scores = lax.dot_general(
        keys_in[:seen, :],
        queries[block * rows : seen, :],
        contract_last,
        preferred_element_type=jnp.float32,
    )
    ids = id_cols[:seen, :]
    mine = id_rows[block][:1, :]
    same = jnp.concatenate(
        [ids == mine[:, start : start + head_dim] for start in range(0, rows, head_dim)], axis=1
    )
    key_at = lax.broadcasted_iota(jnp.int32, (rows, rows), 0)
    query_at = lax.broadcasted_iota(jnp.int32, (rows, rows), 1)
    last = same[seen - rows :] & (key_at <= query_at)
    allowed = last if block == 0 else jnp.concatenate([same[: seen - rows], last], axis=0)
    return jnp.where(allowed, scores * factor, -jnp.inf)


def value_grad_kernel(factor, chips, rows, place_ref, *refs):
    packed, grads, rank_ref = refs[:chips], refs[chips : 2 * chips], refs[2 * chips]
    refs = refs[2 * chips + 1 :]
    out_refs, probs_ref, sums_ref = refs[:chips], refs[chips], refs[chips + 1]
    queries, keys_in, grad_rows, id_rows, id_cols, total_ref = refs[chips + 2 :]
    head_dim = queries.shape[1]
    clusters = rank_ref.shape[1]
    tall = 2 * rows
    place = place_ref[0]
    in_order(place, packed, 0, queries)
    in_order(place, packed, tall, keys_in)
    order_grads(place, grads, rows, grad_rows, id_rows, id_cols)
    total_ref[...] = jnp.zeros_like(total_ref)
    stored = 0
    for block in range(2 * chips):
        seen = (block + 1) * rows
        scores = block_scores(factor, block, rows, queries, keys_in, id_rows, id_cols)
        top = jnp.max(scores, axis=0, keepdims=True)
        expd = jnp.exp2(scores - top)
        total = jnp.sum(expd, axis=0, keepdims=True)
        probs_low = (expd * (1.0 / total)).astype(jnp.bfloat16)
        probs_ref[stored : stored + seen, :] = probs_low
        stored += seen
        total_ref[:seen, :] += jnp.dot(
            probs_low, grad_rows[block * rows : seen, :], preferred_element_type=jnp.float32
        )
    for offset, out_ref in enumerate(out_refs):
        at = pl.multiple_of((place ^ offset) * tall, tall)
        out_ref[...] = total_ref[pl.ds(at, tall), :].astype(jnp.bfloat16)
    sums = jnp.zeros((clusters, head_dim), jnp.float32)
    cluster_at = lax.broadcasted_iota(jnp.int32, (clusters, rows), 0).astype(jnp.float32)
    for block in range(2 * chips):
        keys_float = keys_in[block * rows : (block + 1) * rows, :].astype(jnp.float32)
        unit = keys_float * lax.rsqrt(
            jnp.sum(keys_float * keys_float, axis=1, keepdims=True) + epsilon
        )
        unit_high = unit.astype(jnp.bfloat16)
        unit_low = (unit - unit_high.astype(jnp.float32)).astype(jnp.bfloat16)
        member = jnp.where(cluster_at == id_rows[block][:1, :], 1.0, 0.0).astype(jnp.bfloat16)
        sums += jnp.dot(member, unit_high, preferred_element_type=jnp.float32)
        sums += jnp.dot(member, unit_low, preferred_element_type=jnp.float32)
    rank_at = lax.broadcasted_iota(jnp.int32, (clusters, clusters), 0)
    ordered = jnp.where(rank_at == rank_ref[...], 1.0, 0.0).astype(jnp.bfloat16)
    ranked = jnp.dot(ordered, sums.astype(jnp.bfloat16), preferred_element_type=jnp.float32)
    sums_ref[...] = ranked.astype(jnp.bfloat16)


def query_grad_kernel(scale, chips, rows, place_ref, *refs):
    packed, valued, grads = refs[:chips], refs[chips : 2 * chips], refs[2 * chips : 3 * chips]
    probs_ref, sums_ref = refs[3 * chips : 3 * chips + 2]
    refs = refs[3 * chips + 2 :]
    grad_refs, out_refs, refs = refs[:chips], refs[chips : chips + 2], refs[chips + 2 :]
    queries, keys_in, values, grad_rows, total_ref, dq_ref, attended_ref = refs
    tall = 2 * rows
    place = place_ref[0]
    in_order(place, packed, 0, queries)
    in_order(place, packed, tall, keys_in)
    in_order(place, valued, 0, values)
    order_rows(place, grads, rows, grad_rows)
    total_ref[...] = jnp.zeros_like(total_ref)
    stored = 0
    for block in range(2 * chips):
        seen = (block + 1) * rows
        mine = slice(block * rows, seen)
        probs_low = probs_ref[stored : stored + seen, :]
        stored += seen
        seen_values = values[:seen, :]
        grad_probs = lax.dot_general(
            seen_values, grad_rows[mine, :], contract_last, preferred_element_type=jnp.float32
        )
        flipped = lax.dot_general(
            seen_values, probs_low, contract_first, preferred_element_type=jnp.float32
        )
        attended_ref[mine, :] = flipped.T.astype(jnp.bfloat16)
        probs = probs_low.astype(jnp.float32)
        weighted = probs * grad_probs
        delta = jnp.sum(weighted, axis=0, keepdims=True)
        grad_low = (weighted - probs * delta).astype(jnp.bfloat16)
        total_ref[:seen, :] += jnp.dot(
            grad_low, queries[mine, :], preferred_element_type=jnp.float32
        )
        flipped = lax.dot_general(
            keys_in[:seen, :], grad_low, contract_first, preferred_element_type=jnp.float32
        )
        dq_ref[mine, :] = (flipped.T * scale).astype(jnp.bfloat16)
    for offset in range(chips):
        at = pl.ds(pl.multiple_of((place ^ offset) * tall, tall), tall)
        grad_refs[offset][:tall, :] = dq_ref[at, :]
        grad_refs[offset][tall:, :] = (total_ref[at, :] * scale).astype(jnp.bfloat16)
    owned = sums_ref.shape[0] // (2 * chips)
    for turn, out_ref in enumerate(out_refs):
        for chip in range(chips):
            shard = chip * 2 + (place_ref[1] ^ turn)
            at = pl.ds(pl.multiple_of(shard * rows, rows), rows)
            out_ref[chip, :rows, :] = attended_ref[at, :]
            at = pl.ds(pl.multiple_of(shard * owned, owned), owned)
            out_ref[chip, rows:, :] = sums_ref[at, :]


def join_kernel(*refs):
    parts, out_ref = refs[1:-1], refs[-1]
    for offset, part in enumerate(parts):
        out_ref[offset] = part[...]


def input_kernel(chips, which, place_ref, *refs):
    valued_other_ref, refs = refs[3 * chips], refs[: 3 * chips] + refs[3 * chips + 1 :]
    weights, (out_ref, gathered_ref) = refs[3 * chips : -2], refs[-2:]
    rows, width = out_ref.shape[0], weights[0].shape[1]
    head_dim = width // (2 * chips)
    for turn in range(2):
        parts = refs[turn * chips : (turn + 1) * chips]
        valued = refs[2 * chips : 3 * chips]
        for offset in range(chips):
            head = (place_ref[1] ^ turn) * chips + (place_ref[0] ^ offset)
            for index in range(3):
                source = parts[offset] if index < 2 else valued[offset]
                if index == 2 and turn == 1:
                    source = valued_other_ref.at[offset]
                at = pl.multiple_of((2 * (index % 2) + place_ref[which]) * rows, rows)
                start = pl.multiple_of(index * width + head * head_dim, head_dim)
                gathered_ref[:, pl.ds(start, head_dim)] = source[pl.ds(at, rows), :]
    flipped = None
    for index in range(3):
        term = lax.dot_general(
            weights[index][...],
            gathered_ref[:, index * width : (index + 1) * width],
            contract_last,
            preferred_element_type=jnp.float32,
        )
        flipped = term if flipped is None else flipped + term
    out_ref[...] = flipped.T.astype(out_ref.dtype)


def attended_kernel(chips, place_ref, *refs):
    parts, (attended_ref, sums_ref) = refs[:chips], refs[chips:]
    rows = attended_ref.shape[0]
    head_dim = sums_ref.shape[2]
    height = parts[0].shape[0] // 2
    for core in range(2):
        start = core * height
        for offset, part in enumerate(parts):
            head = core * chips + (place_ref[0] ^ offset)
            at = pl.multiple_of(head * head_dim, head_dim)
            attended_ref[:, pl.ds(at, head_dim)] = part[start : start + rows, :]
            sums_ref[head] = part[start + rows : start + height, :].astype(jnp.float32)


def sum_kernel(place_ref, first_ref, second_ref, kept_ref, hidden_ref):
    keeps = place_ref[2] == place_ref[1]
    second = jnp.where(keeps, kept_ref[...], second_ref[...]).astype(jnp.float32)
    hidden_ref[...] = (first_ref[...].astype(jnp.float32) + second).astype(jnp.bfloat16)


def by_head(hidden, w_query, w_key, w_value, cluster_rank, assign, d_attended):
    rows = hidden.shape[0]
    count = assign.shape[0]
    chips = count // 2
    half, width = w_query.shape
    head_dim = width // count
    tokens = count * rows
    clusters = cluster_rank.shape[0]
    owned = clusters // count
    scale = head_dim ** (-0.5)
    factor = scale * log2_e
    smem = pl.BlockSpec(memory_space=pltpu.SMEM)
    vmem = pl.BlockSpec(memory_space=pltpu.VMEM)
    anywhere = pl.BlockSpec(memory_space=pl.ANY)
    params = pltpu.CompilerParams(vmem_limit_bytes=32 * mebi)
    project_params = pltpu.CompilerParams(vmem_limit_bytes=32 * mebi)
    swap = [(0, 1), (1, 0)]
    chip, side, column = (lax.axis_index(name) for name in ("seq", "sub", "head"))
    place = jnp.stack([chip, side, column, 1 - column])

    def call(kernel, outs, *operands, scratch=(), hbm=0, limits=params, takes=1):
        return pl.pallas_call(
            kernel,
            out_shape=outs,
            in_specs=[smem] + [vmem] * (len(operands) - 1 - hbm) + [anywhere] * hbm,
            out_specs=jax.tree.map(lambda _: vmem, outs),
            scratch_shapes=list(scratch),
            compiler_params=limits,
            cost_estimate=pl.CostEstimate(
                flops=int(takes * 1.15e9), bytes_accessed=mebi, transcendentals=0
            ),
        )(*operands)

    def low(*shape):
        return jax.ShapeDtypeStruct(shape, jnp.bfloat16)

    def buffers(height):
        return (low(height, head_dim),) * chips

    def exchange(parts):
        moved = {
            offset: lax.ppermute(parts[offset], "seq", [(at, at ^ offset) for at in range(chips)])
            for offset in (2, 3, 1)
        }
        return (parts[0], moved[1], moved[2], moved[3])

    def to_sibling(piece):
        return lax.ppermute(piece, "sub", swap)

    def stay(array):
        return pltpu.with_memory_space_constraint(array, pltpu.HBM)

    hidden_other = to_sibling(hidden)
    block = low(chips, rows + id_lines(rows, head_dim), head_dim)
    grads_mine, grads_theirs = call(
        pack_kernel,
        (block, block),
        place,
        stay(d_attended),
        stay(assign),
        scratch=[pltpu.VMEM(assign.shape, jnp.int32), pltpu.SemaphoreType.DMA((count + 1,))],
        hbm=2,
    )
    grads_other = to_sibling(grads_theirs)

    def project(turn, weights, *arrived):
        number = len(weights)
        outs = buffers(2 * number * rows) if turn == 0 else low(number, 2 * rows, width // 2)

        return call(
            partial(project_kernel, number, turn),
            outs,
            place,
            *arrived,
            stay(hidden),
            hidden_other,
            *(stay(weight) for weight in weights),
            scratch=[
                pltpu.VMEM((2 * rows, half), jnp.bfloat16),
                pltpu.VMEM((number, half, width // 2), jnp.bfloat16),
                pltpu.VMEM((2 * rows, width // 2), jnp.bfloat16),
                pltpu.SemaphoreType.DMA((number, 4)),
                pltpu.SemaphoreType.DMA((2,)),
            ],
            hbm=2 + number,
            limits=project_params,
            takes=(8 if number == 2 else 0.1) if turn == 0 else 0.1,
        )

    merged = call(merge_kernel, buffers(2 * block.shape[1]), place, grads_mine, grads_other)
    grads = exchange(merged)
    hidden_other, _ = lax.optimization_barrier((hidden_other, merged[0]))
    early, late = (w_query, w_key), (w_value,)
    early_arrived = to_sibling(project(1, early))
    late_arrived = to_sibling(project(1, late))
    grads = exchange(call(merge_kernel, buffers(2 * block.shape[1]), place, grads_mine, grads_other))
    early_arrived, _ = lax.optimization_barrier((early_arrived, grads[0]))
    early_projected = project(0, early, early_arrived)
    packed = exchange(early_projected)
    late_arrived, _, _ = lax.optimization_barrier((late_arrived, early_projected[0], (grads[2], grads[3])))
    late_projected = project(0, late, late_arrived)
    valued = exchange(late_projected)
    packed = lax.optimization_barrier((*packed, late_projected[0]))[:chips]

    def held(kind):
        return pltpu.VMEM((tokens, head_dim), kind)

    id_scratch = [pltpu.VMEM((count, 8, rows), jnp.float32), held(jnp.float32)]
    *value_grads, probs, sums = call(
        partial(value_grad_kernel, factor, chips, rows),
        (
            *buffers(2 * rows),
            pltpu.VMEM((count * (count + 1) // 2 * rows, rows), jnp.bfloat16),
            low(clusters, head_dim),
        ),
        place,
        *packed,
        *grads,
        cluster_rank.reshape(1, clusters),
        scratch=[held(jnp.bfloat16)] * 3 + id_scratch + [held(jnp.float32)],
        takes=7,
    )
    value_back = exchange(value_grads)
    results = call(
        partial(query_grad_kernel, scale, chips, rows),
        (*buffers(4 * rows), *(low(chips, rows + owned, head_dim),) * 2),
        place,
        *packed,
        *valued,
        *grads,
        probs,
        sums,
        scratch=[held(jnp.bfloat16)] * 4
        + [held(jnp.float32)]
        + [held(jnp.bfloat16)] * 2,
        takes=10,
    )
    *ready, _, _ = lax.optimization_barrier((*results[:chips], value_back[2], value_back[3]))
    back = exchange(ready)

    attended_mine, attended_theirs = results[chips:]
    outputs = call(
        merge_kernel, buffers(2 * (rows + owned)), place, attended_mine, to_sibling(attended_theirs)
    )
    back = (lax.optimization_barrier((back[0], outputs[0]))[0], *back[1:])
    back_other = tuple(to_sibling(part) for part in back)
    value_other = to_sibling(
        call(join_kernel, low(chips, 2 * rows, head_dim), place, *value_back)
    )

    def input_part(which, place):
        return call(
            partial(input_kernel, chips, which),
            low(rows, half),
            place,
            *back,
            *back_other,
            *value_back,
            value_other,
            w_query,
            w_key,
            w_value,
            scratch=[pltpu.VMEM((rows, 3 * width), jnp.bfloat16)],
        )

    *outputs, _, _ = lax.optimization_barrier((*outputs, back[2], back[3]))
    returned = exchange(outputs)
    square = ("head", "sub")
    crossing = input_part(3, place)
    first = lax.ppermute(crossing, square, [(0, 1), (1, 3), (3, 2), (2, 0)])
    kept = input_part(2, lax.optimization_barrier((place, crossing))[0])
    second = lax.ppermute(kept, square, [(1, 2), (2, 1)])
    attended, centroid_sums = call(
        partial(attended_kernel, chips),
        (low(rows, width), jax.ShapeDtypeStruct((count, owned, head_dim), jnp.float32)),
        place,
        *returned,
        takes=8,
    )
    first, second, _ = lax.optimization_barrier((first, second, attended))
    d_hidden = call(sum_kernel, low(rows, half), place, first, second, kept)
    return (attended, d_hidden, centroid_sums)


def per_device(hidden, w_query, w_key, w_value, cluster_rank, assign, d_attended):
    chips = lax.axis_size("seq")
    fits = chips == 4 and lax.axis_size("sub") == 2 and lax.axis_size("head") == 2
    plan = by_head if fits and assign.shape[0] == 2 * chips else by_owner
    return plan(hidden, w_query, w_key, w_value, cluster_rank, assign, d_attended)


def solution(mesh):
    placed = (
        P(("groups", "seq", "sub"), None),
        P("sub", "head"),
        P("sub", "head"),
        P("sub", "head"),
        P("groups"),
        P("head", ("groups", "seq", "sub")),
        P(("groups", "seq", "sub"), "head"),
    )
    return jax.shard_map(
        per_device,
        mesh=mesh,
        in_specs=placed,
        out_specs=(
            P(("groups", "seq", "sub"), "head"),
            P(("groups", "seq", "sub"), "head"),
            P("head", ("groups", "seq", "sub"), None),
        ),
        check_vma=False,
    )
```

```python
from functools import partial

import jax
import jax.numpy as jnp
from jax import lax
from jax.experimental import pallas as pl
from jax.experimental.pallas import tpu as pltpu
from jax.sharding import PartitionSpec as P

epsilon = 1e-06


def keep_mask(filled, cluster_ids, positions):
    count = filled.shape[0]
    same = filled[:, None] & filled[None, :] & (cluster_ids[:, None] == cluster_ids[None, :])
    causal = positions[None, :] <= positions[:, None]
    diagonal = jnp.arange(count)[:, None] == jnp.arange(count)[None, :]
    return same & causal | diagonal


def head_forward(packed, scale):
    queries, keys_in, values, filled, cluster_ids, positions = packed
    scores = (
        lax.dot_general(
            queries, keys_in, (((1,), (1,)), ((), ())), preferred_element_type=jnp.float32
        )
        * scale
    )
    allowed = keep_mask(filled, cluster_ids, positions)
    row_top = jnp.max(jnp.where(allowed, scores, -jnp.inf), axis=1)
    expd = jnp.where(allowed, jnp.exp(scores - row_top[:, None]), 0.0)
    row_total = jnp.sum(expd, axis=1)
    probs_low = (expd / row_total[:, None]).astype(jnp.bfloat16)
    outputs = jnp.dot(probs_low, values, preferred_element_type=jnp.float32).astype(jnp.bfloat16)
    return (outputs, row_top, row_total)


def head_backward(packed, scale):
    queries, keys_in, values, grads_in, filled, cluster_ids, positions, row_top, row_total = packed
    contract_last = (((1,), (1,)), ((), ()))
    contract_first = (((0,), (0,)), ((), ()))
    scores = (
        lax.dot_general(queries, keys_in, contract_last, preferred_element_type=jnp.float32) * scale
    )
    allowed = keep_mask(filled, cluster_ids, positions)
    probs = jnp.where(allowed, jnp.exp(scores - row_top[:, None]), 0.0) / row_total[:, None]
    probs_low = probs.astype(jnp.bfloat16)
    grad_probs = lax.dot_general(
        grads_in, values, contract_last, preferred_element_type=jnp.float32
    )
    delta_rows = jnp.sum(probs * grad_probs, axis=1)
    grad_low = (probs * (grad_probs - delta_rows[:, None]) * scale).astype(jnp.bfloat16)
    grad_query = jnp.dot(grad_low, keys_in, preferred_element_type=jnp.float32).astype(jnp.bfloat16)
    grad_key = lax.dot_general(
        grad_low, queries, contract_first, preferred_element_type=jnp.float32
    ).astype(jnp.bfloat16)
    grad_value = lax.dot_general(
        probs_low, grads_in, contract_first, preferred_element_type=jnp.float32
    ).astype(jnp.bfloat16)
    return (grad_query, grad_key, grad_value)


def by_owner(hidden, w_query, w_key, w_value, cluster_rank, assign, d_attended):
    tok_rows = hidden.shape[0]
    heads_here = assign.shape[0]
    head_dim = w_query.shape[1] // heads_here
    clusters = cluster_rank.shape[0]
    seq_count = lax.axis_size("seq")
    sub_count = lax.axis_size("sub")
    owners = seq_count * sub_count
    capacity = 2 * tok_rows // owners
    slot_count = owners * capacity
    per_owner = clusters // owners
    scale = head_dim ** (-0.5)
    pieces = (
        lax.all_gather(w_query, "sub", axis=0, tiled=True),
        lax.all_gather(w_key, "sub", axis=0, tiled=True),
        lax.all_gather(w_value, "sub", axis=0, tiled=True),
    )
    projected = tuple(
        (
            jnp.dot(hidden, weight_piece, preferred_element_type=jnp.float32)
            for weight_piece in pieces
        )
    )

    def split_heads(matrix):
        return (
            matrix.astype(jnp.bfloat16).reshape(tok_rows, heads_here, head_dim).transpose(1, 0, 2)
        )

    queries, keys_all, values = tuple((split_heads(matrix) for matrix in projected))
    cluster_range = jnp.arange(clusters, dtype=jnp.int32)
    rank_tok = jnp.sum(jnp.where(assign[:, :, None] == cluster_range, cluster_rank, 0), axis=2)
    owner_ids = rank_tok // per_owner
    owner_hot = (owner_ids[:, :, None] == jnp.arange(owners, dtype=jnp.int32)).astype(jnp.int32)
    within = jnp.sum(owner_hot * (jnp.cumsum(owner_hot, axis=1) - 1), axis=2)
    slot_tok = owner_ids * capacity + within
    token_ids = jnp.arange(tok_rows, dtype=jnp.int32)
    slot_range = jnp.arange(slot_count, dtype=jnp.int32)
    slot_match = slot_tok[:, None, :] == slot_range[None, :, None]
    slot_hot = slot_match.astype(jnp.bfloat16)

    def to_slots(rows_in):
        kept = jnp.einsum(
            "hst,htd->hsd", slot_hot, rows_in, preferred_element_type=jnp.float32
        ).astype(jnp.bfloat16)
        return kept.reshape(heads_here, owners, capacity, head_dim)

    def from_slots(slotted):
        flat_slots = slotted.reshape(heads_here, slot_count, head_dim)
        return jnp.einsum(
            "hst,hsd->htd", slot_hot, flat_slots, preferred_element_type=jnp.float32
        ).astype(jnp.bfloat16)

    def exchange_three(first, second, third):
        return (
            lax.all_to_all(first, ("seq", "sub"), split_axis=1, concat_axis=1, tiled=True),
            lax.all_to_all(second, ("seq", "sub"), split_axis=1, concat_axis=1, tiled=True),
            lax.all_to_all(third, ("seq", "sub"), split_axis=1, concat_axis=1, tiled=True),
        )

    sent = exchange_three(to_slots(queries), to_slots(keys_all), to_slots(values))
    tag_tok = assign * tok_rows + token_ids
    slot_tag = jnp.sum(jnp.where(slot_match, tag_tok[:, None, :] + 1, 0), axis=2) - 1
    tags = lax.all_to_all(
        slot_tag.reshape(heads_here, owners, capacity),
        ("seq", "sub"),
        split_axis=1,
        concat_axis=1,
        tiled=True,
    )
    tags = tags.reshape(heads_here, slot_count)
    owner_q, owner_k, owner_v = tuple(
        (member.reshape(heads_here, slot_count, head_dim) for member in sent)
    )
    filled = tags >= 0
    cluster_ids = jnp.where(filled, tags // tok_rows, -1)
    positions = slot_range // capacity * tok_rows + tags % tok_rows
    outputs, row_top, row_total = lax.map(
        partial(head_forward, scale=scale),
        (owner_q, owner_k, owner_v, filled, cluster_ids, positions),
    )
    returned = lax.all_to_all(
        outputs.reshape(heads_here, owners, capacity, head_dim),
        ("seq", "sub"),
        split_axis=1,
        concat_axis=1,
        tiled=True,
    )

    def merge_heads(slotted):
        return from_slots(slotted).transpose(1, 0, 2).reshape(tok_rows, heads_here * head_dim)

    attended = merge_heads(returned)
    grads_tok = d_attended.reshape(tok_rows, heads_here, head_dim).transpose(1, 0, 2)
    owner_g = lax.all_to_all(
        to_slots(grads_tok), ("seq", "sub"), split_axis=1, concat_axis=1, tiled=True
    ).reshape(heads_here, slot_count, head_dim)
    grad_q, grad_k, grad_v = lax.map(
        partial(head_backward, scale=scale),
        (owner_q, owner_k, owner_v, owner_g, filled, cluster_ids, positions, row_top, row_total),
    )
    shape_four = (heads_here, owners, capacity, head_dim)
    back = exchange_three(
        grad_q.reshape(shape_four), grad_k.reshape(shape_four), grad_v.reshape(shape_four)
    )
    token_grads = tuple((merge_heads(member) for member in back))
    pieces = lax.all_gather((w_query, w_key, w_value), "sub", axis=0, tiled=True)
    terms = [
        jnp.einsum("tc,rc->tr", grad_rows_in, weight_piece, preferred_element_type=jnp.float32)
        for grad_rows_in, weight_piece in zip(token_grads, pieces)
    ]
    partial_grad = terms[0] + terms[1] + terms[2]
    d_hidden = lax.psum_scatter(
        partial_grad.astype(jnp.bfloat16), "head", scatter_dimension=1, tiled=True
    )
    keys_float = keys_all.astype(jnp.float32)
    unit_keys = keys_float * lax.rsqrt(
        jnp.sum(keys_float * keys_float, axis=2, keepdims=True) + epsilon
    )
    member_hot = (rank_tok[:, :, None] == cluster_range).astype(jnp.float32)
    local_sums = jnp.einsum("htr,htd->hrd", member_hot, unit_keys, precision=lax.Precision.HIGHEST)
    centroid_sums = lax.psum_scatter(
        local_sums.astype(jnp.bfloat16), ("seq", "sub"), scatter_dimension=1, tiled=True
    ).astype(jnp.float32)
    return (attended, d_hidden, centroid_sums)


contract_last = (((1,), (1,)), ((), ()))
contract_first = (((0,), (0,)), ((), ()))
log2_e = 1.4426950408889634
mebi = 1024 * 1024


def id_lines(rows, head_dim):
    return -(-(rows // head_dim) // 16) * 16


def pack_kernel(place_ref, grads_ref, assign_ref, mine_ref, theirs_ref, ids_ref, sems):
    chips, padded, head_dim = mine_ref.shape
    rows = grads_ref.shape[0]
    spare = padded - rows - rows // head_dim
    copies = [pltpu.make_async_copy(assign_ref, ids_ref, sems.at[2 * chips])]
    for turn, out_ref in enumerate((mine_ref, theirs_ref)):
        for chip in range(chips):
            head = (place_ref[1] ^ turn) * chips + chip
            at = pl.multiple_of(head * head_dim, head_dim)
            copies.append(
                pltpu.make_async_copy(
                    grads_ref.at[:, pl.ds(at, head_dim)],
                    out_ref.at[chip, pl.ds(0, rows)],
                    sems.at[turn * chips + chip],
                )
            )
    for copy in copies:
        copy.start()
    copies[0].wait()
    for turn, out_ref in enumerate((mine_ref, theirs_ref)):
        for chip in range(chips):
            head = (place_ref[1] ^ turn) * chips + chip
            ids = ids_ref[pl.ds(head, 1), :].astype(jnp.float32)
            lines = [
                ids[:, start : start + head_dim] for start in range(0, rows, head_dim)
            ] + [jnp.zeros((spare, head_dim), jnp.float32)]
            out_ref[chip, rows:, :] = jnp.concatenate(lines, axis=0).astype(jnp.bfloat16)
    for copy in copies[1:]:
        copy.wait()


def merge_kernel(place_ref, mine_ref, theirs_ref, *out_refs):
    height = mine_ref.shape[1]
    for turn, held_ref in enumerate((mine_ref, theirs_ref)):
        at = pl.ds(pl.multiple_of((place_ref[1] ^ turn) * height, height), height)
        for offset, out_ref in enumerate(out_refs):
            out_ref[at, :] = held_ref[place_ref[0] ^ offset]


def fetch_columns(half, weights, held_ref, sems):
    chunks = sems.shape[1]
    columns = held_ref.shape[2]
    rows = held_ref.shape[1] // chunks
    at = pl.ds(pl.multiple_of(half * columns, columns), columns)
    copies = []
    for index, weight in enumerate(weights):
        for chunk in range(chunks):
            lines = pl.ds(chunk * rows, rows)
            copy = pltpu.make_async_copy(
                weight.at[lines, at], held_ref.at[index, lines], sems.at[index, chunk]
            )
            copy.start()
            copies.append(copy)
    return copies


def project_kernel(count, turn, place_ref, *refs):
    if turn == 0:
        arrived_ref, refs = refs[0], refs[1:]
    tokens, weights, refs = refs[:2], refs[2 : 2 + count], refs[2 + count :]
    out_refs, (joined_ref, held_ref, low_ref, sems, token_sems) = refs[:-5], refs[-5:]
    side = place_ref[1]
    tall, depth = joined_ref.shape
    rows = tall // 2
    near = pl.ds(pl.multiple_of(side * depth, depth), depth)
    joins = []
    for core, source in enumerate(tokens):
        at = pl.ds(pl.multiple_of((side ^ core) * rows, rows), rows)
        joins.append(
            pltpu.make_async_copy(source.at[:, near], joined_ref.at[at], token_sems.at[core])
        )
        joins[core].start()
    copies = fetch_columns(side ^ turn, weights, held_ref, sems)
    for copy in joins:
        copy.wait()
    chunks = sems.shape[1]
    for index in range(count):
        for chunk in range(chunks):
            copies[index * chunks + chunk].wait()
        total = jnp.dot(joined_ref[...], held_ref[index], preferred_element_type=jnp.float32)
        if turn == 1:
            out_refs[0][index] = total.astype(jnp.bfloat16)
            continue
        low_ref[...] = (total + arrived_ref[index].astype(jnp.float32)).astype(jnp.bfloat16)
        for offset, out_ref in enumerate(out_refs):
            head_dim = out_ref.shape[1]
            at = pl.multiple_of((place_ref[0] ^ offset) * head_dim, head_dim)
            out_ref[index * tall : (index + 1) * tall, :] = low_ref[:, pl.ds(at, head_dim)]


def in_order(place, parts, start, ordered):
    for offset, part in enumerate(parts):
        tall = ordered.shape[0] // len(parts)
        at = pl.ds(pl.multiple_of((place ^ offset) * tall, tall), tall)
        ordered[at, :] = part[start : start + tall, :]


def order_grads(place, parts, rows, grad_rows, id_rows, id_cols):
    head_dim = grad_rows.shape[1]
    height = parts[0].shape[0] // 2
    for offset, part in enumerate(parts):
        for core in range(2):
            block = (place ^ offset) * 2 + core
            at = pl.ds(pl.multiple_of(block * rows, rows), rows)
            start = core * height
            grad_rows[at, :] = part[start : start + rows, :]
            lines = part[start + rows : start + rows + 16, :].astype(jnp.float32)
            ids = jnp.concatenate(
                [lines[line : line + 1, :] for line in range(rows // head_dim)], axis=1
            )
            id_rows[block] = jnp.broadcast_to(ids, id_rows.shape[1:])
            id_cols[at, :] = jnp.broadcast_to(ids, (head_dim, rows)).T


def order_rows(place, parts, rows, ordered):
    height = parts[0].shape[0] // 2
    for offset, part in enumerate(parts):
        for core in range(2):
            at = pl.ds(pl.multiple_of(((place ^ offset) * 2 + core) * rows, rows), rows)
            ordered[at, :] = part[core * height : core * height + rows, :]


def block_scores(factor, block, rows, queries, keys_in, id_rows, id_cols):
    head_dim = queries.shape[1]
    seen = (block + 1) * rows
    scores = lax.dot_general(
        keys_in[:seen, :],
        queries[block * rows : seen, :],
        contract_last,
        preferred_element_type=jnp.float32,
    )
    ids = id_cols[:seen, :]
    mine = id_rows[block][:1, :]
    same = jnp.concatenate(
        [ids == mine[:, start : start + head_dim] for start in range(0, rows, head_dim)], axis=1
    )
    key_at = lax.broadcasted_iota(jnp.int32, (rows, rows), 0)
    query_at = lax.broadcasted_iota(jnp.int32, (rows, rows), 1)
    last = same[seen - rows :] & (key_at <= query_at)
    allowed = last if block == 0 else jnp.concatenate([same[: seen - rows], last], axis=0)
    return jnp.where(allowed, scores * factor, -jnp.inf)


def value_grad_kernel(factor, chips, rows, place_ref, *refs):
    packed, grads, rank_ref = refs[:chips], refs[chips : 2 * chips], refs[2 * chips]
    refs = refs[2 * chips + 1 :]
    out_refs, probs_ref, sums_ref = refs[:chips], refs[chips], refs[chips + 1]
    queries, keys_in, grad_rows, id_rows, id_cols, total_ref = refs[chips + 2 :]
    head_dim = queries.shape[1]
    clusters = rank_ref.shape[1]
    tall = 2 * rows
    place = place_ref[0]
    in_order(place, packed, 0, queries)
    in_order(place, packed, tall, keys_in)
    order_grads(place, grads, rows, grad_rows, id_rows, id_cols)
    total_ref[...] = jnp.zeros_like(total_ref)
    stored = 0
    for block in range(2 * chips):
        seen = (block + 1) * rows
        scores = block_scores(factor, block, rows, queries, keys_in, id_rows, id_cols)
        top = jnp.max(scores, axis=0, keepdims=True)
        expd = jnp.exp2(scores - top)
        total = jnp.sum(expd, axis=0, keepdims=True)
        probs_low = (expd * (1.0 / total)).astype(jnp.bfloat16)
        probs_ref[stored : stored + seen, :] = probs_low
        stored += seen
        total_ref[:seen, :] += jnp.dot(
            probs_low, grad_rows[block * rows : seen, :], preferred_element_type=jnp.float32
        )
    for offset, out_ref in enumerate(out_refs):
        at = pl.multiple_of((place ^ offset) * tall, tall)
        out_ref[...] = total_ref[pl.ds(at, tall), :].astype(jnp.bfloat16)
    sums = jnp.zeros((clusters, head_dim), jnp.float32)
    cluster_at = lax.broadcasted_iota(jnp.int32, (clusters, rows), 0).astype(jnp.float32)
    for block in range(2 * chips):
        keys_float = keys_in[block * rows : (block + 1) * rows, :].astype(jnp.float32)
        unit = keys_float * lax.rsqrt(
            jnp.sum(keys_float * keys_float, axis=1, keepdims=True) + epsilon
        )
        unit_high = unit.astype(jnp.bfloat16)
        unit_low = (unit - unit_high.astype(jnp.float32)).astype(jnp.bfloat16)
        member = jnp.where(cluster_at == id_rows[block][:1, :], 1.0, 0.0).astype(jnp.bfloat16)
        sums += jnp.dot(member, unit_high, preferred_element_type=jnp.float32)
        sums += jnp.dot(member, unit_low, preferred_element_type=jnp.float32)
    rank_at = lax.broadcasted_iota(jnp.int32, (clusters, clusters), 0)
    ordered = jnp.where(rank_at == rank_ref[...], 1.0, 0.0).astype(jnp.bfloat16)
    ranked = jnp.dot(ordered, sums.astype(jnp.bfloat16), preferred_element_type=jnp.float32)
    sums_ref[...] = ranked.astype(jnp.bfloat16)


def query_grad_kernel(scale, chips, rows, place_ref, *refs):
    packed, valued, grads = refs[:chips], refs[chips : 2 * chips], refs[2 * chips : 3 * chips]
    probs_ref, sums_ref = refs[3 * chips : 3 * chips + 2]
    refs = refs[3 * chips + 2 :]
    grad_refs, out_refs, refs = refs[:chips], refs[chips : chips + 2], refs[chips + 2 :]
    queries, keys_in, values, grad_rows, total_ref, dq_ref, attended_ref = refs
    tall = 2 * rows
    place = place_ref[0]
    in_order(place, packed, 0, queries)
    in_order(place, packed, tall, keys_in)
    in_order(place, valued, 0, values)
    order_rows(place, grads, rows, grad_rows)
    total_ref[...] = jnp.zeros_like(total_ref)
    stored = 0
    for block in range(2 * chips):
        seen = (block + 1) * rows
        mine = slice(block * rows, seen)
        probs_low = probs_ref[stored : stored + seen, :]
        stored += seen
        seen_values = values[:seen, :]
        grad_probs = lax.dot_general(
            seen_values, grad_rows[mine, :], contract_last, preferred_element_type=jnp.float32
        )
        flipped = lax.dot_general(
            seen_values, probs_low, contract_first, preferred_element_type=jnp.float32
        )
        attended_ref[mine, :] = flipped.T.astype(jnp.bfloat16)
        probs = probs_low.astype(jnp.float32)
        weighted = probs * grad_probs
        delta = jnp.sum(weighted, axis=0, keepdims=True)
        grad_low = (weighted - probs * delta).astype(jnp.bfloat16)
        total_ref[:seen, :] += jnp.dot(
            grad_low, queries[mine, :], preferred_element_type=jnp.float32
        )
        flipped = lax.dot_general(
            keys_in[:seen, :], grad_low, contract_first, preferred_element_type=jnp.float32
        )
        dq_ref[mine, :] = (flipped.T * scale).astype(jnp.bfloat16)
    for offset in range(chips):
        at = pl.ds(pl.multiple_of((place ^ offset) * tall, tall), tall)
        grad_refs[offset][:tall, :] = dq_ref[at, :]
        grad_refs[offset][tall:, :] = (total_ref[at, :] * scale).astype(jnp.bfloat16)
    owned = sums_ref.shape[0] // (2 * chips)
    for turn, out_ref in enumerate(out_refs):
        for chip in range(chips):
            shard = chip * 2 + (place_ref[1] ^ turn)
            at = pl.ds(pl.multiple_of(shard * rows, rows), rows)
            out_ref[chip, :rows, :] = attended_ref[at, :]
            at = pl.ds(pl.multiple_of(shard * owned, owned), owned)
            out_ref[chip, rows:, :] = sums_ref[at, :]


def join_kernel(*refs):
    parts, out_ref = refs[1:-1], refs[-1]
    for offset, part in enumerate(parts):
        out_ref[offset] = part[...]


def input_kernel(chips, which, place_ref, *refs):
    valued_other_ref, refs = refs[3 * chips], refs[: 3 * chips] + refs[3 * chips + 1 :]
    weights, (out_ref, gathered_ref) = refs[3 * chips : -2], refs[-2:]
    rows, width = out_ref.shape[0], weights[0].shape[1]
    head_dim = width // (2 * chips)
    for turn in range(2):
        parts = refs[turn * chips : (turn + 1) * chips]
        valued = refs[2 * chips : 3 * chips]
        for offset in range(chips):
            head = (place_ref[1] ^ turn) * chips + (place_ref[0] ^ offset)
            for index in range(3):
                source = parts[offset] if index < 2 else valued[offset]
                if index == 2 and turn == 1:
                    source = valued_other_ref.at[offset]
                at = pl.multiple_of((2 * (index % 2) + place_ref[which]) * rows, rows)
                start = pl.multiple_of(index * width + head * head_dim, head_dim)
                gathered_ref[:, pl.ds(start, head_dim)] = source[pl.ds(at, rows), :]
    flipped = None
    for index in range(3):
        term = lax.dot_general(
            weights[index][...],
            gathered_ref[:, index * width : (index + 1) * width],
            contract_last,
            preferred_element_type=jnp.float32,
        )
        flipped = term if flipped is None else flipped + term
    out_ref[...] = flipped.T.astype(out_ref.dtype)


def attended_kernel(chips, place_ref, *refs):
    parts, (attended_ref, sums_ref) = refs[:chips], refs[chips:]
    rows = attended_ref.shape[0]
    head_dim = sums_ref.shape[2]
    height = parts[0].shape[0] // 2
    for core in range(2):
        start = core * height
        for offset, part in enumerate(parts):
            head = core * chips + (place_ref[0] ^ offset)
            at = pl.multiple_of(head * head_dim, head_dim)
            attended_ref[:, pl.ds(at, head_dim)] = part[start : start + rows, :]
            sums_ref[head] = part[start + rows : start + height, :].astype(jnp.float32)


def sum_kernel(place_ref, first_ref, second_ref, kept_ref, hidden_ref):
    keeps = place_ref[2] == place_ref[1]
    second = jnp.where(keeps, kept_ref[...], second_ref[...]).astype(jnp.float32)
    hidden_ref[...] = (first_ref[...].astype(jnp.float32) + second).astype(jnp.bfloat16)


def by_head(hidden, w_query, w_key, w_value, cluster_rank, assign, d_attended):
    rows = hidden.shape[0]
    count = assign.shape[0]
    chips = count // 2
    half, width = w_query.shape
    head_dim = width // count
    tokens = count * rows
    clusters = cluster_rank.shape[0]
    owned = clusters // count
    scale = head_dim ** (-0.5)
    factor = scale * log2_e
    smem = pl.BlockSpec(memory_space=pltpu.SMEM)
    vmem = pl.BlockSpec(memory_space=pltpu.VMEM)
    anywhere = pl.BlockSpec(memory_space=pl.ANY)
    params = pltpu.CompilerParams(vmem_limit_bytes=32 * mebi)
    project_params = pltpu.CompilerParams(vmem_limit_bytes=32 * mebi)
    swap = [(0, 1), (1, 0)]
    chip, side, column = (lax.axis_index(name) for name in ("seq", "sub", "head"))
    place = jnp.stack([chip, side, column, 1 - column])

    def call(kernel, outs, *operands, scratch=(), hbm=0, limits=params, takes=1):
        return pl.pallas_call(
            kernel,
            out_shape=outs,
            in_specs=[smem] + [vmem] * (len(operands) - 1 - hbm) + [anywhere] * hbm,
            out_specs=jax.tree.map(lambda _: vmem, outs),
            scratch_shapes=list(scratch),
            compiler_params=limits,
            cost_estimate=pl.CostEstimate(
                flops=int(takes * 1.15e9), bytes_accessed=mebi, transcendentals=0
            ),
        )(*operands)

    def low(*shape):
        return jax.ShapeDtypeStruct(shape, jnp.bfloat16)

    def buffers(height):
        return (low(height, head_dim),) * chips

    def exchange(parts):
        moved = {
            offset: lax.ppermute(parts[offset], "seq", [(at, at ^ offset) for at in range(chips)])
            for offset in (2, 3, 1)
        }
        return (parts[0], moved[1], moved[2], moved[3])

    def to_sibling(piece):
        return lax.ppermute(piece, "sub", swap)

    def stay(array):
        return pltpu.with_memory_space_constraint(array, pltpu.HBM)

    hidden_other = to_sibling(hidden)
    block = low(chips, rows + id_lines(rows, head_dim), head_dim)
    grads_mine, grads_theirs = call(
        pack_kernel,
        (block, block),
        place,
        stay(d_attended),
        stay(assign),
        scratch=[pltpu.VMEM(assign.shape, jnp.int32), pltpu.SemaphoreType.DMA((count + 1,))],
        hbm=2,
    )
    grads_other = to_sibling(grads_theirs)

    def project(turn, weights, *arrived):
        number = len(weights)
        outs = buffers(2 * number * rows) if turn == 0 else low(number, 2 * rows, width // 2)

        return call(
            partial(project_kernel, number, turn),
            outs,
            place,
            *arrived,
            stay(hidden),
            hidden_other,
            *(stay(weight) for weight in weights),
            scratch=[
                pltpu.VMEM((2 * rows, half), jnp.bfloat16),
                pltpu.VMEM((number, half, width // 2), jnp.bfloat16),
                pltpu.VMEM((2 * rows, width // 2), jnp.bfloat16),
                pltpu.SemaphoreType.DMA((number, 4)),
                pltpu.SemaphoreType.DMA((2,)),
            ],
            hbm=2 + number,
            limits=project_params,
            takes=(8 if number == 2 else 0.1) if turn == 0 else 0.1,
        )

    merged = call(merge_kernel, buffers(2 * block.shape[1]), place, grads_mine, grads_other)
    grads = exchange(merged)
    hidden_other, _ = lax.optimization_barrier((hidden_other, merged[0]))
    early, late = (w_query, w_key), (w_value,)
    early_arrived = to_sibling(project(1, early))
    late_arrived = to_sibling(project(1, late))
    grads = exchange(call(merge_kernel, buffers(2 * block.shape[1]), place, grads_mine, grads_other))
    early_arrived, _ = lax.optimization_barrier((early_arrived, grads[0]))
    early_projected = project(0, early, early_arrived)
    packed = exchange(early_projected)
    late_arrived, _, _ = lax.optimization_barrier((late_arrived, early_projected[0], (grads[2], grads[3])))
    late_projected = project(0, late, late_arrived)
    valued = exchange(late_projected)
    packed = lax.optimization_barrier((*packed, late_projected[0]))[:chips]

    def held(kind):
        return pltpu.VMEM((tokens, head_dim), kind)

    id_scratch = [pltpu.VMEM((count, 8, rows), jnp.float32), held(jnp.float32)]
    *value_grads, probs, sums = call(
        partial(value_grad_kernel, factor, chips, rows),
        (
            *buffers(2 * rows),
            pltpu.VMEM((count * (count + 1) // 2 * rows, rows), jnp.bfloat16),
            low(clusters, head_dim),
        ),
        place,
        *packed,
        *grads,
        cluster_rank.reshape(1, clusters),
        scratch=[held(jnp.bfloat16)] * 3 + id_scratch + [held(jnp.float32)],
        takes=7,
    )
    value_back = exchange(value_grads)
    results = call(
        partial(query_grad_kernel, scale, chips, rows),
        (*buffers(4 * rows), *(low(chips, rows + owned, head_dim),) * 2),
        place,
        *packed,
        *valued,
        *grads,
        probs,
        sums,
        scratch=[held(jnp.bfloat16)] * 4
        + [held(jnp.float32)]
        + [held(jnp.bfloat16)] * 2,
        takes=10,
    )
    *ready, _ = lax.optimization_barrier((*results[:chips], value_back[2]))
    back = exchange(ready)

    attended_mine, attended_theirs = results[chips:]
    outputs = call(
        merge_kernel, buffers(2 * (rows + owned)), place, attended_mine, to_sibling(attended_theirs)
    )
    back = (lax.optimization_barrier((back[0], outputs[0]))[0], *back[1:])
    back_other = tuple(to_sibling(part) for part in back)
    value_other = to_sibling(
        call(join_kernel, low(chips, 2 * rows, head_dim), place, *value_back)
    )

    def input_part(which, place):
        return call(
            partial(input_kernel, chips, which),
            low(rows, half),
            place,
            *back,
            *back_other,
            *value_back,
            value_other,
            w_query,
            w_key,
            w_value,
            scratch=[pltpu.VMEM((rows, 3 * width), jnp.bfloat16)],
        )

    *outputs, _, _ = lax.optimization_barrier((*outputs, back[2], back[3]))
    returned = exchange(outputs)
    square = ("head", "sub")
    crossing = input_part(3, place)
    first = lax.ppermute(crossing, square, [(0, 1), (1, 3), (3, 2), (2, 0)])
    kept = input_part(2, lax.optimization_barrier((place, crossing))[0])
    second = lax.ppermute(kept, square, [(1, 2), (2, 1)])
    attended, centroid_sums = call(
        partial(attended_kernel, chips),
        (low(rows, width), jax.ShapeDtypeStruct((count, owned, head_dim), jnp.float32)),
        place,
        *returned,
        takes=8,
    )
    first, second, _ = lax.optimization_barrier((first, second, attended))
    d_hidden = call(sum_kernel, low(rows, half), place, first, second, kept)
    return (attended, d_hidden, centroid_sums)


def per_device(hidden, w_query, w_key, w_value, cluster_rank, assign, d_attended):
    chips = lax.axis_size("seq")
    fits = chips == 4 and lax.axis_size("sub") == 2 and lax.axis_size("head") == 2
    plan = by_head if fits and assign.shape[0] == 2 * chips else by_owner
    return plan(hidden, w_query, w_key, w_value, cluster_rank, assign, d_attended)


def solution(mesh):
    placed = (
        P(("groups", "seq", "sub"), None),
        P("sub", "head"),
        P("sub", "head"),
        P("sub", "head"),
        P("groups"),
        P("head", ("groups", "seq", "sub")),
        P(("groups", "seq", "sub"), "head"),
    )
    return jax.shard_map(
        per_device,
        mesh=mesh,
        in_specs=placed,
        out_specs=(
            P(("groups", "seq", "sub"), "head"),
            P(("groups", "seq", "sub"), "head"),
            P("head", ("groups", "seq", "sub"), None),
        ),
        check_vma=False,
    )
```

```python
from functools import partial

import jax
import jax.numpy as jnp
from jax import lax
from jax.experimental import pallas as pl
from jax.experimental.pallas import tpu as pltpu
from jax.sharding import PartitionSpec as P

epsilon = 1e-06


def keep_mask(filled, cluster_ids, positions):
    count = filled.shape[0]
    same = filled[:, None] & filled[None, :] & (cluster_ids[:, None] == cluster_ids[None, :])
    causal = positions[None, :] <= positions[:, None]
    diagonal = jnp.arange(count)[:, None] == jnp.arange(count)[None, :]
    return same & causal | diagonal


def head_forward(packed, scale):
    queries, keys_in, values, filled, cluster_ids, positions = packed
    scores = (
        lax.dot_general(
            queries, keys_in, (((1,), (1,)), ((), ())), preferred_element_type=jnp.float32
        )
        * scale
    )
    allowed = keep_mask(filled, cluster_ids, positions)
    row_top = jnp.max(jnp.where(allowed, scores, -jnp.inf), axis=1)
    expd = jnp.where(allowed, jnp.exp(scores - row_top[:, None]), 0.0)
    row_total = jnp.sum(expd, axis=1)
    probs_low = (expd / row_total[:, None]).astype(jnp.bfloat16)
    outputs = jnp.dot(probs_low, values, preferred_element_type=jnp.float32).astype(jnp.bfloat16)
    return (outputs, row_top, row_total)


def head_backward(packed, scale):
    queries, keys_in, values, grads_in, filled, cluster_ids, positions, row_top, row_total = packed
    contract_last = (((1,), (1,)), ((), ()))
    contract_first = (((0,), (0,)), ((), ()))
    scores = (
        lax.dot_general(queries, keys_in, contract_last, preferred_element_type=jnp.float32) * scale
    )
    allowed = keep_mask(filled, cluster_ids, positions)
    probs = jnp.where(allowed, jnp.exp(scores - row_top[:, None]), 0.0) / row_total[:, None]
    probs_low = probs.astype(jnp.bfloat16)
    grad_probs = lax.dot_general(
        grads_in, values, contract_last, preferred_element_type=jnp.float32
    )
    delta_rows = jnp.sum(probs * grad_probs, axis=1)
    grad_low = (probs * (grad_probs - delta_rows[:, None]) * scale).astype(jnp.bfloat16)
    grad_query = jnp.dot(grad_low, keys_in, preferred_element_type=jnp.float32).astype(jnp.bfloat16)
    grad_key = lax.dot_general(
        grad_low, queries, contract_first, preferred_element_type=jnp.float32
    ).astype(jnp.bfloat16)
    grad_value = lax.dot_general(
        probs_low, grads_in, contract_first, preferred_element_type=jnp.float32
    ).astype(jnp.bfloat16)
    return (grad_query, grad_key, grad_value)


def by_owner(hidden, w_query, w_key, w_value, cluster_rank, assign, d_attended):
    tok_rows = hidden.shape[0]
    heads_here = assign.shape[0]
    head_dim = w_query.shape[1] // heads_here
    clusters = cluster_rank.shape[0]
    seq_count = lax.axis_size("seq")
    sub_count = lax.axis_size("sub")
    owners = seq_count * sub_count
    capacity = 2 * tok_rows // owners
    slot_count = owners * capacity
    per_owner = clusters // owners
    scale = head_dim ** (-0.5)
    pieces = (
        lax.all_gather(w_query, "sub", axis=0, tiled=True),
        lax.all_gather(w_key, "sub", axis=0, tiled=True),
        lax.all_gather(w_value, "sub", axis=0, tiled=True),
    )
    projected = tuple(
        (
            jnp.dot(hidden, weight_piece, preferred_element_type=jnp.float32)
            for weight_piece in pieces
        )
    )

    def split_heads(matrix):
        return (
            matrix.astype(jnp.bfloat16).reshape(tok_rows, heads_here, head_dim).transpose(1, 0, 2)
        )

    queries, keys_all, values = tuple((split_heads(matrix) for matrix in projected))
    cluster_range = jnp.arange(clusters, dtype=jnp.int32)
    rank_tok = jnp.sum(jnp.where(assign[:, :, None] == cluster_range, cluster_rank, 0), axis=2)
    owner_ids = rank_tok // per_owner
    owner_hot = (owner_ids[:, :, None] == jnp.arange(owners, dtype=jnp.int32)).astype(jnp.int32)
    within = jnp.sum(owner_hot * (jnp.cumsum(owner_hot, axis=1) - 1), axis=2)
    slot_tok = owner_ids * capacity + within
    token_ids = jnp.arange(tok_rows, dtype=jnp.int32)
    slot_range = jnp.arange(slot_count, dtype=jnp.int32)
    slot_match = slot_tok[:, None, :] == slot_range[None, :, None]
    slot_hot = slot_match.astype(jnp.bfloat16)

    def to_slots(rows_in):
        kept = jnp.einsum(
            "hst,htd->hsd", slot_hot, rows_in, preferred_element_type=jnp.float32
        ).astype(jnp.bfloat16)
        return kept.reshape(heads_here, owners, capacity, head_dim)

    def from_slots(slotted):
        flat_slots = slotted.reshape(heads_here, slot_count, head_dim)
        return jnp.einsum(
            "hst,hsd->htd", slot_hot, flat_slots, preferred_element_type=jnp.float32
        ).astype(jnp.bfloat16)

    def exchange_three(first, second, third):
        return (
            lax.all_to_all(first, ("seq", "sub"), split_axis=1, concat_axis=1, tiled=True),
            lax.all_to_all(second, ("seq", "sub"), split_axis=1, concat_axis=1, tiled=True),
            lax.all_to_all(third, ("seq", "sub"), split_axis=1, concat_axis=1, tiled=True),
        )

    sent = exchange_three(to_slots(queries), to_slots(keys_all), to_slots(values))
    tag_tok = assign * tok_rows + token_ids
    slot_tag = jnp.sum(jnp.where(slot_match, tag_tok[:, None, :] + 1, 0), axis=2) - 1
    tags = lax.all_to_all(
        slot_tag.reshape(heads_here, owners, capacity),
        ("seq", "sub"),
        split_axis=1,
        concat_axis=1,
        tiled=True,
    )
    tags = tags.reshape(heads_here, slot_count)
    owner_q, owner_k, owner_v = tuple(
        (member.reshape(heads_here, slot_count, head_dim) for member in sent)
    )
    filled = tags >= 0
    cluster_ids = jnp.where(filled, tags // tok_rows, -1)
    positions = slot_range // capacity * tok_rows + tags % tok_rows
    outputs, row_top, row_total = lax.map(
        partial(head_forward, scale=scale),
        (owner_q, owner_k, owner_v, filled, cluster_ids, positions),
    )
    returned = lax.all_to_all(
        outputs.reshape(heads_here, owners, capacity, head_dim),
        ("seq", "sub"),
        split_axis=1,
        concat_axis=1,
        tiled=True,
    )

    def merge_heads(slotted):
        return from_slots(slotted).transpose(1, 0, 2).reshape(tok_rows, heads_here * head_dim)

    attended = merge_heads(returned)
    grads_tok = d_attended.reshape(tok_rows, heads_here, head_dim).transpose(1, 0, 2)
    owner_g = lax.all_to_all(
        to_slots(grads_tok), ("seq", "sub"), split_axis=1, concat_axis=1, tiled=True
    ).reshape(heads_here, slot_count, head_dim)
    grad_q, grad_k, grad_v = lax.map(
        partial(head_backward, scale=scale),
        (owner_q, owner_k, owner_v, owner_g, filled, cluster_ids, positions, row_top, row_total),
    )
    shape_four = (heads_here, owners, capacity, head_dim)
    back = exchange_three(
        grad_q.reshape(shape_four), grad_k.reshape(shape_four), grad_v.reshape(shape_four)
    )
    token_grads = tuple((merge_heads(member) for member in back))
    pieces = lax.all_gather((w_query, w_key, w_value), "sub", axis=0, tiled=True)
    terms = [
        jnp.einsum("tc,rc->tr", grad_rows_in, weight_piece, preferred_element_type=jnp.float32)
        for grad_rows_in, weight_piece in zip(token_grads, pieces)
    ]
    partial_grad = terms[0] + terms[1] + terms[2]
    d_hidden = lax.psum_scatter(
        partial_grad.astype(jnp.bfloat16), "head", scatter_dimension=1, tiled=True
    )
    keys_float = keys_all.astype(jnp.float32)
    unit_keys = keys_float * lax.rsqrt(
        jnp.sum(keys_float * keys_float, axis=2, keepdims=True) + epsilon
    )
    member_hot = (rank_tok[:, :, None] == cluster_range).astype(jnp.float32)
    local_sums = jnp.einsum("htr,htd->hrd", member_hot, unit_keys, precision=lax.Precision.HIGHEST)
    centroid_sums = lax.psum_scatter(
        local_sums.astype(jnp.bfloat16), ("seq", "sub"), scatter_dimension=1, tiled=True
    ).astype(jnp.float32)
    return (attended, d_hidden, centroid_sums)


contract_last = (((1,), (1,)), ((), ()))
contract_first = (((0,), (0,)), ((), ()))
log2_e = 1.4426950408889634
mebi = 1024 * 1024


def id_lines(rows, head_dim):
    return -(-(rows // head_dim) // 16) * 16


def pack_kernel(place_ref, grads_ref, assign_ref, mine_ref, theirs_ref, ids_ref, sems):
    chips, padded, head_dim = mine_ref.shape
    rows = grads_ref.shape[0]
    spare = padded - rows - rows // head_dim
    copies = [pltpu.make_async_copy(assign_ref, ids_ref, sems.at[2 * chips])]
    for turn, out_ref in enumerate((mine_ref, theirs_ref)):
        for chip in range(chips):
            head = (place_ref[1] ^ turn) * chips + chip
            at = pl.multiple_of(head * head_dim, head_dim)
            copies.append(
                pltpu.make_async_copy(
                    grads_ref.at[:, pl.ds(at, head_dim)],
                    out_ref.at[chip, pl.ds(0, rows)],
                    sems.at[turn * chips + chip],
                )
            )
    for copy in copies:
        copy.start()
    copies[0].wait()
    for turn, out_ref in enumerate((mine_ref, theirs_ref)):
        for chip in range(chips):
            head = (place_ref[1] ^ turn) * chips + chip
            ids = ids_ref[pl.ds(head, 1), :].astype(jnp.float32)
            lines = [
                ids[:, start : start + head_dim] for start in range(0, rows, head_dim)
            ] + [jnp.zeros((spare, head_dim), jnp.float32)]
            out_ref[chip, rows:, :] = jnp.concatenate(lines, axis=0).astype(jnp.bfloat16)
    for copy in copies[1:]:
        copy.wait()


def merge_kernel(place_ref, mine_ref, theirs_ref, *out_refs):
    height = mine_ref.shape[1]
    for turn, held_ref in enumerate((mine_ref, theirs_ref)):
        at = pl.ds(pl.multiple_of((place_ref[1] ^ turn) * height, height), height)
        for offset, out_ref in enumerate(out_refs):
            out_ref[at, :] = held_ref[place_ref[0] ^ offset]


def fetch_columns(half, weights, held_ref, sems):
    chunks = sems.shape[1]
    columns = held_ref.shape[2]
    rows = held_ref.shape[1] // chunks
    at = pl.ds(pl.multiple_of(half * columns, columns), columns)
    copies = []
    for index, weight in enumerate(weights):
        for chunk in range(chunks):
            lines = pl.ds(chunk * rows, rows)
            copy = pltpu.make_async_copy(
                weight.at[lines, at], held_ref.at[index, lines], sems.at[index, chunk]
            )
            copy.start()
            copies.append(copy)
    return copies


def project_kernel(count, turn, place_ref, *refs):
    if turn == 0:
        arrived_ref, refs = refs[0], refs[1:]
    tokens, weights, refs = refs[:2], refs[2 : 2 + count], refs[2 + count :]
    out_refs, (joined_ref, held_ref, low_ref, sems, token_sems) = refs[:-5], refs[-5:]
    side = place_ref[1]
    tall, depth = joined_ref.shape
    rows = tall // 2
    near = pl.ds(pl.multiple_of(side * depth, depth), depth)
    joins = []
    for core, source in enumerate(tokens):
        at = pl.ds(pl.multiple_of((side ^ core) * rows, rows), rows)
        joins.append(
            pltpu.make_async_copy(source.at[:, near], joined_ref.at[at], token_sems.at[core])
        )
        joins[core].start()
    copies = fetch_columns(side ^ turn, weights, held_ref, sems)
    for copy in joins:
        copy.wait()
    chunks = sems.shape[1]
    for index in range(count):
        for chunk in range(chunks):
            copies[index * chunks + chunk].wait()
        total = jnp.dot(joined_ref[...], held_ref[index], preferred_element_type=jnp.float32)
        if turn == 1:
            out_refs[0][index] = total.astype(jnp.bfloat16)
            continue
        low_ref[...] = (total + arrived_ref[index].astype(jnp.float32)).astype(jnp.bfloat16)
        for offset, out_ref in enumerate(out_refs):
            head_dim = out_ref.shape[1]
            at = pl.multiple_of((place_ref[0] ^ offset) * head_dim, head_dim)
            out_ref[index * tall : (index + 1) * tall, :] = low_ref[:, pl.ds(at, head_dim)]


def fetch_kernel(turn, place_ref, *refs):
    weights, (held_ref, sems) = refs[:-2], refs[-2:]
    for copy in fetch_columns(place_ref[1] ^ turn, weights, held_ref, sems):
        copy.wait()


def opening_kernel(place_ref, held_ref, mine_ref, theirs_ref, *refs):
    tokens, refs = refs[:2], refs[2:]
    out_refs, (part_ref, joined_ref, sems) = refs[:-3], refs[-3:]
    side = place_ref[1]
    tall, depth = joined_ref.shape
    rows = tall // 2
    near = pl.ds(pl.multiple_of(side * depth, depth), depth)
    joins = []
    for core, source in enumerate(tokens):
        at = pl.ds(pl.multiple_of((side ^ core) * rows, rows), rows)
        joins.append(pltpu.make_async_copy(source.at[:, near], joined_ref.at[at], sems.at[core]))
        joins[core].start()
    merge_kernel(place_ref, mine_ref, theirs_ref, *out_refs)
    for copy in joins:
        copy.wait()
    for index in range(held_ref.shape[0]):
        total = jnp.dot(joined_ref[...], held_ref[index], preferred_element_type=jnp.float32)
        part_ref[index] = total.astype(jnp.bfloat16)


def in_order(place, parts, start, ordered):
    for offset, part in enumerate(parts):
        tall = ordered.shape[0] // len(parts)
        at = pl.ds(pl.multiple_of((place ^ offset) * tall, tall), tall)
        ordered[at, :] = part[start : start + tall, :]


def order_grads(place, parts, rows, grad_rows, id_rows, id_cols):
    head_dim = grad_rows.shape[1]
    height = parts[0].shape[0] // 2
    for offset, part in enumerate(parts):
        for core in range(2):
            block = (place ^ offset) * 2 + core
            at = pl.ds(pl.multiple_of(block * rows, rows), rows)
            start = core * height
            grad_rows[at, :] = part[start : start + rows, :]
            lines = part[start + rows : start + rows + 16, :].astype(jnp.float32)
            ids = jnp.concatenate(
                [lines[line : line + 1, :] for line in range(rows // head_dim)], axis=1
            )
            id_rows[block] = jnp.broadcast_to(ids, id_rows.shape[1:])
            id_cols[at, :] = jnp.broadcast_to(ids, (head_dim, rows)).T


def order_rows(place, parts, rows, ordered):
    height = parts[0].shape[0] // 2
    for offset, part in enumerate(parts):
        for core in range(2):
            at = pl.ds(pl.multiple_of(((place ^ offset) * 2 + core) * rows, rows), rows)
            ordered[at, :] = part[core * height : core * height + rows, :]


def block_scores(factor, block, rows, queries, keys_in, id_rows, id_cols):
    head_dim = queries.shape[1]
    seen = (block + 1) * rows
    scores = lax.dot_general(
        keys_in[:seen, :],
        queries[block * rows : seen, :],
        contract_last,
        preferred_element_type=jnp.float32,
    )
    ids = id_cols[:seen, :]
    mine = id_rows[block][:1, :]
    same = jnp.concatenate(
        [ids == mine[:, start : start + head_dim] for start in range(0, rows, head_dim)], axis=1
    )
    key_at = lax.broadcasted_iota(jnp.int32, (rows, rows), 0)
    query_at = lax.broadcasted_iota(jnp.int32, (rows, rows), 1)
    last = same[seen - rows :] & (key_at <= query_at)
    allowed = last if block == 0 else jnp.concatenate([same[: seen - rows], last], axis=0)
    return jnp.where(allowed, scores * factor, -jnp.inf)


def value_grad_kernel(factor, chips, rows, place_ref, *refs):
    packed, grads, rank_ref = refs[:chips], refs[chips : 2 * chips], refs[2 * chips]
    refs = refs[2 * chips + 1 :]
    out_refs, probs_ref, sums_ref = refs[:chips], refs[chips], refs[chips + 1]
    queries, keys_in, grad_rows, id_rows, id_cols, total_ref = refs[chips + 2 :]
    head_dim = queries.shape[1]
    clusters = rank_ref.shape[1]
    tall = 2 * rows
    place = place_ref[0]
    in_order(place, packed, 0, queries)
    in_order(place, packed, tall, keys_in)
    order_grads(place, grads, rows, grad_rows, id_rows, id_cols)
    total_ref[...] = jnp.zeros_like(total_ref)
    stored = 0
    for block in range(2 * chips):
        seen = (block + 1) * rows
        scores = block_scores(factor, block, rows, queries, keys_in, id_rows, id_cols)
        top = jnp.max(scores, axis=0, keepdims=True)
        expd = jnp.exp2(scores - top)
        total = jnp.sum(expd, axis=0, keepdims=True)
        probs_low = (expd * (1.0 / total)).astype(jnp.bfloat16)
        probs_ref[stored : stored + seen, :] = probs_low
        stored += seen
        total_ref[:seen, :] += jnp.dot(
            probs_low, grad_rows[block * rows : seen, :], preferred_element_type=jnp.float32
        )
    for offset, out_ref in enumerate(out_refs):
        at = pl.multiple_of((place ^ offset) * tall, tall)
        out_ref[...] = total_ref[pl.ds(at, tall), :].astype(jnp.bfloat16)
    sums = jnp.zeros((clusters, head_dim), jnp.float32)
    cluster_at = lax.broadcasted_iota(jnp.int32, (clusters, rows), 0).astype(jnp.float32)
    for block in range(2 * chips):
        keys_float = keys_in[block * rows : (block + 1) * rows, :].astype(jnp.float32)
        unit = keys_float * lax.rsqrt(
            jnp.sum(keys_float * keys_float, axis=1, keepdims=True) + epsilon
        )
        unit_high = unit.astype(jnp.bfloat16)
        unit_low = (unit - unit_high.astype(jnp.float32)).astype(jnp.bfloat16)
        member = jnp.where(cluster_at == id_rows[block][:1, :], 1.0, 0.0).astype(jnp.bfloat16)
        sums += jnp.dot(member, unit_high, preferred_element_type=jnp.float32)
        sums += jnp.dot(member, unit_low, preferred_element_type=jnp.float32)
    rank_at = lax.broadcasted_iota(jnp.int32, (clusters, clusters), 0)
    ordered = jnp.where(rank_at == rank_ref[...], 1.0, 0.0).astype(jnp.bfloat16)
    ranked = jnp.dot(ordered, sums.astype(jnp.bfloat16), preferred_element_type=jnp.float32)
    sums_ref[...] = ranked.astype(jnp.bfloat16)


def query_grad_kernel(scale, chips, rows, place_ref, *refs):
    packed, valued, grads = refs[:chips], refs[chips : 2 * chips], refs[2 * chips : 3 * chips]
    probs_ref, sums_ref = refs[3 * chips : 3 * chips + 2]
    refs = refs[3 * chips + 2 :]
    grad_refs, out_refs, refs = refs[:chips], refs[chips : chips + 2], refs[chips + 2 :]
    queries, keys_in, values, grad_rows, total_ref, dq_ref, attended_ref = refs
    tall = 2 * rows
    place = place_ref[0]
    in_order(place, packed, 0, queries)
    in_order(place, packed, tall, keys_in)
    in_order(place, valued, 0, values)
    order_rows(place, grads, rows, grad_rows)
    total_ref[...] = jnp.zeros_like(total_ref)
    stored = 0
    for block in range(2 * chips):
        seen = (block + 1) * rows
        mine = slice(block * rows, seen)
        probs_low = probs_ref[stored : stored + seen, :]
        stored += seen
        seen_values = values[:seen, :]
        grad_probs = lax.dot_general(
            seen_values, grad_rows[mine, :], contract_last, preferred_element_type=jnp.float32
        )
        flipped = lax.dot_general(
            seen_values, probs_low, contract_first, preferred_element_type=jnp.float32
        )
        attended_ref[mine, :] = flipped.T.astype(jnp.bfloat16)
        probs = probs_low.astype(jnp.float32)
        weighted = probs * grad_probs
        delta = jnp.sum(weighted, axis=0, keepdims=True)
        grad_low = (weighted - probs * delta).astype(jnp.bfloat16)
        total_ref[:seen, :] += jnp.dot(
            grad_low, queries[mine, :], preferred_element_type=jnp.float32
        )
        flipped = lax.dot_general(
            keys_in[:seen, :], grad_low, contract_first, preferred_element_type=jnp.float32
        )
        dq_ref[mine, :] = (flipped.T * scale).astype(jnp.bfloat16)
    for offset in range(chips):
        at = pl.ds(pl.multiple_of((place ^ offset) * tall, tall), tall)
        grad_refs[offset][:tall, :] = dq_ref[at, :]
        grad_refs[offset][tall:, :] = (total_ref[at, :] * scale).astype(jnp.bfloat16)
    owned = sums_ref.shape[0] // (2 * chips)
    for turn, out_ref in enumerate(out_refs):
        for chip in range(chips):
            shard = chip * 2 + (place_ref[1] ^ turn)
            at = pl.ds(pl.multiple_of(shard * rows, rows), rows)
            out_ref[chip, :rows, :] = attended_ref[at, :]
            at = pl.ds(pl.multiple_of(shard * owned, owned), owned)
            out_ref[chip, rows:, :] = sums_ref[at, :]


def join_kernel(*refs):
    parts, out_ref = refs[1:-1], refs[-1]
    for offset, part in enumerate(parts):
        out_ref[offset] = part[...]


def input_kernel(chips, which, place_ref, *refs):
    valued_other_ref, refs = refs[3 * chips], refs[: 3 * chips] + refs[3 * chips + 1 :]
    weights, (out_ref, gathered_ref) = refs[3 * chips : -2], refs[-2:]
    rows, width = out_ref.shape[0], weights[0].shape[1]
    head_dim = width // (2 * chips)
    for turn in range(2):
        parts = refs[turn * chips : (turn + 1) * chips]
        valued = refs[2 * chips : 3 * chips]
        for offset in range(chips):
            head = (place_ref[1] ^ turn) * chips + (place_ref[0] ^ offset)
            for index in range(3):
                source = parts[offset] if index < 2 else valued[offset]
                if index == 2 and turn == 1:
                    source = valued_other_ref.at[offset]
                at = pl.multiple_of((2 * (index % 2) + place_ref[which]) * rows, rows)
                start = pl.multiple_of(index * width + head * head_dim, head_dim)
                gathered_ref[:, pl.ds(start, head_dim)] = source[pl.ds(at, rows), :]
    flipped = None
    for index in range(3):
        term = lax.dot_general(
            weights[index][...],
            gathered_ref[:, index * width : (index + 1) * width],
            contract_last,
            preferred_element_type=jnp.float32,
        )
        flipped = term if flipped is None else flipped + term
    out_ref[...] = flipped.T.astype(out_ref.dtype)


def attended_kernel(chips, place_ref, *refs):
    parts, (attended_ref, sums_ref, sems) = refs[:chips], refs[chips:]
    rows = attended_ref.shape[0]
    head_dim = sums_ref.shape[2]
    height = parts[0].shape[0] // 2
    heads = [
        (part, core * height, core * chips + (place_ref[0] ^ offset))
        for core in range(2)
        for offset, part in enumerate(parts)
    ]
    copies = []
    for index, (part, start, head) in enumerate(heads):
        at = pl.ds(pl.multiple_of(head * head_dim, head_dim), head_dim)
        copies.append(
            pltpu.make_async_copy(
                part.at[pl.ds(start, rows)], attended_ref.at[:, at], sems.at[index]
            )
        )
        copies[index].start()
    for part, start, head in heads:
        sums_ref[head] = part[start + rows : start + height, :].astype(jnp.float32)
    for copy in copies:
        copy.wait()


def sum_kernel(place_ref, first_ref, second_ref, kept_ref, hidden_ref):
    keeps = place_ref[2] == place_ref[1]
    second = jnp.where(keeps, kept_ref[...], second_ref[...]).astype(jnp.float32)
    hidden_ref[...] = (first_ref[...].astype(jnp.float32) + second).astype(jnp.bfloat16)


def by_head(hidden, w_query, w_key, w_value, cluster_rank, assign, d_attended):
    rows = hidden.shape[0]
    count = assign.shape[0]
    chips = count // 2
    half, width = w_query.shape
    head_dim = width // count
    tokens = count * rows
    clusters = cluster_rank.shape[0]
    owned = clusters // count
    scale = head_dim ** (-0.5)
    factor = scale * log2_e
    smem = pl.BlockSpec(memory_space=pltpu.SMEM)
    vmem = pl.BlockSpec(memory_space=pltpu.VMEM)
    anywhere = pl.BlockSpec(memory_space=pl.ANY)
    params = pltpu.CompilerParams(vmem_limit_bytes=32 * mebi)
    project_params = pltpu.CompilerParams(vmem_limit_bytes=32 * mebi)
    swap = [(0, 1), (1, 0)]
    chip, side, column = (lax.axis_index(name) for name in ("seq", "sub", "head"))
    place = jnp.stack([chip, side, column, 1 - column])

    def call(kernel, outs, *operands, scratch=(), hbm=0, limits=params, outside=None, takes=1):
        return pl.pallas_call(
            kernel,
            out_shape=outs,
            in_specs=[smem] + [vmem] * (len(operands) - 1 - hbm) + [anywhere] * hbm,
            out_specs=outside or jax.tree.map(lambda _: vmem, outs),
            scratch_shapes=list(scratch),
            compiler_params=limits,
            cost_estimate=pl.CostEstimate(
                flops=int(takes * 1.15e9), bytes_accessed=mebi, transcendentals=0
            ),
        )(*operands)

    def low(*shape):
        return jax.ShapeDtypeStruct(shape, jnp.bfloat16)

    def buffers(height):
        return (low(height, head_dim),) * chips

    def exchange(parts):
        moved = {
            offset: lax.ppermute(parts[offset], "seq", [(at, at ^ offset) for at in range(chips)])
            for offset in (2, 3, 1)
        }
        return (parts[0], moved[1], moved[2], moved[3])

    def to_sibling(piece):
        return lax.ppermute(piece, "sub", swap)

    def stay(array):
        return pltpu.with_memory_space_constraint(array, pltpu.HBM)

    hidden_other = to_sibling(hidden)
    block = low(chips, rows + id_lines(rows, head_dim), head_dim)
    grads_mine, grads_theirs = call(
        pack_kernel,
        (block, block),
        place,
        stay(d_attended),
        stay(assign),
        scratch=[pltpu.VMEM(assign.shape, jnp.int32), pltpu.SemaphoreType.DMA((count + 1,))],
        hbm=2,
    )
    grads_other = to_sibling(grads_theirs)

    def project(turn, weights, tokens_other, *arrived):
        number = len(weights)
        outs = buffers(2 * number * rows) if turn == 0 else low(number, 2 * rows, width // 2)

        return call(
            partial(project_kernel, number, turn),
            outs,
            place,
            *arrived,
            stay(hidden),
            tokens_other,
            *(stay(weight) for weight in weights),
            scratch=[
                pltpu.VMEM((2 * rows, half), jnp.bfloat16),
                pltpu.VMEM((number, half, width // 2), jnp.bfloat16),
                pltpu.VMEM((2 * rows, width // 2), jnp.bfloat16),
                pltpu.SemaphoreType.DMA((number, 4)),
                pltpu.SemaphoreType.DMA((2,)),
            ],
            hbm=2 + number,
            limits=project_params,
            takes=(8 if number == 2 else 0.1) if turn == 0 else 0.1,
        )

    early, late = (w_query, w_key), (w_value,)
    fetched = call(
        partial(fetch_kernel, 1),
        pltpu.VMEM((2, half, width // 2), jnp.bfloat16),
        place,
        *(stay(weight) for weight in early),
        scratch=[pltpu.SemaphoreType.DMA((2, 4))],
        hbm=2,
    )
    *merged, early_part = call(
        opening_kernel,
        (*buffers(2 * block.shape[1]), low(2, 2 * rows, width // 2)),
        place,
        fetched,
        grads_mine,
        grads_other,
        stay(hidden),
        hidden_other,
        scratch=[pltpu.VMEM((2 * rows, half), jnp.bfloat16), pltpu.SemaphoreType.DMA((2,))],
        hbm=2,
        takes=0.1,
    )
    grads = exchange(merged)
    early_arrived = to_sibling(early_part)
    early_projected = project(0, early, hidden_other, early_arrived)
    packed = exchange(early_projected)
    late_tokens, *_ = lax.optimization_barrier((hidden_other, early_arrived))
    late_arrived = to_sibling(project(1, late, late_tokens))
    late_arrived, *_ = lax.optimization_barrier((late_arrived, grads[2], grads[3]))
    late_projected = project(0, late, late_tokens, late_arrived)
    valued = exchange(late_projected)
    packed = lax.optimization_barrier((*packed, late_projected[0]))[:chips]

    def held(kind):
        return pltpu.VMEM((tokens, head_dim), kind)

    id_scratch = [pltpu.VMEM((count, 8, rows), jnp.float32), held(jnp.float32)]
    *value_grads, probs, sums = call(
        partial(value_grad_kernel, factor, chips, rows),
        (
            *buffers(2 * rows),
            pltpu.VMEM((count * (count + 1) // 2 * rows, rows), jnp.bfloat16),
            low(clusters, head_dim),
        ),
        place,
        *packed,
        *grads,
        cluster_rank.reshape(1, clusters),
        scratch=[held(jnp.bfloat16)] * 3 + id_scratch + [held(jnp.float32)],
        takes=7,
    )
    value_back = exchange(value_grads)
    results = call(
        partial(query_grad_kernel, scale, chips, rows),
        (*buffers(4 * rows), *(low(chips, rows + owned, head_dim),) * 2),
        place,
        *packed,
        *valued,
        *grads,
        probs,
        sums,
        scratch=[held(jnp.bfloat16)] * 4
        + [held(jnp.float32)]
        + [held(jnp.bfloat16)] * 2,
        takes=10,
    )
    *ready, _ = lax.optimization_barrier((*results[:chips], value_back[2]))
    back = exchange(ready)

    attended_mine, attended_theirs = results[chips:]
    outputs = call(
        merge_kernel, buffers(2 * (rows + owned)), place, attended_mine, to_sibling(attended_theirs)
    )
    back = (lax.optimization_barrier((back[0], outputs[0]))[0], *back[1:])
    back_other = tuple(to_sibling(part) for part in back)
    value_other = to_sibling(
        call(join_kernel, low(chips, 2 * rows, head_dim), place, *value_back)
    )

    def input_part(which, place):
        return call(
            partial(input_kernel, chips, which),
            low(rows, half),
            place,
            *back,
            *back_other,
            *value_back,
            value_other,
            w_query,
            w_key,
            w_value,
            scratch=[pltpu.VMEM((rows, 3 * width), jnp.bfloat16)],
        )

    *outputs, _, _ = lax.optimization_barrier((*outputs, back[2], back[3]))
    returned = exchange(outputs)
    square = ("head", "sub")
    crossing = input_part(3, place)
    first = lax.ppermute(crossing, square, [(0, 1), (1, 3), (3, 2), (2, 0)])
    kept = input_part(2, lax.optimization_barrier((place, crossing))[0])
    second = lax.ppermute(kept, square, [(1, 2), (2, 1)])
    attended, centroid_sums = call(
        partial(attended_kernel, chips),
        (low(rows, width), jax.ShapeDtypeStruct((count, owned, head_dim), jnp.float32)),
        place,
        *returned,
        scratch=[pltpu.SemaphoreType.DMA((count,))],
        outside=(anywhere, vmem),
        takes=8,
    )
    first, second, _ = lax.optimization_barrier((first, second, attended))
    d_hidden = call(sum_kernel, low(rows, half), place, first, second, kept)
    return (attended, d_hidden, centroid_sums)


def per_device(hidden, w_query, w_key, w_value, cluster_rank, assign, d_attended):
    chips = lax.axis_size("seq")
    fits = chips == 4 and lax.axis_size("sub") == 2 and lax.axis_size("head") == 2
    plan = by_head if fits and assign.shape[0] == 2 * chips else by_owner
    return plan(hidden, w_query, w_key, w_value, cluster_rank, assign, d_attended)


def solution(mesh):
    placed = (
        P(("groups", "seq", "sub"), None),
        P("sub", "head"),
        P("sub", "head"),
        P("sub", "head"),
        P("groups"),
        P("head", ("groups", "seq", "sub")),
        P(("groups", "seq", "sub"), "head"),
    )
    return jax.shard_map(
        per_device,
        mesh=mesh,
        in_specs=placed,
        out_specs=(
            P(("groups", "seq", "sub"), "head"),
            P(("groups", "seq", "sub"), "head"),
            P("head", ("groups", "seq", "sub"), None),
        ),
        check_vma=False,
    )
```

```python
from functools import partial

import jax
import jax.numpy as jnp
from jax import lax
from jax.experimental import pallas as pl
from jax.experimental.pallas import tpu as pltpu
from jax.sharding import PartitionSpec as P

epsilon = 1e-06


def keep_mask(filled, cluster_ids, positions):
    count = filled.shape[0]
    same = filled[:, None] & filled[None, :] & (cluster_ids[:, None] == cluster_ids[None, :])
    causal = positions[None, :] <= positions[:, None]
    diagonal = jnp.arange(count)[:, None] == jnp.arange(count)[None, :]
    return same & causal | diagonal


def head_forward(packed, scale):
    queries, keys_in, values, filled, cluster_ids, positions = packed
    scores = (
        lax.dot_general(
            queries, keys_in, (((1,), (1,)), ((), ())), preferred_element_type=jnp.float32
        )
        * scale
    )
    allowed = keep_mask(filled, cluster_ids, positions)
    row_top = jnp.max(jnp.where(allowed, scores, -jnp.inf), axis=1)
    expd = jnp.where(allowed, jnp.exp(scores - row_top[:, None]), 0.0)
    row_total = jnp.sum(expd, axis=1)
    probs_low = (expd / row_total[:, None]).astype(jnp.bfloat16)
    outputs = jnp.dot(probs_low, values, preferred_element_type=jnp.float32).astype(jnp.bfloat16)
    return (outputs, row_top, row_total)


def head_backward(packed, scale):
    queries, keys_in, values, grads_in, filled, cluster_ids, positions, row_top, row_total = packed
    contract_last = (((1,), (1,)), ((), ()))
    contract_first = (((0,), (0,)), ((), ()))
    scores = (
        lax.dot_general(queries, keys_in, contract_last, preferred_element_type=jnp.float32) * scale
    )
    allowed = keep_mask(filled, cluster_ids, positions)
    probs = jnp.where(allowed, jnp.exp(scores - row_top[:, None]), 0.0) / row_total[:, None]
    probs_low = probs.astype(jnp.bfloat16)
    grad_probs = lax.dot_general(
        grads_in, values, contract_last, preferred_element_type=jnp.float32
    )
    delta_rows = jnp.sum(probs * grad_probs, axis=1)
    grad_low = (probs * (grad_probs - delta_rows[:, None]) * scale).astype(jnp.bfloat16)
    grad_query = jnp.dot(grad_low, keys_in, preferred_element_type=jnp.float32).astype(jnp.bfloat16)
    grad_key = lax.dot_general(
        grad_low, queries, contract_first, preferred_element_type=jnp.float32
    ).astype(jnp.bfloat16)
    grad_value = lax.dot_general(
        probs_low, grads_in, contract_first, preferred_element_type=jnp.float32
    ).astype(jnp.bfloat16)
    return (grad_query, grad_key, grad_value)


def by_owner(hidden, w_query, w_key, w_value, cluster_rank, assign, d_attended):
    tok_rows = hidden.shape[0]
    heads_here = assign.shape[0]
    head_dim = w_query.shape[1] // heads_here
    clusters = cluster_rank.shape[0]
    seq_count = lax.axis_size("seq")
    sub_count = lax.axis_size("sub")
    owners = seq_count * sub_count
    capacity = 2 * tok_rows // owners
    slot_count = owners * capacity
    per_owner = clusters // owners
    scale = head_dim ** (-0.5)
    pieces = (
        lax.all_gather(w_query, "sub", axis=0, tiled=True),
        lax.all_gather(w_key, "sub", axis=0, tiled=True),
        lax.all_gather(w_value, "sub", axis=0, tiled=True),
    )
    projected = tuple(
        (
            jnp.dot(hidden, weight_piece, preferred_element_type=jnp.float32)
            for weight_piece in pieces
        )
    )

    def split_heads(matrix):
        return (
            matrix.astype(jnp.bfloat16).reshape(tok_rows, heads_here, head_dim).transpose(1, 0, 2)
        )

    queries, keys_all, values = tuple((split_heads(matrix) for matrix in projected))
    cluster_range = jnp.arange(clusters, dtype=jnp.int32)
    rank_tok = jnp.sum(jnp.where(assign[:, :, None] == cluster_range, cluster_rank, 0), axis=2)
    owner_ids = rank_tok // per_owner
    owner_hot = (owner_ids[:, :, None] == jnp.arange(owners, dtype=jnp.int32)).astype(jnp.int32)
    within = jnp.sum(owner_hot * (jnp.cumsum(owner_hot, axis=1) - 1), axis=2)
    slot_tok = owner_ids * capacity + within
    token_ids = jnp.arange(tok_rows, dtype=jnp.int32)
    slot_range = jnp.arange(slot_count, dtype=jnp.int32)
    slot_match = slot_tok[:, None, :] == slot_range[None, :, None]
    slot_hot = slot_match.astype(jnp.bfloat16)

    def to_slots(rows_in):
        kept = jnp.einsum(
            "hst,htd->hsd", slot_hot, rows_in, preferred_element_type=jnp.float32
        ).astype(jnp.bfloat16)
        return kept.reshape(heads_here, owners, capacity, head_dim)

    def from_slots(slotted):
        flat_slots = slotted.reshape(heads_here, slot_count, head_dim)
        return jnp.einsum(
            "hst,hsd->htd", slot_hot, flat_slots, preferred_element_type=jnp.float32
        ).astype(jnp.bfloat16)

    def exchange_three(first, second, third):
        return (
            lax.all_to_all(first, ("seq", "sub"), split_axis=1, concat_axis=1, tiled=True),
            lax.all_to_all(second, ("seq", "sub"), split_axis=1, concat_axis=1, tiled=True),
            lax.all_to_all(third, ("seq", "sub"), split_axis=1, concat_axis=1, tiled=True),
        )

    sent = exchange_three(to_slots(queries), to_slots(keys_all), to_slots(values))
    tag_tok = assign * tok_rows + token_ids
    slot_tag = jnp.sum(jnp.where(slot_match, tag_tok[:, None, :] + 1, 0), axis=2) - 1
    tags = lax.all_to_all(
        slot_tag.reshape(heads_here, owners, capacity),
        ("seq", "sub"),
        split_axis=1,
        concat_axis=1,
        tiled=True,
    )
    tags = tags.reshape(heads_here, slot_count)
    owner_q, owner_k, owner_v = tuple(
        (member.reshape(heads_here, slot_count, head_dim) for member in sent)
    )
    filled = tags >= 0
    cluster_ids = jnp.where(filled, tags // tok_rows, -1)
    positions = slot_range // capacity * tok_rows + tags % tok_rows
    outputs, row_top, row_total = lax.map(
        partial(head_forward, scale=scale),
        (owner_q, owner_k, owner_v, filled, cluster_ids, positions),
    )
    returned = lax.all_to_all(
        outputs.reshape(heads_here, owners, capacity, head_dim),
        ("seq", "sub"),
        split_axis=1,
        concat_axis=1,
        tiled=True,
    )

    def merge_heads(slotted):
        return from_slots(slotted).transpose(1, 0, 2).reshape(tok_rows, heads_here * head_dim)

    attended = merge_heads(returned)
    grads_tok = d_attended.reshape(tok_rows, heads_here, head_dim).transpose(1, 0, 2)
    owner_g = lax.all_to_all(
        to_slots(grads_tok), ("seq", "sub"), split_axis=1, concat_axis=1, tiled=True
    ).reshape(heads_here, slot_count, head_dim)
    grad_q, grad_k, grad_v = lax.map(
        partial(head_backward, scale=scale),
        (owner_q, owner_k, owner_v, owner_g, filled, cluster_ids, positions, row_top, row_total),
    )
    shape_four = (heads_here, owners, capacity, head_dim)
    back = exchange_three(
        grad_q.reshape(shape_four), grad_k.reshape(shape_four), grad_v.reshape(shape_four)
    )
    token_grads = tuple((merge_heads(member) for member in back))
    pieces = lax.all_gather((w_query, w_key, w_value), "sub", axis=0, tiled=True)
    terms = [
        jnp.einsum("tc,rc->tr", grad_rows_in, weight_piece, preferred_element_type=jnp.float32)
        for grad_rows_in, weight_piece in zip(token_grads, pieces)
    ]
    partial_grad = terms[0] + terms[1] + terms[2]
    d_hidden = lax.psum_scatter(
        partial_grad.astype(jnp.bfloat16), "head", scatter_dimension=1, tiled=True
    )
    keys_float = keys_all.astype(jnp.float32)
    unit_keys = keys_float * lax.rsqrt(
        jnp.sum(keys_float * keys_float, axis=2, keepdims=True) + epsilon
    )
    member_hot = (rank_tok[:, :, None] == cluster_range).astype(jnp.float32)
    local_sums = jnp.einsum("htr,htd->hrd", member_hot, unit_keys, precision=lax.Precision.HIGHEST)
    centroid_sums = lax.psum_scatter(
        local_sums.astype(jnp.bfloat16), ("seq", "sub"), scatter_dimension=1, tiled=True
    ).astype(jnp.float32)
    return (attended, d_hidden, centroid_sums)


contract_last = (((1,), (1,)), ((), ()))
contract_first = (((0,), (0,)), ((), ()))
log2_e = 1.4426950408889634
mebi = 1024 * 1024


def id_lines(rows, head_dim):
    return -(-(rows // head_dim) // 16) * 16


def pack_kernel(place_ref, grads_ref, assign_ref, mine_ref, theirs_ref, ids_ref, sems):
    chips, padded, head_dim = mine_ref.shape
    rows = grads_ref.shape[0]
    spare = padded - rows - rows // head_dim
    copies = [pltpu.make_async_copy(assign_ref, ids_ref, sems.at[2 * chips])]
    for turn, out_ref in enumerate((mine_ref, theirs_ref)):
        for chip in range(chips):
            head = (place_ref[1] ^ turn) * chips + chip
            at = pl.multiple_of(head * head_dim, head_dim)
            copies.append(
                pltpu.make_async_copy(
                    grads_ref.at[:, pl.ds(at, head_dim)],
                    out_ref.at[chip, pl.ds(0, rows)],
                    sems.at[turn * chips + chip],
                )
            )
    for copy in copies:
        copy.start()
    copies[0].wait()
    for turn, out_ref in enumerate((mine_ref, theirs_ref)):
        for chip in range(chips):
            head = (place_ref[1] ^ turn) * chips + chip
            ids = ids_ref[pl.ds(head, 1), :].astype(jnp.float32)
            lines = [
                ids[:, start : start + head_dim] for start in range(0, rows, head_dim)
            ] + [jnp.zeros((spare, head_dim), jnp.float32)]
            out_ref[chip, rows:, :] = jnp.concatenate(lines, axis=0).astype(jnp.bfloat16)
    for copy in copies[1:]:
        copy.wait()


def merge_kernel(place_ref, mine_ref, theirs_ref, *out_refs):
    height = mine_ref.shape[1]
    for turn, held_ref in enumerate((mine_ref, theirs_ref)):
        at = pl.ds(pl.multiple_of((place_ref[1] ^ turn) * height, height), height)
        for offset, out_ref in enumerate(out_refs):
            out_ref[at, :] = held_ref[place_ref[0] ^ offset]


def fetch_columns(half, weights, held_ref, sems):
    chunks = sems.shape[1]
    columns = held_ref.shape[2]
    rows = held_ref.shape[1] // chunks
    at = pl.ds(pl.multiple_of(half * columns, columns), columns)
    copies = []
    for index, weight in enumerate(weights):
        for chunk in range(chunks):
            lines = pl.ds(chunk * rows, rows)
            copy = pltpu.make_async_copy(
                weight.at[lines, at], held_ref.at[index, lines], sems.at[index, chunk]
            )
            copy.start()
            copies.append(copy)
    return copies


def project_kernel(count, turn, place_ref, *refs):
    if turn == 0:
        arrived_ref, refs = refs[0], refs[1:]
    tokens, weights, refs = refs[:2], refs[2 : 2 + count], refs[2 + count :]
    out_refs, (joined_ref, held_ref, low_ref, sems, token_sems) = refs[:-5], refs[-5:]
    side = place_ref[1]
    tall, depth = joined_ref.shape
    rows = tall // 2
    near = pl.ds(pl.multiple_of(side * depth, depth), depth)
    joins = []
    for core, source in enumerate(tokens):
        at = pl.ds(pl.multiple_of((side ^ core) * rows, rows), rows)
        joins.append(
            pltpu.make_async_copy(source.at[:, near], joined_ref.at[at], token_sems.at[core])
        )
        joins[core].start()
    copies = fetch_columns(side ^ turn, weights, held_ref, sems)
    for copy in joins:
        copy.wait()
    chunks = sems.shape[1]
    for index in range(count):
        for chunk in range(chunks):
            copies[index * chunks + chunk].wait()
        total = jnp.dot(joined_ref[...], held_ref[index], preferred_element_type=jnp.float32)
        if turn == 1:
            out_refs[0][index] = total.astype(jnp.bfloat16)
            continue
        low_ref[...] = (total + arrived_ref[index].astype(jnp.float32)).astype(jnp.bfloat16)
        for offset, out_ref in enumerate(out_refs):
            head_dim = out_ref.shape[1]
            at = pl.multiple_of((place_ref[0] ^ offset) * head_dim, head_dim)
            out_ref[index * tall : (index + 1) * tall, :] = low_ref[:, pl.ds(at, head_dim)]


def fetch_kernel(turn, place_ref, *refs):
    weights, (held_ref, sems) = refs[:-2], refs[-2:]
    for copy in fetch_columns(place_ref[1] ^ turn, weights, held_ref, sems):
        copy.wait()


def opening_kernel(place_ref, held_ref, mine_ref, theirs_ref, *refs):
    tokens, refs = refs[:2], refs[2:]
    out_refs, (part_ref, joined_ref, sems) = refs[:-3], refs[-3:]
    side = place_ref[1]
    tall, depth = joined_ref.shape
    rows = tall // 2
    near = pl.ds(pl.multiple_of(side * depth, depth), depth)
    joins = []
    for core, source in enumerate(tokens):
        at = pl.ds(pl.multiple_of((side ^ core) * rows, rows), rows)
        joins.append(pltpu.make_async_copy(source.at[:, near], joined_ref.at[at], sems.at[core]))
        joins[core].start()
    merge_kernel(place_ref, mine_ref, theirs_ref, *out_refs)
    for copy in joins:
        copy.wait()
    for index in range(held_ref.shape[0]):
        total = jnp.dot(joined_ref[...], held_ref[index], preferred_element_type=jnp.float32)
        part_ref[index] = total.astype(jnp.bfloat16)


def in_order(place, parts, start, ordered):
    for offset, part in enumerate(parts):
        tall = ordered.shape[0] // len(parts)
        at = pl.ds(pl.multiple_of((place ^ offset) * tall, tall), tall)
        ordered[at, :] = part[start : start + tall, :]


def order_grads(place, parts, rows, grad_rows, id_rows, id_cols):
    head_dim = grad_rows.shape[1]
    height = parts[0].shape[0] // 2
    for offset, part in enumerate(parts):
        for core in range(2):
            block = (place ^ offset) * 2 + core
            at = pl.ds(pl.multiple_of(block * rows, rows), rows)
            start = core * height
            grad_rows[at, :] = part[start : start + rows, :]
            lines = part[start + rows : start + rows + 16, :].astype(jnp.float32)
            ids = jnp.concatenate(
                [lines[line : line + 1, :] for line in range(rows // head_dim)], axis=1
            )
            id_rows[block] = jnp.broadcast_to(ids, id_rows.shape[1:])
            id_cols[at, :] = jnp.broadcast_to(ids, (head_dim, rows)).T


def order_rows(place, parts, rows, ordered):
    height = parts[0].shape[0] // 2
    for offset, part in enumerate(parts):
        for core in range(2):
            at = pl.ds(pl.multiple_of(((place ^ offset) * 2 + core) * rows, rows), rows)
            ordered[at, :] = part[core * height : core * height + rows, :]


def block_scores(factor, block, rows, queries, keys_in, id_rows, id_cols):
    head_dim = queries.shape[1]
    seen = (block + 1) * rows
    scores = lax.dot_general(
        keys_in[:seen, :],
        queries[block * rows : seen, :],
        contract_last,
        preferred_element_type=jnp.float32,
    )
    ids = id_cols[:seen, :]
    mine = id_rows[block][:1, :]
    same = jnp.concatenate(
        [ids == mine[:, start : start + head_dim] for start in range(0, rows, head_dim)], axis=1
    )
    key_at = lax.broadcasted_iota(jnp.int32, (rows, rows), 0)
    query_at = lax.broadcasted_iota(jnp.int32, (rows, rows), 1)
    last = same[seen - rows :] & (key_at <= query_at)
    allowed = last if block == 0 else jnp.concatenate([same[: seen - rows], last], axis=0)
    return jnp.where(allowed, scores * factor, -jnp.inf)


def value_grad_kernel(factor, chips, rows, place_ref, *refs):
    packed, grads, rank_ref = refs[:chips], refs[chips : 2 * chips], refs[2 * chips]
    refs = refs[2 * chips + 1 :]
    out_refs, probs_ref, sums_ref = refs[:chips], refs[chips], refs[chips + 1]
    queries, keys_in, grad_rows, id_rows, id_cols, total_ref = refs[chips + 2 :]
    head_dim = queries.shape[1]
    clusters = rank_ref.shape[1]
    tall = 2 * rows
    place = place_ref[0]
    in_order(place, packed, 0, queries)
    in_order(place, packed, tall, keys_in)
    order_grads(place, grads, rows, grad_rows, id_rows, id_cols)
    total_ref[...] = jnp.zeros_like(total_ref)
    stored = 0
    for block in range(2 * chips):
        seen = (block + 1) * rows
        scores = block_scores(factor, block, rows, queries, keys_in, id_rows, id_cols)
        top = jnp.max(scores, axis=0, keepdims=True)
        expd = jnp.exp2(scores - top)
        total = jnp.sum(expd, axis=0, keepdims=True)
        probs_low = (expd * (1.0 / total)).astype(jnp.bfloat16)
        probs_ref[stored : stored + seen, :] = probs_low
        stored += seen
        total_ref[:seen, :] += jnp.dot(
            probs_low, grad_rows[block * rows : seen, :], preferred_element_type=jnp.float32
        )
    for offset, out_ref in enumerate(out_refs):
        at = pl.multiple_of((place ^ offset) * tall, tall)
        out_ref[...] = total_ref[pl.ds(at, tall), :].astype(jnp.bfloat16)
    sums = jnp.zeros((clusters, head_dim), jnp.float32)
    cluster_at = lax.broadcasted_iota(jnp.int32, (clusters, rows), 0).astype(jnp.float32)
    for block in range(2 * chips):
        keys_float = keys_in[block * rows : (block + 1) * rows, :].astype(jnp.float32)
        unit = keys_float * lax.rsqrt(
            jnp.sum(keys_float * keys_float, axis=1, keepdims=True) + epsilon
        )
        unit_high = unit.astype(jnp.bfloat16)
        unit_low = (unit - unit_high.astype(jnp.float32)).astype(jnp.bfloat16)
        member = jnp.where(cluster_at == id_rows[block][:1, :], 1.0, 0.0).astype(jnp.bfloat16)
        sums += jnp.dot(member, unit_high, preferred_element_type=jnp.float32)
        sums += jnp.dot(member, unit_low, preferred_element_type=jnp.float32)
    rank_at = lax.broadcasted_iota(jnp.int32, (clusters, clusters), 0)
    ordered = jnp.where(rank_at == rank_ref[...], 1.0, 0.0).astype(jnp.bfloat16)
    ranked = jnp.dot(ordered, sums.astype(jnp.bfloat16), preferred_element_type=jnp.float32)
    sums_ref[...] = ranked.astype(jnp.bfloat16)


def query_grad_kernel(scale, chips, rows, place_ref, *refs):
    packed, valued, grads = refs[:chips], refs[chips : 2 * chips], refs[2 * chips : 3 * chips]
    probs_ref, sums_ref = refs[3 * chips : 3 * chips + 2]
    refs = refs[3 * chips + 2 :]
    grad_refs, out_refs, refs = refs[:chips], refs[chips : chips + 2], refs[chips + 2 :]
    queries, keys_in, values, grad_rows, total_ref, dq_ref, attended_ref = refs
    tall = 2 * rows
    place = place_ref[0]
    in_order(place, packed, 0, queries)
    in_order(place, packed, tall, keys_in)
    in_order(place, valued, 0, values)
    order_rows(place, grads, rows, grad_rows)
    total_ref[...] = jnp.zeros_like(total_ref)
    stored = 0
    for block in range(2 * chips):
        seen = (block + 1) * rows
        mine = slice(block * rows, seen)
        probs_low = probs_ref[stored : stored + seen, :]
        stored += seen
        seen_values = values[:seen, :]
        grad_probs = lax.dot_general(
            seen_values, grad_rows[mine, :], contract_last, preferred_element_type=jnp.float32
        )
        flipped = lax.dot_general(
            seen_values, probs_low, contract_first, preferred_element_type=jnp.float32
        )
        attended_ref[mine, :] = flipped.T.astype(jnp.bfloat16)
        probs = probs_low.astype(jnp.float32)
        weighted = probs * grad_probs
        delta = jnp.sum(weighted, axis=0, keepdims=True)
        grad_low = (weighted - probs * delta).astype(jnp.bfloat16)
        total_ref[:seen, :] += jnp.dot(
            grad_low, queries[mine, :], preferred_element_type=jnp.float32
        )
        flipped = lax.dot_general(
            keys_in[:seen, :], grad_low, contract_first, preferred_element_type=jnp.float32
        )
        dq_ref[mine, :] = (flipped.T * scale).astype(jnp.bfloat16)
    for offset in range(chips):
        at = pl.ds(pl.multiple_of((place ^ offset) * tall, tall), tall)
        grad_refs[offset][:tall, :] = dq_ref[at, :]
        grad_refs[offset][tall:, :] = (total_ref[at, :] * scale).astype(jnp.bfloat16)
    owned = sums_ref.shape[0] // (2 * chips)
    for turn, out_ref in enumerate(out_refs):
        for chip in range(chips):
            shard = chip * 2 + (place_ref[1] ^ turn)
            at = pl.ds(pl.multiple_of(shard * rows, rows), rows)
            out_ref[chip, :rows, :] = attended_ref[at, :]
            at = pl.ds(pl.multiple_of(shard * owned, owned), owned)
            out_ref[chip, rows:, :] = sums_ref[at, :]


def join_kernel(*refs):
    parts, out_ref = refs[1:-1], refs[-1]
    for offset, part in enumerate(parts):
        out_ref[offset] = part[...]


def input_kernel(chips, which, place_ref, *refs):
    valued_other_ref, refs = refs[3 * chips], refs[: 3 * chips] + refs[3 * chips + 1 :]
    weights, (out_ref, gathered_ref) = refs[3 * chips : -2], refs[-2:]
    rows, width = out_ref.shape[0], weights[0].shape[1]
    head_dim = width // (2 * chips)
    for turn in range(2):
        parts = refs[turn * chips : (turn + 1) * chips]
        valued = refs[2 * chips : 3 * chips]
        for offset in range(chips):
            head = (place_ref[1] ^ turn) * chips + (place_ref[0] ^ offset)
            for index in range(3):
                source = parts[offset] if index < 2 else valued[offset]
                if index == 2 and turn == 1:
                    source = valued_other_ref.at[offset]
                at = pl.multiple_of((2 * (index % 2) + place_ref[which]) * rows, rows)
                start = pl.multiple_of(index * width + head * head_dim, head_dim)
                gathered_ref[:, pl.ds(start, head_dim)] = source[pl.ds(at, rows), :]
    flipped = None
    for index in range(3):
        term = lax.dot_general(
            weights[index][...],
            gathered_ref[:, index * width : (index + 1) * width],
            contract_last,
            preferred_element_type=jnp.float32,
        )
        flipped = term if flipped is None else flipped + term
    out_ref[...] = flipped.T.astype(out_ref.dtype)


def attended_kernel(chips, place_ref, *refs):
    parts, (attended_ref, sums_ref) = refs[:chips], refs[chips:]
    rows = attended_ref.shape[0]
    head_dim = sums_ref.shape[2]
    height = parts[0].shape[0] // 2
    for core in range(2):
        start = core * height
        for offset, part in enumerate(parts):
            head = core * chips + (place_ref[0] ^ offset)
            at = pl.multiple_of(head * head_dim, head_dim)
            attended_ref[:, pl.ds(at, head_dim)] = part[start : start + rows, :]
            sums_ref[head] = part[start + rows : start + height, :].astype(jnp.float32)


def sum_kernel(place_ref, first_ref, second_ref, kept_ref, hidden_ref):
    keeps = place_ref[2] == place_ref[1]
    second = jnp.where(keeps, kept_ref[...], second_ref[...]).astype(jnp.float32)
    hidden_ref[...] = (first_ref[...].astype(jnp.float32) + second).astype(jnp.bfloat16)


def by_head(hidden, w_query, w_key, w_value, cluster_rank, assign, d_attended):
    rows = hidden.shape[0]
    count = assign.shape[0]
    chips = count // 2
    half, width = w_query.shape
    head_dim = width // count
    tokens = count * rows
    clusters = cluster_rank.shape[0]
    owned = clusters // count
    scale = head_dim ** (-0.5)
    factor = scale * log2_e
    smem = pl.BlockSpec(memory_space=pltpu.SMEM)
    vmem = pl.BlockSpec(memory_space=pltpu.VMEM)
    anywhere = pl.BlockSpec(memory_space=pl.ANY)
    params = pltpu.CompilerParams(vmem_limit_bytes=32 * mebi)
    project_params = pltpu.CompilerParams(vmem_limit_bytes=32 * mebi)
    swap = [(0, 1), (1, 0)]
    chip, side, column = (lax.axis_index(name) for name in ("seq", "sub", "head"))
    place = jnp.stack([chip, side, column, 1 - column])

    def call(kernel, outs, *operands, scratch=(), hbm=0, limits=params, takes=1):
        return pl.pallas_call(
            kernel,
            out_shape=outs,
            in_specs=[smem] + [vmem] * (len(operands) - 1 - hbm) + [anywhere] * hbm,
            out_specs=jax.tree.map(lambda _: vmem, outs),
            scratch_shapes=list(scratch),
            compiler_params=limits,
            cost_estimate=pl.CostEstimate(
                flops=int(takes * 1.15e9), bytes_accessed=mebi, transcendentals=0
            ),
        )(*operands)

    def low(*shape):
        return jax.ShapeDtypeStruct(shape, jnp.bfloat16)

    def buffers(height):
        return (low(height, head_dim),) * chips

    def exchange(parts):
        moved = {
            offset: lax.ppermute(parts[offset], "seq", [(at, at ^ offset) for at in range(chips)])
            for offset in (2, 3, 1)
        }
        return (parts[0], moved[1], moved[2], moved[3])

    def to_sibling(piece):
        return lax.ppermute(piece, "sub", swap)

    def stay(array):
        return pltpu.with_memory_space_constraint(array, pltpu.HBM)

    hidden_other = to_sibling(hidden)
    block = low(chips, rows + id_lines(rows, head_dim), head_dim)
    grads_mine, grads_theirs = call(
        pack_kernel,
        (block, block),
        place,
        stay(d_attended),
        stay(assign),
        scratch=[pltpu.VMEM(assign.shape, jnp.int32), pltpu.SemaphoreType.DMA((count + 1,))],
        hbm=2,
    )
    grads_other = to_sibling(grads_theirs)

    def project(turn, weights, tokens_other, *arrived):
        number = len(weights)
        outs = buffers(2 * number * rows) if turn == 0 else low(number, 2 * rows, width // 2)

        return call(
            partial(project_kernel, number, turn),
            outs,
            place,
            *arrived,
            stay(hidden),
            tokens_other,
            *(stay(weight) for weight in weights),
            scratch=[
                pltpu.VMEM((2 * rows, half), jnp.bfloat16),
                pltpu.VMEM((number, half, width // 2), jnp.bfloat16),
                pltpu.VMEM((2 * rows, width // 2), jnp.bfloat16),
                pltpu.SemaphoreType.DMA((number, 4)),
                pltpu.SemaphoreType.DMA((2,)),
            ],
            hbm=2 + number,
            limits=project_params,
            takes=(8 if number == 2 else 0.1) if turn == 0 else 0.1,
        )

    early, late = (w_query, w_key), (w_value,)
    fetched = call(
        partial(fetch_kernel, 1),
        pltpu.VMEM((2, half, width // 2), jnp.bfloat16),
        place,
        *(stay(weight) for weight in early),
        scratch=[pltpu.SemaphoreType.DMA((2, 4))],
        hbm=2,
    )
    *merged, early_part = call(
        opening_kernel,
        (*buffers(2 * block.shape[1]), low(2, 2 * rows, width // 2)),
        place,
        fetched,
        grads_mine,
        grads_other,
        stay(hidden),
        hidden_other,
        scratch=[pltpu.VMEM((2 * rows, half), jnp.bfloat16), pltpu.SemaphoreType.DMA((2,))],
        hbm=2,
        takes=0.1,
    )
    grads = exchange(merged)
    early_arrived = to_sibling(early_part)
    early_projected = project(0, early, hidden_other, early_arrived)
    packed = exchange(early_projected)
    late_tokens, *_ = lax.optimization_barrier((hidden_other, early_arrived))
    late_arrived = to_sibling(project(1, late, late_tokens))
    late_arrived, *_ = lax.optimization_barrier((late_arrived, grads[2], grads[3]))
    late_projected = project(0, late, late_tokens, late_arrived)
    valued = exchange(late_projected)
    packed = lax.optimization_barrier((*packed, late_projected[0]))[:chips]

    def held(kind):
        return pltpu.VMEM((tokens, head_dim), kind)

    id_scratch = [pltpu.VMEM((count, 8, rows), jnp.float32), held(jnp.float32)]
    *value_grads, probs, sums = call(
        partial(value_grad_kernel, factor, chips, rows),
        (
            *buffers(2 * rows),
            pltpu.VMEM((count * (count + 1) // 2 * rows, rows), jnp.bfloat16),
            low(clusters, head_dim),
        ),
        place,
        *packed,
        *grads,
        cluster_rank.reshape(1, clusters),
        scratch=[held(jnp.bfloat16)] * 3 + id_scratch + [held(jnp.float32)],
        takes=7,
    )
    value_back = exchange(value_grads)
    results = call(
        partial(query_grad_kernel, scale, chips, rows),
        (*buffers(4 * rows), *(low(chips, rows + owned, head_dim),) * 2),
        place,
        *packed,
        *valued,
        *grads,
        probs,
        sums,
        scratch=[held(jnp.bfloat16)] * 4
        + [held(jnp.float32)]
        + [held(jnp.bfloat16)] * 2,
        takes=10,
    )
    *ready, _ = lax.optimization_barrier((*results[:chips], value_back[2]))
    back = exchange(ready)

    attended_mine, attended_theirs = results[chips:]
    outputs = call(
        merge_kernel, buffers(2 * (rows + owned)), place, attended_mine, to_sibling(attended_theirs)
    )
    early_back, _ = lax.optimization_barrier((back[2], outputs[0]))
    back_other = tuple(
        to_sibling(early_back if offset == 2 else part) for offset, part in enumerate(back)
    )
    value_other = to_sibling(
        call(join_kernel, low(chips, 2 * rows, head_dim), place, *value_back)
    )

    def input_part(which, place):
        return call(
            partial(input_kernel, chips, which),
            low(rows, half),
            place,
            *back,
            *back_other,
            *value_back,
            value_other,
            w_query,
            w_key,
            w_value,
            scratch=[pltpu.VMEM((rows, 3 * width), jnp.bfloat16)],
        )

    *outputs, _, _ = lax.optimization_barrier((*outputs, back[2], back[3]))
    returned = exchange(outputs)
    square = ("head", "sub")
    crossing = input_part(3, place)
    first = lax.ppermute(crossing, square, [(0, 1), (1, 3), (3, 2), (2, 0)])
    kept = input_part(2, lax.optimization_barrier((place, crossing))[0])
    second = lax.ppermute(kept, square, [(1, 2), (2, 1)])
    attended, centroid_sums = call(
        partial(attended_kernel, chips),
        (low(rows, width), jax.ShapeDtypeStruct((count, owned, head_dim), jnp.float32)),
        place,
        *returned,
        takes=8,
    )
    first, second, _ = lax.optimization_barrier((first, second, attended))
    d_hidden = call(sum_kernel, low(rows, half), place, first, second, kept)
    return (attended, d_hidden, centroid_sums)


def per_device(hidden, w_query, w_key, w_value, cluster_rank, assign, d_attended):
    chips = lax.axis_size("seq")
    fits = chips == 4 and lax.axis_size("sub") == 2 and lax.axis_size("head") == 2
    plan = by_head if fits and assign.shape[0] == 2 * chips else by_owner
    return plan(hidden, w_query, w_key, w_value, cluster_rank, assign, d_attended)


def solution(mesh):
    placed = (
        P(("groups", "seq", "sub"), None),
        P("sub", "head"),
        P("sub", "head"),
        P("sub", "head"),
        P("groups"),
        P("head", ("groups", "seq", "sub")),
        P(("groups", "seq", "sub"), "head"),
    )
    return jax.shard_map(
        per_device,
        mesh=mesh,
        in_specs=placed,
        out_specs=(
            P(("groups", "seq", "sub"), "head"),
            P(("groups", "seq", "sub"), "head"),
            P("head", ("groups", "seq", "sub"), None),
        ),
        check_vma=False,
    )
```

```python
from functools import partial

import jax
import jax.numpy as jnp
from jax import lax
from jax.experimental import pallas as pl
from jax.experimental.pallas import tpu as pltpu
from jax.sharding import PartitionSpec as P

epsilon = 1e-06


def keep_mask(filled, cluster_ids, positions):
    count = filled.shape[0]
    same = filled[:, None] & filled[None, :] & (cluster_ids[:, None] == cluster_ids[None, :])
    causal = positions[None, :] <= positions[:, None]
    diagonal = jnp.arange(count)[:, None] == jnp.arange(count)[None, :]
    return same & causal | diagonal


def head_forward(packed, scale):
    queries, keys_in, values, filled, cluster_ids, positions = packed
    scores = (
        lax.dot_general(
            queries, keys_in, (((1,), (1,)), ((), ())), preferred_element_type=jnp.float32
        )
        * scale
    )
    allowed = keep_mask(filled, cluster_ids, positions)
    row_top = jnp.max(jnp.where(allowed, scores, -jnp.inf), axis=1)
    expd = jnp.where(allowed, jnp.exp(scores - row_top[:, None]), 0.0)
    row_total = jnp.sum(expd, axis=1)
    probs_low = (expd / row_total[:, None]).astype(jnp.bfloat16)
    outputs = jnp.dot(probs_low, values, preferred_element_type=jnp.float32).astype(jnp.bfloat16)
    return (outputs, row_top, row_total)


def head_backward(packed, scale):
    queries, keys_in, values, grads_in, filled, cluster_ids, positions, row_top, row_total = packed
    contract_last = (((1,), (1,)), ((), ()))
    contract_first = (((0,), (0,)), ((), ()))
    scores = (
        lax.dot_general(queries, keys_in, contract_last, preferred_element_type=jnp.float32) * scale
    )
    allowed = keep_mask(filled, cluster_ids, positions)
    probs = jnp.where(allowed, jnp.exp(scores - row_top[:, None]), 0.0) / row_total[:, None]
    probs_low = probs.astype(jnp.bfloat16)
    grad_probs = lax.dot_general(
        grads_in, values, contract_last, preferred_element_type=jnp.float32
    )
    delta_rows = jnp.sum(probs * grad_probs, axis=1)
    grad_low = (probs * (grad_probs - delta_rows[:, None]) * scale).astype(jnp.bfloat16)
    grad_query = jnp.dot(grad_low, keys_in, preferred_element_type=jnp.float32).astype(jnp.bfloat16)
    grad_key = lax.dot_general(
        grad_low, queries, contract_first, preferred_element_type=jnp.float32
    ).astype(jnp.bfloat16)
    grad_value = lax.dot_general(
        probs_low, grads_in, contract_first, preferred_element_type=jnp.float32
    ).astype(jnp.bfloat16)
    return (grad_query, grad_key, grad_value)


def by_owner(hidden, w_query, w_key, w_value, cluster_rank, assign, d_attended):
    tok_rows = hidden.shape[0]
    heads_here = assign.shape[0]
    head_dim = w_query.shape[1] // heads_here
    clusters = cluster_rank.shape[0]
    seq_count = lax.axis_size("seq")
    sub_count = lax.axis_size("sub")
    owners = seq_count * sub_count
    capacity = 2 * tok_rows // owners
    slot_count = owners * capacity
    per_owner = clusters // owners
    scale = head_dim ** (-0.5)
    pieces = (
        lax.all_gather(w_query, "sub", axis=0, tiled=True),
        lax.all_gather(w_key, "sub", axis=0, tiled=True),
        lax.all_gather(w_value, "sub", axis=0, tiled=True),
    )
    projected = tuple(
        (
            jnp.dot(hidden, weight_piece, preferred_element_type=jnp.float32)
            for weight_piece in pieces
        )
    )

    def split_heads(matrix):
        return (
            matrix.astype(jnp.bfloat16).reshape(tok_rows, heads_here, head_dim).transpose(1, 0, 2)
        )

    queries, keys_all, values = tuple((split_heads(matrix) for matrix in projected))
    cluster_range = jnp.arange(clusters, dtype=jnp.int32)
    rank_tok = jnp.sum(jnp.where(assign[:, :, None] == cluster_range, cluster_rank, 0), axis=2)
    owner_ids = rank_tok // per_owner
    owner_hot = (owner_ids[:, :, None] == jnp.arange(owners, dtype=jnp.int32)).astype(jnp.int32)
    within = jnp.sum(owner_hot * (jnp.cumsum(owner_hot, axis=1) - 1), axis=2)
    slot_tok = owner_ids * capacity + within
    token_ids = jnp.arange(tok_rows, dtype=jnp.int32)
    slot_range = jnp.arange(slot_count, dtype=jnp.int32)
    slot_match = slot_tok[:, None, :] == slot_range[None, :, None]
    slot_hot = slot_match.astype(jnp.bfloat16)

    def to_slots(rows_in):
        kept = jnp.einsum(
            "hst,htd->hsd", slot_hot, rows_in, preferred_element_type=jnp.float32
        ).astype(jnp.bfloat16)
        return kept.reshape(heads_here, owners, capacity, head_dim)

    def from_slots(slotted):
        flat_slots = slotted.reshape(heads_here, slot_count, head_dim)
        return jnp.einsum(
            "hst,hsd->htd", slot_hot, flat_slots, preferred_element_type=jnp.float32
        ).astype(jnp.bfloat16)

    def exchange_three(first, second, third):
        return (
            lax.all_to_all(first, ("seq", "sub"), split_axis=1, concat_axis=1, tiled=True),
            lax.all_to_all(second, ("seq", "sub"), split_axis=1, concat_axis=1, tiled=True),
            lax.all_to_all(third, ("seq", "sub"), split_axis=1, concat_axis=1, tiled=True),
        )

    sent = exchange_three(to_slots(queries), to_slots(keys_all), to_slots(values))
    tag_tok = assign * tok_rows + token_ids
    slot_tag = jnp.sum(jnp.where(slot_match, tag_tok[:, None, :] + 1, 0), axis=2) - 1
    tags = lax.all_to_all(
        slot_tag.reshape(heads_here, owners, capacity),
        ("seq", "sub"),
        split_axis=1,
        concat_axis=1,
        tiled=True,
    )
    tags = tags.reshape(heads_here, slot_count)
    owner_q, owner_k, owner_v = tuple(
        (member.reshape(heads_here, slot_count, head_dim) for member in sent)
    )
    filled = tags >= 0
    cluster_ids = jnp.where(filled, tags // tok_rows, -1)
    positions = slot_range // capacity * tok_rows + tags % tok_rows
    outputs, row_top, row_total = lax.map(
        partial(head_forward, scale=scale),
        (owner_q, owner_k, owner_v, filled, cluster_ids, positions),
    )
    returned = lax.all_to_all(
        outputs.reshape(heads_here, owners, capacity, head_dim),
        ("seq", "sub"),
        split_axis=1,
        concat_axis=1,
        tiled=True,
    )

    def merge_heads(slotted):
        return from_slots(slotted).transpose(1, 0, 2).reshape(tok_rows, heads_here * head_dim)

    attended = merge_heads(returned)
    grads_tok = d_attended.reshape(tok_rows, heads_here, head_dim).transpose(1, 0, 2)
    owner_g = lax.all_to_all(
        to_slots(grads_tok), ("seq", "sub"), split_axis=1, concat_axis=1, tiled=True
    ).reshape(heads_here, slot_count, head_dim)
    grad_q, grad_k, grad_v = lax.map(
        partial(head_backward, scale=scale),
        (owner_q, owner_k, owner_v, owner_g, filled, cluster_ids, positions, row_top, row_total),
    )
    shape_four = (heads_here, owners, capacity, head_dim)
    back = exchange_three(
        grad_q.reshape(shape_four), grad_k.reshape(shape_four), grad_v.reshape(shape_four)
    )
    token_grads = tuple((merge_heads(member) for member in back))
    pieces = lax.all_gather((w_query, w_key, w_value), "sub", axis=0, tiled=True)
    terms = [
        jnp.einsum("tc,rc->tr", grad_rows_in, weight_piece, preferred_element_type=jnp.float32)
        for grad_rows_in, weight_piece in zip(token_grads, pieces)
    ]
    partial_grad = terms[0] + terms[1] + terms[2]
    d_hidden = lax.psum_scatter(
        partial_grad.astype(jnp.bfloat16), "head", scatter_dimension=1, tiled=True
    )
    keys_float = keys_all.astype(jnp.float32)
    unit_keys = keys_float * lax.rsqrt(
        jnp.sum(keys_float * keys_float, axis=2, keepdims=True) + epsilon
    )
    member_hot = (rank_tok[:, :, None] == cluster_range).astype(jnp.float32)
    local_sums = jnp.einsum("htr,htd->hrd", member_hot, unit_keys, precision=lax.Precision.HIGHEST)
    centroid_sums = lax.psum_scatter(
        local_sums.astype(jnp.bfloat16), ("seq", "sub"), scatter_dimension=1, tiled=True
    ).astype(jnp.float32)
    return (attended, d_hidden, centroid_sums)


contract_last = (((1,), (1,)), ((), ()))
contract_first = (((0,), (0,)), ((), ()))
log2_e = 1.4426950408889634
mebi = 1024 * 1024


def id_lines(rows, head_dim):
    return -(-(rows // head_dim) // 16) * 16


def pack_kernel(place_ref, grads_ref, assign_ref, mine_ref, theirs_ref, ids_ref, sems):
    chips, padded, head_dim = mine_ref.shape
    rows = grads_ref.shape[0]
    spare = padded - rows - rows // head_dim
    copies = [pltpu.make_async_copy(assign_ref, ids_ref, sems.at[2 * chips])]
    for turn, out_ref in enumerate((mine_ref, theirs_ref)):
        for chip in range(chips):
            head = (place_ref[1] ^ turn) * chips + chip
            at = pl.multiple_of(head * head_dim, head_dim)
            copies.append(
                pltpu.make_async_copy(
                    grads_ref.at[:, pl.ds(at, head_dim)],
                    out_ref.at[chip, pl.ds(0, rows)],
                    sems.at[turn * chips + chip],
                )
            )
    for copy in copies:
        copy.start()
    copies[0].wait()
    for turn, out_ref in enumerate((mine_ref, theirs_ref)):
        for chip in range(chips):
            head = (place_ref[1] ^ turn) * chips + chip
            ids = ids_ref[pl.ds(head, 1), :].astype(jnp.float32)
            lines = [
                ids[:, start : start + head_dim] for start in range(0, rows, head_dim)
            ] + [jnp.zeros((spare, head_dim), jnp.float32)]
            out_ref[chip, rows:, :] = jnp.concatenate(lines, axis=0).astype(jnp.bfloat16)
    for copy in copies[1:]:
        copy.wait()


def merge_kernel(place_ref, mine_ref, theirs_ref, *out_refs):
    height = mine_ref.shape[1]
    for turn, held_ref in enumerate((mine_ref, theirs_ref)):
        at = pl.ds(pl.multiple_of((place_ref[1] ^ turn) * height, height), height)
        for offset, out_ref in enumerate(out_refs):
            out_ref[at, :] = held_ref[place_ref[0] ^ offset]


def fetch_columns(half, weights, held_ref, sems):
    chunks = sems.shape[1]
    columns = held_ref.shape[2]
    rows = held_ref.shape[1] // chunks
    at = pl.ds(pl.multiple_of(half * columns, columns), columns)
    copies = []
    for index, weight in enumerate(weights):
        for chunk in range(chunks):
            lines = pl.ds(chunk * rows, rows)
            copy = pltpu.make_async_copy(
                weight.at[lines, at], held_ref.at[index, lines], sems.at[index, chunk]
            )
            copy.start()
            copies.append(copy)
    return copies


def project_kernel(count, turn, place_ref, *refs):
    if turn == 0:
        arrived_ref, refs = refs[0], refs[1:]
    tokens, weights, refs = refs[:2], refs[2 : 2 + count], refs[2 + count :]
    out_refs, (joined_ref, held_ref, low_ref, sems, token_sems) = refs[:-5], refs[-5:]
    side = place_ref[1]
    tall, depth = joined_ref.shape
    rows = tall // 2
    near = pl.ds(pl.multiple_of(side * depth, depth), depth)
    joins = []
    for core, source in enumerate(tokens):
        at = pl.ds(pl.multiple_of((side ^ core) * rows, rows), rows)
        joins.append(
            pltpu.make_async_copy(source.at[:, near], joined_ref.at[at], token_sems.at[core])
        )
        joins[core].start()
    copies = fetch_columns(side ^ turn, weights, held_ref, sems)
    for copy in joins:
        copy.wait()
    chunks = sems.shape[1]
    for index in range(count):
        for chunk in range(chunks):
            copies[index * chunks + chunk].wait()
        total = jnp.dot(joined_ref[...], held_ref[index], preferred_element_type=jnp.float32)
        if turn == 1:
            out_refs[0][index] = total.astype(jnp.bfloat16)
            continue
        low_ref[...] = (total + arrived_ref[index].astype(jnp.float32)).astype(jnp.bfloat16)
        for offset, out_ref in enumerate(out_refs):
            head_dim = out_ref.shape[1]
            at = pl.multiple_of((place_ref[0] ^ offset) * head_dim, head_dim)
            out_ref[index * tall : (index + 1) * tall, :] = low_ref[:, pl.ds(at, head_dim)]


def fetch_kernel(place_ref, mine_ref, theirs_ref, weight_ref, joined_ref, held_ref, sems, token_sems):
    side = place_ref[1]
    tall, depth = joined_ref.shape
    rows = tall // 2
    near = pl.ds(pl.multiple_of(side * depth, depth), depth)
    joins = []
    for core, source in enumerate((mine_ref, theirs_ref)):
        at = pl.ds(pl.multiple_of((side ^ core) * rows, rows), rows)
        joins.append(
            pltpu.make_async_copy(source.at[:, near], joined_ref.at[at], token_sems.at[core])
        )
        joins[core].start()
    for copy in (*fetch_columns(1 - side, (weight_ref,), held_ref, sems), *joins):
        copy.wait()


def opening_kernel(place_ref, joined_ref, held_ref, mine_ref, theirs_ref, weight_ref, *refs):
    out_refs, (part_ref, second_ref, sems) = refs[:-3], refs[-3:]
    copies = fetch_columns(1 - place_ref[1], (weight_ref,), second_ref, sems)
    merge_kernel(place_ref, mine_ref, theirs_ref, *out_refs)
    total = jnp.dot(joined_ref[...], held_ref[0], preferred_element_type=jnp.float32)
    part_ref[0] = total.astype(jnp.bfloat16)
    for copy in copies:
        copy.wait()
    total = jnp.dot(joined_ref[...], second_ref[0], preferred_element_type=jnp.float32)
    part_ref[1] = total.astype(jnp.bfloat16)


def in_order(place, parts, start, ordered):
    for offset, part in enumerate(parts):
        tall = ordered.shape[0] // len(parts)
        at = pl.ds(pl.multiple_of((place ^ offset) * tall, tall), tall)
        ordered[at, :] = part[start : start + tall, :]


def order_grads(place, parts, rows, grad_rows, id_rows, id_cols):
    head_dim = grad_rows.shape[1]
    height = parts[0].shape[0] // 2
    for offset, part in enumerate(parts):
        for core in range(2):
            block = (place ^ offset) * 2 + core
            at = pl.ds(pl.multiple_of(block * rows, rows), rows)
            start = core * height
            grad_rows[at, :] = part[start : start + rows, :]
            lines = part[start + rows : start + rows + 16, :].astype(jnp.float32)
            ids = jnp.concatenate(
                [lines[line : line + 1, :] for line in range(rows // head_dim)], axis=1
            )
            id_rows[block] = jnp.broadcast_to(ids, id_rows.shape[1:])
            id_cols[at, :] = jnp.broadcast_to(ids, (head_dim, rows)).T


def order_rows(place, parts, rows, ordered):
    height = parts[0].shape[0] // 2
    for offset, part in enumerate(parts):
        for core in range(2):
            at = pl.ds(pl.multiple_of(((place ^ offset) * 2 + core) * rows, rows), rows)
            ordered[at, :] = part[core * height : core * height + rows, :]


def block_scores(factor, block, rows, queries, keys_in, id_rows, id_cols):
    head_dim = queries.shape[1]
    seen = (block + 1) * rows
    scores = lax.dot_general(
        keys_in[:seen, :],
        queries[block * rows : seen, :],
        contract_last,
        preferred_element_type=jnp.float32,
    )
    ids = id_cols[:seen, :]
    mine = id_rows[block][:1, :]
    same = jnp.concatenate(
        [ids == mine[:, start : start + head_dim] for start in range(0, rows, head_dim)], axis=1
    )
    key_at = lax.broadcasted_iota(jnp.int32, (rows, rows), 0)
    query_at = lax.broadcasted_iota(jnp.int32, (rows, rows), 1)
    last = same[seen - rows :] & (key_at <= query_at)
    allowed = last if block == 0 else jnp.concatenate([same[: seen - rows], last], axis=0)
    return jnp.where(allowed, scores * factor, -jnp.inf)


def value_grad_kernel(factor, chips, rows, place_ref, *refs):
    packed, grads, rank_ref = refs[:chips], refs[chips : 2 * chips], refs[2 * chips]
    refs = refs[2 * chips + 1 :]
    out_refs, probs_ref, sums_ref = refs[:chips], refs[chips], refs[chips + 1]
    queries, keys_in, grad_rows, id_rows, id_cols, total_ref = refs[chips + 2 :]
    head_dim = queries.shape[1]
    clusters = rank_ref.shape[1]
    tall = 2 * rows
    place = place_ref[0]
    in_order(place, packed, 0, queries)
    in_order(place, packed, tall, keys_in)
    order_grads(place, grads, rows, grad_rows, id_rows, id_cols)
    total_ref[...] = jnp.zeros_like(total_ref)
    stored = 0
    for block in range(2 * chips):
        seen = (block + 1) * rows
        scores = block_scores(factor, block, rows, queries, keys_in, id_rows, id_cols)
        top = jnp.max(scores, axis=0, keepdims=True)
        expd = jnp.exp2(scores - top)
        total = jnp.sum(expd, axis=0, keepdims=True)
        probs_low = (expd * (1.0 / total)).astype(jnp.bfloat16)
        probs_ref[stored : stored + seen, :] = probs_low
        stored += seen
        total_ref[:seen, :] += jnp.dot(
            probs_low, grad_rows[block * rows : seen, :], preferred_element_type=jnp.float32
        )
    for offset, out_ref in enumerate(out_refs):
        at = pl.multiple_of((place ^ offset) * tall, tall)
        out_ref[...] = total_ref[pl.ds(at, tall), :].astype(jnp.bfloat16)
    sums = jnp.zeros((clusters, head_dim), jnp.float32)
    cluster_at = lax.broadcasted_iota(jnp.int32, (clusters, rows), 0).astype(jnp.float32)
    for block in range(2 * chips):
        keys_float = keys_in[block * rows : (block + 1) * rows, :].astype(jnp.float32)
        unit = keys_float * lax.rsqrt(
            jnp.sum(keys_float * keys_float, axis=1, keepdims=True) + epsilon
        )
        unit_high = unit.astype(jnp.bfloat16)
        unit_low = (unit - unit_high.astype(jnp.float32)).astype(jnp.bfloat16)
        member = jnp.where(cluster_at == id_rows[block][:1, :], 1.0, 0.0).astype(jnp.bfloat16)
        sums += jnp.dot(member, unit_high, preferred_element_type=jnp.float32)
        sums += jnp.dot(member, unit_low, preferred_element_type=jnp.float32)
    rank_at = lax.broadcasted_iota(jnp.int32, (clusters, clusters), 0)
    ordered = jnp.where(rank_at == rank_ref[...], 1.0, 0.0).astype(jnp.bfloat16)
    ranked = jnp.dot(ordered, sums.astype(jnp.bfloat16), preferred_element_type=jnp.float32)
    sums_ref[...] = ranked.astype(jnp.bfloat16)


def query_grad_kernel(scale, chips, rows, place_ref, *refs):
    packed, valued, grads = refs[:chips], refs[chips : 2 * chips], refs[2 * chips : 3 * chips]
    probs_ref, sums_ref = refs[3 * chips : 3 * chips + 2]
    refs = refs[3 * chips + 2 :]
    grad_refs, out_refs, refs = refs[:chips], refs[chips : chips + 2], refs[chips + 2 :]
    queries, keys_in, values, grad_rows, total_ref, dq_ref, attended_ref = refs
    tall = 2 * rows
    place = place_ref[0]
    in_order(place, packed, 0, queries)
    in_order(place, packed, tall, keys_in)
    in_order(place, valued, 0, values)
    order_rows(place, grads, rows, grad_rows)
    total_ref[...] = jnp.zeros_like(total_ref)
    stored = 0
    for block in range(2 * chips):
        seen = (block + 1) * rows
        mine = slice(block * rows, seen)
        probs_low = probs_ref[stored : stored + seen, :]
        stored += seen
        seen_values = values[:seen, :]
        grad_probs = lax.dot_general(
            seen_values, grad_rows[mine, :], contract_last, preferred_element_type=jnp.float32
        )
        flipped = lax.dot_general(
            seen_values, probs_low, contract_first, preferred_element_type=jnp.float32
        )
        attended_ref[mine, :] = flipped.T.astype(jnp.bfloat16)
        probs = probs_low.astype(jnp.float32)
        weighted = probs * grad_probs
        delta = jnp.sum(weighted, axis=0, keepdims=True)
        grad_low = (weighted - probs * delta).astype(jnp.bfloat16)
        total_ref[:seen, :] += jnp.dot(
            grad_low, queries[mine, :], preferred_element_type=jnp.float32
        )
        flipped = lax.dot_general(
            keys_in[:seen, :], grad_low, contract_first, preferred_element_type=jnp.float32
        )
        dq_ref[mine, :] = (flipped.T * scale).astype(jnp.bfloat16)
    for offset in range(chips):
        at = pl.ds(pl.multiple_of((place ^ offset) * tall, tall), tall)
        grad_refs[offset][:tall, :] = dq_ref[at, :]
        grad_refs[offset][tall:, :] = (total_ref[at, :] * scale).astype(jnp.bfloat16)
    owned = sums_ref.shape[0] // (2 * chips)
    for turn, out_ref in enumerate(out_refs):
        for chip in range(chips):
            shard = chip * 2 + (place_ref[1] ^ turn)
            at = pl.ds(pl.multiple_of(shard * rows, rows), rows)
            out_ref[chip, :rows, :] = attended_ref[at, :]
            at = pl.ds(pl.multiple_of(shard * owned, owned), owned)
            out_ref[chip, rows:, :] = sums_ref[at, :]


def join_kernel(*refs):
    parts, out_ref = refs[1:-1], refs[-1]
    for offset, part in enumerate(parts):
        out_ref[offset] = part[...]


def input_kernel(chips, which, place_ref, *refs):
    valued_other_ref, refs = refs[3 * chips], refs[: 3 * chips] + refs[3 * chips + 1 :]
    weights, (out_ref, gathered_ref) = refs[3 * chips : -2], refs[-2:]
    rows, width = out_ref.shape[0], weights[0].shape[1]
    head_dim = width // (2 * chips)
    for turn in range(2):
        parts = refs[turn * chips : (turn + 1) * chips]
        valued = refs[2 * chips : 3 * chips]
        for offset in range(chips):
            head = (place_ref[1] ^ turn) * chips + (place_ref[0] ^ offset)
            for index in range(3):
                source = parts[offset] if index < 2 else valued[offset]
                if index == 2 and turn == 1:
                    source = valued_other_ref.at[offset]
                at = pl.multiple_of((2 * (index % 2) + place_ref[which]) * rows, rows)
                start = pl.multiple_of(index * width + head * head_dim, head_dim)
                gathered_ref[:, pl.ds(start, head_dim)] = source[pl.ds(at, rows), :]
    flipped = None
    for index in range(3):
        term = lax.dot_general(
            weights[index][...],
            gathered_ref[:, index * width : (index + 1) * width],
            contract_last,
            preferred_element_type=jnp.float32,
        )
        flipped = term if flipped is None else flipped + term
    out_ref[...] = flipped.T.astype(out_ref.dtype)


def attended_kernel(chips, place_ref, *refs):
    parts, (attended_ref, sums_ref) = refs[:chips], refs[chips:]
    rows = attended_ref.shape[0]
    head_dim = sums_ref.shape[2]
    height = parts[0].shape[0] // 2
    for core in range(2):
        start = core * height
        for offset, part in enumerate(parts):
            head = core * chips + (place_ref[0] ^ offset)
            at = pl.multiple_of(head * head_dim, head_dim)
            attended_ref[:, pl.ds(at, head_dim)] = part[start : start + rows, :]
            sums_ref[head] = part[start + rows : start + height, :].astype(jnp.float32)


def sum_kernel(place_ref, first_ref, second_ref, kept_ref, hidden_ref):
    keeps = place_ref[2] == place_ref[1]
    second = jnp.where(keeps, kept_ref[...], second_ref[...]).astype(jnp.float32)
    hidden_ref[...] = (first_ref[...].astype(jnp.float32) + second).astype(jnp.bfloat16)


def by_head(hidden, w_query, w_key, w_value, cluster_rank, assign, d_attended):
    rows = hidden.shape[0]
    count = assign.shape[0]
    chips = count // 2
    half, width = w_query.shape
    head_dim = width // count
    tokens = count * rows
    clusters = cluster_rank.shape[0]
    owned = clusters // count
    scale = head_dim ** (-0.5)
    factor = scale * log2_e
    smem = pl.BlockSpec(memory_space=pltpu.SMEM)
    vmem = pl.BlockSpec(memory_space=pltpu.VMEM)
    anywhere = pl.BlockSpec(memory_space=pl.ANY)
    params = pltpu.CompilerParams(vmem_limit_bytes=32 * mebi)
    project_params = pltpu.CompilerParams(vmem_limit_bytes=32 * mebi)
    swap = [(0, 1), (1, 0)]
    chip, side, column = (lax.axis_index(name) for name in ("seq", "sub", "head"))
    place = jnp.stack([chip, side, column, 1 - column])

    def call(kernel, outs, *operands, scratch=(), hbm=0, limits=params, takes=1):
        return pl.pallas_call(
            kernel,
            out_shape=outs,
            in_specs=[smem] + [vmem] * (len(operands) - 1 - hbm) + [anywhere] * hbm,
            out_specs=jax.tree.map(lambda _: vmem, outs),
            scratch_shapes=list(scratch),
            compiler_params=limits,
            cost_estimate=pl.CostEstimate(
                flops=int(takes * 1.15e9), bytes_accessed=mebi, transcendentals=0
            ),
        )(*operands)

    def low(*shape):
        return jax.ShapeDtypeStruct(shape, jnp.bfloat16)

    def buffers(height):
        return (low(height, head_dim),) * chips

    def exchange(parts):
        moved = {
            offset: lax.ppermute(parts[offset], "seq", [(at, at ^ offset) for at in range(chips)])
            for offset in (2, 3, 1)
        }
        return (parts[0], moved[1], moved[2], moved[3])

    def to_sibling(piece):
        return lax.ppermute(piece, "sub", swap)

    def stay(array):
        return pltpu.with_memory_space_constraint(array, pltpu.HBM)

    hidden_other = to_sibling(hidden)
    block = low(chips, rows + id_lines(rows, head_dim), head_dim)
    grads_mine, grads_theirs = call(
        pack_kernel,
        (block, block),
        place,
        stay(d_attended),
        stay(assign),
        scratch=[pltpu.VMEM(assign.shape, jnp.int32), pltpu.SemaphoreType.DMA((count + 1,))],
        hbm=2,
    )
    grads_other = to_sibling(grads_theirs)

    def project(turn, weights, tokens_other, *arrived):
        number = len(weights)
        outs = buffers(2 * number * rows) if turn == 0 else low(number, 2 * rows, width // 2)

        return call(
            partial(project_kernel, number, turn),
            outs,
            place,
            *arrived,
            stay(hidden),
            tokens_other,
            *(stay(weight) for weight in weights),
            scratch=[
                pltpu.VMEM((2 * rows, half), jnp.bfloat16),
                pltpu.VMEM((number, half, width // 2), jnp.bfloat16),
                pltpu.VMEM((2 * rows, width // 2), jnp.bfloat16),
                pltpu.SemaphoreType.DMA((number, 4)),
                pltpu.SemaphoreType.DMA((2,)),
            ],
            hbm=2 + number,
            limits=project_params,
            takes=(8 if number == 2 else 0.1) if turn == 0 else 0.1,
        )

    early, late = (w_query, w_key), (w_value,)
    half_columns = (1, half, width // 2)
    joined, fetched = call(
        fetch_kernel,
        (pltpu.VMEM((2 * rows, half), jnp.bfloat16), pltpu.VMEM(half_columns, jnp.bfloat16)),
        place,
        stay(hidden),
        hidden_other,
        stay(w_query),
        scratch=[pltpu.SemaphoreType.DMA((1, 4)), pltpu.SemaphoreType.DMA((2,))],
        hbm=3,
    )
    *merged, early_part = call(
        opening_kernel,
        (*buffers(2 * block.shape[1]), low(2, 2 * rows, width // 2)),
        place,
        joined,
        fetched,
        grads_mine,
        grads_other,
        stay(w_key),
        scratch=[pltpu.VMEM(half_columns, jnp.bfloat16), pltpu.SemaphoreType.DMA((1, 4))],
        hbm=1,
        takes=0.1,
    )
    grads = exchange(merged)
    early_arrived = to_sibling(early_part)
    early_projected = project(0, early, hidden_other, early_arrived)
    packed = exchange(early_projected)
    late_tokens, *_ = lax.optimization_barrier((hidden_other, early_arrived))
    late_arrived = to_sibling(project(1, late, late_tokens))
    late_arrived, *_ = lax.optimization_barrier((late_arrived, grads[2], grads[3]))
    late_projected = project(0, late, late_tokens, late_arrived)
    valued = exchange(late_projected)
    packed = lax.optimization_barrier((*packed, late_projected[0]))[:chips]

    def held(kind):
        return pltpu.VMEM((tokens, head_dim), kind)

    id_scratch = [pltpu.VMEM((count, 8, rows), jnp.float32), held(jnp.float32)]
    *value_grads, probs, sums = call(
        partial(value_grad_kernel, factor, chips, rows),
        (
            *buffers(2 * rows),
            pltpu.VMEM((count * (count + 1) // 2 * rows, rows), jnp.bfloat16),
            low(clusters, head_dim),
        ),
        place,
        *packed,
        *grads,
        cluster_rank.reshape(1, clusters),
        scratch=[held(jnp.bfloat16)] * 3 + id_scratch + [held(jnp.float32)],
        takes=7,
    )
    value_back = exchange(value_grads)
    results = call(
        partial(query_grad_kernel, scale, chips, rows),
        (*buffers(4 * rows), *(low(chips, rows + owned, head_dim),) * 2),
        place,
        *packed,
        *valued,
        *grads,
        probs,
        sums,
        scratch=[held(jnp.bfloat16)] * 4
        + [held(jnp.float32)]
        + [held(jnp.bfloat16)] * 2,
        takes=10,
    )
    *ready, _ = lax.optimization_barrier((*results[:chips], value_back[2]))
    back = exchange(ready)

    attended_mine, attended_theirs = results[chips:]
    outputs = call(
        merge_kernel, buffers(2 * (rows + owned)), place, attended_mine, to_sibling(attended_theirs)
    )
    early_back, _ = lax.optimization_barrier((back[2], outputs[0]))
    back_other = tuple(
        to_sibling(early_back if offset == 2 else part) for offset, part in enumerate(back)
    )
    value_other = to_sibling(
        call(join_kernel, low(chips, 2 * rows, head_dim), place, *value_back)
    )

    def input_part(which, place):
        return call(
            partial(input_kernel, chips, which),
            low(rows, half),
            place,
            *back,
            *back_other,
            *value_back,
            value_other,
            w_query,
            w_key,
            w_value,
            scratch=[pltpu.VMEM((rows, 3 * width), jnp.bfloat16)],
        )

    *outputs, _, _ = lax.optimization_barrier((*outputs, back[2], back[3]))
    returned = exchange(outputs)
    square = ("head", "sub")
    crossing = input_part(3, place)
    first = lax.ppermute(crossing, square, [(0, 1), (1, 3), (3, 2), (2, 0)])
    kept = input_part(2, lax.optimization_barrier((place, crossing))[0])
    second = lax.ppermute(kept, square, [(1, 2), (2, 1)])
    attended, centroid_sums = call(
        partial(attended_kernel, chips),
        (low(rows, width), jax.ShapeDtypeStruct((count, owned, head_dim), jnp.float32)),
        place,
        *returned,
        takes=8,
    )
    first, second, _ = lax.optimization_barrier((first, second, attended))
    d_hidden = call(sum_kernel, low(rows, half), place, first, second, kept)
    return (attended, d_hidden, centroid_sums)


def per_device(hidden, w_query, w_key, w_value, cluster_rank, assign, d_attended):
    chips = lax.axis_size("seq")
    fits = chips == 4 and lax.axis_size("sub") == 2 and lax.axis_size("head") == 2
    plan = by_head if fits and assign.shape[0] == 2 * chips else by_owner
    return plan(hidden, w_query, w_key, w_value, cluster_rank, assign, d_attended)


def solution(mesh):
    placed = (
        P(("groups", "seq", "sub"), None),
        P("sub", "head"),
        P("sub", "head"),
        P("sub", "head"),
        P("groups"),
        P("head", ("groups", "seq", "sub")),
        P(("groups", "seq", "sub"), "head"),
    )
    return jax.shard_map(
        per_device,
        mesh=mesh,
        in_specs=placed,
        out_specs=(
            P(("groups", "seq", "sub"), "head"),
            P(("groups", "seq", "sub"), "head"),
            P("head", ("groups", "seq", "sub"), None),
        ),
        check_vma=False,
    )
```

```python
from functools import partial

import jax
import jax.numpy as jnp
from jax import lax
from jax.experimental import pallas as pl
from jax.experimental.pallas import tpu as pltpu
from jax.sharding import PartitionSpec as P

epsilon = 1e-06


def keep_mask(filled, cluster_ids, positions):
    count = filled.shape[0]
    same = filled[:, None] & filled[None, :] & (cluster_ids[:, None] == cluster_ids[None, :])
    causal = positions[None, :] <= positions[:, None]
    diagonal = jnp.arange(count)[:, None] == jnp.arange(count)[None, :]
    return same & causal | diagonal


def head_forward(packed, scale):
    queries, keys_in, values, filled, cluster_ids, positions = packed
    scores = (
        lax.dot_general(
            queries, keys_in, (((1,), (1,)), ((), ())), preferred_element_type=jnp.float32
        )
        * scale
    )
    allowed = keep_mask(filled, cluster_ids, positions)
    row_top = jnp.max(jnp.where(allowed, scores, -jnp.inf), axis=1)
    expd = jnp.where(allowed, jnp.exp(scores - row_top[:, None]), 0.0)
    row_total = jnp.sum(expd, axis=1)
    probs_low = (expd / row_total[:, None]).astype(jnp.bfloat16)
    outputs = jnp.dot(probs_low, values, preferred_element_type=jnp.float32).astype(jnp.bfloat16)
    return (outputs, row_top, row_total)


def head_backward(packed, scale):
    queries, keys_in, values, grads_in, filled, cluster_ids, positions, row_top, row_total = packed
    contract_last = (((1,), (1,)), ((), ()))
    contract_first = (((0,), (0,)), ((), ()))
    scores = (
        lax.dot_general(queries, keys_in, contract_last, preferred_element_type=jnp.float32) * scale
    )
    allowed = keep_mask(filled, cluster_ids, positions)
    probs = jnp.where(allowed, jnp.exp(scores - row_top[:, None]), 0.0) / row_total[:, None]
    probs_low = probs.astype(jnp.bfloat16)
    grad_probs = lax.dot_general(
        grads_in, values, contract_last, preferred_element_type=jnp.float32
    )
    delta_rows = jnp.sum(probs * grad_probs, axis=1)
    grad_low = (probs * (grad_probs - delta_rows[:, None]) * scale).astype(jnp.bfloat16)
    grad_query = jnp.dot(grad_low, keys_in, preferred_element_type=jnp.float32).astype(jnp.bfloat16)
    grad_key = lax.dot_general(
        grad_low, queries, contract_first, preferred_element_type=jnp.float32
    ).astype(jnp.bfloat16)
    grad_value = lax.dot_general(
        probs_low, grads_in, contract_first, preferred_element_type=jnp.float32
    ).astype(jnp.bfloat16)
    return (grad_query, grad_key, grad_value)


def by_owner(hidden, w_query, w_key, w_value, cluster_rank, assign, d_attended):
    tok_rows = hidden.shape[0]
    heads_here = assign.shape[0]
    head_dim = w_query.shape[1] // heads_here
    clusters = cluster_rank.shape[0]
    seq_count = lax.axis_size("seq")
    sub_count = lax.axis_size("sub")
    owners = seq_count * sub_count
    capacity = 2 * tok_rows // owners
    slot_count = owners * capacity
    per_owner = clusters // owners
    scale = head_dim ** (-0.5)
    pieces = (
        lax.all_gather(w_query, "sub", axis=0, tiled=True),
        lax.all_gather(w_key, "sub", axis=0, tiled=True),
        lax.all_gather(w_value, "sub", axis=0, tiled=True),
    )
    projected = tuple(
        (
            jnp.dot(hidden, weight_piece, preferred_element_type=jnp.float32)
            for weight_piece in pieces
        )
    )

    def split_heads(matrix):
        return (
            matrix.astype(jnp.bfloat16).reshape(tok_rows, heads_here, head_dim).transpose(1, 0, 2)
        )

    queries, keys_all, values = tuple((split_heads(matrix) for matrix in projected))
    cluster_range = jnp.arange(clusters, dtype=jnp.int32)
    rank_tok = jnp.sum(jnp.where(assign[:, :, None] == cluster_range, cluster_rank, 0), axis=2)
    owner_ids = rank_tok // per_owner
    owner_hot = (owner_ids[:, :, None] == jnp.arange(owners, dtype=jnp.int32)).astype(jnp.int32)
    within = jnp.sum(owner_hot * (jnp.cumsum(owner_hot, axis=1) - 1), axis=2)
    slot_tok = owner_ids * capacity + within
    token_ids = jnp.arange(tok_rows, dtype=jnp.int32)
    slot_range = jnp.arange(slot_count, dtype=jnp.int32)
    slot_match = slot_tok[:, None, :] == slot_range[None, :, None]
    slot_hot = slot_match.astype(jnp.bfloat16)

    def to_slots(rows_in):
        kept = jnp.einsum(
            "hst,htd->hsd", slot_hot, rows_in, preferred_element_type=jnp.float32
        ).astype(jnp.bfloat16)
        return kept.reshape(heads_here, owners, capacity, head_dim)

    def from_slots(slotted):
        flat_slots = slotted.reshape(heads_here, slot_count, head_dim)
        return jnp.einsum(
            "hst,hsd->htd", slot_hot, flat_slots, preferred_element_type=jnp.float32
        ).astype(jnp.bfloat16)

    def exchange_three(first, second, third):
        return (
            lax.all_to_all(first, ("seq", "sub"), split_axis=1, concat_axis=1, tiled=True),
            lax.all_to_all(second, ("seq", "sub"), split_axis=1, concat_axis=1, tiled=True),
            lax.all_to_all(third, ("seq", "sub"), split_axis=1, concat_axis=1, tiled=True),
        )

    sent = exchange_three(to_slots(queries), to_slots(keys_all), to_slots(values))
    tag_tok = assign * tok_rows + token_ids
    slot_tag = jnp.sum(jnp.where(slot_match, tag_tok[:, None, :] + 1, 0), axis=2) - 1
    tags = lax.all_to_all(
        slot_tag.reshape(heads_here, owners, capacity),
        ("seq", "sub"),
        split_axis=1,
        concat_axis=1,
        tiled=True,
    )
    tags = tags.reshape(heads_here, slot_count)
    owner_q, owner_k, owner_v = tuple(
        (member.reshape(heads_here, slot_count, head_dim) for member in sent)
    )
    filled = tags >= 0
    cluster_ids = jnp.where(filled, tags // tok_rows, -1)
    positions = slot_range // capacity * tok_rows + tags % tok_rows
    outputs, row_top, row_total = lax.map(
        partial(head_forward, scale=scale),
        (owner_q, owner_k, owner_v, filled, cluster_ids, positions),
    )
    returned = lax.all_to_all(
        outputs.reshape(heads_here, owners, capacity, head_dim),
        ("seq", "sub"),
        split_axis=1,
        concat_axis=1,
        tiled=True,
    )

    def merge_heads(slotted):
        return from_slots(slotted).transpose(1, 0, 2).reshape(tok_rows, heads_here * head_dim)

    attended = merge_heads(returned)
    grads_tok = d_attended.reshape(tok_rows, heads_here, head_dim).transpose(1, 0, 2)
    owner_g = lax.all_to_all(
        to_slots(grads_tok), ("seq", "sub"), split_axis=1, concat_axis=1, tiled=True
    ).reshape(heads_here, slot_count, head_dim)
    grad_q, grad_k, grad_v = lax.map(
        partial(head_backward, scale=scale),
        (owner_q, owner_k, owner_v, owner_g, filled, cluster_ids, positions, row_top, row_total),
    )
    shape_four = (heads_here, owners, capacity, head_dim)
    back = exchange_three(
        grad_q.reshape(shape_four), grad_k.reshape(shape_four), grad_v.reshape(shape_four)
    )
    token_grads = tuple((merge_heads(member) for member in back))
    pieces = lax.all_gather((w_query, w_key, w_value), "sub", axis=0, tiled=True)
    terms = [
        jnp.einsum("tc,rc->tr", grad_rows_in, weight_piece, preferred_element_type=jnp.float32)
        for grad_rows_in, weight_piece in zip(token_grads, pieces)
    ]
    partial_grad = terms[0] + terms[1] + terms[2]
    d_hidden = lax.psum_scatter(
        partial_grad.astype(jnp.bfloat16), "head", scatter_dimension=1, tiled=True
    )
    keys_float = keys_all.astype(jnp.float32)
    unit_keys = keys_float * lax.rsqrt(
        jnp.sum(keys_float * keys_float, axis=2, keepdims=True) + epsilon
    )
    member_hot = (rank_tok[:, :, None] == cluster_range).astype(jnp.float32)
    local_sums = jnp.einsum("htr,htd->hrd", member_hot, unit_keys, precision=lax.Precision.HIGHEST)
    centroid_sums = lax.psum_scatter(
        local_sums.astype(jnp.bfloat16), ("seq", "sub"), scatter_dimension=1, tiled=True
    ).astype(jnp.float32)
    return (attended, d_hidden, centroid_sums)


contract_last = (((1,), (1,)), ((), ()))
contract_first = (((0,), (0,)), ((), ()))
log2_e = 1.4426950408889634
mebi = 1024 * 1024


def id_lines(rows, head_dim):
    return -(-(rows // head_dim) // 16) * 16


def pack_kernel(place_ref, grads_ref, assign_ref, mine_ref, theirs_ref, ids_ref, sems):
    chips, padded, head_dim = mine_ref.shape
    rows = grads_ref.shape[0]
    spare = padded - rows - rows // head_dim
    copies = [pltpu.make_async_copy(assign_ref, ids_ref, sems.at[2 * chips])]
    for turn, out_ref in enumerate((mine_ref, theirs_ref)):
        for chip in range(chips):
            head = (place_ref[1] ^ turn) * chips + chip
            at = pl.multiple_of(head * head_dim, head_dim)
            copies.append(
                pltpu.make_async_copy(
                    grads_ref.at[:, pl.ds(at, head_dim)],
                    out_ref.at[chip, pl.ds(0, rows)],
                    sems.at[turn * chips + chip],
                )
            )
    for copy in copies:
        copy.start()
    copies[0].wait()
    for turn, out_ref in enumerate((mine_ref, theirs_ref)):
        for chip in range(chips):
            head = (place_ref[1] ^ turn) * chips + chip
            ids = ids_ref[pl.ds(head, 1), :].astype(jnp.float32)
            lines = [
                ids[:, start : start + head_dim] for start in range(0, rows, head_dim)
            ] + [jnp.zeros((spare, head_dim), jnp.float32)]
            out_ref[chip, rows:, :] = jnp.concatenate(lines, axis=0).astype(jnp.bfloat16)
    for copy in copies[1:]:
        copy.wait()


def merge_kernel(place_ref, mine_ref, theirs_ref, *out_refs):
    height = mine_ref.shape[1]
    for turn, held_ref in enumerate((mine_ref, theirs_ref)):
        at = pl.ds(pl.multiple_of((place_ref[1] ^ turn) * height, height), height)
        for offset, out_ref in enumerate(out_refs):
            out_ref[at, :] = held_ref[place_ref[0] ^ offset]


def fetch_columns(half, weights, held_ref, sems):
    chunks = sems.shape[1]
    columns = held_ref.shape[2]
    rows = held_ref.shape[1] // chunks
    at = pl.ds(pl.multiple_of(half * columns, columns), columns)
    copies = []
    for index, weight in enumerate(weights):
        for chunk in range(chunks):
            lines = pl.ds(chunk * rows, rows)
            copy = pltpu.make_async_copy(
                weight.at[lines, at], held_ref.at[index, lines], sems.at[index, chunk]
            )
            copy.start()
            copies.append(copy)
    return copies


def project_kernel(count, turn, place_ref, *refs):
    if turn == 0:
        arrived_ref, refs = refs[0], refs[1:]
    tokens, weights, refs = refs[:2], refs[2 : 2 + count], refs[2 + count :]
    out_refs, (joined_ref, held_ref, low_ref, sems, token_sems) = refs[:-5], refs[-5:]
    side = place_ref[1]
    tall, depth = joined_ref.shape
    rows = tall // 2
    near = pl.ds(pl.multiple_of(side * depth, depth), depth)
    joins = []
    for core, source in enumerate(tokens):
        at = pl.ds(pl.multiple_of((side ^ core) * rows, rows), rows)
        joins.append(
            pltpu.make_async_copy(source.at[:, near], joined_ref.at[at], token_sems.at[core])
        )
        joins[core].start()
    copies = fetch_columns(side ^ turn, weights, held_ref, sems)
    for copy in joins:
        copy.wait()
    chunks = sems.shape[1]
    for index in range(count):
        for chunk in range(chunks):
            copies[index * chunks + chunk].wait()
        total = jnp.dot(joined_ref[...], held_ref[index], preferred_element_type=jnp.float32)
        if turn == 1:
            out_refs[0][index] = total.astype(jnp.bfloat16)
            continue
        low_ref[...] = (total + arrived_ref[index].astype(jnp.float32)).astype(jnp.bfloat16)
        for offset, out_ref in enumerate(out_refs):
            head_dim = out_ref.shape[1]
            at = pl.multiple_of((place_ref[0] ^ offset) * head_dim, head_dim)
            out_ref[index * tall : (index + 1) * tall, :] = low_ref[:, pl.ds(at, head_dim)]


def fetch_kernel(turn, place_ref, *refs):
    weights, (held_ref, sems) = refs[:-2], refs[-2:]
    for copy in fetch_columns(place_ref[1] ^ turn, weights, held_ref, sems):
        copy.wait()


def opening_kernel(place_ref, held_ref, mine_ref, theirs_ref, *refs):
    tokens, refs = refs[:2], refs[2:]
    out_refs, (part_ref, joined_ref, sems) = refs[:-3], refs[-3:]
    side = place_ref[1]
    tall, depth = joined_ref.shape
    rows = tall // 2
    near = pl.ds(pl.multiple_of(side * depth, depth), depth)
    joins = []
    for core, source in enumerate(tokens):
        at = pl.ds(pl.multiple_of((side ^ core) * rows, rows), rows)
        joins.append(pltpu.make_async_copy(source.at[:, near], joined_ref.at[at], sems.at[core]))
        joins[core].start()
    merge_kernel(place_ref, mine_ref, theirs_ref, *out_refs)
    for copy in joins:
        copy.wait()
    for index in range(held_ref.shape[0]):
        total = jnp.dot(joined_ref[...], held_ref[index], preferred_element_type=jnp.float32)
        part_ref[index] = total.astype(jnp.bfloat16)


def in_order(place, parts, start, ordered):
    for offset, part in enumerate(parts):
        tall = ordered.shape[0] // len(parts)
        at = pl.ds(pl.multiple_of((place ^ offset) * tall, tall), tall)
        ordered[at, :] = part[start : start + tall, :]


def order_grads(place, parts, rows, grad_rows, id_rows, id_cols):
    head_dim = grad_rows.shape[1]
    height = parts[0].shape[0] // 2
    for offset, part in enumerate(parts):
        for core in range(2):
            block = (place ^ offset) * 2 + core
            at = pl.ds(pl.multiple_of(block * rows, rows), rows)
            start = core * height
            grad_rows[at, :] = part[start : start + rows, :]
            lines = part[start + rows : start + rows + 16, :].astype(jnp.float32)
            ids = jnp.concatenate(
                [lines[line : line + 1, :] for line in range(rows // head_dim)], axis=1
            )
            id_rows[block] = jnp.broadcast_to(ids, id_rows.shape[1:])
            id_cols[at, :] = jnp.broadcast_to(ids, (head_dim, rows)).T


def order_rows(place, parts, rows, ordered):
    height = parts[0].shape[0] // 2
    for offset, part in enumerate(parts):
        for core in range(2):
            at = pl.ds(pl.multiple_of(((place ^ offset) * 2 + core) * rows, rows), rows)
            ordered[at, :] = part[core * height : core * height + rows, :]


def block_scores(factor, block, rows, queries, keys_in, id_rows, id_cols):
    head_dim = queries.shape[1]
    seen = (block + 1) * rows
    scores = lax.dot_general(
        keys_in[:seen, :],
        queries[block * rows : seen, :],
        contract_last,
        preferred_element_type=jnp.float32,
    )
    ids = id_cols[:seen, :]
    mine = id_rows[block][:1, :]
    same = jnp.concatenate(
        [ids == mine[:, start : start + head_dim] for start in range(0, rows, head_dim)], axis=1
    )
    key_at = lax.broadcasted_iota(jnp.int32, (rows, rows), 0)
    query_at = lax.broadcasted_iota(jnp.int32, (rows, rows), 1)
    last = same[seen - rows :] & (key_at <= query_at)
    allowed = last if block == 0 else jnp.concatenate([same[: seen - rows], last], axis=0)
    return jnp.where(allowed, scores * factor, -jnp.inf)


def value_grad_kernel(factor, chips, rows, place_ref, *refs):
    packed, grads, rank_ref = refs[:chips], refs[chips : 2 * chips], refs[2 * chips]
    refs = refs[2 * chips + 1 :]
    out_refs, probs_ref, sums_ref = refs[:chips], refs[chips], refs[chips + 1]
    queries, keys_in, grad_rows, id_rows, id_cols, total_ref = refs[chips + 2 :]
    head_dim = queries.shape[1]
    clusters = rank_ref.shape[1]
    tall = 2 * rows
    place = place_ref[0]
    in_order(place, packed, 0, queries)
    in_order(place, packed, tall, keys_in)
    order_grads(place, grads, rows, grad_rows, id_rows, id_cols)
    total_ref[...] = jnp.zeros_like(total_ref)
    stored = 0
    for block in range(2 * chips):
        seen = (block + 1) * rows
        scores = block_scores(factor, block, rows, queries, keys_in, id_rows, id_cols)
        top = jnp.max(scores, axis=0, keepdims=True)
        expd = jnp.exp2(scores - top)
        total = jnp.sum(expd, axis=0, keepdims=True)
        probs_low = (expd * (1.0 / total)).astype(jnp.bfloat16)
        probs_ref[stored : stored + seen, :] = probs_low
        stored += seen
        total_ref[:seen, :] += jnp.dot(
            probs_low, grad_rows[block * rows : seen, :], preferred_element_type=jnp.float32
        )
    for offset, out_ref in enumerate(out_refs):
        at = pl.multiple_of((place ^ offset) * tall, tall)
        out_ref[...] = total_ref[pl.ds(at, tall), :].astype(jnp.bfloat16)
    sums = jnp.zeros((clusters, head_dim), jnp.float32)
    cluster_at = lax.broadcasted_iota(jnp.int32, (clusters, rows), 0).astype(jnp.float32)
    for block in range(2 * chips):
        keys_float = keys_in[block * rows : (block + 1) * rows, :].astype(jnp.float32)
        unit = keys_float * lax.rsqrt(
            jnp.sum(keys_float * keys_float, axis=1, keepdims=True) + epsilon
        )
        unit_high = unit.astype(jnp.bfloat16)
        unit_low = (unit - unit_high.astype(jnp.float32)).astype(jnp.bfloat16)
        member = jnp.where(cluster_at == id_rows[block][:1, :], 1.0, 0.0).astype(jnp.bfloat16)
        sums += jnp.dot(member, unit_high, preferred_element_type=jnp.float32)
        sums += jnp.dot(member, unit_low, preferred_element_type=jnp.float32)
    rank_at = lax.broadcasted_iota(jnp.int32, (clusters, clusters), 0)
    ordered = jnp.where(rank_at == rank_ref[...], 1.0, 0.0).astype(jnp.bfloat16)
    ranked = jnp.dot(ordered, sums.astype(jnp.bfloat16), preferred_element_type=jnp.float32)
    sums_ref[...] = ranked.astype(jnp.bfloat16)


def query_grad_kernel(scale, chips, rows, place_ref, *refs):
    packed, valued, grads = refs[:chips], refs[chips : 2 * chips], refs[2 * chips : 3 * chips]
    probs_ref, sums_ref = refs[3 * chips : 3 * chips + 2]
    refs = refs[3 * chips + 2 :]
    grad_refs, out_refs, refs = refs[:chips], refs[chips : chips + 2], refs[chips + 2 :]
    queries, keys_in, values, grad_rows, total_ref, dq_ref, attended_ref = refs
    tall = 2 * rows
    place = place_ref[0]
    in_order(place, packed, 0, queries)
    in_order(place, packed, tall, keys_in)
    in_order(place, valued, 0, values)
    order_rows(place, grads, rows, grad_rows)
    total_ref[...] = jnp.zeros_like(total_ref)
    stored = 0
    for block in range(2 * chips):
        seen = (block + 1) * rows
        mine = slice(block * rows, seen)
        probs_low = probs_ref[stored : stored + seen, :]
        stored += seen
        seen_values = values[:seen, :]
        grad_probs = lax.dot_general(
            seen_values, grad_rows[mine, :], contract_last, preferred_element_type=jnp.float32
        )
        flipped = lax.dot_general(
            seen_values, probs_low, contract_first, preferred_element_type=jnp.float32
        )
        attended_ref[mine, :] = flipped.T.astype(jnp.bfloat16)
        probs = probs_low.astype(jnp.float32)
        weighted = probs * grad_probs
        delta = jnp.sum(weighted, axis=0, keepdims=True)
        grad_low = (weighted - probs * delta).astype(jnp.bfloat16)
        total_ref[:seen, :] += jnp.dot(
            grad_low, queries[mine, :], preferred_element_type=jnp.float32
        )
        flipped = lax.dot_general(
            keys_in[:seen, :], grad_low, contract_first, preferred_element_type=jnp.float32
        )
        dq_ref[mine, :] = (flipped.T * scale).astype(jnp.bfloat16)
    for offset in range(chips):
        at = pl.ds(pl.multiple_of((place ^ offset) * tall, tall), tall)
        grad_refs[offset][:tall, :] = dq_ref[at, :]
        grad_refs[offset][tall:, :] = (total_ref[at, :] * scale).astype(jnp.bfloat16)
    owned = sums_ref.shape[0] // (2 * chips)
    for turn, out_ref in enumerate(out_refs):
        for chip in range(chips):
            shard = chip * 2 + (place_ref[1] ^ turn)
            at = pl.ds(pl.multiple_of(shard * rows, rows), rows)
            out_ref[chip, :rows, :] = attended_ref[at, :]
            at = pl.ds(pl.multiple_of(shard * owned, owned), owned)
            out_ref[chip, rows:, :] = sums_ref[at, :]


def join_kernel(*refs):
    parts, out_ref = refs[1:-1], refs[-1]
    for offset, part in enumerate(parts):
        out_ref[offset] = part[...]


def input_kernel(chips, which, place_ref, *refs):
    valued_other_ref, refs = refs[3 * chips], refs[: 3 * chips] + refs[3 * chips + 1 :]
    weights, (out_ref, gathered_ref) = refs[3 * chips : -2], refs[-2:]
    rows, width = out_ref.shape[0], weights[0].shape[1]
    head_dim = width // (2 * chips)
    for turn in range(2):
        parts = refs[turn * chips : (turn + 1) * chips]
        valued = refs[2 * chips : 3 * chips]
        for offset in range(chips):
            head = (place_ref[1] ^ turn) * chips + (place_ref[0] ^ offset)
            for index in range(3):
                source = parts[offset] if index < 2 else valued[offset]
                if index == 2 and turn == 1:
                    source = valued_other_ref.at[offset]
                at = pl.multiple_of((2 * (index % 2) + place_ref[which]) * rows, rows)
                start = pl.multiple_of(index * width + head * head_dim, head_dim)
                gathered_ref[:, pl.ds(start, head_dim)] = source[pl.ds(at, rows), :]
    flipped = None
    for index in range(3):
        term = lax.dot_general(
            weights[index][...],
            gathered_ref[:, index * width : (index + 1) * width],
            contract_last,
            preferred_element_type=jnp.float32,
        )
        flipped = term if flipped is None else flipped + term
    out_ref[...] = flipped.T.astype(out_ref.dtype)


def attended_kernel(chips, place_ref, *refs):
    parts, (attended_ref, sums_ref) = refs[:chips], refs[chips:]
    rows = attended_ref.shape[0]
    head_dim = sums_ref.shape[2]
    height = parts[0].shape[0] // 2
    for core in range(2):
        start = core * height
        for offset, part in enumerate(parts):
            head = core * chips + (place_ref[0] ^ offset)
            at = pl.multiple_of(head * head_dim, head_dim)
            attended_ref[:, pl.ds(at, head_dim)] = part[start : start + rows, :]
            sums_ref[head] = part[start + rows : start + height, :].astype(jnp.float32)


def sum_kernel(place_ref, first_ref, second_ref, kept_ref, hidden_ref):
    keeps = place_ref[2] == place_ref[1]
    second = jnp.where(keeps, kept_ref[...], second_ref[...]).astype(jnp.float32)
    hidden_ref[...] = (first_ref[...].astype(jnp.float32) + second).astype(jnp.bfloat16)


def by_head(hidden, w_query, w_key, w_value, cluster_rank, assign, d_attended):
    rows = hidden.shape[0]
    count = assign.shape[0]
    chips = count // 2
    half, width = w_query.shape
    head_dim = width // count
    tokens = count * rows
    clusters = cluster_rank.shape[0]
    owned = clusters // count
    scale = head_dim ** (-0.5)
    factor = scale * log2_e
    smem = pl.BlockSpec(memory_space=pltpu.SMEM)
    vmem = pl.BlockSpec(memory_space=pltpu.VMEM)
    anywhere = pl.BlockSpec(memory_space=pl.ANY)
    params = pltpu.CompilerParams(vmem_limit_bytes=32 * mebi)
    project_params = pltpu.CompilerParams(vmem_limit_bytes=32 * mebi)
    swap = [(0, 1), (1, 0)]
    chip, side, column = (lax.axis_index(name) for name in ("seq", "sub", "head"))
    place = jnp.stack([chip, side, column, 1 - column])

    def call(kernel, outs, *operands, scratch=(), hbm=0, limits=params, takes=1):
        return pl.pallas_call(
            kernel,
            out_shape=outs,
            in_specs=[smem] + [vmem] * (len(operands) - 1 - hbm) + [anywhere] * hbm,
            out_specs=jax.tree.map(lambda _: vmem, outs),
            scratch_shapes=list(scratch),
            compiler_params=limits,
            cost_estimate=pl.CostEstimate(
                flops=int(takes * 1.15e9), bytes_accessed=mebi, transcendentals=0
            ),
        )(*operands)

    def low(*shape):
        return jax.ShapeDtypeStruct(shape, jnp.bfloat16)

    def buffers(height):
        return (low(height, head_dim),) * chips

    def exchange(parts):
        moved = {
            offset: lax.ppermute(parts[offset], "seq", [(at, at ^ offset) for at in range(chips)])
            for offset in (2, 3, 1)
        }
        return (parts[0], moved[1], moved[2], moved[3])

    def to_sibling(piece):
        return lax.ppermute(piece, "sub", swap)

    def stay(array):
        return pltpu.with_memory_space_constraint(array, pltpu.HBM)

    hidden_other = to_sibling(hidden)
    block = low(chips, rows + id_lines(rows, head_dim), head_dim)
    grads_mine, grads_theirs = call(
        pack_kernel,
        (block, block),
        place,
        stay(d_attended),
        stay(assign),
        scratch=[pltpu.VMEM(assign.shape, jnp.int32), pltpu.SemaphoreType.DMA((count + 1,))],
        hbm=2,
    )
    grads_other = to_sibling(grads_theirs)

    def project(turn, weights, tokens_other, *arrived):
        number = len(weights)
        outs = buffers(2 * number * rows) if turn == 0 else low(number, 2 * rows, width // 2)

        return call(
            partial(project_kernel, number, turn),
            outs,
            place,
            *arrived,
            stay(hidden),
            tokens_other,
            *(stay(weight) for weight in weights),
            scratch=[
                pltpu.VMEM((2 * rows, half), jnp.bfloat16),
                pltpu.VMEM((number, half, width // 2), jnp.bfloat16),
                pltpu.VMEM((2 * rows, width // 2), jnp.bfloat16),
                pltpu.SemaphoreType.DMA((number, 4)),
                pltpu.SemaphoreType.DMA((2,)),
            ],
            hbm=2 + number,
            limits=project_params,
            takes=(8 if number == 2 else 0.1) if turn == 0 else 0.1,
        )

    early, late = (w_query, w_key), (w_value,)
    fetched = call(
        partial(fetch_kernel, 1),
        pltpu.VMEM((2, half, width // 2), jnp.bfloat16),
        place,
        *(stay(weight) for weight in early),
        scratch=[pltpu.SemaphoreType.DMA((2, 4))],
        hbm=2,
    )
    *merged, early_part = call(
        opening_kernel,
        (*buffers(2 * block.shape[1]), low(2, 2 * rows, width // 2)),
        place,
        fetched,
        grads_mine,
        grads_other,
        stay(hidden),
        hidden_other,
        scratch=[pltpu.VMEM((2 * rows, half), jnp.bfloat16), pltpu.SemaphoreType.DMA((2,))],
        hbm=2,
        takes=0.1,
    )
    grads = exchange(merged)
    early_arrived = to_sibling(early_part)
    early_projected = project(0, early, hidden_other, early_arrived)
    packed = exchange(early_projected)
    late_tokens, *_ = lax.optimization_barrier((hidden_other, early_arrived))
    late_arrived = to_sibling(project(1, late, late_tokens))
    late_arrived, *_ = lax.optimization_barrier((late_arrived, grads[2], grads[3]))
    late_projected = project(0, late, late_tokens, late_arrived)
    valued = exchange(late_projected)
    packed = lax.optimization_barrier((*packed, late_projected[0]))[:chips]

    def held(kind):
        return pltpu.VMEM((tokens, head_dim), kind)

    id_scratch = [pltpu.VMEM((count, 8, rows), jnp.float32), held(jnp.float32)]
    *value_grads, probs, sums = call(
        partial(value_grad_kernel, factor, chips, rows),
        (
            *buffers(2 * rows),
            pltpu.VMEM((count * (count + 1) // 2 * rows, rows), jnp.bfloat16),
            low(clusters, head_dim),
        ),
        place,
        *packed,
        *grads,
        cluster_rank.reshape(1, clusters),
        scratch=[held(jnp.bfloat16)] * 3 + id_scratch + [held(jnp.float32)],
        takes=7,
    )
    value_back = exchange(value_grads)
    results = call(
        partial(query_grad_kernel, scale, chips, rows),
        (*buffers(4 * rows), *(low(chips, rows + owned, head_dim),) * 2),
        place,
        *packed,
        *valued,
        *grads,
        probs,
        sums,
        scratch=[held(jnp.bfloat16)] * 4
        + [held(jnp.float32)]
        + [held(jnp.bfloat16)] * 2,
        takes=10,
    )
    *ready, _ = lax.optimization_barrier((*results[:chips], value_back[2]))
    back = exchange(ready)

    attended_mine, attended_theirs = results[chips:]
    outputs = call(
        merge_kernel, buffers(2 * (rows + owned)), place, attended_mine, to_sibling(attended_theirs)
    )
    value_other = to_sibling(
        call(join_kernel, low(chips, 2 * rows, head_dim), place, *value_back)
    )
    zero, one, three = (to_sibling(back[offset]) for offset in (0, 1, 3))
    last, *_ = lax.optimization_barrier((back[2], outputs[0], zero, one, three, value_other))
    back_other = (zero, one, to_sibling(last), three)

    def input_part(which, place):
        return call(
            partial(input_kernel, chips, which),
            low(rows, half),
            place,
            *back,
            *back_other,
            *value_back,
            value_other,
            w_query,
            w_key,
            w_value,
            scratch=[pltpu.VMEM((rows, 3 * width), jnp.bfloat16)],
        )

    *outputs, _ = lax.optimization_barrier((*outputs, back[3]))
    returned = exchange(outputs)
    square = ("head", "sub")
    crossing = input_part(3, place)
    first = lax.ppermute(crossing, square, [(0, 1), (1, 3), (3, 2), (2, 0)])
    kept = input_part(2, lax.optimization_barrier((place, crossing))[0])
    second = lax.ppermute(kept, square, [(1, 2), (2, 1)])
    attended, centroid_sums = call(
        partial(attended_kernel, chips),
        (low(rows, width), jax.ShapeDtypeStruct((count, owned, head_dim), jnp.float32)),
        place,
        *returned,
        takes=20,
    )
    first, second, _ = lax.optimization_barrier((first, second, attended))
    d_hidden = call(sum_kernel, low(rows, half), place, first, second, kept)
    return (attended, d_hidden, centroid_sums)


def per_device(hidden, w_query, w_key, w_value, cluster_rank, assign, d_attended):
    chips = lax.axis_size("seq")
    fits = chips == 4 and lax.axis_size("sub") == 2 and lax.axis_size("head") == 2
    plan = by_head if fits and assign.shape[0] == 2 * chips else by_owner
    return plan(hidden, w_query, w_key, w_value, cluster_rank, assign, d_attended)


def solution(mesh):
    placed = (
        P(("groups", "seq", "sub"), None),
        P("sub", "head"),
        P("sub", "head"),
        P("sub", "head"),
        P("groups"),
        P("head", ("groups", "seq", "sub")),
        P(("groups", "seq", "sub"), "head"),
    )
    return jax.shard_map(
        per_device,
        mesh=mesh,
        in_specs=placed,
        out_specs=(
            P(("groups", "seq", "sub"), "head"),
            P(("groups", "seq", "sub"), "head"),
            P("head", ("groups", "seq", "sub"), None),
        ),
        check_vma=False,
    )
```

```python
from functools import partial

import jax
import jax.numpy as jnp
from jax import lax
from jax.experimental import pallas as pl
from jax.experimental.pallas import tpu as pltpu
from jax.sharding import PartitionSpec as P

epsilon = 1e-06


def keep_mask(filled, cluster_ids, positions):
    count = filled.shape[0]
    same = filled[:, None] & filled[None, :] & (cluster_ids[:, None] == cluster_ids[None, :])
    causal = positions[None, :] <= positions[:, None]
    diagonal = jnp.arange(count)[:, None] == jnp.arange(count)[None, :]
    return same & causal | diagonal


def head_forward(packed, scale):
    queries, keys_in, values, filled, cluster_ids, positions = packed
    scores = (
        lax.dot_general(
            queries, keys_in, (((1,), (1,)), ((), ())), preferred_element_type=jnp.float32
        )
        * scale
    )
    allowed = keep_mask(filled, cluster_ids, positions)
    row_top = jnp.max(jnp.where(allowed, scores, -jnp.inf), axis=1)
    expd = jnp.where(allowed, jnp.exp(scores - row_top[:, None]), 0.0)
    row_total = jnp.sum(expd, axis=1)
    probs_low = (expd / row_total[:, None]).astype(jnp.bfloat16)
    outputs = jnp.dot(probs_low, values, preferred_element_type=jnp.float32).astype(jnp.bfloat16)
    return (outputs, row_top, row_total)


def head_backward(packed, scale):
    queries, keys_in, values, grads_in, filled, cluster_ids, positions, row_top, row_total = packed
    contract_last = (((1,), (1,)), ((), ()))
    contract_first = (((0,), (0,)), ((), ()))
    scores = (
        lax.dot_general(queries, keys_in, contract_last, preferred_element_type=jnp.float32) * scale
    )
    allowed = keep_mask(filled, cluster_ids, positions)
    probs = jnp.where(allowed, jnp.exp(scores - row_top[:, None]), 0.0) / row_total[:, None]
    probs_low = probs.astype(jnp.bfloat16)
    grad_probs = lax.dot_general(
        grads_in, values, contract_last, preferred_element_type=jnp.float32
    )
    delta_rows = jnp.sum(probs * grad_probs, axis=1)
    grad_low = (probs * (grad_probs - delta_rows[:, None]) * scale).astype(jnp.bfloat16)
    grad_query = jnp.dot(grad_low, keys_in, preferred_element_type=jnp.float32).astype(jnp.bfloat16)
    grad_key = lax.dot_general(
        grad_low, queries, contract_first, preferred_element_type=jnp.float32
    ).astype(jnp.bfloat16)
    grad_value = lax.dot_general(
        probs_low, grads_in, contract_first, preferred_element_type=jnp.float32
    ).astype(jnp.bfloat16)
    return (grad_query, grad_key, grad_value)


def by_owner(hidden, w_query, w_key, w_value, cluster_rank, assign, d_attended):
    tok_rows = hidden.shape[0]
    heads_here = assign.shape[0]
    head_dim = w_query.shape[1] // heads_here
    clusters = cluster_rank.shape[0]
    seq_count = lax.axis_size("seq")
    sub_count = lax.axis_size("sub")
    owners = seq_count * sub_count
    capacity = 2 * tok_rows // owners
    slot_count = owners * capacity
    per_owner = clusters // owners
    scale = head_dim ** (-0.5)
    pieces = (
        lax.all_gather(w_query, "sub", axis=0, tiled=True),
        lax.all_gather(w_key, "sub", axis=0, tiled=True),
        lax.all_gather(w_value, "sub", axis=0, tiled=True),
    )
    projected = tuple(
        (
            jnp.dot(hidden, weight_piece, preferred_element_type=jnp.float32)
            for weight_piece in pieces
        )
    )

    def split_heads(matrix):
        return (
            matrix.astype(jnp.bfloat16).reshape(tok_rows, heads_here, head_dim).transpose(1, 0, 2)
        )

    queries, keys_all, values = tuple((split_heads(matrix) for matrix in projected))
    cluster_range = jnp.arange(clusters, dtype=jnp.int32)
    rank_tok = jnp.sum(jnp.where(assign[:, :, None] == cluster_range, cluster_rank, 0), axis=2)
    owner_ids = rank_tok // per_owner
    owner_hot = (owner_ids[:, :, None] == jnp.arange(owners, dtype=jnp.int32)).astype(jnp.int32)
    within = jnp.sum(owner_hot * (jnp.cumsum(owner_hot, axis=1) - 1), axis=2)
    slot_tok = owner_ids * capacity + within
    token_ids = jnp.arange(tok_rows, dtype=jnp.int32)
    slot_range = jnp.arange(slot_count, dtype=jnp.int32)
    slot_match = slot_tok[:, None, :] == slot_range[None, :, None]
    slot_hot = slot_match.astype(jnp.bfloat16)

    def to_slots(rows_in):
        kept = jnp.einsum(
            "hst,htd->hsd", slot_hot, rows_in, preferred_element_type=jnp.float32
        ).astype(jnp.bfloat16)
        return kept.reshape(heads_here, owners, capacity, head_dim)

    def from_slots(slotted):
        flat_slots = slotted.reshape(heads_here, slot_count, head_dim)
        return jnp.einsum(
            "hst,hsd->htd", slot_hot, flat_slots, preferred_element_type=jnp.float32
        ).astype(jnp.bfloat16)

    def exchange_three(first, second, third):
        return (
            lax.all_to_all(first, ("seq", "sub"), split_axis=1, concat_axis=1, tiled=True),
            lax.all_to_all(second, ("seq", "sub"), split_axis=1, concat_axis=1, tiled=True),
            lax.all_to_all(third, ("seq", "sub"), split_axis=1, concat_axis=1, tiled=True),
        )

    sent = exchange_three(to_slots(queries), to_slots(keys_all), to_slots(values))
    tag_tok = assign * tok_rows + token_ids
    slot_tag = jnp.sum(jnp.where(slot_match, tag_tok[:, None, :] + 1, 0), axis=2) - 1
    tags = lax.all_to_all(
        slot_tag.reshape(heads_here, owners, capacity),
        ("seq", "sub"),
        split_axis=1,
        concat_axis=1,
        tiled=True,
    )
    tags = tags.reshape(heads_here, slot_count)
    owner_q, owner_k, owner_v = tuple(
        (member.reshape(heads_here, slot_count, head_dim) for member in sent)
    )
    filled = tags >= 0
    cluster_ids = jnp.where(filled, tags // tok_rows, -1)
    positions = slot_range // capacity * tok_rows + tags % tok_rows
    outputs, row_top, row_total = lax.map(
        partial(head_forward, scale=scale),
        (owner_q, owner_k, owner_v, filled, cluster_ids, positions),
    )
    returned = lax.all_to_all(
        outputs.reshape(heads_here, owners, capacity, head_dim),
        ("seq", "sub"),
        split_axis=1,
        concat_axis=1,
        tiled=True,
    )

    def merge_heads(slotted):
        return from_slots(slotted).transpose(1, 0, 2).reshape(tok_rows, heads_here * head_dim)

    attended = merge_heads(returned)
    grads_tok = d_attended.reshape(tok_rows, heads_here, head_dim).transpose(1, 0, 2)
    owner_g = lax.all_to_all(
        to_slots(grads_tok), ("seq", "sub"), split_axis=1, concat_axis=1, tiled=True
    ).reshape(heads_here, slot_count, head_dim)
    grad_q, grad_k, grad_v = lax.map(
        partial(head_backward, scale=scale),
        (owner_q, owner_k, owner_v, owner_g, filled, cluster_ids, positions, row_top, row_total),
    )
    shape_four = (heads_here, owners, capacity, head_dim)
    back = exchange_three(
        grad_q.reshape(shape_four), grad_k.reshape(shape_four), grad_v.reshape(shape_four)
    )
    token_grads = tuple((merge_heads(member) for member in back))
    pieces = lax.all_gather((w_query, w_key, w_value), "sub", axis=0, tiled=True)
    terms = [
        jnp.einsum("tc,rc->tr", grad_rows_in, weight_piece, preferred_element_type=jnp.float32)
        for grad_rows_in, weight_piece in zip(token_grads, pieces)
    ]
    partial_grad = terms[0] + terms[1] + terms[2]
    d_hidden = lax.psum_scatter(
        partial_grad.astype(jnp.bfloat16), "head", scatter_dimension=1, tiled=True
    )
    keys_float = keys_all.astype(jnp.float32)
    unit_keys = keys_float * lax.rsqrt(
        jnp.sum(keys_float * keys_float, axis=2, keepdims=True) + epsilon
    )
    member_hot = (rank_tok[:, :, None] == cluster_range).astype(jnp.float32)
    local_sums = jnp.einsum("htr,htd->hrd", member_hot, unit_keys, precision=lax.Precision.HIGHEST)
    centroid_sums = lax.psum_scatter(
        local_sums.astype(jnp.bfloat16), ("seq", "sub"), scatter_dimension=1, tiled=True
    ).astype(jnp.float32)
    return (attended, d_hidden, centroid_sums)


contract_last = (((1,), (1,)), ((), ()))
contract_first = (((0,), (0,)), ((), ()))
log2_e = 1.4426950408889634
mebi = 1024 * 1024


def id_lines(rows, head_dim):
    return -(-(rows // head_dim) // 16) * 16


def pack_kernel(place_ref, grads_ref, assign_ref, mine_ref, theirs_ref, ids_ref, sems):
    chips, padded, head_dim = mine_ref.shape
    rows = grads_ref.shape[0]
    spare = padded - rows - rows // head_dim
    copies = [pltpu.make_async_copy(assign_ref, ids_ref, sems.at[2 * chips])]
    for turn, out_ref in enumerate((mine_ref, theirs_ref)):
        for chip in range(chips):
            head = (place_ref[1] ^ turn) * chips + chip
            at = pl.multiple_of(head * head_dim, head_dim)
            copies.append(
                pltpu.make_async_copy(
                    grads_ref.at[:, pl.ds(at, head_dim)],
                    out_ref.at[chip, pl.ds(0, rows)],
                    sems.at[turn * chips + chip],
                )
            )
    for copy in copies:
        copy.start()
    copies[0].wait()
    for turn, out_ref in enumerate((mine_ref, theirs_ref)):
        for chip in range(chips):
            head = (place_ref[1] ^ turn) * chips + chip
            ids = ids_ref[pl.ds(head, 1), :].astype(jnp.float32)
            lines = [ids[:, start : start + head_dim] for start in range(0, rows, head_dim)]
            gap = [jnp.zeros((len(lines), head_dim), jnp.float32)]
            rest = [jnp.zeros((spare - len(lines), head_dim), jnp.float32)]
            first = jnp.concatenate(lines + gap + rest, axis=0)
            second = jnp.concatenate(gap + lines + rest, axis=0)
            tile = jnp.where(place_ref[1] == 0, first, second)
            out_ref[chip, rows:, :] = tile.astype(jnp.bfloat16)
    for copy in copies[1:]:
        copy.wait()


def merge_kernel(place_ref, mine_ref, theirs_ref, *out_refs):
    height = mine_ref.shape[1]
    for turn, held_ref in enumerate((mine_ref, theirs_ref)):
        at = pl.ds(pl.multiple_of((place_ref[1] ^ turn) * height, height), height)
        for offset, out_ref in enumerate(out_refs):
            out_ref[at, :] = held_ref[place_ref[0] ^ offset]


def merge_grads(place_ref, mine_ref, theirs_ref, out_refs):
    rows = out_refs[0].shape[0] - mine_ref.shape[1]
    for offset, out_ref in enumerate(out_refs):
        chip = place_ref[0] ^ offset
        for turn, held_ref in enumerate((mine_ref, theirs_ref)):
            at = pl.ds(pl.multiple_of((place_ref[1] ^ turn) * rows, rows), rows)
            out_ref[at, :] = held_ref[chip, :rows, :]
        out_ref[2 * rows :, :] = mine_ref[chip, rows:, :] + theirs_ref[chip, rows:, :]


def fetch_columns(half, weights, held_ref, sems):
    chunks = sems.shape[1]
    columns = held_ref.shape[2]
    rows = held_ref.shape[1] // chunks
    at = pl.ds(pl.multiple_of(half * columns, columns), columns)
    copies = []
    for index, weight in enumerate(weights):
        for chunk in range(chunks):
            lines = pl.ds(chunk * rows, rows)
            copy = pltpu.make_async_copy(
                weight.at[lines, at], held_ref.at[index, lines], sems.at[index, chunk]
            )
            copy.start()
            copies.append(copy)
    return copies


def project_kernel(count, turn, place_ref, *refs):
    if turn == 0:
        arrived_ref, refs = refs[0], refs[1:]
    tokens, weights, refs = refs[:2], refs[2 : 2 + count], refs[2 + count :]
    out_refs, (joined_ref, held_ref, low_ref, sems, token_sems) = refs[:-5], refs[-5:]
    side = place_ref[1]
    tall, depth = joined_ref.shape
    rows = tall // 2
    near = pl.ds(pl.multiple_of(side * depth, depth), depth)
    joins = []
    for core, source in enumerate(tokens):
        at = pl.ds(pl.multiple_of((side ^ core) * rows, rows), rows)
        joins.append(
            pltpu.make_async_copy(source.at[:, near], joined_ref.at[at], token_sems.at[core])
        )
        joins[core].start()
    copies = fetch_columns(side ^ turn, weights, held_ref, sems)
    for copy in joins:
        copy.wait()
    chunks = sems.shape[1]
    for index in range(count):
        for chunk in range(chunks):
            copies[index * chunks + chunk].wait()
        total = jnp.dot(joined_ref[...], held_ref[index], preferred_element_type=jnp.float32)
        if turn == 1:
            out_refs[0][index] = total.astype(jnp.bfloat16)
            continue
        low_ref[...] = (total + arrived_ref[index].astype(jnp.float32)).astype(jnp.bfloat16)
        for offset, out_ref in enumerate(out_refs):
            head_dim = out_ref.shape[1]
            at = pl.multiple_of((place_ref[0] ^ offset) * head_dim, head_dim)
            out_ref[index * tall : (index + 1) * tall, :] = low_ref[:, pl.ds(at, head_dim)]


def fetch_kernel(turn, place_ref, *refs):
    weights, (held_ref, sems) = refs[:-2], refs[-2:]
    for copy in fetch_columns(place_ref[1] ^ turn, weights, held_ref, sems):
        copy.wait()


def opening_kernel(place_ref, held_ref, mine_ref, theirs_ref, *refs):
    tokens, refs = refs[:2], refs[2:]
    out_refs, (part_ref, joined_ref, sems) = refs[:-3], refs[-3:]
    side = place_ref[1]
    tall, depth = joined_ref.shape
    rows = tall // 2
    near = pl.ds(pl.multiple_of(side * depth, depth), depth)
    joins = []
    for core, source in enumerate(tokens):
        at = pl.ds(pl.multiple_of((side ^ core) * rows, rows), rows)
        joins.append(pltpu.make_async_copy(source.at[:, near], joined_ref.at[at], sems.at[core]))
        joins[core].start()
    merge_grads(place_ref, mine_ref, theirs_ref, out_refs)
    for copy in joins:
        copy.wait()
    for index in range(held_ref.shape[0]):
        total = jnp.dot(joined_ref[...], held_ref[index], preferred_element_type=jnp.float32)
        part_ref[index] = total.astype(jnp.bfloat16)


def in_order(place, parts, start, ordered):
    for offset, part in enumerate(parts):
        tall = ordered.shape[0] // len(parts)
        at = pl.ds(pl.multiple_of((place ^ offset) * tall, tall), tall)
        ordered[at, :] = part[start : start + tall, :]


def order_grads(place, parts, rows, grad_rows, id_rows, id_cols):
    head_dim = grad_rows.shape[1]
    count = rows // head_dim
    for offset, part in enumerate(parts):
        lines = part[2 * rows :, :].astype(jnp.float32)
        for core in range(2):
            block = (place ^ offset) * 2 + core
            at = pl.ds(pl.multiple_of(block * rows, rows), rows)
            grad_rows[at, :] = part[core * rows : (core + 1) * rows, :]
            first = core * count
            ids = jnp.concatenate(
                [lines[line : line + 1, :] for line in range(first, first + count)], axis=1
            )
            id_rows[block] = jnp.broadcast_to(ids, id_rows.shape[1:])
            id_cols[at, :] = jnp.broadcast_to(ids, (head_dim, rows)).T


def order_rows(place, parts, rows, ordered):
    for offset, part in enumerate(parts):
        at = pl.ds(pl.multiple_of((place ^ offset) * 2 * rows, 2 * rows), 2 * rows)
        ordered[at, :] = part[: 2 * rows, :]


def block_scores(factor, block, rows, queries, keys_in, id_rows, id_cols):
    head_dim = queries.shape[1]
    seen = (block + 1) * rows
    scores = lax.dot_general(
        keys_in[:seen, :],
        queries[block * rows : seen, :],
        contract_last,
        preferred_element_type=jnp.float32,
    )
    ids = id_cols[:seen, :]
    mine = id_rows[block][:1, :]
    same = jnp.concatenate(
        [ids == mine[:, start : start + head_dim] for start in range(0, rows, head_dim)], axis=1
    )
    key_at = lax.broadcasted_iota(jnp.int32, (rows, rows), 0)
    query_at = lax.broadcasted_iota(jnp.int32, (rows, rows), 1)
    last = same[seen - rows :] & (key_at <= query_at)
    allowed = last if block == 0 else jnp.concatenate([same[: seen - rows], last], axis=0)
    return jnp.where(allowed, scores * factor, -jnp.inf)


def value_grad_kernel(factor, chips, rows, place_ref, *refs):
    packed, grads, rank_ref = refs[:chips], refs[chips : 2 * chips], refs[2 * chips]
    refs = refs[2 * chips + 1 :]
    out_refs, probs_ref, sums_ref = refs[:chips], refs[chips], refs[chips + 1]
    queries, keys_in, grad_rows, id_rows, id_cols, total_ref = refs[chips + 2 :]
    head_dim = queries.shape[1]
    clusters = rank_ref.shape[1]
    tall = 2 * rows
    place = place_ref[0]
    in_order(place, packed, 0, queries)
    in_order(place, packed, tall, keys_in)
    order_grads(place, grads, rows, grad_rows, id_rows, id_cols)
    total_ref[...] = jnp.zeros_like(total_ref)
    stored = 0
    for block in range(2 * chips):
        seen = (block + 1) * rows
        scores = block_scores(factor, block, rows, queries, keys_in, id_rows, id_cols)
        top = jnp.max(scores, axis=0, keepdims=True)
        expd = jnp.exp2(scores - top)
        total = jnp.sum(expd, axis=0, keepdims=True)
        probs_low = (expd * (1.0 / total)).astype(jnp.bfloat16)
        probs_ref[stored : stored + seen, :] = probs_low
        stored += seen
        total_ref[:seen, :] += jnp.dot(
            probs_low, grad_rows[block * rows : seen, :], preferred_element_type=jnp.float32
        )
    for offset, out_ref in enumerate(out_refs):
        at = pl.multiple_of((place ^ offset) * tall, tall)
        out_ref[...] = total_ref[pl.ds(at, tall), :].astype(jnp.bfloat16)
    sums = jnp.zeros((clusters, head_dim), jnp.float32)
    cluster_at = lax.broadcasted_iota(jnp.int32, (clusters, rows), 0).astype(jnp.float32)
    for block in range(2 * chips):
        keys_float = keys_in[block * rows : (block + 1) * rows, :].astype(jnp.float32)
        unit = keys_float * lax.rsqrt(
            jnp.sum(keys_float * keys_float, axis=1, keepdims=True) + epsilon
        )
        unit_high = unit.astype(jnp.bfloat16)
        unit_low = (unit - unit_high.astype(jnp.float32)).astype(jnp.bfloat16)
        member = jnp.where(cluster_at == id_rows[block][:1, :], 1.0, 0.0).astype(jnp.bfloat16)
        sums += jnp.dot(member, unit_high, preferred_element_type=jnp.float32)
        sums += jnp.dot(member, unit_low, preferred_element_type=jnp.float32)
    rank_at = lax.broadcasted_iota(jnp.int32, (clusters, clusters), 0)
    ordered = jnp.where(rank_at == rank_ref[...], 1.0, 0.0).astype(jnp.bfloat16)
    ranked = jnp.dot(ordered, sums.astype(jnp.bfloat16), preferred_element_type=jnp.float32)
    sums_ref[...] = ranked.astype(jnp.bfloat16)


def query_grad_kernel(scale, chips, rows, place_ref, *refs):
    packed, valued, grads = refs[:chips], refs[chips : 2 * chips], refs[2 * chips : 3 * chips]
    probs_ref, sums_ref = refs[3 * chips : 3 * chips + 2]
    refs = refs[3 * chips + 2 :]
    grad_refs, out_refs, refs = refs[:chips], refs[chips : chips + 2], refs[chips + 2 :]
    queries, keys_in, values, grad_rows, total_ref, dq_ref, attended_ref = refs
    tall = 2 * rows
    place = place_ref[0]
    in_order(place, packed, 0, queries)
    in_order(place, packed, tall, keys_in)
    in_order(place, valued, 0, values)
    order_rows(place, grads, rows, grad_rows)
    total_ref[...] = jnp.zeros_like(total_ref)
    stored = 0
    for block in range(2 * chips):
        seen = (block + 1) * rows
        mine = slice(block * rows, seen)
        probs_low = probs_ref[stored : stored + seen, :]
        stored += seen
        seen_values = values[:seen, :]
        grad_probs = lax.dot_general(
            seen_values, grad_rows[mine, :], contract_last, preferred_element_type=jnp.float32
        )
        flipped = lax.dot_general(
            seen_values, probs_low, contract_first, preferred_element_type=jnp.float32
        )
        attended_ref[mine, :] = flipped.T.astype(jnp.bfloat16)
        probs = probs_low.astype(jnp.float32)
        weighted = probs * grad_probs
        delta = jnp.sum(weighted, axis=0, keepdims=True)
        grad_low = (weighted - probs * delta).astype(jnp.bfloat16)
        total_ref[:seen, :] += jnp.dot(
            grad_low, queries[mine, :], preferred_element_type=jnp.float32
        )
        flipped = lax.dot_general(
            keys_in[:seen, :], grad_low, contract_first, preferred_element_type=jnp.float32
        )
        dq_ref[mine, :] = (flipped.T * scale).astype(jnp.bfloat16)
    for offset in range(chips):
        at = pl.ds(pl.multiple_of((place ^ offset) * tall, tall), tall)
        grad_refs[offset][:tall, :] = dq_ref[at, :]
        grad_refs[offset][tall:, :] = (total_ref[at, :] * scale).astype(jnp.bfloat16)
    owned = sums_ref.shape[0] // (2 * chips)
    for turn, out_ref in enumerate(out_refs):
        for chip in range(chips):
            shard = chip * 2 + (place_ref[1] ^ turn)
            at = pl.ds(pl.multiple_of(shard * rows, rows), rows)
            out_ref[chip, :rows, :] = attended_ref[at, :]
            at = pl.ds(pl.multiple_of(shard * owned, owned), owned)
            out_ref[chip, rows:, :] = sums_ref[at, :]


def join_kernel(*refs):
    parts, out_ref = refs[1:-1], refs[-1]
    for offset, part in enumerate(parts):
        out_ref[offset] = part[...]


def input_kernel(chips, which, place_ref, *refs):
    valued_other_ref, refs = refs[3 * chips], refs[: 3 * chips] + refs[3 * chips + 1 :]
    weights, (out_ref, gathered_ref) = refs[3 * chips : -2], refs[-2:]
    rows, width = out_ref.shape[0], weights[0].shape[1]
    head_dim = width // (2 * chips)
    for turn in range(2):
        parts = refs[turn * chips : (turn + 1) * chips]
        valued = refs[2 * chips : 3 * chips]
        for offset in range(chips):
            head = (place_ref[1] ^ turn) * chips + (place_ref[0] ^ offset)
            for index in range(3):
                source = parts[offset] if index < 2 else valued[offset]
                if index == 2 and turn == 1:
                    source = valued_other_ref.at[offset]
                at = pl.multiple_of((2 * (index % 2) + place_ref[which]) * rows, rows)
                start = pl.multiple_of(index * width + head * head_dim, head_dim)
                gathered_ref[:, pl.ds(start, head_dim)] = source[pl.ds(at, rows), :]
    flipped = None
    for index in range(3):
        term = lax.dot_general(
            weights[index][...],
            gathered_ref[:, index * width : (index + 1) * width],
            contract_last,
            preferred_element_type=jnp.float32,
        )
        flipped = term if flipped is None else flipped + term
    out_ref[...] = flipped.T.astype(out_ref.dtype)


def attended_kernel(chips, place_ref, *refs):
    parts, (attended_ref, sums_ref) = refs[:chips], refs[chips:]
    rows = attended_ref.shape[0]
    head_dim = sums_ref.shape[2]
    height = parts[0].shape[0] // 2
    for core in range(2):
        start = core * height
        for offset, part in enumerate(parts):
            head = core * chips + (place_ref[0] ^ offset)
            at = pl.multiple_of(head * head_dim, head_dim)
            attended_ref[:, pl.ds(at, head_dim)] = part[start : start + rows, :]
            sums_ref[head] = part[start + rows : start + height, :].astype(jnp.float32)


def sum_kernel(place_ref, first_ref, second_ref, kept_ref, hidden_ref):
    keeps = place_ref[2] == place_ref[1]
    second = jnp.where(keeps, kept_ref[...], second_ref[...]).astype(jnp.float32)
    hidden_ref[...] = (first_ref[...].astype(jnp.float32) + second).astype(jnp.bfloat16)


def by_head(hidden, w_query, w_key, w_value, cluster_rank, assign, d_attended):
    rows = hidden.shape[0]
    count = assign.shape[0]
    chips = count // 2
    half, width = w_query.shape
    head_dim = width // count
    tokens = count * rows
    clusters = cluster_rank.shape[0]
    owned = clusters // count
    scale = head_dim ** (-0.5)
    factor = scale * log2_e
    smem = pl.BlockSpec(memory_space=pltpu.SMEM)
    vmem = pl.BlockSpec(memory_space=pltpu.VMEM)
    anywhere = pl.BlockSpec(memory_space=pl.ANY)
    params = pltpu.CompilerParams(vmem_limit_bytes=32 * mebi)
    project_params = pltpu.CompilerParams(vmem_limit_bytes=32 * mebi)
    swap = [(0, 1), (1, 0)]
    chip, side, column = (lax.axis_index(name) for name in ("seq", "sub", "head"))
    place = jnp.stack([chip, side, column, 1 - column])

    def call(kernel, outs, *operands, scratch=(), hbm=0, limits=params, takes=1):
        return pl.pallas_call(
            kernel,
            out_shape=outs,
            in_specs=[smem] + [vmem] * (len(operands) - 1 - hbm) + [anywhere] * hbm,
            out_specs=jax.tree.map(lambda _: vmem, outs),
            scratch_shapes=list(scratch),
            compiler_params=limits,
            cost_estimate=pl.CostEstimate(
                flops=int(takes * 1.15e9), bytes_accessed=mebi, transcendentals=0
            ),
        )(*operands)

    def low(*shape):
        return jax.ShapeDtypeStruct(shape, jnp.bfloat16)

    def buffers(height):
        return (low(height, head_dim),) * chips

    def exchange(parts):
        moved = {
            offset: lax.ppermute(parts[offset], "seq", [(at, at ^ offset) for at in range(chips)])
            for offset in (2, 3, 1)
        }
        return (parts[0], moved[1], moved[2], moved[3])

    def to_sibling(piece):
        return lax.ppermute(piece, "sub", swap)

    def stay(array):
        return pltpu.with_memory_space_constraint(array, pltpu.HBM)

    hidden_other = to_sibling(hidden)
    block = low(chips, rows + id_lines(2 * rows, head_dim), head_dim)
    grads_mine, grads_theirs = call(
        pack_kernel,
        (block, block),
        place,
        stay(d_attended),
        stay(assign),
        scratch=[pltpu.VMEM(assign.shape, jnp.int32), pltpu.SemaphoreType.DMA((count + 1,))],
        hbm=2,
    )
    grads_other = to_sibling(grads_theirs)

    def project(turn, weights, tokens_other, *arrived):
        number = len(weights)
        outs = buffers(2 * number * rows) if turn == 0 else low(number, 2 * rows, width // 2)

        return call(
            partial(project_kernel, number, turn),
            outs,
            place,
            *arrived,
            stay(hidden),
            tokens_other,
            *(stay(weight) for weight in weights),
            scratch=[
                pltpu.VMEM((2 * rows, half), jnp.bfloat16),
                pltpu.VMEM((number, half, width // 2), jnp.bfloat16),
                pltpu.VMEM((2 * rows, width // 2), jnp.bfloat16),
                pltpu.SemaphoreType.DMA((number, 4)),
                pltpu.SemaphoreType.DMA((2,)),
            ],
            hbm=2 + number,
            limits=project_params,
            takes=(8 if number == 2 else 0.1) if turn == 0 else 0.1,
        )

    early, late = (w_query, w_key), (w_value,)
    fetched = call(
        partial(fetch_kernel, 1),
        pltpu.VMEM((2, half, width // 2), jnp.bfloat16),
        place,
        *(stay(weight) for weight in early),
        scratch=[pltpu.SemaphoreType.DMA((2, 4))],
        hbm=2,
    )
    *merged, early_part = call(
        opening_kernel,
        (*buffers(rows + block.shape[1]), low(2, 2 * rows, width // 2)),
        place,
        fetched,
        grads_mine,
        grads_other,
        stay(hidden),
        hidden_other,
        scratch=[pltpu.VMEM((2 * rows, half), jnp.bfloat16), pltpu.SemaphoreType.DMA((2,))],
        hbm=2,
        takes=0.1,
    )
    grads = exchange(merged)
    early_arrived = to_sibling(early_part)
    early_projected = project(0, early, hidden_other, early_arrived)
    packed = exchange(early_projected)
    late_tokens, *_ = lax.optimization_barrier((hidden_other, early_arrived))
    late_arrived = to_sibling(project(1, late, late_tokens))
    late_arrived, *_ = lax.optimization_barrier((late_arrived, grads[2], grads[3]))
    late_projected = project(0, late, late_tokens, late_arrived)
    valued = exchange(late_projected)
    packed = lax.optimization_barrier((*packed, late_projected[0]))[:chips]

    def held(kind):
        return pltpu.VMEM((tokens, head_dim), kind)

    id_scratch = [pltpu.VMEM((count, 8, rows), jnp.float32), held(jnp.float32)]
    *value_grads, probs, sums = call(
        partial(value_grad_kernel, factor, chips, rows),
        (
            *buffers(2 * rows),
            pltpu.VMEM((count * (count + 1) // 2 * rows, rows), jnp.bfloat16),
            low(clusters, head_dim),
        ),
        place,
        *packed,
        *grads,
        cluster_rank.reshape(1, clusters),
        scratch=[held(jnp.bfloat16)] * 3 + id_scratch + [held(jnp.float32)],
        takes=7,
    )
    value_back = exchange(value_grads)
    results = call(
        partial(query_grad_kernel, scale, chips, rows),
        (*buffers(4 * rows), *(low(chips, rows + owned, head_dim),) * 2),
        place,
        *packed,
        *valued,
        *grads,
        probs,
        sums,
        scratch=[held(jnp.bfloat16)] * 4
        + [held(jnp.float32)]
        + [held(jnp.bfloat16)] * 2,
        takes=10,
    )
    *ready, _ = lax.optimization_barrier((*results[:chips], value_back[2]))
    back = exchange(ready)

    attended_mine, attended_theirs = results[chips:]
    outputs = call(
        merge_kernel, buffers(2 * (rows + owned)), place, attended_mine, to_sibling(attended_theirs)
    )
    early_back, _ = lax.optimization_barrier((back[2], outputs[0]))
    back_other = tuple(
        to_sibling(early_back if offset == 2 else part) for offset, part in enumerate(back)
    )
    value_other = to_sibling(
        call(join_kernel, low(chips, 2 * rows, head_dim), place, *value_back)
    )

    def input_part(which, place):
        return call(
            partial(input_kernel, chips, which),
            low(rows, half),
            place,
            *back,
            *back_other,
            *value_back,
            value_other,
            w_query,
            w_key,
            w_value,
            scratch=[pltpu.VMEM((rows, 3 * width), jnp.bfloat16)],
        )

    *outputs, _, _ = lax.optimization_barrier((*outputs, back[2], back[3]))
    returned = exchange(outputs)
    square = ("head", "sub")
    crossing = input_part(3, place)
    first = lax.ppermute(crossing, square, [(0, 1), (1, 3), (3, 2), (2, 0)])
    kept = input_part(2, lax.optimization_barrier((place, crossing))[0])
    second = lax.ppermute(kept, square, [(1, 2), (2, 1)])
    attended, centroid_sums = call(
        partial(attended_kernel, chips),
        (low(rows, width), jax.ShapeDtypeStruct((count, owned, head_dim), jnp.float32)),
        place,
        *returned,
        takes=8,
    )
    first, second, _ = lax.optimization_barrier((first, second, attended))
    d_hidden = call(sum_kernel, low(rows, half), place, first, second, kept)
    return (attended, d_hidden, centroid_sums)


def per_device(hidden, w_query, w_key, w_value, cluster_rank, assign, d_attended):
    chips = lax.axis_size("seq")
    fits = chips == 4 and lax.axis_size("sub") == 2 and lax.axis_size("head") == 2
    plan = by_head if fits and assign.shape[0] == 2 * chips else by_owner
    return plan(hidden, w_query, w_key, w_value, cluster_rank, assign, d_attended)


def solution(mesh):
    placed = (
        P(("groups", "seq", "sub"), None),
        P("sub", "head"),
        P("sub", "head"),
        P("sub", "head"),
        P("groups"),
        P("head", ("groups", "seq", "sub")),
        P(("groups", "seq", "sub"), "head"),
    )
    return jax.shard_map(
        per_device,
        mesh=mesh,
        in_specs=placed,
        out_specs=(
            P(("groups", "seq", "sub"), "head"),
            P(("groups", "seq", "sub"), "head"),
            P("head", ("groups", "seq", "sub"), None),
        ),
        check_vma=False,
    )
```

```python
from functools import partial

import jax
import jax.numpy as jnp
from jax import lax
from jax.experimental import pallas as pl
from jax.experimental.pallas import tpu as pltpu
from jax.sharding import PartitionSpec as P

epsilon = 1e-06


def keep_mask(filled, cluster_ids, positions):
    count = filled.shape[0]
    same = filled[:, None] & filled[None, :] & (cluster_ids[:, None] == cluster_ids[None, :])
    causal = positions[None, :] <= positions[:, None]
    diagonal = jnp.arange(count)[:, None] == jnp.arange(count)[None, :]
    return same & causal | diagonal


def head_forward(packed, scale):
    queries, keys_in, values, filled, cluster_ids, positions = packed
    scores = (
        lax.dot_general(
            queries, keys_in, (((1,), (1,)), ((), ())), preferred_element_type=jnp.float32
        )
        * scale
    )
    allowed = keep_mask(filled, cluster_ids, positions)
    row_top = jnp.max(jnp.where(allowed, scores, -jnp.inf), axis=1)
    expd = jnp.where(allowed, jnp.exp(scores - row_top[:, None]), 0.0)
    row_total = jnp.sum(expd, axis=1)
    probs_low = (expd / row_total[:, None]).astype(jnp.bfloat16)
    outputs = jnp.dot(probs_low, values, preferred_element_type=jnp.float32).astype(jnp.bfloat16)
    return (outputs, row_top, row_total)


def head_backward(packed, scale):
    queries, keys_in, values, grads_in, filled, cluster_ids, positions, row_top, row_total = packed
    contract_last = (((1,), (1,)), ((), ()))
    contract_first = (((0,), (0,)), ((), ()))
    scores = (
        lax.dot_general(queries, keys_in, contract_last, preferred_element_type=jnp.float32) * scale
    )
    allowed = keep_mask(filled, cluster_ids, positions)
    probs = jnp.where(allowed, jnp.exp(scores - row_top[:, None]), 0.0) / row_total[:, None]
    probs_low = probs.astype(jnp.bfloat16)
    grad_probs = lax.dot_general(
        grads_in, values, contract_last, preferred_element_type=jnp.float32
    )
    delta_rows = jnp.sum(probs * grad_probs, axis=1)
    grad_low = (probs * (grad_probs - delta_rows[:, None]) * scale).astype(jnp.bfloat16)
    grad_query = jnp.dot(grad_low, keys_in, preferred_element_type=jnp.float32).astype(jnp.bfloat16)
    grad_key = lax.dot_general(
        grad_low, queries, contract_first, preferred_element_type=jnp.float32
    ).astype(jnp.bfloat16)
    grad_value = lax.dot_general(
        probs_low, grads_in, contract_first, preferred_element_type=jnp.float32
    ).astype(jnp.bfloat16)
    return (grad_query, grad_key, grad_value)


def by_owner(hidden, w_query, w_key, w_value, cluster_rank, assign, d_attended):
    tok_rows = hidden.shape[0]
    heads_here = assign.shape[0]
    head_dim = w_query.shape[1] // heads_here
    clusters = cluster_rank.shape[0]
    seq_count = lax.axis_size("seq")
    sub_count = lax.axis_size("sub")
    owners = seq_count * sub_count
    capacity = 2 * tok_rows // owners
    slot_count = owners * capacity
    per_owner = clusters // owners
    scale = head_dim ** (-0.5)
    pieces = (
        lax.all_gather(w_query, "sub", axis=0, tiled=True),
        lax.all_gather(w_key, "sub", axis=0, tiled=True),
        lax.all_gather(w_value, "sub", axis=0, tiled=True),
    )
    projected = tuple(
        (
            jnp.dot(hidden, weight_piece, preferred_element_type=jnp.float32)
            for weight_piece in pieces
        )
    )

    def split_heads(matrix):
        return (
            matrix.astype(jnp.bfloat16).reshape(tok_rows, heads_here, head_dim).transpose(1, 0, 2)
        )

    queries, keys_all, values = tuple((split_heads(matrix) for matrix in projected))
    cluster_range = jnp.arange(clusters, dtype=jnp.int32)
    rank_tok = jnp.sum(jnp.where(assign[:, :, None] == cluster_range, cluster_rank, 0), axis=2)
    owner_ids = rank_tok // per_owner
    owner_hot = (owner_ids[:, :, None] == jnp.arange(owners, dtype=jnp.int32)).astype(jnp.int32)
    within = jnp.sum(owner_hot * (jnp.cumsum(owner_hot, axis=1) - 1), axis=2)
    slot_tok = owner_ids * capacity + within
    token_ids = jnp.arange(tok_rows, dtype=jnp.int32)
    slot_range = jnp.arange(slot_count, dtype=jnp.int32)
    slot_match = slot_tok[:, None, :] == slot_range[None, :, None]
    slot_hot = slot_match.astype(jnp.bfloat16)

    def to_slots(rows_in):
        kept = jnp.einsum(
            "hst,htd->hsd", slot_hot, rows_in, preferred_element_type=jnp.float32
        ).astype(jnp.bfloat16)
        return kept.reshape(heads_here, owners, capacity, head_dim)

    def from_slots(slotted):
        flat_slots = slotted.reshape(heads_here, slot_count, head_dim)
        return jnp.einsum(
            "hst,hsd->htd", slot_hot, flat_slots, preferred_element_type=jnp.float32
        ).astype(jnp.bfloat16)

    def exchange_three(first, second, third):
        return (
            lax.all_to_all(first, ("seq", "sub"), split_axis=1, concat_axis=1, tiled=True),
            lax.all_to_all(second, ("seq", "sub"), split_axis=1, concat_axis=1, tiled=True),
            lax.all_to_all(third, ("seq", "sub"), split_axis=1, concat_axis=1, tiled=True),
        )

    sent = exchange_three(to_slots(queries), to_slots(keys_all), to_slots(values))
    tag_tok = assign * tok_rows + token_ids
    slot_tag = jnp.sum(jnp.where(slot_match, tag_tok[:, None, :] + 1, 0), axis=2) - 1
    tags = lax.all_to_all(
        slot_tag.reshape(heads_here, owners, capacity),
        ("seq", "sub"),
        split_axis=1,
        concat_axis=1,
        tiled=True,
    )
    tags = tags.reshape(heads_here, slot_count)
    owner_q, owner_k, owner_v = tuple(
        (member.reshape(heads_here, slot_count, head_dim) for member in sent)
    )
    filled = tags >= 0
    cluster_ids = jnp.where(filled, tags // tok_rows, -1)
    positions = slot_range // capacity * tok_rows + tags % tok_rows
    outputs, row_top, row_total = lax.map(
        partial(head_forward, scale=scale),
        (owner_q, owner_k, owner_v, filled, cluster_ids, positions),
    )
    returned = lax.all_to_all(
        outputs.reshape(heads_here, owners, capacity, head_dim),
        ("seq", "sub"),
        split_axis=1,
        concat_axis=1,
        tiled=True,
    )

    def merge_heads(slotted):
        return from_slots(slotted).transpose(1, 0, 2).reshape(tok_rows, heads_here * head_dim)

    attended = merge_heads(returned)
    grads_tok = d_attended.reshape(tok_rows, heads_here, head_dim).transpose(1, 0, 2)
    owner_g = lax.all_to_all(
        to_slots(grads_tok), ("seq", "sub"), split_axis=1, concat_axis=1, tiled=True
    ).reshape(heads_here, slot_count, head_dim)
    grad_q, grad_k, grad_v = lax.map(
        partial(head_backward, scale=scale),
        (owner_q, owner_k, owner_v, owner_g, filled, cluster_ids, positions, row_top, row_total),
    )
    shape_four = (heads_here, owners, capacity, head_dim)
    back = exchange_three(
        grad_q.reshape(shape_four), grad_k.reshape(shape_four), grad_v.reshape(shape_four)
    )
    token_grads = tuple((merge_heads(member) for member in back))
    pieces = lax.all_gather((w_query, w_key, w_value), "sub", axis=0, tiled=True)
    terms = [
        jnp.einsum("tc,rc->tr", grad_rows_in, weight_piece, preferred_element_type=jnp.float32)
        for grad_rows_in, weight_piece in zip(token_grads, pieces)
    ]
    partial_grad = terms[0] + terms[1] + terms[2]
    d_hidden = lax.psum_scatter(
        partial_grad.astype(jnp.bfloat16), "head", scatter_dimension=1, tiled=True
    )
    keys_float = keys_all.astype(jnp.float32)
    unit_keys = keys_float * lax.rsqrt(
        jnp.sum(keys_float * keys_float, axis=2, keepdims=True) + epsilon
    )
    member_hot = (rank_tok[:, :, None] == cluster_range).astype(jnp.float32)
    local_sums = jnp.einsum("htr,htd->hrd", member_hot, unit_keys, precision=lax.Precision.HIGHEST)
    centroid_sums = lax.psum_scatter(
        local_sums.astype(jnp.bfloat16), ("seq", "sub"), scatter_dimension=1, tiled=True
    ).astype(jnp.float32)
    return (attended, d_hidden, centroid_sums)


contract_last = (((1,), (1,)), ((), ()))
contract_first = (((0,), (0,)), ((), ()))
log2_e = 1.4426950408889634
mebi = 1024 * 1024


def id_lines(rows, head_dim):
    return -(-(rows // head_dim) // 16) * 16


def id_tile(side, ids, spare):
    head_dim = 128 if ids.shape[1] % 128 == 0 else ids.shape[1]
    lines = [ids[:, at : at + head_dim] for at in range(0, ids.shape[1], head_dim)]
    gap = [jnp.zeros((len(lines), head_dim), jnp.float32)]
    rest = [jnp.zeros((spare - len(lines), head_dim), jnp.float32)]
    first = jnp.concatenate(lines + gap + rest, axis=0)
    second = jnp.concatenate(gap + lines + rest, axis=0)
    return jnp.where(side == 0, first, second).astype(jnp.bfloat16)


def pack_kernel(place_ref, grads_ref, assign_ref, theirs_ref, ids_ref, sems):
    chips, padded, head_dim = theirs_ref.shape
    rows = grads_ref.shape[0]
    spare = padded - rows - rows // head_dim
    copies = [pltpu.make_async_copy(assign_ref, ids_ref, sems.at[chips])]
    for chip in range(chips):
        head = (1 - place_ref[1]) * chips + chip
        at = pl.multiple_of(head * head_dim, head_dim)
        copies.append(
            pltpu.make_async_copy(
                grads_ref.at[:, pl.ds(at, head_dim)],
                theirs_ref.at[chip, pl.ds(0, rows)],
                sems.at[chip],
            )
        )
    for copy in copies:
        copy.start()
    copies[0].wait()
    for chip in range(chips):
        head = (1 - place_ref[1]) * chips + chip
        ids = ids_ref[pl.ds(head, 1), :].astype(jnp.float32)
        theirs_ref[chip, rows:, :] = id_tile(place_ref[1], ids, spare)
    for copy in copies[1:]:
        copy.wait()


def merge_kernel(place_ref, mine_ref, theirs_ref, *out_refs):
    height = mine_ref.shape[1]
    for turn, held_ref in enumerate((mine_ref, theirs_ref)):
        at = pl.ds(pl.multiple_of((place_ref[1] ^ turn) * height, height), height)
        for offset, out_ref in enumerate(out_refs):
            out_ref[at, :] = held_ref[place_ref[0] ^ offset]


def fetch_columns(half, weights, held_ref, sems):
    chunks = sems.shape[1]
    columns = held_ref.shape[2]
    rows = held_ref.shape[1] // chunks
    at = pl.ds(pl.multiple_of(half * columns, columns), columns)
    copies = []
    for index, weight in enumerate(weights):
        for chunk in range(chunks):
            lines = pl.ds(chunk * rows, rows)
            copy = pltpu.make_async_copy(
                weight.at[lines, at], held_ref.at[index, lines], sems.at[index, chunk]
            )
            copy.start()
            copies.append(copy)
    return copies


def project_kernel(count, turn, place_ref, *refs):
    if turn == 0:
        arrived_ref, refs = refs[0], refs[1:]
    tokens, weights, refs = refs[:2], refs[2 : 2 + count], refs[2 + count :]
    out_refs, (joined_ref, held_ref, low_ref, sems, token_sems) = refs[:-5], refs[-5:]
    side = place_ref[1]
    tall, depth = joined_ref.shape
    rows = tall // 2
    near = pl.ds(pl.multiple_of(side * depth, depth), depth)
    joins = []
    for core, source in enumerate(tokens):
        at = pl.ds(pl.multiple_of((side ^ core) * rows, rows), rows)
        joins.append(
            pltpu.make_async_copy(source.at[:, near], joined_ref.at[at], token_sems.at[core])
        )
        joins[core].start()
    copies = fetch_columns(side ^ turn, weights, held_ref, sems)
    for copy in joins:
        copy.wait()
    chunks = sems.shape[1]
    for index in range(count):
        for chunk in range(chunks):
            copies[index * chunks + chunk].wait()
        total = jnp.dot(joined_ref[...], held_ref[index], preferred_element_type=jnp.float32)
        if turn == 1:
            out_refs[0][index] = total.astype(jnp.bfloat16)
            continue
        low_ref[...] = (total + arrived_ref[index].astype(jnp.float32)).astype(jnp.bfloat16)
        for offset, out_ref in enumerate(out_refs):
            head_dim = out_ref.shape[1]
            at = pl.multiple_of((place_ref[0] ^ offset) * head_dim, head_dim)
            out_ref[index * tall : (index + 1) * tall, :] = low_ref[:, pl.ds(at, head_dim)]


def fetch_kernel(turn, place_ref, *refs):
    weights, (held_ref, sems) = refs[:-2], refs[-2:]
    for copy in fetch_columns(place_ref[1] ^ turn, weights, held_ref, sems):
        copy.wait()


def opening_kernel(place_ref, held_ref, theirs_ref, *refs):
    tokens, (grads_ref, assign_ref), refs = refs[:2], refs[2:4], refs[4:]
    out_refs, (part_ref, joined_ref, ids_ref, sems, grad_sems) = refs[:-5], refs[-5:]
    side = place_ref[1]
    chips = len(out_refs)
    tall, depth = joined_ref.shape
    rows = tall // 2
    head_dim = out_refs[0].shape[1]
    near = pl.ds(pl.multiple_of(side * depth, depth), depth)
    joins = []
    for core, source in enumerate(tokens):
        at = pl.ds(pl.multiple_of((side ^ core) * rows, rows), rows)
        joins.append(pltpu.make_async_copy(source.at[:, near], joined_ref.at[at], sems.at[core]))
        joins[core].start()
    copies = [pltpu.make_async_copy(assign_ref, ids_ref, grad_sems.at[chips])]
    mine = pl.ds(pl.multiple_of(side * rows, rows), rows)
    other = pl.ds(pl.multiple_of((1 - side) * rows, rows), rows)
    for offset, out_ref in enumerate(out_refs):
        head = side * chips + (place_ref[0] ^ offset)
        at = pl.multiple_of(head * head_dim, head_dim)
        copies.append(
            pltpu.make_async_copy(
                grads_ref.at[:, pl.ds(at, head_dim)], out_ref.at[mine], grad_sems.at[offset]
            )
        )
    for copy in copies:
        copy.start()
    copies[0].wait()
    for offset, out_ref in enumerate(out_refs):
        chip = place_ref[0] ^ offset
        ids = ids_ref[pl.ds(side * chips + chip, 1), :].astype(jnp.float32)
        spare = theirs_ref.shape[1] - rows - rows // head_dim
        out_ref[other, :] = theirs_ref[chip, :rows, :]
        out_ref[tall:, :] = theirs_ref[chip, rows:, :] + id_tile(side, ids, spare)
    for copy in joins:
        copy.wait()
    for index in range(held_ref.shape[0]):
        total = jnp.dot(joined_ref[...], held_ref[index], preferred_element_type=jnp.float32)
        part_ref[index] = total.astype(jnp.bfloat16)
    for copy in copies[1:]:
        copy.wait()


def in_order(place, parts, start, ordered):
    for offset, part in enumerate(parts):
        tall = ordered.shape[0] // len(parts)
        at = pl.ds(pl.multiple_of((place ^ offset) * tall, tall), tall)
        ordered[at, :] = part[start : start + tall, :]


def order_grads(place, parts, rows, grad_rows, id_rows, id_cols):
    head_dim = grad_rows.shape[1]
    count = rows // head_dim
    for offset, part in enumerate(parts):
        lines = part[2 * rows :, :].astype(jnp.float32)
        for core in range(2):
            block = (place ^ offset) * 2 + core
            at = pl.ds(pl.multiple_of(block * rows, rows), rows)
            grad_rows[at, :] = part[core * rows : (core + 1) * rows, :]
            first = core * count
            ids = jnp.concatenate(
                [lines[line : line + 1, :] for line in range(first, first + count)], axis=1
            )
            id_rows[block] = jnp.broadcast_to(ids, id_rows.shape[1:])
            id_cols[at, :] = jnp.broadcast_to(ids, (head_dim, rows)).T


def order_rows(place, parts, rows, ordered):
    for offset, part in enumerate(parts):
        at = pl.ds(pl.multiple_of((place ^ offset) * 2 * rows, 2 * rows), 2 * rows)
        ordered[at, :] = part[: 2 * rows, :]


def block_scores(factor, block, rows, queries, keys_in, id_rows, id_cols):
    head_dim = queries.shape[1]
    seen = (block + 1) * rows
    scores = lax.dot_general(
        keys_in[:seen, :],
        queries[block * rows : seen, :],
        contract_last,
        preferred_element_type=jnp.float32,
    )
    ids = id_cols[:seen, :]
    mine = id_rows[block][:1, :]
    same = jnp.concatenate(
        [ids == mine[:, start : start + head_dim] for start in range(0, rows, head_dim)], axis=1
    )
    key_at = lax.broadcasted_iota(jnp.int32, (rows, rows), 0)
    query_at = lax.broadcasted_iota(jnp.int32, (rows, rows), 1)
    last = same[seen - rows :] & (key_at <= query_at)
    allowed = last if block == 0 else jnp.concatenate([same[: seen - rows], last], axis=0)
    return jnp.where(allowed, scores * factor, -jnp.inf)


def value_grad_kernel(factor, chips, rows, place_ref, *refs):
    packed, grads, rank_ref = refs[:chips], refs[chips : 2 * chips], refs[2 * chips]
    refs = refs[2 * chips + 1 :]
    out_refs, probs_ref, sums_ref = refs[:chips], refs[chips], refs[chips + 1]
    queries, keys_in, grad_rows, id_rows, id_cols, total_ref = refs[chips + 2 :]
    head_dim = queries.shape[1]
    clusters = rank_ref.shape[1]
    tall = 2 * rows
    place = place_ref[0]
    in_order(place, packed, 0, queries)
    in_order(place, packed, tall, keys_in)
    order_grads(place, grads, rows, grad_rows, id_rows, id_cols)
    total_ref[...] = jnp.zeros_like(total_ref)
    stored = 0
    for block in range(2 * chips):
        seen = (block + 1) * rows
        scores = block_scores(factor, block, rows, queries, keys_in, id_rows, id_cols)
        top = jnp.max(scores, axis=0, keepdims=True)
        expd = jnp.exp2(scores - top)
        total = jnp.sum(expd, axis=0, keepdims=True)
        probs_low = (expd * (1.0 / total)).astype(jnp.bfloat16)
        probs_ref[stored : stored + seen, :] = probs_low
        stored += seen
        total_ref[:seen, :] += jnp.dot(
            probs_low, grad_rows[block * rows : seen, :], preferred_element_type=jnp.float32
        )
    for offset, out_ref in enumerate(out_refs):
        at = pl.multiple_of((place ^ offset) * tall, tall)
        out_ref[...] = total_ref[pl.ds(at, tall), :].astype(jnp.bfloat16)
    sums = jnp.zeros((clusters, head_dim), jnp.float32)
    cluster_at = lax.broadcasted_iota(jnp.int32, (clusters, rows), 0).astype(jnp.float32)
    for block in range(2 * chips):
        keys_float = keys_in[block * rows : (block + 1) * rows, :].astype(jnp.float32)
        unit = keys_float * lax.rsqrt(
            jnp.sum(keys_float * keys_float, axis=1, keepdims=True) + epsilon
        )
        unit_high = unit.astype(jnp.bfloat16)
        unit_low = (unit - unit_high.astype(jnp.float32)).astype(jnp.bfloat16)
        member = jnp.where(cluster_at == id_rows[block][:1, :], 1.0, 0.0).astype(jnp.bfloat16)
        sums += jnp.dot(member, unit_high, preferred_element_type=jnp.float32)
        sums += jnp.dot(member, unit_low, preferred_element_type=jnp.float32)
    rank_at = lax.broadcasted_iota(jnp.int32, (clusters, clusters), 0)
    ordered = jnp.where(rank_at == rank_ref[...], 1.0, 0.0).astype(jnp.bfloat16)
    ranked = jnp.dot(ordered, sums.astype(jnp.bfloat16), preferred_element_type=jnp.float32)
    sums_ref[...] = ranked.astype(jnp.bfloat16)


def query_grad_kernel(scale, chips, rows, place_ref, *refs):
    packed, valued, grads = refs[:chips], refs[chips : 2 * chips], refs[2 * chips : 3 * chips]
    probs_ref, sums_ref = refs[3 * chips : 3 * chips + 2]
    refs = refs[3 * chips + 2 :]
    grad_refs, out_refs, refs = refs[:chips], refs[chips : chips + 2], refs[chips + 2 :]
    queries, keys_in, values, grad_rows, total_ref, dq_ref, attended_ref = refs
    tall = 2 * rows
    place = place_ref[0]
    in_order(place, packed, 0, queries)
    in_order(place, packed, tall, keys_in)
    in_order(place, valued, 0, values)
    order_rows(place, grads, rows, grad_rows)
    total_ref[...] = jnp.zeros_like(total_ref)
    stored = 0
    for block in range(2 * chips):
        seen = (block + 1) * rows
        mine = slice(block * rows, seen)
        probs_low = probs_ref[stored : stored + seen, :]
        stored += seen
        seen_values = values[:seen, :]
        grad_probs = lax.dot_general(
            seen_values, grad_rows[mine, :], contract_last, preferred_element_type=jnp.float32
        )
        flipped = lax.dot_general(
            seen_values, probs_low, contract_first, preferred_element_type=jnp.float32
        )
        attended_ref[mine, :] = flipped.T.astype(jnp.bfloat16)
        probs = probs_low.astype(jnp.float32)
        weighted = probs * grad_probs
        delta = jnp.sum(weighted, axis=0, keepdims=True)
        grad_low = (weighted - probs * delta).astype(jnp.bfloat16)
        total_ref[:seen, :] += jnp.dot(
            grad_low, queries[mine, :], preferred_element_type=jnp.float32
        )
        flipped = lax.dot_general(
            keys_in[:seen, :], grad_low, contract_first, preferred_element_type=jnp.float32
        )
        dq_ref[mine, :] = (flipped.T * scale).astype(jnp.bfloat16)
    for offset in range(chips):
        at = pl.ds(pl.multiple_of((place ^ offset) * tall, tall), tall)
        grad_refs[offset][:tall, :] = dq_ref[at, :]
        grad_refs[offset][tall:, :] = (total_ref[at, :] * scale).astype(jnp.bfloat16)
    owned = sums_ref.shape[0] // (2 * chips)
    for turn, out_ref in enumerate(out_refs):
        for chip in range(chips):
            shard = chip * 2 + (place_ref[1] ^ turn)
            at = pl.ds(pl.multiple_of(shard * rows, rows), rows)
            out_ref[chip, :rows, :] = attended_ref[at, :]
            at = pl.ds(pl.multiple_of(shard * owned, owned), owned)
            out_ref[chip, rows:, :] = sums_ref[at, :]


def join_kernel(*refs):
    parts, out_ref = refs[1:-1], refs[-1]
    for offset, part in enumerate(parts):
        out_ref[offset] = part[...]


def input_kernel(chips, which, place_ref, *refs):
    valued_other_ref, refs = refs[3 * chips], refs[: 3 * chips] + refs[3 * chips + 1 :]
    weights, (out_ref, gathered_ref) = refs[3 * chips : -2], refs[-2:]
    rows, width = out_ref.shape[0], weights[0].shape[1]
    head_dim = width // (2 * chips)
    for turn in range(2):
        parts = refs[turn * chips : (turn + 1) * chips]
        valued = refs[2 * chips : 3 * chips]
        for offset in range(chips):
            head = (place_ref[1] ^ turn) * chips + (place_ref[0] ^ offset)
            for index in range(3):
                source = parts[offset] if index < 2 else valued[offset]
                if index == 2 and turn == 1:
                    source = valued_other_ref.at[offset]
                at = pl.multiple_of((2 * (index % 2) + place_ref[which]) * rows, rows)
                start = pl.multiple_of(index * width + head * head_dim, head_dim)
                gathered_ref[:, pl.ds(start, head_dim)] = source[pl.ds(at, rows), :]
    flipped = None
    for index in range(3):
        term = lax.dot_general(
            weights[index][...],
            gathered_ref[:, index * width : (index + 1) * width],
            contract_last,
            preferred_element_type=jnp.float32,
        )
        flipped = term if flipped is None else flipped + term
    out_ref[...] = flipped.T.astype(out_ref.dtype)


def attended_kernel(chips, place_ref, *refs):
    parts, (attended_ref, sums_ref) = refs[:chips], refs[chips:]
    rows = attended_ref.shape[0]
    head_dim = sums_ref.shape[2]
    height = parts[0].shape[0] // 2
    for core in range(2):
        start = core * height
        for offset, part in enumerate(parts):
            head = core * chips + (place_ref[0] ^ offset)
            at = pl.multiple_of(head * head_dim, head_dim)
            attended_ref[:, pl.ds(at, head_dim)] = part[start : start + rows, :]
            sums_ref[head] = part[start + rows : start + height, :].astype(jnp.float32)


def sum_kernel(place_ref, first_ref, second_ref, kept_ref, hidden_ref):
    keeps = place_ref[2] == place_ref[1]
    second = jnp.where(keeps, kept_ref[...], second_ref[...]).astype(jnp.float32)
    hidden_ref[...] = (first_ref[...].astype(jnp.float32) + second).astype(jnp.bfloat16)


def by_head(hidden, w_query, w_key, w_value, cluster_rank, assign, d_attended):
    rows = hidden.shape[0]
    count = assign.shape[0]
    chips = count // 2
    half, width = w_query.shape
    head_dim = width // count
    tokens = count * rows
    clusters = cluster_rank.shape[0]
    owned = clusters // count
    scale = head_dim ** (-0.5)
    factor = scale * log2_e
    smem = pl.BlockSpec(memory_space=pltpu.SMEM)
    vmem = pl.BlockSpec(memory_space=pltpu.VMEM)
    anywhere = pl.BlockSpec(memory_space=pl.ANY)
    params = pltpu.CompilerParams(vmem_limit_bytes=32 * mebi)
    project_params = pltpu.CompilerParams(vmem_limit_bytes=32 * mebi)
    swap = [(0, 1), (1, 0)]
    chip, side, column = (lax.axis_index(name) for name in ("seq", "sub", "head"))
    place = jnp.stack([chip, side, column, 1 - column])

    def call(kernel, outs, *operands, scratch=(), hbm=0, limits=params, takes=1):
        return pl.pallas_call(
            kernel,
            out_shape=outs,
            in_specs=[smem] + [vmem] * (len(operands) - 1 - hbm) + [anywhere] * hbm,
            out_specs=jax.tree.map(lambda _: vmem, outs),
            scratch_shapes=list(scratch),
            compiler_params=limits,
            cost_estimate=pl.CostEstimate(
                flops=int(takes * 1.15e9), bytes_accessed=mebi, transcendentals=0
            ),
        )(*operands)

    def low(*shape):
        return jax.ShapeDtypeStruct(shape, jnp.bfloat16)

    def buffers(height):
        return (low(height, head_dim),) * chips

    def exchange(parts):
        moved = {
            offset: lax.ppermute(parts[offset], "seq", [(at, at ^ offset) for at in range(chips)])
            for offset in (2, 3, 1)
        }
        return (parts[0], moved[1], moved[2], moved[3])

    def to_sibling(piece):
        return lax.ppermute(piece, "sub", swap)

    def stay(array):
        return pltpu.with_memory_space_constraint(array, pltpu.HBM)

    hidden_other = to_sibling(hidden)
    block = low(chips, rows + id_lines(2 * rows, head_dim), head_dim)
    grads_theirs = call(
        pack_kernel,
        block,
        place,
        stay(d_attended),
        stay(assign),
        scratch=[pltpu.VMEM(assign.shape, jnp.int32), pltpu.SemaphoreType.DMA((chips + 1,))],
        hbm=2,
    )
    grads_other = to_sibling(grads_theirs)

    def project(turn, weights, tokens_other, *arrived):
        number = len(weights)
        outs = buffers(2 * number * rows) if turn == 0 else low(number, 2 * rows, width // 2)

        return call(
            partial(project_kernel, number, turn),
            outs,
            place,
            *arrived,
            stay(hidden),
            tokens_other,
            *(stay(weight) for weight in weights),
            scratch=[
                pltpu.VMEM((2 * rows, half), jnp.bfloat16),
                pltpu.VMEM((number, half, width // 2), jnp.bfloat16),
                pltpu.VMEM((2 * rows, width // 2), jnp.bfloat16),
                pltpu.SemaphoreType.DMA((number, 4)),
                pltpu.SemaphoreType.DMA((2,)),
            ],
            hbm=2 + number,
            limits=project_params,
            takes=(8 if number == 2 else 0.1) if turn == 0 else 0.1,
        )

    early, late = (w_query, w_key), (w_value,)
    fetched = call(
        partial(fetch_kernel, 1),
        pltpu.VMEM((2, half, width // 2), jnp.bfloat16),
        place,
        *(stay(weight) for weight in early),
        scratch=[pltpu.SemaphoreType.DMA((2, 4))],
        hbm=2,
    )
    *merged, early_part = call(
        opening_kernel,
        (*buffers(rows + block.shape[1]), low(2, 2 * rows, width // 2)),
        place,
        fetched,
        grads_other,
        stay(hidden),
        hidden_other,
        stay(d_attended),
        stay(assign),
        scratch=[
            pltpu.VMEM((2 * rows, half), jnp.bfloat16),
            pltpu.VMEM(assign.shape, jnp.int32),
            pltpu.SemaphoreType.DMA((2,)),
            pltpu.SemaphoreType.DMA((chips + 1,)),
        ],
        hbm=4,
        takes=0.1,
    )
    grads = exchange(merged)
    early_arrived = to_sibling(early_part)
    early_projected = project(0, early, hidden_other, early_arrived)
    packed = exchange(early_projected)
    late_tokens, *_ = lax.optimization_barrier((hidden_other, early_arrived))
    late_arrived = to_sibling(project(1, late, late_tokens))
    late_arrived, *_ = lax.optimization_barrier((late_arrived, grads[2], grads[3]))
    late_projected = project(0, late, late_tokens, late_arrived)
    valued = exchange(late_projected)
    packed = lax.optimization_barrier((*packed, late_projected[0]))[:chips]

    def held(kind):
        return pltpu.VMEM((tokens, head_dim), kind)

    id_scratch = [pltpu.VMEM((count, 8, rows), jnp.float32), held(jnp.float32)]
    *value_grads, probs, sums = call(
        partial(value_grad_kernel, factor, chips, rows),
        (
            *buffers(2 * rows),
            pltpu.VMEM((count * (count + 1) // 2 * rows, rows), jnp.bfloat16),
            low(clusters, head_dim),
        ),
        place,
        *packed,
        *grads,
        cluster_rank.reshape(1, clusters),
        scratch=[held(jnp.bfloat16)] * 3 + id_scratch + [held(jnp.float32)],
        takes=7,
    )
    value_back = exchange(value_grads)
    results = call(
        partial(query_grad_kernel, scale, chips, rows),
        (*buffers(4 * rows), *(low(chips, rows + owned, head_dim),) * 2),
        place,
        *packed,
        *valued,
        *grads,
        probs,
        sums,
        scratch=[held(jnp.bfloat16)] * 4
        + [held(jnp.float32)]
        + [held(jnp.bfloat16)] * 2,
        takes=10,
    )
    *ready, _ = lax.optimization_barrier((*results[:chips], value_back[2]))
    back = exchange(ready)

    attended_mine, attended_theirs = results[chips:]
    outputs = call(
        merge_kernel, buffers(2 * (rows + owned)), place, attended_mine, to_sibling(attended_theirs)
    )
    early_back, _ = lax.optimization_barrier((back[2], outputs[0]))
    back_other = tuple(
        to_sibling(early_back if offset == 2 else part) for offset, part in enumerate(back)
    )
    value_other = to_sibling(
        call(join_kernel, low(chips, 2 * rows, head_dim), place, *value_back)
    )

    def input_part(which, place):
        return call(
            partial(input_kernel, chips, which),
            low(rows, half),
            place,
            *back,
            *back_other,
            *value_back,
            value_other,
            w_query,
            w_key,
            w_value,
            scratch=[pltpu.VMEM((rows, 3 * width), jnp.bfloat16)],
        )

    *outputs, _, _ = lax.optimization_barrier((*outputs, back[2], back[3]))
    returned = exchange(outputs)
    square = ("head", "sub")
    crossing = input_part(3, place)
    first = lax.ppermute(crossing, square, [(0, 1), (1, 3), (3, 2), (2, 0)])
    kept = input_part(2, lax.optimization_barrier((place, crossing))[0])
    second = lax.ppermute(kept, square, [(1, 2), (2, 1)])
    attended, centroid_sums = call(
        partial(attended_kernel, chips),
        (low(rows, width), jax.ShapeDtypeStruct((count, owned, head_dim), jnp.float32)),
        place,
        *returned,
        takes=8,
    )
    first, second, _ = lax.optimization_barrier((first, second, attended))
    d_hidden = call(sum_kernel, low(rows, half), place, first, second, kept)
    return (attended, d_hidden, centroid_sums)


def per_device(hidden, w_query, w_key, w_value, cluster_rank, assign, d_attended):
    chips = lax.axis_size("seq")
    fits = chips == 4 and lax.axis_size("sub") == 2 and lax.axis_size("head") == 2
    plan = by_head if fits and assign.shape[0] == 2 * chips else by_owner
    return plan(hidden, w_query, w_key, w_value, cluster_rank, assign, d_attended)


def solution(mesh):
    placed = (
        P(("groups", "seq", "sub"), None),
        P("sub", "head"),
        P("sub", "head"),
        P("sub", "head"),
        P("groups"),
        P("head", ("groups", "seq", "sub")),
        P(("groups", "seq", "sub"), "head"),
    )
    return jax.shard_map(
        per_device,
        mesh=mesh,
        in_specs=placed,
        out_specs=(
            P(("groups", "seq", "sub"), "head"),
            P(("groups", "seq", "sub"), "head"),
            P("head", ("groups", "seq", "sub"), None),
        ),
        check_vma=False,
    )
```

```python
from functools import partial

import jax
import jax.numpy as jnp
from jax import lax
from jax.experimental import pallas as pl
from jax.experimental.pallas import tpu as pltpu
from jax.sharding import PartitionSpec as P

epsilon = 1e-06


def keep_mask(filled, cluster_ids, positions):
    count = filled.shape[0]
    same = filled[:, None] & filled[None, :] & (cluster_ids[:, None] == cluster_ids[None, :])
    causal = positions[None, :] <= positions[:, None]
    diagonal = jnp.arange(count)[:, None] == jnp.arange(count)[None, :]
    return same & causal | diagonal


def head_forward(packed, scale):
    queries, keys_in, values, filled, cluster_ids, positions = packed
    scores = (
        lax.dot_general(
            queries, keys_in, (((1,), (1,)), ((), ())), preferred_element_type=jnp.float32
        )
        * scale
    )
    allowed = keep_mask(filled, cluster_ids, positions)
    row_top = jnp.max(jnp.where(allowed, scores, -jnp.inf), axis=1)
    expd = jnp.where(allowed, jnp.exp(scores - row_top[:, None]), 0.0)
    row_total = jnp.sum(expd, axis=1)
    probs_low = (expd / row_total[:, None]).astype(jnp.bfloat16)
    outputs = jnp.dot(probs_low, values, preferred_element_type=jnp.float32).astype(jnp.bfloat16)
    return (outputs, row_top, row_total)


def head_backward(packed, scale):
    queries, keys_in, values, grads_in, filled, cluster_ids, positions, row_top, row_total = packed
    contract_last = (((1,), (1,)), ((), ()))
    contract_first = (((0,), (0,)), ((), ()))
    scores = (
        lax.dot_general(queries, keys_in, contract_last, preferred_element_type=jnp.float32) * scale
    )
    allowed = keep_mask(filled, cluster_ids, positions)
    probs = jnp.where(allowed, jnp.exp(scores - row_top[:, None]), 0.0) / row_total[:, None]
    probs_low = probs.astype(jnp.bfloat16)
    grad_probs = lax.dot_general(
        grads_in, values, contract_last, preferred_element_type=jnp.float32
    )
    delta_rows = jnp.sum(probs * grad_probs, axis=1)
    grad_low = (probs * (grad_probs - delta_rows[:, None]) * scale).astype(jnp.bfloat16)
    grad_query = jnp.dot(grad_low, keys_in, preferred_element_type=jnp.float32).astype(jnp.bfloat16)
    grad_key = lax.dot_general(
        grad_low, queries, contract_first, preferred_element_type=jnp.float32
    ).astype(jnp.bfloat16)
    grad_value = lax.dot_general(
        probs_low, grads_in, contract_first, preferred_element_type=jnp.float32
    ).astype(jnp.bfloat16)
    return (grad_query, grad_key, grad_value)


def by_owner(hidden, w_query, w_key, w_value, cluster_rank, assign, d_attended):
    tok_rows = hidden.shape[0]
    heads_here = assign.shape[0]
    head_dim = w_query.shape[1] // heads_here
    clusters = cluster_rank.shape[0]
    seq_count = lax.axis_size("seq")
    sub_count = lax.axis_size("sub")
    owners = seq_count * sub_count
    capacity = 2 * tok_rows // owners
    slot_count = owners * capacity
    per_owner = clusters // owners
    scale = head_dim ** (-0.5)
    pieces = (
        lax.all_gather(w_query, "sub", axis=0, tiled=True),
        lax.all_gather(w_key, "sub", axis=0, tiled=True),
        lax.all_gather(w_value, "sub", axis=0, tiled=True),
    )
    projected = tuple(
        (
            jnp.dot(hidden, weight_piece, preferred_element_type=jnp.float32)
            for weight_piece in pieces
        )
    )

    def split_heads(matrix):
        return (
            matrix.astype(jnp.bfloat16).reshape(tok_rows, heads_here, head_dim).transpose(1, 0, 2)
        )

    queries, keys_all, values = tuple((split_heads(matrix) for matrix in projected))
    cluster_range = jnp.arange(clusters, dtype=jnp.int32)
    rank_tok = jnp.sum(jnp.where(assign[:, :, None] == cluster_range, cluster_rank, 0), axis=2)
    owner_ids = rank_tok // per_owner
    owner_hot = (owner_ids[:, :, None] == jnp.arange(owners, dtype=jnp.int32)).astype(jnp.int32)
    within = jnp.sum(owner_hot * (jnp.cumsum(owner_hot, axis=1) - 1), axis=2)
    slot_tok = owner_ids * capacity + within
    token_ids = jnp.arange(tok_rows, dtype=jnp.int32)
    slot_range = jnp.arange(slot_count, dtype=jnp.int32)
    slot_match = slot_tok[:, None, :] == slot_range[None, :, None]
    slot_hot = slot_match.astype(jnp.bfloat16)

    def to_slots(rows_in):
        kept = jnp.einsum(
            "hst,htd->hsd", slot_hot, rows_in, preferred_element_type=jnp.float32
        ).astype(jnp.bfloat16)
        return kept.reshape(heads_here, owners, capacity, head_dim)

    def from_slots(slotted):
        flat_slots = slotted.reshape(heads_here, slot_count, head_dim)
        return jnp.einsum(
            "hst,hsd->htd", slot_hot, flat_slots, preferred_element_type=jnp.float32
        ).astype(jnp.bfloat16)

    def exchange_three(first, second, third):
        return (
            lax.all_to_all(first, ("seq", "sub"), split_axis=1, concat_axis=1, tiled=True),
            lax.all_to_all(second, ("seq", "sub"), split_axis=1, concat_axis=1, tiled=True),
            lax.all_to_all(third, ("seq", "sub"), split_axis=1, concat_axis=1, tiled=True),
        )

    sent = exchange_three(to_slots(queries), to_slots(keys_all), to_slots(values))
    tag_tok = assign * tok_rows + token_ids
    slot_tag = jnp.sum(jnp.where(slot_match, tag_tok[:, None, :] + 1, 0), axis=2) - 1
    tags = lax.all_to_all(
        slot_tag.reshape(heads_here, owners, capacity),
        ("seq", "sub"),
        split_axis=1,
        concat_axis=1,
        tiled=True,
    )
    tags = tags.reshape(heads_here, slot_count)
    owner_q, owner_k, owner_v = tuple(
        (member.reshape(heads_here, slot_count, head_dim) for member in sent)
    )
    filled = tags >= 0
    cluster_ids = jnp.where(filled, tags // tok_rows, -1)
    positions = slot_range // capacity * tok_rows + tags % tok_rows
    outputs, row_top, row_total = lax.map(
        partial(head_forward, scale=scale),
        (owner_q, owner_k, owner_v, filled, cluster_ids, positions),
    )
    returned = lax.all_to_all(
        outputs.reshape(heads_here, owners, capacity, head_dim),
        ("seq", "sub"),
        split_axis=1,
        concat_axis=1,
        tiled=True,
    )

    def merge_heads(slotted):
        return from_slots(slotted).transpose(1, 0, 2).reshape(tok_rows, heads_here * head_dim)

    attended = merge_heads(returned)
    grads_tok = d_attended.reshape(tok_rows, heads_here, head_dim).transpose(1, 0, 2)
    owner_g = lax.all_to_all(
        to_slots(grads_tok), ("seq", "sub"), split_axis=1, concat_axis=1, tiled=True
    ).reshape(heads_here, slot_count, head_dim)
    grad_q, grad_k, grad_v = lax.map(
        partial(head_backward, scale=scale),
        (owner_q, owner_k, owner_v, owner_g, filled, cluster_ids, positions, row_top, row_total),
    )
    shape_four = (heads_here, owners, capacity, head_dim)
    back = exchange_three(
        grad_q.reshape(shape_four), grad_k.reshape(shape_four), grad_v.reshape(shape_four)
    )
    token_grads = tuple((merge_heads(member) for member in back))
    pieces = lax.all_gather((w_query, w_key, w_value), "sub", axis=0, tiled=True)
    terms = [
        jnp.einsum("tc,rc->tr", grad_rows_in, weight_piece, preferred_element_type=jnp.float32)
        for grad_rows_in, weight_piece in zip(token_grads, pieces)
    ]
    partial_grad = terms[0] + terms[1] + terms[2]
    d_hidden = lax.psum_scatter(
        partial_grad.astype(jnp.bfloat16), "head", scatter_dimension=1, tiled=True
    )
    keys_float = keys_all.astype(jnp.float32)
    unit_keys = keys_float * lax.rsqrt(
        jnp.sum(keys_float * keys_float, axis=2, keepdims=True) + epsilon
    )
    member_hot = (rank_tok[:, :, None] == cluster_range).astype(jnp.float32)
    local_sums = jnp.einsum("htr,htd->hrd", member_hot, unit_keys, precision=lax.Precision.HIGHEST)
    centroid_sums = lax.psum_scatter(
        local_sums.astype(jnp.bfloat16), ("seq", "sub"), scatter_dimension=1, tiled=True
    ).astype(jnp.float32)
    return (attended, d_hidden, centroid_sums)


contract_last = (((1,), (1,)), ((), ()))
contract_first = (((0,), (0,)), ((), ()))
log2_e = 1.4426950408889634
mebi = 1024 * 1024


def id_lines(rows, head_dim):
    return -(-(rows // head_dim) // 16) * 16


def id_tile(side, ids, spare):
    head_dim = 128 if ids.shape[1] % 128 == 0 else ids.shape[1]
    lines = [ids[:, at : at + head_dim] for at in range(0, ids.shape[1], head_dim)]
    gap = [jnp.zeros((len(lines), head_dim), jnp.float32)]
    rest = [jnp.zeros((spare - len(lines), head_dim), jnp.float32)]
    first = jnp.concatenate(lines + gap + rest, axis=0)
    second = jnp.concatenate(gap + lines + rest, axis=0)
    return jnp.where(side == 0, first, second).astype(jnp.bfloat16)


def pack_kernel(place_ref, grads_ref, assign_ref, theirs_ref, ids_ref, sems):
    chips, padded, head_dim = theirs_ref.shape
    rows = grads_ref.shape[0]
    spare = padded - rows - rows // head_dim
    copies = [pltpu.make_async_copy(assign_ref, ids_ref, sems.at[chips])]
    for chip in range(chips):
        head = (1 - place_ref[1]) * chips + chip
        at = pl.multiple_of(head * head_dim, head_dim)
        copies.append(
            pltpu.make_async_copy(
                grads_ref.at[:, pl.ds(at, head_dim)],
                theirs_ref.at[chip, pl.ds(0, rows)],
                sems.at[chip],
            )
        )
    for copy in copies:
        copy.start()
    copies[0].wait()
    for chip in range(chips):
        head = (1 - place_ref[1]) * chips + chip
        ids = ids_ref[pl.ds(head, 1), :].astype(jnp.float32)
        theirs_ref[chip, rows:, :] = id_tile(place_ref[1], ids, spare)
    for copy in copies[1:]:
        copy.wait()


def merge_kernel(place_ref, mine_ref, theirs_ref, *out_refs):
    height = mine_ref.shape[1]
    for turn, held_ref in enumerate((mine_ref, theirs_ref)):
        at = pl.ds(pl.multiple_of((place_ref[1] ^ turn) * height, height), height)
        for offset, out_ref in enumerate(out_refs):
            out_ref[at, :] = held_ref[place_ref[0] ^ offset]


def fetch_columns(half, weights, held_ref, sems):
    chunks = sems.shape[1]
    columns = held_ref.shape[2]
    rows = held_ref.shape[1] // chunks
    at = pl.ds(pl.multiple_of(half * columns, columns), columns)
    copies = []
    for index, weight in enumerate(weights):
        for chunk in range(chunks):
            lines = pl.ds(chunk * rows, rows)
            copy = pltpu.make_async_copy(
                weight.at[lines, at], held_ref.at[index, lines], sems.at[index, chunk]
            )
            copy.start()
            copies.append(copy)
    return copies


def project_kernel(count, turn, place_ref, *refs):
    if turn == 0:
        arrived_ref, refs = refs[0], refs[1:]
    tokens, weights, refs = refs[:2], refs[2 : 2 + count], refs[2 + count :]
    out_refs, (joined_ref, held_ref, low_ref, sems, token_sems) = refs[:-5], refs[-5:]
    side = place_ref[1]
    tall, depth = joined_ref.shape
    rows = tall // 2
    near = pl.ds(pl.multiple_of(side * depth, depth), depth)
    joins = []
    for core, source in enumerate(tokens):
        at = pl.ds(pl.multiple_of((side ^ core) * rows, rows), rows)
        joins.append(
            pltpu.make_async_copy(source.at[:, near], joined_ref.at[at], token_sems.at[core])
        )
        joins[core].start()
    copies = fetch_columns(side ^ turn, weights, held_ref, sems)
    for copy in joins:
        copy.wait()
    chunks = sems.shape[1]
    for index in range(count):
        for chunk in range(chunks):
            copies[index * chunks + chunk].wait()
        total = jnp.dot(joined_ref[...], held_ref[index], preferred_element_type=jnp.float32)
        if turn == 1:
            out_refs[0][index] = total.astype(jnp.bfloat16)
            continue
        low_ref[...] = (total + arrived_ref[index].astype(jnp.float32)).astype(jnp.bfloat16)
        for offset, out_ref in enumerate(out_refs):
            head_dim = out_ref.shape[1]
            at = pl.multiple_of((place_ref[0] ^ offset) * head_dim, head_dim)
            out_ref[index * tall : (index + 1) * tall, :] = low_ref[:, pl.ds(at, head_dim)]


def fetch_kernel(turn, place_ref, *refs):
    weights, (held_ref, sems) = refs[:-2], refs[-2:]
    for copy in fetch_columns(place_ref[1] ^ turn, weights, held_ref, sems):
        copy.wait()


def opening_kernel(place_ref, held_ref, theirs_ref, *refs):
    tokens, (grads_ref, assign_ref), refs = refs[:2], refs[2:4], refs[4:]
    out_refs, (part_ref, joined_ref, ids_ref, sems, grad_sems) = refs[:-5], refs[-5:]
    side = place_ref[1]
    chips = len(out_refs)
    tall, depth = joined_ref.shape
    rows = tall // 2
    head_dim = out_refs[0].shape[1]
    near = pl.ds(pl.multiple_of(side * depth, depth), depth)
    joins = []
    for core, source in enumerate(tokens):
        at = pl.ds(pl.multiple_of((side ^ core) * rows, rows), rows)
        joins.append(pltpu.make_async_copy(source.at[:, near], joined_ref.at[at], sems.at[core]))
        joins[core].start()
    copies = [pltpu.make_async_copy(assign_ref, ids_ref, grad_sems.at[chips])]
    mine = pl.ds(pl.multiple_of(side * rows, rows), rows)
    other = pl.ds(pl.multiple_of((1 - side) * rows, rows), rows)
    for offset, out_ref in enumerate(out_refs):
        head = side * chips + (place_ref[0] ^ offset)
        at = pl.multiple_of(head * head_dim, head_dim)
        copies.append(
            pltpu.make_async_copy(
                grads_ref.at[:, pl.ds(at, head_dim)], out_ref.at[mine], grad_sems.at[offset]
            )
        )
    for copy in copies:
        copy.start()
    copies[0].wait()
    for offset, out_ref in enumerate(out_refs):
        chip = place_ref[0] ^ offset
        ids = ids_ref[pl.ds(side * chips + chip, 1), :].astype(jnp.float32)
        spare = theirs_ref.shape[1] - rows - rows // head_dim
        out_ref[other, :] = theirs_ref[chip, :rows, :]
        out_ref[tall:, :] = theirs_ref[chip, rows:, :] + id_tile(side, ids, spare)
    for copy in joins:
        copy.wait()
    for index in range(held_ref.shape[0]):
        total = jnp.dot(joined_ref[...], held_ref[index], preferred_element_type=jnp.float32)
        part_ref[index] = total.astype(jnp.bfloat16)
    for copy in copies[1:]:
        copy.wait()


def in_order(place, parts, start, ordered):
    for offset, part in enumerate(parts):
        tall = ordered.shape[0] // len(parts)
        at = pl.ds(pl.multiple_of((place ^ offset) * tall, tall), tall)
        ordered[at, :] = part[start : start + tall, :]


def order_grads(place, parts, rows, grad_rows, id_rows, id_cols):
    head_dim = grad_rows.shape[1]
    count = rows // head_dim
    for offset, part in enumerate(parts):
        lines = part[2 * rows :, :].astype(jnp.float32)
        for core in range(2):
            block = (place ^ offset) * 2 + core
            at = pl.ds(pl.multiple_of(block * rows, rows), rows)
            grad_rows[at, :] = part[core * rows : (core + 1) * rows, :]
            first = core * count
            ids = jnp.concatenate(
                [lines[line : line + 1, :] for line in range(first, first + count)], axis=1
            )
            id_rows[block] = jnp.broadcast_to(ids, id_rows.shape[1:])
            id_cols[at, :] = jnp.broadcast_to(ids, (head_dim, rows)).T


def order_rows(place, parts, rows, ordered):
    for offset, part in enumerate(parts):
        at = pl.ds(pl.multiple_of((place ^ offset) * 2 * rows, 2 * rows), 2 * rows)
        ordered[at, :] = part[: 2 * rows, :]


def block_scores(factor, block, rows, queries, keys_in, id_rows, id_cols):
    head_dim = queries.shape[1]
    seen = (block + 1) * rows
    scores = lax.dot_general(
        keys_in[:seen, :],
        queries[block * rows : seen, :],
        contract_last,
        preferred_element_type=jnp.float32,
    )
    ids = id_cols[:seen, :]
    mine = id_rows[block][:1, :]
    same = jnp.concatenate(
        [ids == mine[:, start : start + head_dim] for start in range(0, rows, head_dim)], axis=1
    )
    key_at = lax.broadcasted_iota(jnp.int32, (rows, rows), 0)
    query_at = lax.broadcasted_iota(jnp.int32, (rows, rows), 1)
    last = same[seen - rows :] & (key_at <= query_at)
    allowed = last if block == 0 else jnp.concatenate([same[: seen - rows], last], axis=0)
    return jnp.where(allowed, scores * factor, -jnp.inf)


def value_grad_kernel(factor, chips, rows, place_ref, *refs):
    packed, grads, rank_ref = refs[:chips], refs[chips : 2 * chips], refs[2 * chips]
    refs = refs[2 * chips + 1 :]
    out_refs, probs_ref, sums_ref = refs[:chips], refs[chips], refs[chips + 1]
    queries, keys_in, grad_rows, id_rows, id_cols, total_ref = refs[chips + 2 :]
    head_dim = queries.shape[1]
    clusters = rank_ref.shape[1]
    tall = 2 * rows
    place = place_ref[0]
    in_order(place, packed, 0, queries)
    in_order(place, packed, tall, keys_in)
    order_grads(place, grads, rows, grad_rows, id_rows, id_cols)
    total_ref[...] = jnp.zeros_like(total_ref)
    stored = 0
    for block in range(2 * chips):
        seen = (block + 1) * rows
        scores = block_scores(factor, block, rows, queries, keys_in, id_rows, id_cols)
        top = jnp.max(scores, axis=0, keepdims=True)
        expd = jnp.exp2(scores - top)
        total = jnp.sum(expd, axis=0, keepdims=True)
        probs_low = (expd * (1.0 / total)).astype(jnp.bfloat16)
        probs_ref[stored : stored + seen, :] = probs_low
        stored += seen
        total_ref[:seen, :] += jnp.dot(
            probs_low, grad_rows[block * rows : seen, :], preferred_element_type=jnp.float32
        )
    for offset, out_ref in enumerate(out_refs):
        at = pl.multiple_of((place ^ offset) * tall, tall)
        out_ref[...] = total_ref[pl.ds(at, tall), :].astype(jnp.bfloat16)
    sums = jnp.zeros((clusters, head_dim), jnp.float32)
    cluster_at = lax.broadcasted_iota(jnp.int32, (clusters, rows), 0).astype(jnp.float32)
    for block in range(2 * chips):
        keys_float = keys_in[block * rows : (block + 1) * rows, :].astype(jnp.float32)
        unit = keys_float * lax.rsqrt(
            jnp.sum(keys_float * keys_float, axis=1, keepdims=True) + epsilon
        )
        unit_high = unit.astype(jnp.bfloat16)
        unit_low = (unit - unit_high.astype(jnp.float32)).astype(jnp.bfloat16)
        member = jnp.where(cluster_at == id_rows[block][:1, :], 1.0, 0.0).astype(jnp.bfloat16)
        sums += jnp.dot(member, unit_high, preferred_element_type=jnp.float32)
        sums += jnp.dot(member, unit_low, preferred_element_type=jnp.float32)
    rank_at = lax.broadcasted_iota(jnp.int32, (clusters, clusters), 0)
    ordered = jnp.where(rank_at == rank_ref[...], 1.0, 0.0).astype(jnp.bfloat16)
    ranked = jnp.dot(ordered, sums.astype(jnp.bfloat16), preferred_element_type=jnp.float32)
    sums_ref[...] = ranked.astype(jnp.bfloat16)


def query_grad_kernel(scale, chips, rows, place_ref, *refs):
    packed, valued, grads = refs[:chips], refs[chips : 2 * chips], refs[2 * chips : 3 * chips]
    probs_ref, sums_ref = refs[3 * chips : 3 * chips + 2]
    refs = refs[3 * chips + 2 :]
    grad_refs, out_refs, refs = refs[:chips], refs[chips : chips + 2], refs[chips + 2 :]
    queries, keys_in, values, grad_rows, total_ref, dq_ref, attended_ref = refs
    tall = 2 * rows
    place = place_ref[0]
    in_order(place, packed, 0, queries)
    in_order(place, packed, tall, keys_in)
    in_order(place, valued, 0, values)
    order_rows(place, grads, rows, grad_rows)
    total_ref[...] = jnp.zeros_like(total_ref)
    stored = 0
    for block in range(2 * chips):
        seen = (block + 1) * rows
        mine = slice(block * rows, seen)
        probs_low = probs_ref[stored : stored + seen, :]
        stored += seen
        seen_values = values[:seen, :]
        grad_probs = lax.dot_general(
            seen_values, grad_rows[mine, :], contract_last, preferred_element_type=jnp.float32
        )
        flipped = lax.dot_general(
            seen_values, probs_low, contract_first, preferred_element_type=jnp.float32
        )
        attended_ref[mine, :] = flipped.T.astype(jnp.bfloat16)
        probs = probs_low.astype(jnp.float32)
        weighted = probs * grad_probs
        delta = jnp.sum(weighted, axis=0, keepdims=True)
        grad_low = (weighted - probs * delta).astype(jnp.bfloat16)
        total_ref[:seen, :] += jnp.dot(
            grad_low, queries[mine, :], preferred_element_type=jnp.float32
        )
        flipped = lax.dot_general(
            keys_in[:seen, :], grad_low, contract_first, preferred_element_type=jnp.float32
        )
        dq_ref[mine, :] = (flipped.T * scale).astype(jnp.bfloat16)
    for offset in range(chips):
        at = pl.ds(pl.multiple_of((place ^ offset) * tall, tall), tall)
        grad_refs[offset][:tall, :] = dq_ref[at, :]
        grad_refs[offset][tall:, :] = (total_ref[at, :] * scale).astype(jnp.bfloat16)
    owned = sums_ref.shape[0] // (2 * chips)
    for turn, out_ref in enumerate(out_refs):
        for chip in range(chips):
            shard = chip * 2 + (place_ref[1] ^ turn)
            at = pl.ds(pl.multiple_of(shard * rows, rows), rows)
            out_ref[chip, :rows, :] = attended_ref[at, :]
            at = pl.ds(pl.multiple_of(shard * owned, owned), owned)
            out_ref[chip, rows:, :] = sums_ref[at, :]


def join_kernel(*refs):
    parts, out_ref = refs[1:-1], refs[-1]
    for offset, part in enumerate(parts):
        out_ref[offset] = part[...]


def input_kernel(chips, which, place_ref, *refs):
    valued_other_ref, refs = refs[3 * chips], refs[: 3 * chips] + refs[3 * chips + 1 :]
    weights, (out_ref, gathered_ref) = refs[3 * chips : -2], refs[-2:]
    rows, width = out_ref.shape[0], weights[0].shape[1]
    head_dim = width // (2 * chips)
    for turn in range(2):
        parts = refs[turn * chips : (turn + 1) * chips]
        valued = refs[2 * chips : 3 * chips]
        for offset in range(chips):
            head = (place_ref[1] ^ turn) * chips + (place_ref[0] ^ offset)
            for index in range(3):
                source = parts[offset] if index < 2 else valued[offset]
                if index == 2 and turn == 1:
                    source = valued_other_ref.at[offset]
                at = pl.multiple_of((2 * (index % 2) + place_ref[which]) * rows, rows)
                start = pl.multiple_of(index * width + head * head_dim, head_dim)
                gathered_ref[:, pl.ds(start, head_dim)] = source[pl.ds(at, rows), :]
    flipped = None
    for index in range(3):
        term = lax.dot_general(
            weights[index][...],
            gathered_ref[:, index * width : (index + 1) * width],
            contract_last,
            preferred_element_type=jnp.float32,
        )
        flipped = term if flipped is None else flipped + term
    out_ref[...] = flipped.T.astype(out_ref.dtype)


def attended_kernel(chips, place_ref, *refs):
    parts, (attended_ref, sums_ref) = refs[:chips], refs[chips:]
    rows = attended_ref.shape[0]
    head_dim = sums_ref.shape[2]
    height = parts[0].shape[0] // 2
    for core in range(2):
        start = core * height
        for offset, part in enumerate(parts):
            head = core * chips + (place_ref[0] ^ offset)
            at = pl.multiple_of(head * head_dim, head_dim)
            attended_ref[:, pl.ds(at, head_dim)] = part[start : start + rows, :]
            sums_ref[head] = part[start + rows : start + height, :].astype(jnp.float32)


def sum_kernel(place_ref, first_ref, second_ref, kept_ref, hidden_ref):
    keeps = place_ref[2] == place_ref[1]
    second = jnp.where(keeps, kept_ref[...], second_ref[...]).astype(jnp.float32)
    hidden_ref[...] = (first_ref[...].astype(jnp.float32) + second).astype(jnp.bfloat16)


def by_head(hidden, w_query, w_key, w_value, cluster_rank, assign, d_attended):
    rows = hidden.shape[0]
    count = assign.shape[0]
    chips = count // 2
    half, width = w_query.shape
    head_dim = width // count
    tokens = count * rows
    clusters = cluster_rank.shape[0]
    owned = clusters // count
    scale = head_dim ** (-0.5)
    factor = scale * log2_e
    smem = pl.BlockSpec(memory_space=pltpu.SMEM)
    vmem = pl.BlockSpec(memory_space=pltpu.VMEM)
    anywhere = pl.BlockSpec(memory_space=pl.ANY)
    params = pltpu.CompilerParams(vmem_limit_bytes=32 * mebi)
    project_params = pltpu.CompilerParams(vmem_limit_bytes=32 * mebi)
    swap = [(0, 1), (1, 0)]
    chip, side, column = (lax.axis_index(name) for name in ("seq", "sub", "head"))
    place = jnp.stack([chip, side, column, 1 - column])

    def call(kernel, outs, *operands, scratch=(), hbm=0, limits=params, takes=1):
        return pl.pallas_call(
            kernel,
            out_shape=outs,
            in_specs=[smem] + [vmem] * (len(operands) - 1 - hbm) + [anywhere] * hbm,
            out_specs=jax.tree.map(lambda _: vmem, outs),
            scratch_shapes=list(scratch),
            compiler_params=limits,
            cost_estimate=pl.CostEstimate(
                flops=int(takes * 1.15e9), bytes_accessed=mebi, transcendentals=0
            ),
        )(*operands)

    def low(*shape):
        return jax.ShapeDtypeStruct(shape, jnp.bfloat16)

    def buffers(height):
        return (low(height, head_dim),) * chips

    def exchange(parts):
        moved = {
            offset: lax.ppermute(parts[offset], "seq", [(at, at ^ offset) for at in range(chips)])
            for offset in (2, 3, 1)
        }
        return (parts[0], moved[1], moved[2], moved[3])

    def to_sibling(piece):
        return lax.ppermute(piece, "sub", swap)

    def stay(array):
        return pltpu.with_memory_space_constraint(array, pltpu.HBM)

    hidden_other = to_sibling(hidden)
    block = low(chips, rows + id_lines(2 * rows, head_dim), head_dim)
    grads_theirs = call(
        pack_kernel,
        block,
        place,
        stay(d_attended),
        stay(assign),
        scratch=[pltpu.VMEM(assign.shape, jnp.int32), pltpu.SemaphoreType.DMA((chips + 1,))],
        hbm=2,
    )
    grads_other = to_sibling(grads_theirs)

    def project(turn, weights, tokens_other, *arrived):
        number = len(weights)
        outs = buffers(2 * number * rows) if turn == 0 else low(number, 2 * rows, width // 2)

        return call(
            partial(project_kernel, number, turn),
            outs,
            place,
            *arrived,
            stay(hidden),
            tokens_other,
            *(stay(weight) for weight in weights),
            scratch=[
                pltpu.VMEM((2 * rows, half), jnp.bfloat16),
                pltpu.VMEM((number, half, width // 2), jnp.bfloat16),
                pltpu.VMEM((2 * rows, width // 2), jnp.bfloat16),
                pltpu.SemaphoreType.DMA((number, 8)),
                pltpu.SemaphoreType.DMA((2,)),
            ],
            hbm=2 + number,
            limits=project_params,
            takes=(8 if number == 2 else 0.1) if turn == 0 else 0.1,
        )

    early, late = (w_query, w_key), (w_value,)
    fetched = call(
        partial(fetch_kernel, 1),
        pltpu.VMEM((2, half, width // 2), jnp.bfloat16),
        place,
        *(stay(weight) for weight in early),
        scratch=[pltpu.SemaphoreType.DMA((2, 8))],
        hbm=2,
    )
    *merged, early_part = call(
        opening_kernel,
        (*buffers(rows + block.shape[1]), low(2, 2 * rows, width // 2)),
        place,
        fetched,
        grads_other,
        stay(hidden),
        hidden_other,
        stay(d_attended),
        stay(assign),
        scratch=[
            pltpu.VMEM((2 * rows, half), jnp.bfloat16),
            pltpu.VMEM(assign.shape, jnp.int32),
            pltpu.SemaphoreType.DMA((2,)),
            pltpu.SemaphoreType.DMA((chips + 1,)),
        ],
        hbm=4,
        takes=0.1,
    )
    grads = exchange(merged)
    early_arrived = to_sibling(early_part)
    early_projected = project(0, early, hidden_other, early_arrived)
    packed = exchange(early_projected)
    late_tokens, *_ = lax.optimization_barrier((hidden_other, early_arrived))
    late_arrived = to_sibling(project(1, late, late_tokens))
    late_arrived, *_ = lax.optimization_barrier((late_arrived, grads[2], grads[3]))
    late_projected = project(0, late, late_tokens, late_arrived)
    valued = exchange(late_projected)
    packed = lax.optimization_barrier((*packed, late_projected[0]))[:chips]

    def held(kind):
        return pltpu.VMEM((tokens, head_dim), kind)

    id_scratch = [pltpu.VMEM((count, 8, rows), jnp.float32), held(jnp.float32)]
    *value_grads, probs, sums = call(
        partial(value_grad_kernel, factor, chips, rows),
        (
            *buffers(2 * rows),
            pltpu.VMEM((count * (count + 1) // 2 * rows, rows), jnp.bfloat16),
            low(clusters, head_dim),
        ),
        place,
        *packed,
        *grads,
        cluster_rank.reshape(1, clusters),
        scratch=[held(jnp.bfloat16)] * 3 + id_scratch + [held(jnp.float32)],
        takes=7,
    )
    value_back = exchange(value_grads)
    results = call(
        partial(query_grad_kernel, scale, chips, rows),
        (*buffers(4 * rows), *(low(chips, rows + owned, head_dim),) * 2),
        place,
        *packed,
        *valued,
        *grads,
        probs,
        sums,
        scratch=[held(jnp.bfloat16)] * 4
        + [held(jnp.float32)]
        + [held(jnp.bfloat16)] * 2,
        takes=10,
    )
    *ready, _ = lax.optimization_barrier((*results[:chips], value_back[2]))
    back = exchange(ready)

    attended_mine, attended_theirs = results[chips:]
    outputs = call(
        merge_kernel, buffers(2 * (rows + owned)), place, attended_mine, to_sibling(attended_theirs)
    )
    early_back, _ = lax.optimization_barrier((back[2], outputs[0]))
    back_other = tuple(
        to_sibling(early_back if offset == 2 else part) for offset, part in enumerate(back)
    )
    value_other = to_sibling(
        call(join_kernel, low(chips, 2 * rows, head_dim), place, *value_back)
    )

    def input_part(which, place):
        return call(
            partial(input_kernel, chips, which),
            low(rows, half),
            place,
            *back,
            *back_other,
            *value_back,
            value_other,
            w_query,
            w_key,
            w_value,
            scratch=[pltpu.VMEM((rows, 3 * width), jnp.bfloat16)],
        )

    *outputs, _, _ = lax.optimization_barrier((*outputs, back[2], back[3]))
    returned = exchange(outputs)
    square = ("head", "sub")
    crossing = input_part(3, place)
    first = lax.ppermute(crossing, square, [(0, 1), (1, 3), (3, 2), (2, 0)])
    kept = input_part(2, lax.optimization_barrier((place, crossing))[0])
    second = lax.ppermute(kept, square, [(1, 2), (2, 1)])
    attended, centroid_sums = call(
        partial(attended_kernel, chips),
        (low(rows, width), jax.ShapeDtypeStruct((count, owned, head_dim), jnp.float32)),
        place,
        *returned,
        takes=8,
    )
    first, second, _ = lax.optimization_barrier((first, second, attended))
    d_hidden = call(sum_kernel, low(rows, half), place, first, second, kept)
    return (attended, d_hidden, centroid_sums)


def per_device(hidden, w_query, w_key, w_value, cluster_rank, assign, d_attended):
    chips = lax.axis_size("seq")
    fits = chips == 4 and lax.axis_size("sub") == 2 and lax.axis_size("head") == 2
    plan = by_head if fits and assign.shape[0] == 2 * chips else by_owner
    return plan(hidden, w_query, w_key, w_value, cluster_rank, assign, d_attended)


def solution(mesh):
    placed = (
        P(("groups", "seq", "sub"), None),
        P("sub", "head"),
        P("sub", "head"),
        P("sub", "head"),
        P("groups"),
        P("head", ("groups", "seq", "sub")),
        P(("groups", "seq", "sub"), "head"),
    )
    return jax.shard_map(
        per_device,
        mesh=mesh,
        in_specs=placed,
        out_specs=(
            P(("groups", "seq", "sub"), "head"),
            P(("groups", "seq", "sub"), "head"),
            P("head", ("groups", "seq", "sub"), None),
        ),
        check_vma=False,
    )
```
